32 devices in a mesh: seq: 8 (over z, x), head: 4 (over y, core).
Axes of the slice: x: 2, y: 2, z: 4, core: 2. Of those that a mesh axis runs over, the one named last changes fastest.
Arguments:
- query: bfloat16 [4096, 16, 128], P('seq', 'head'), may hold values from -6 to 6
- key: bfloat16 [4096, 16, 128], P('seq', 'head'), may hold values from -6 to 6
- value: bfloat16 [4096, 16, 128], P('seq', 'head'), may hold values from -1.5 to 1.5
- beta: float32 [16, 4096], P('head', 'seq'), may hold values from 0.1 to 2
- log_decay: float32 [16, 4096], P('head', 'seq')
- out_weight: bfloat16 [2048, 2048], P('head'), may hold values from -0.125 to 0.125
Outputs:
- mixed: bfloat16 [4096, 2048], P(('seq', 'head'))
The draws below stay inside these ranges and needn't reach their ends.
All inputs are finite; a program needn't handle non-finite values.
Results may differ from the reference program's by a relative error of at most 0.0075.
Values may be sent and summed in bfloat16 or wider, within the bound.
No kernel may reach another device: no remote copies, remote signals or barrier semaphores. Data moves between devices by JAX's collectives and lax.ppermute only.
A program may use at most 128 MiB of HBM per device.

```python
import math
import jax
import jax.numpy as jnp
from jax import lax

HEAD_TOTAL = 16
DK = 128
DV = 128
D = 2048
TOK_DEV = 512
SEQUENCE_TOKENS = 4096


def lasting_heads(key, lasting_count):
    order = jax.random.permutation(jax.random.fold_in(key, 7), HEAD_TOTAL)
    return order < lasting_count


def draw_beta(key, part):
    lasting = lasting_heads(key, HEAD_TOTAL // 2)
    key = jax.random.fold_in(key, 1)
    key_quick, key_lasting = jax.random.split(key)
    quick = jax.random.uniform(key_quick, (HEAD_TOTAL, SEQUENCE_TOKENS), jnp.float32, 0.1, 2.0)
    kept = 2.0 - jax.random.uniform(key_lasting, (HEAD_TOTAL, SEQUENCE_TOKENS), jnp.float32) * (32.0 / SEQUENCE_TOKENS)
    return jnp.where(lasting[:, None], kept, quick)


def draw_log_decay(key, part):
    lasting = lasting_heads(key, HEAD_TOTAL // 2)
    key = jax.random.fold_in(key, 2)
    random_subkeys = jax.random.split(key, 6)
    quick_rate = jnp.exp(jax.random.uniform(random_subkeys[0], (HEAD_TOTAL,), jnp.float32, math.log(1.0 / 50.0), math.log(1.0 / 30.0)))
    lasting_rate = jax.random.uniform(random_subkeys[1], (HEAD_TOTAL,), jnp.float32, 0.25, 0.5) / SEQUENCE_TOKENS
    baseline_rate = jnp.where(lasting, lasting_rate, quick_rate)
    jitter_level = jax.random.uniform(random_subkeys[2], (HEAD_TOTAL, SEQUENCE_TOKENS), jnp.float32, 0.5, 1.5)
    processor_factor = jnp.exp(jax.random.uniform(random_subkeys[3], (HEAD_TOTAL, SEQUENCE_TOKENS // TOK_DEV, 1), jnp.float32, math.log(0.5), math.log(2.0)))
    processor_factor = jnp.broadcast_to(processor_factor, (HEAD_TOTAL, SEQUENCE_TOKENS // TOK_DEV, TOK_DEV)).reshape(HEAD_TOTAL, SEQUENCE_TOKENS)
    spike_position = jax.random.randint(random_subkeys[4], (HEAD_TOTAL, 1, 2), 0, SEQUENCE_TOKENS)
    falloff_amount = jax.random.uniform(random_subkeys[5], (HEAD_TOTAL, 1, 2), jnp.float32, math.log(0.5), math.log(0.8))
    token_position = jnp.arange(SEQUENCE_TOKENS)[None, :, None]
    spike_events = jnp.sum(jnp.where(token_position == spike_position, falloff_amount, 0.0), axis=-1)
    return spike_events - baseline_rate[:, None] * jitter_level * processor_factor


def block_scale(stream_key, extent, cuts, least, high):
    factor_of = 1.0
    for dim, shards_of in cuts:
        steps = jax.random.uniform(jax.random.fold_in(jax.random.fold_in(stream_key, 6), dim), (shards_of,), jnp.float32, least / len(cuts), high / len(cuts))
        factor_of = factor_of * jnp.repeat(jnp.exp(steps), extent[dim] // shards_of).reshape((-1,) + (1,) * (len(extent) - 1 - dim))
    return factor_of


def bell_draw(rng, extent, spread, most, pieces=(), held_as=jnp.bfloat16):
    result = spread * jax.random.normal(rng, extent, jnp.float32)
    if pieces:
        result = result * block_scale(rng, extent, pieces, -0.22, 0.18)
    return jnp.clip(result, -most, most).astype(held_as)


def setup_inputs(seed: int = 0) -> dict:
    seeds = jax.random.split(jax.random.key(seed), 7)
    query = bell_draw(seeds[0], (SEQUENCE_TOKENS, HEAD_TOTAL, DK), 1.0, 6.0, ((0, 8), (1, 4)))
    key = bell_draw(seeds[1], (SEQUENCE_TOKENS, HEAD_TOTAL, DK), 1.0, 6.0, ((0, 8), (1, 4)))
    value = bell_draw(seeds[2], (SEQUENCE_TOKENS, HEAD_TOTAL, DV), (16.0 * SEQUENCE_TOKENS ** -0.5), 1.5, ((0, 8), (1, 4)))
    beta = draw_beta(jax.random.fold_in(seeds[6], 71), 0)
    log_decay = draw_log_decay(jax.random.fold_in(seeds[6], 71), 0)
    out_weight = bell_draw(seeds[5], (HEAD_TOTAL * DV, D), (HEAD_TOTAL * DV) ** -0.5, 0.125, ((0, 4),))
    return dict(query=query, key=key, value=value, beta=beta, log_decay=log_decay, out_weight=out_weight)


def unit_rows(tensor):
    widened = tensor.astype(jnp.float32)
    return widened * lax.rsqrt(lax.optimization_barrier(jnp.sum(widened * widened, axis=-1, keepdims=True)) + 1e-06)

def reference(query, key, value, beta, log_decay, out_weight):
    queries = unit_rows(query)
    keys_all = unit_rows(key)
    values_all = value.astype(jnp.float32)
    decays = jnp.exp(log_decay).T
    strengths = beta.T

    def advance_token(running_state, token_slice):
        query_current, key_current, value_t, strength_t, decay_t = token_slice
        retrieved_values = jnp.einsum('in,inc->ic', key_current, running_state, precision=lax.Precision.HIGHEST)
        erased = running_state - strength_t[:, None, None] * key_current[:, :, None] * retrieved_values[:, None, :]
        running_state = decay_t[:, None, None] * erased + strength_t[:, None, None] * key_current[:, :, None] * value_t[:, None, :]
        output_current = jnp.einsum('in,inc->ic', query_current, running_state, precision=lax.Precision.HIGHEST)
        return (running_state, output_current)
    initial = jnp.zeros((HEAD_TOTAL, DK, DV), jnp.float32)
    final_state, per_token = lax.scan(advance_token, initial, (queries, keys_all, values_all, strengths, decays))
    attended = per_token.reshape(SEQUENCE_TOKENS, HEAD_TOTAL * DV).astype(jnp.bfloat16)
    return jnp.dot(attended, out_weight, preferred_element_type=jnp.float32).astype(jnp.bfloat16)
```

```python
import functools

import jax
import jax.numpy as jnp
from jax import lax
from jax.experimental import pallas as pl
from jax.experimental.pallas import tpu as pltpu
from jax.sharding import PartitionSpec as P

C = 128
F32 = jnp.float32
BF16 = jnp.bfloat16
NN = (((1,), (0,)), ((), ()))
NT = (((1,), (1,)), ((), ()))
TN = (((0,), (0,)), ((), ()))
VMEM_LIMIT = 56 * 1024 * 1024


def dot(a, b, dims=NN):
    return lax.dot_general(a, b, dims, preferred_element_type=F32)


def split(x):
    high = x.astype(BF16)
    return high, (x - high.astype(F32)).astype(BF16)


def dot3(a, b, dims=NN):
    (ah, al), (bh, bl) = a, b
    return dot(ah, bh, dims) + (dot(al, bh, dims) + dot(ah, bl, dims))


def iotas():
    return (
        lax.broadcasted_iota(jnp.int32, (C, C), 0),
        lax.broadcasted_iota(jnp.int32, (C, C), 1),
    )


def to_column(row, eye):
    return jnp.sum(jnp.where(eye, row, 0.0), axis=1, keepdims=True)


def to_row(column, eye):
    return jnp.sum(jnp.where(eye, column, 0.0), axis=0, keepdims=True)


def head_row(ref, head, c):
    block = ref[:, c * C : (c + 1) * C]
    index = lax.broadcasted_iota(jnp.int32, block.shape, 0)
    return jnp.sum(jnp.where(index == head, block, 0.0), axis=0, keepdims=True)


def inverse_scale(rows):
    return lax.rsqrt(jnp.sum(rows * rows, axis=1, keepdims=True) + 1e-06)


def decay_parts(log_row, within, eye):
    column = jnp.sum(jnp.where(within, log_row, 0.0), axis=1, keepdims=True)
    row = to_row(column, eye)
    decay = jnp.where(within, jnp.exp(jnp.where(within, column - row, 0.0)), 0.0)
    return column, decay


def inverses(lowers, row, col):
    eye = jnp.where(row == col, 1.0, 0.0)
    found = [eye - jnp.where((row // 2) == (col // 2), a, 0.0) for a in lowers]
    parts = [split(a) for a in lowers]
    size = 2
    while size < C:
        mask = ((row // (2 * size)) == (col // (2 * size))) & ((row // size) != (col // size))
        zero = jnp.zeros((), BF16)
        blocks = [(jnp.where(mask, h, zero), jnp.where(mask, l, zero)) for h, l in parts]
        halves = [split(x) for x in found]
        middle = [split(dot3(a, x)) for a, x in zip(blocks, halves)]
        found = [x - dot3(h, y) for x, h, y in zip(found, halves, middle)]
        size *= 2
    return found


def local_kernel(heads, step_heads, k_ref, v_ref, beta_ref, log_ref, m_ref, ut_ref, wu_ref, n_ref, k32, v32):
    step = pl.program_id(0)
    chunks = beta_ref.shape[1] // C

    @pl.when(step == 0)
    def _():
        k32[...] = k_ref[...].astype(F32)
        v32[...] = v_ref[...].astype(F32)

    row, col = iotas()
    eye = row == col
    within = row >= col
    strict = row > col
    jobs = [(j, c) for j in range(step_heads) for c in range(chunks)]
    lowers, sides, fades, ends = [], [], [], []
    for j, c in jobs:
        head = step * step_heads + j
        rows = pl.ds(c * C * heads + head, C, stride=heads)
        raw = k32[rows, :]
        value = v32[rows, :]
        beta = to_column(head_row(beta_ref, head, c), eye)
        column, decay = decay_parts(head_row(log_ref, head, c), within, eye)
        scale = inverse_scale(raw)
        raw16 = raw.astype(BF16)
        gram = dot(raw16, raw16, NT)
        lowers.append(jnp.where(strict, gram * decay * (beta * scale) * to_row(scale, eye), 0.0))
        unit = raw * scale
        last = column[C - 1 : C, :]
        sides.append(jnp.concatenate([unit * (beta * jnp.exp(column)), value * beta], axis=1))
        fades.append(unit * jnp.exp(last - column))
        ends.append(jnp.exp(last))
    solved = [dot3(split(x), split(s)) for x, s in zip(inverses(lowers, row, col), sides)]
    maps = []
    for i, (j, c) in enumerate(jobs):
        wu_ref[j * chunks + c] = solved[i]
        both = dot3(split(fades[i]), split(solved[i]), TN)
        maps.append((jnp.where(eye, ends[i], 0.0) - both[:, :C], both[:, C:]))
    for j in range(step_heads):
        state = jnp.concatenate(maps[j * chunks], axis=1)
        for c in range(1, chunks):
            n_ref[j * chunks + c] = state
            moved, fresh = maps[j * chunks + c]
            state = dot3(split(moved), split(state))
            state = jnp.concatenate([state[:, :C], state[:, C:] + fresh], axis=1)
        m_ref[j] = state[:, :C].astype(m_ref.dtype)
        ut_ref[j] = state[:, C:].T.astype(ut_ref.dtype)


def local_maps(key, value, beta, log_decay, heads, step_heads):
    tokens = beta.shape[1]
    chunks = tokens // C
    whole = lambda shape: pl.BlockSpec(shape, lambda i: (0,) * len(shape))
    part = lambda shape: pl.BlockSpec(shape, lambda i: (i,) + (0,) * (len(shape) - 1))
    return pl.pallas_call(
        functools.partial(local_kernel, heads, step_heads),
        grid=(heads // step_heads,),
        in_specs=[
            whole((tokens * heads, C)),
            whole((tokens * heads, C)),
            whole((heads, tokens)),
            whole((heads, tokens)),
        ],
        out_specs=[
            part((step_heads, C, C)),
            part((step_heads, C, C)),
            part((step_heads * chunks, C, 2 * C)),
            part((step_heads * chunks, C, 2 * C)),
        ],
        out_shape=[
            jax.ShapeDtypeStruct((heads, C, C), BF16),
            jax.ShapeDtypeStruct((heads, C, C), BF16),
            jax.ShapeDtypeStruct((heads * chunks, C, 2 * C), F32),
            jax.ShapeDtypeStruct((heads * chunks, C, 2 * C), F32),
        ],
        scratch_shapes=[pltpu.VMEM((tokens * heads, C), F32), pltpu.VMEM((tokens * heads, C), F32)],
        compiler_params=pltpu.CompilerParams(vmem_limit_bytes=VMEM_LIMIT),
        name="local_maps",
    )(key, value, beta, log_decay)


def rows_kernel(heads, step_heads, q_ref, k_ref, log_ref, wu_ref, n_ref, out_ref, q32, k32):
    step = pl.program_id(0)
    chunks = log_ref.shape[1] // C

    @pl.when(step == 0)
    def _():
        q32[...] = q_ref[...].astype(F32)
        k32[...] = k_ref[...].astype(F32)

    row, col = iotas()
    eye = row == col
    within = row >= col
    for j in range(step_heads):
        head = step * step_heads + j
        for c in range(chunks):
            rows = pl.ds(c * C * heads + head, C, stride=heads)
            query, raw = q32[rows, :], k32[rows, :]
            column, decay = decay_parts(head_row(log_ref, head, c), within, eye)
            scale = inverse_scale(query)
            pairs = dot(query.astype(BF16), raw.astype(BF16), NT)
            pairs = pairs * decay * scale * to_row(inverse_scale(raw), eye)
            both = dot3(split(pairs), split(wu_ref[j * chunks + c]))
            reach = query * (scale * jnp.exp(column)) - both[:, :C]
            fresh = both[:, C:]
            if c > 0:
                earlier = dot3(split(reach), split(n_ref[j * chunks + c]))
                reach = earlier[:, :C]
                fresh = fresh + earlier[:, C:]
            out_ref[j, c * C : (c + 1) * C, :] = jnp.concatenate([reach, fresh], axis=1)


def row_maps(query, key, log_decay, wu, states, heads, step_heads):
    tokens = log_decay.shape[1]
    chunks = tokens // C
    whole = lambda shape: pl.BlockSpec(shape, lambda i: (0,) * len(shape))
    part = lambda shape: pl.BlockSpec(shape, lambda i: (i,) + (0,) * (len(shape) - 1))
    return pl.pallas_call(
        functools.partial(rows_kernel, heads, step_heads),
        grid=(heads // step_heads,),
        in_specs=[
            whole((tokens * heads, C)),
            whole((tokens * heads, C)),
            whole((heads, tokens)),
            part((step_heads * chunks, C, 2 * C)),
            part((step_heads * chunks, C, 2 * C)),
        ],
        out_specs=part((step_heads, tokens, 2 * C)),
        out_shape=jax.ShapeDtypeStruct((heads, tokens, 2 * C), F32),
        scratch_shapes=[pltpu.VMEM((tokens * heads, C), F32), pltpu.VMEM((tokens * heads, C), F32)],
        compiler_params=pltpu.CompilerParams(vmem_limit_bytes=VMEM_LIMIT),
        name="row_maps",
    )(query, key, log_decay, wu, states)


def chain_kernel(blocks, m_ref, ut_ref, out_ref):
    width = ut_ref.shape[1]
    state = jnp.zeros((width, C), F32)
    for d in range(blocks):
        out_ref[d] = state.astype(out_ref.dtype)
        if d + 1 < blocks:
            if d == 0:
                state = ut_ref[0].astype(F32)
            else:
                both = dot(jnp.concatenate(split(state), axis=0), m_ref[d], NT)
                state = both[:width] + both[width:] + ut_ref[d].astype(F32)


def chain(maps, adds):
    blocks, width = adds.shape[:2]
    return pl.pallas_call(
        functools.partial(chain_kernel, blocks),
        out_shape=jax.ShapeDtypeStruct((blocks, width, C), BF16),
        compiler_params=pltpu.CompilerParams(vmem_limit_bytes=VMEM_LIMIT),
        name="chain",
    )(maps, adds)


def apply_kernel(heads, rows_ref, st_ref, w_ref, out_ref):
    attended = []
    for h in range(heads):
        reach, fresh = rows_ref[h, :, :C], rows_ref[h, :, C:]
        high, low = split(reach)
        state = st_ref[h]
        attended.append((fresh + dot(high, state, NT) + dot(low, state, NT)).astype(BF16))
    out_ref[0] = dot(jnp.concatenate(attended, axis=1), w_ref[...]).astype(BF16)


def apply_and_project(rows, states_t, weight, groups):
    heads, tokens, _ = rows.shape
    block = tokens // groups
    depth, width = weight.shape
    return pl.pallas_call(
        functools.partial(apply_kernel, heads),
        grid=(groups,),
        in_specs=[
            pl.BlockSpec((heads, block, 2 * C), lambda i: (0, i, 0)),
            pl.BlockSpec((heads, C, C), lambda i: (0, 0, 0)),
            pl.BlockSpec((depth, width), lambda i: (0, 0)),
        ],
        out_specs=pl.BlockSpec((1, block, width), lambda i: (i, 0, 0)),
        out_shape=jax.ShapeDtypeStruct((groups, block, width), BF16),
        compiler_params=pltpu.CompilerParams(vmem_limit_bytes=VMEM_LIMIT),
        name="apply_and_project",
    )(rows, states_t, weight)


def body(query, key, value, beta, log_decay, out_weight):
    tokens, heads, _ = key.shape
    blocks = lax.axis_size("seq")
    groups = lax.axis_size("head")
    flat = lambda x: x.reshape(tokens * heads, C)
    q2, k2, v2 = flat(query), flat(key), flat(value)
    share = blocks // heads
    moved, added_t, wu, states = local_maps(k2, v2, beta, log_decay, heads, 1)
    send_m = jnp.broadcast_to(moved[:, None], (heads, share, C, C)).reshape(blocks, C, C)
    send_u = added_t.reshape(blocks, C // share, C)
    sent = lax.all_to_all(jnp.concatenate([send_m, send_u], axis=1), "seq", 0, 0, tiled=True)
    rows = row_maps(q2, k2, log_decay, wu, states, heads, 1)
    entering = chain(sent[:, :C], sent[:, C:])
    entering = lax.all_to_all(entering, "seq", 0, 0, tiled=True)
    parts = apply_and_project(rows, entering.reshape(heads, C, C), out_weight, groups)
    parts = lax.all_to_all(parts, "head", 0, 0, tiled=True)
    return jnp.sum(parts.astype(F32), axis=0).astype(BF16)


def solution(mesh):
    in_specs = (
        P("seq", "head", None),
        P("seq", "head", None),
        P("seq", "head", None),
        P("head", "seq"),
        P("head", "seq"),
        P("head", None),
    )
    out_specs = P(("seq", "head"), None)
    return jax.shard_map(body, mesh=mesh, in_specs=in_specs, out_specs=out_specs, check_vma=False)
```

```python
import functools

import jax
import jax.numpy as jnp
from jax import lax
from jax.experimental import pallas as pl
from jax.experimental.pallas import tpu as pltpu
from jax.sharding import PartitionSpec as P

C = 128
F32 = jnp.float32
BF16 = jnp.bfloat16
NN = (((1,), (0,)), ((), ()))
NT = (((1,), (1,)), ((), ()))
TN = (((0,), (0,)), ((), ()))
MIB = 1024 * 1024


def dot(a, b, dims=NN):
    return lax.dot_general(a, b, dims, preferred_element_type=F32)


def split(x):
    high = x.astype(BF16)
    return high, (x - high.astype(F32)).astype(BF16)


def dot3(a, b, dims=NN):
    (ah, al), (bh, bl) = a, b
    return dot(ah, bh, dims) + (dot(al, bh, dims) + dot(ah, bl, dims))


def iotas():
    return (
        lax.broadcasted_iota(jnp.int32, (C, C), 0),
        lax.broadcasted_iota(jnp.int32, (C, C), 1),
    )


def to_column(row, eye):
    return jnp.sum(jnp.where(eye, row, 0.0), axis=1, keepdims=True)


def to_row(column, eye):
    return jnp.sum(jnp.where(eye, column, 0.0), axis=0, keepdims=True)


def head_row(ref, head, c):
    block = ref[:, c * C : (c + 1) * C]
    index = lax.broadcasted_iota(jnp.int32, block.shape, 0)
    return jnp.sum(jnp.where(index == head, block, 0.0), axis=0, keepdims=True)


def inverse_scale(rows):
    return lax.rsqrt(jnp.sum(rows * rows, axis=1, keepdims=True) + 1e-06)


def decay_parts(log_row, within, eye):
    column = jnp.sum(jnp.where(within, log_row, 0.0), axis=1, keepdims=True)
    row = to_row(column, eye)
    decay = jnp.where(within, jnp.exp(jnp.where(within, column - row, 0.0)), 0.0)
    return column, decay


def inverses(lowers, row, col):
    eye = jnp.where(row == col, 1.0, 0.0)
    found = [eye - jnp.where((row // 2) == (col // 2), a, 0.0) for a in lowers]
    parts = [split(a) for a in lowers]
    size = 2
    while size < C:
        mask = ((row // (2 * size)) == (col // (2 * size))) & ((row // size) != (col // size))
        zero = jnp.zeros((), BF16)
        blocks = [(jnp.where(mask, h, zero), jnp.where(mask, l, zero)) for h, l in parts]
        halves = [split(x) for x in found]
        middle = [split(dot3(a, x)) for a, x in zip(blocks, halves)]
        found = [x - dot3(h, y) for x, h, y in zip(found, halves, middle)]
        size *= 2
    return found


def local_kernel(heads, step_heads, blocks, k_ref, v_ref, beta_ref, log_ref, wu_ref, n_ref, m_ref, ut_ref, *rest):
    sends, (k32, v32) = rest[:blocks], rest[blocks:]
    step = pl.program_id(0)
    chunks = beta_ref.shape[1] // C

    @pl.when(step == 0)
    def _():
        k32[...] = k_ref[...].astype(F32)
        v32[...] = v_ref[...].astype(F32)

    row, col = iotas()
    eye = row == col
    within = row >= col
    strict = row > col
    jobs = [(j, c) for j in range(step_heads) for c in range(chunks)]
    lowers, sides, fades, ends = [], [], [], []
    for j, c in jobs:
        head = step * step_heads + j
        rows = pl.ds(c * C * heads + head, C, stride=heads)
        raw = k32[rows, :]
        value = v32[rows, :]
        beta = to_column(head_row(beta_ref, head, c), eye)
        column, decay = decay_parts(head_row(log_ref, head, c), within, eye)
        scale = inverse_scale(raw)
        raw16 = raw.astype(BF16)
        gram = dot(raw16, raw16, NT)
        lowers.append(jnp.where(strict, gram * decay * (beta * scale) * to_row(scale, eye), 0.0))
        unit = raw * scale
        last = column[C - 1 : C, :]
        sides.append(jnp.concatenate([unit * (beta * jnp.exp(column)), value * beta], axis=1))
        fades.append(unit * jnp.exp(last - column))
        ends.append(jnp.exp(last))
    solved = [dot3(split(x), split(s)) for x, s in zip(inverses(lowers, row, col), sides)]
    maps = []
    for i, (j, c) in enumerate(jobs):
        wu_ref[j * chunks + c] = solved[i]
        both = dot3(split(fades[i]), split(solved[i]), TN)
        maps.append((jnp.where(eye, ends[i], 0.0) - both[:, :C], both[:, C:]))
    for j in range(step_heads):
        state = jnp.concatenate(maps[j * chunks], axis=1)
        for c in range(1, chunks):
            n_ref[j * chunks + c] = state
            moved, fresh = maps[j * chunks + c]
            state = dot3(split(moved), split(state))
            state = jnp.concatenate([state[:, :C], state[:, C:] + fresh], axis=1)
        m_ref[step * step_heads + j] = state[:, :C].astype(BF16)
        ut_ref[step * step_heads + j] = state[:, C:].T.astype(BF16)

    if not blocks:
        return

    @pl.when(step == heads // step_heads - 1)
    def _():
        share = blocks // heads
        width = C // share
        for r in range(blocks):
            target = lax.rem(lax.axis_index("seq") + blocks - r, blocks)
            head, piece = target // share, lax.rem(target, share)
            sends[r][:C, :] = m_ref[head]
            sends[r][C:, :] = ut_ref[head, pl.ds(pl.multiple_of(piece * width, width), width), :]


def local_maps(key, value, beta, log_decay, heads, step_heads, blocks):
    tokens = beta.shape[1]
    tall = C + C * heads // blocks if blocks else 0
    chunks = tokens // C
    whole = lambda shape: pl.BlockSpec(shape, lambda i: (0,) * len(shape))
    part = lambda shape: pl.BlockSpec(shape, lambda i: (i,) + (0,) * (len(shape) - 1))
    return pl.pallas_call(
        functools.partial(local_kernel, heads, step_heads, blocks),
        grid=(heads // step_heads,),
        in_specs=[
            whole((tokens * heads, C)),
            whole((tokens * heads, C)),
            whole((heads, tokens)),
            whole((heads, tokens)),
        ],
        out_specs=[
            part((step_heads * chunks, C, 2 * C)),
            part((step_heads * chunks, C, 2 * C)),
            whole((heads, C, C)),
            whole((heads, C, C)),
        ]
        + [whole((tall, C))] * blocks,
        out_shape=[
            jax.ShapeDtypeStruct((heads * chunks, C, 2 * C), F32),
            jax.ShapeDtypeStruct((heads * chunks, C, 2 * C), F32),
            jax.ShapeDtypeStruct((heads, C, C), BF16),
            jax.ShapeDtypeStruct((heads, C, C), BF16),
        ]
        + [jax.ShapeDtypeStruct((tall, C), BF16)] * blocks,
        scratch_shapes=[
            pltpu.VMEM((tokens * heads, C), F32),
            pltpu.VMEM((tokens * heads, C), F32),
        ],
        compiler_params=pltpu.CompilerParams(vmem_limit_bytes=24 * MIB),
        name="local_maps",
    )(key, value, beta, log_decay)


def rows_kernel(heads, step_heads, q_ref, k_ref, log_ref, wu_ref, n_ref, out_ref, q32, k32):
    step = pl.program_id(0)
    chunks = log_ref.shape[1] // C

    @pl.when(step == 0)
    def _():
        q32[...] = q_ref[...].astype(F32)
        k32[...] = k_ref[...].astype(F32)

    row, col = iotas()
    eye = row == col
    within = row >= col
    for j in range(step_heads):
        head = step * step_heads + j
        for c in range(chunks):
            rows = pl.ds(c * C * heads + head, C, stride=heads)
            query, raw = q32[rows, :], k32[rows, :]
            column, decay = decay_parts(head_row(log_ref, head, c), within, eye)
            scale = inverse_scale(query)
            pairs = dot(query.astype(BF16), raw.astype(BF16), NT)
            pairs = pairs * decay * scale * to_row(inverse_scale(raw), eye)
            both = dot3(split(pairs), split(wu_ref[j * chunks + c]))
            reach = query * (scale * jnp.exp(column)) - both[:, :C]
            fresh = both[:, C:]
            if c > 0:
                earlier = dot3(split(reach), split(n_ref[j * chunks + c]))
                reach = earlier[:, :C]
                fresh = fresh + earlier[:, C:]
            out_ref[j, c * C : (c + 1) * C, :] = jnp.concatenate([reach, fresh], axis=1)


def row_maps(query, key, log_decay, wu, states, heads, step_heads):
    tokens = log_decay.shape[1]
    chunks = tokens // C
    whole = lambda shape: pl.BlockSpec(shape, lambda i: (0,) * len(shape))
    part = lambda shape: pl.BlockSpec(shape, lambda i: (i,) + (0,) * (len(shape) - 1))
    return pl.pallas_call(
        functools.partial(rows_kernel, heads, step_heads),
        grid=(heads // step_heads,),
        in_specs=[
            whole((tokens * heads, C)),
            whole((tokens * heads, C)),
            whole((heads, tokens)),
            part((step_heads * chunks, C, 2 * C)),
            part((step_heads * chunks, C, 2 * C)),
        ],
        out_specs=part((step_heads, tokens, 2 * C)),
        out_shape=jax.ShapeDtypeStruct((heads, tokens, 2 * C), F32),
        scratch_shapes=[pltpu.VMEM((tokens * heads, C), F32), pltpu.VMEM((tokens * heads, C), F32)],
        compiler_params=pltpu.CompilerParams(vmem_limit_bytes=24 * MIB),
        cost_estimate=pl.CostEstimate(flops=4000000000, bytes_accessed=10000000, transcendentals=0),
        name="row_maps",
    )(query, key, log_decay, wu, states)


def chain_kernel(blocks, *refs):
    sends, outs, (held,) = refs[:blocks], refs[blocks : 2 * blocks], refs[2 * blocks :]
    me = lax.axis_index("seq")
    width = held.shape[1] - C
    for r in range(blocks):
        held[lax.rem(me + r, blocks)] = sends[r][...]
    state = jnp.zeros((width, C), F32)
    states = []
    for d in range(blocks):
        states.append(state)
        if d + 1 < blocks:
            added = held[d, C:, :].astype(F32)
            if d == 0:
                state = added
            else:
                both = dot(jnp.concatenate(split(state), axis=0), held[d, :C, :], NT)
                state = both[:width] + both[width:] + added
    for d in range(blocks):
        held[d, :width, :] = states[d].astype(BF16)
    for r in range(blocks):
        outs[r][...] = held[lax.rem(me + r, blocks), :width, :]


def chain(sent):
    blocks = len(sent)
    tall = sent[0].shape[0]
    return pl.pallas_call(
        functools.partial(chain_kernel, blocks),
        out_shape=[jax.ShapeDtypeStruct((tall - C, C), BF16)] * blocks,
        scratch_shapes=[pltpu.VMEM((blocks, tall, C), BF16)],
        compiler_params=pltpu.CompilerParams(vmem_limit_bytes=4 * MIB),
        name="chain",
    )(*sent)


def apply_kernel(heads, blocks, rows_ref, *refs):
    entering, (keep_ref, send_ref, st_ref) = refs[:blocks], refs[blocks:]
    step = pl.program_id(0)

    @pl.when(step == 0)
    def _():
        if blocks == 1:
            st_ref[...] = entering[0][...]
            return
        me = lax.axis_index("seq")
        share = blocks // heads
        width = C // share
        for r in range(blocks):
            source = lax.rem(me + blocks - r, blocks)
            place = pl.multiple_of(lax.rem(source, share) * width, width)
            st_ref[source // share, pl.ds(place, width), :] = entering[r][...]

    attended = []
    for h in range(heads):
        reach, fresh = rows_ref[h, :, :C], rows_ref[h, :, C:]
        high, low = split(reach)
        state = st_ref[h]
        attended.append((fresh + dot(high, state, NT) + dot(low, state, NT)).astype(BF16))
    attended = jnp.concatenate(attended, axis=1)
    mine = lax.rem(step, 2) == lax.rem(lax.axis_index("head"), 2)

    @pl.when(mine)
    def _():
        keep_ref[step // 2] = attended

    @pl.when(jnp.logical_not(mine))
    def _():
        send_ref[step // 2] = attended


def apply(rows, entering, groups):
    heads, tokens, _ = rows.shape
    block = tokens // groups
    blocks = len(entering)
    out = jax.ShapeDtypeStruct((groups // 2, block, heads * C), BF16)
    return pl.pallas_call(
        functools.partial(apply_kernel, heads, blocks),
        grid=(groups,),
        in_specs=[pl.BlockSpec((heads, block, 2 * C), lambda i: (0, i, 0))]
        + [pl.BlockSpec(x.shape, lambda i, n=x.ndim: (0,) * n) for x in entering],
        out_specs=[pl.BlockSpec(out.shape, lambda i: (0, 0, 0))] * 2,
        out_shape=[out, out],
        scratch_shapes=[pltpu.VMEM((heads, C, C), BF16)],
        compiler_params=pltpu.CompilerParams(vmem_limit_bytes=14 * MIB),
        name="apply",
    )(rows, *entering)


def project_kernel(other, keep_ref, got_ref, w_ref, w2_ref, out_ref):
    pair = lax.axis_index("head") // 2
    index = 1 - pair if other else pair
    out_ref[...] = (dot(keep_ref[index], w_ref[...]) + dot(got_ref[index], w2_ref[...])).astype(out_ref.dtype)


def project(other, keep, got, weight, weight2):
    _, block, depth = keep.shape
    width = weight.shape[1]
    return pl.pallas_call(
        functools.partial(project_kernel, other),
        out_shape=jax.ShapeDtypeStruct((block, width), BF16 if other else F32),
        compiler_params=pltpu.CompilerParams(vmem_limit_bytes=20 * MIB),
        cost_estimate=pl.CostEstimate(
            flops=4 * block * depth * width, bytes_accessed=4 * depth * width, transcendentals=0
        ),
        name="project",
    )(keep, got, weight, weight2)


def swap(x, axis, bit):
    count = lax.axis_size(axis)
    return lax.ppermute(x, axis, [(i, i ^ bit) for i in range(count)])


def shift(x, axis, amount):
    count = lax.axis_size(axis)
    return lax.ppermute(x, axis, [(i, (i + amount) % count) for i in range(count)])


def prefix(moved, added):
    me = lax.axis_index("seq")
    moved, added = lax.all_gather(moved, "seq"), lax.all_gather(added, "seq")

    def step(d, state):
        both = jnp.stack(split(state))
        both = jnp.einsum("phwk,hik->phwi", both, moved[d], preferred_element_type=F32)
        return jnp.where(d < me, both[0] + both[1] + added[d].astype(F32), state)

    start = jnp.zeros(added.shape[1:], F32)
    return lax.fori_loop(0, moved.shape[0] - 1, step, start).astype(BF16)


def body(query, key, value, beta, log_decay, out_weight):
    tokens, heads, _ = key.shape
    blocks = lax.axis_size("seq")
    groups = lax.axis_size("head")
    flat = lambda x: x.reshape(tokens * heads, C)
    q2, k2, v2 = flat(query), flat(key), flat(value)
    weight2 = swap(out_weight, "head", 1)
    direct = blocks % heads == 0 and C * heads // blocks >= 64
    wu, states, moved, added, *sends = local_maps(k2, v2, beta, log_decay, heads, 1, blocks if direct else 0)
    rows = row_maps(q2, k2, log_decay, wu, states, heads, 1)
    if direct:
        sent = [x if r == 0 else shift(x, "seq", -r) for r, x in enumerate(sends)]
        sent, rows = lax.optimization_barrier((sent, rows))
        entering = chain(sent)
        entering = [x if r == 0 else shift(x, "seq", r) for r, x in enumerate(entering)]
    else:
        entering = [prefix(moved, added)]
    keep, away = apply(rows, entering, groups)
    got = swap(away, "head", 1)
    theirs = swap(project(True, keep, got, out_weight, weight2), "head", 2)
    mine = project(False, keep, got, out_weight, weight2)
    return (mine + theirs.astype(F32)).astype(BF16)


def solution(mesh):
    in_specs = (
        P("seq", "head", None),
        P("seq", "head", None),
        P("seq", "head", None),
        P("head", "seq"),
        P("head", "seq"),
        P("head", None),
    )
    out_specs = P(("seq", "head"), None)
    return jax.shard_map(body, mesh=mesh, in_specs=in_specs, out_specs=out_specs, check_vma=False)
```

```python
import functools

import jax
import jax.numpy as jnp
from jax import lax
from jax.experimental import pallas as pl
from jax.experimental.pallas import tpu as pltpu
from jax.sharding import PartitionSpec as P

C = 128
B = 16
F32 = jnp.float32
BF16 = jnp.bfloat16
NN = (((1,), (0,)), ((), ()))
NT = (((1,), (1,)), ((), ()))
TN = (((0,), (0,)), ((), ()))
MIB = 1024 * 1024


def dot(a, b, dims=NN):
    return lax.dot_general(a, b, dims, preferred_element_type=F32)


def split(x):
    high = x.astype(BF16)
    return high, (x - high.astype(F32)).astype(BF16)


def twice(x):
    return jnp.concatenate([x, x], axis=0)


def dot3(a, b):
    (ah, al), (bh, bl) = a, b
    width = bh.shape[1]
    left = jnp.concatenate([ah, al], axis=1)
    if width > C:
        return dot(left, twice(bh)) + dot(ah, bl)
    both = dot(left, twice(jnp.concatenate([bh, bl], axis=1)))
    return both[:, :width] + both[:, width:]


def iotas():
    return (
        lax.broadcasted_iota(jnp.int32, (C, C), 0),
        lax.broadcasted_iota(jnp.int32, (C, C), 1),
    )


def to_column(row, eye):
    return jnp.sum(jnp.where(eye, row, 0.0), axis=1, keepdims=True)


def to_row(column, eye):
    return jnp.sum(jnp.where(eye, column, 0.0), axis=0, keepdims=True)


def head_row(ref, head, c):
    block = ref[:, c * C : (c + 1) * C]
    index = lax.broadcasted_iota(jnp.int32, block.shape, 0)
    return jnp.sum(jnp.where(index == head, block, 0.0), axis=0, keepdims=True)


def inverse_scale(rows):
    return lax.rsqrt(jnp.sum(rows * rows, axis=1, keepdims=True) + 1e-06)


def decay_parts(log_row, within, eye):
    column = jnp.sum(jnp.where(within, log_row, 0.0), axis=1, keepdims=True)
    row = to_row(column, eye)
    decay = jnp.where(within, jnp.exp(jnp.where(within, column - row, 0.0)), 0.0)
    return column, decay


def base_inverse(lower, row, col):
    on_block = (row // B) == (col // B)
    blocks = jnp.where(on_block, lower, 0.0)
    packed = sum(blocks[i * B : (i + 1) * B] for i in range(1, C // B)) + blocks[:B]
    r, c = row[:B], col[:B]
    found = jnp.where(r == c % B, 1.0, 0.0)
    first = (c // B) * B
    for j in range(B - 1):
        factor = jnp.take_along_axis(packed, first + j, axis=1)
        found = found - factor * found[j : j + 1]
    return jnp.where(on_block, jnp.concatenate([found] * (C // B), axis=0), 0.0)


def odd_rows(x, size):
    return jnp.concatenate([x[i : i + size] for i in range(size, C, 2 * size)], axis=0)


def weave(even, odd, size):
    parts = []
    for i in range(0, C // 2, size):
        parts += [even[i : i + size], odd[i : i + size]]
    return jnp.concatenate(parts, axis=0)


def even_rows(x, size):
    return jnp.concatenate([x[i : i + size] for i in range(0, C, 2 * size)], axis=0)


def inverses(lowers, row, col):
    found = [base_inverse(a, row, col) for a in lowers]
    parts = [split(a) for a in lowers]
    size = B
    while size < C:
        r, c = odd_rows(row, size), odd_rows(col, size)
        mask = ((r // (2 * size)) == (c // (2 * size))) & ((r // size) != (c // size))
        nothing = jnp.zeros((C // 2, C), BF16)
        joins = [tuple(jnp.where(mask, odd_rows(x, size), nothing) for x in part) for part in parts]
        halves = [split(x) for x in found]
        middle = [split(dot3(a, x)) for a, x in zip(joins, halves)]
        middle = [tuple(weave(nothing, x, size) for x in part) for part in middle]
        lows = [dot3(tuple(odd_rows(x, size) for x in h), y) for h, y in zip(halves, middle)]
        found = [weave(even_rows(x, size), odd_rows(x, size) - y, size) for x, y in zip(found, lows)]
        size *= 2
    return found


def local_kernel(heads, batch, blocks, k_hbm, v_hbm, beta_hbm, log_hbm, wu_ref, n_ref, m_ref, ut_ref, *rest):
    sends, (k16, v16, beta_ref, log_ref, k32, v32, sems) = rest[:blocks], rest[blocks:]
    pairs = ((k_hbm, k16), (log_hbm, log_ref), (beta_hbm, beta_ref), (v_hbm, v16))
    copies = [pltpu.make_async_copy(x, y, sems.at[i]) for i, (x, y) in enumerate(pairs)]
    for copy in copies:
        copy.start()
    for copy in copies:
        copy.wait()
    k32[...] = k16[...].astype(F32)
    v32[...] = v16[...].astype(F32)
    chunks = beta_ref.shape[1] // C
    row, col = iotas()
    eye = row == col
    within = row >= col
    strict = row > col
    for start in range(0, heads, batch):
        jobs = [(head, c) for head in range(start, start + batch) for c in range(chunks)]
        lowers, sides, fades, ends = [], [], [], []
        for head, c in jobs:
            rows = pl.ds(c * C * heads + head, C, stride=heads)
            raw = k32[rows, :]
            value = v32[rows, :]
            beta = to_column(beta_ref[head : head + 1, c * C : (c + 1) * C], eye)
            column, decay = decay_parts(log_ref[head : head + 1, c * C : (c + 1) * C], within, eye)
            scale = inverse_scale(raw)
            raw16 = raw.astype(BF16)
            gram = dot(raw16, raw16, NT)
            lowers.append(jnp.where(strict, gram * decay * (beta * scale) * to_row(scale, eye), 0.0))
            unit = raw * scale
            last = column[C - 1 : C, :]
            sides.append(jnp.concatenate([unit * (beta * jnp.exp(column)), value * beta], axis=1))
            fades.append((unit * jnp.exp(last - column)).T)
            ends.append(jnp.exp(last))
        solved = [dot3(split(x), split(s)) for x, s in zip(inverses(lowers, row, col), sides)]
        maps = []
        for i, (head, c) in enumerate(jobs):
            wu_ref[head * chunks + c] = solved[i]
            both = dot3(split(fades[i]), split(solved[i]))
            maps.append((jnp.where(eye, ends[i], 0.0) - both[:, :C], both[:, C:]))
        for j in range(batch):
            head = start + j
            state = jnp.concatenate(maps[j * chunks], axis=1)
            for c in range(1, chunks):
                n_ref[head * chunks + c] = state
                moved, fresh = maps[j * chunks + c]
                state = dot3(split(moved), split(state))
                state = jnp.concatenate([state[:, :C], state[:, C:] + fresh], axis=1)
            m_ref[head] = state[:, :C].astype(BF16)
            ut_ref[head] = state[:, C:].T.astype(BF16)
    if not blocks:
        return
    share = blocks // heads
    width = C // share
    for r in range(blocks):
        target = lax.rem(lax.axis_index("seq") + blocks - r, blocks)
        head, piece = target // share, lax.rem(target, share)
        sends[r][:C, :] = m_ref[head]
        sends[r][C:, :] = ut_ref[head, pl.ds(pl.multiple_of(piece * width, width), width), :]


def local_maps(key, value, beta, log_decay, heads, batch, blocks):
    tokens = beta.shape[1]
    tall = C + C * heads // blocks if blocks else 0
    chunks = tokens // C
    here = pl.BlockSpec(memory_space=pltpu.VMEM)
    return pl.pallas_call(
        functools.partial(local_kernel, heads, batch, blocks),
        in_specs=[pl.BlockSpec(memory_space=pltpu.HBM)] * 4,
        out_specs=[here] * (4 + blocks),
        out_shape=[
            jax.ShapeDtypeStruct((heads * chunks, C, 2 * C), F32),
            jax.ShapeDtypeStruct((heads * chunks, C, 2 * C), F32),
            jax.ShapeDtypeStruct((heads, C, C), BF16),
            jax.ShapeDtypeStruct((heads, C, C), BF16),
        ]
        + [jax.ShapeDtypeStruct((tall, C), BF16)] * blocks,
        scratch_shapes=[
            pltpu.VMEM((tokens * heads, C), BF16),
            pltpu.VMEM((tokens * heads, C), BF16),
            pltpu.VMEM((heads, tokens), F32),
            pltpu.VMEM((heads, tokens), F32),
            pltpu.VMEM((tokens * heads, C), F32),
            pltpu.VMEM((tokens * heads, C), F32),
            pltpu.SemaphoreType.DMA((4,)),
        ],
        compiler_params=pltpu.CompilerParams(vmem_limit_bytes=32 * MIB),
        name="local_maps",
    )(key, value, beta, log_decay)


def rows_kernel(heads, step_heads, q_ref, k_ref, log_ref, wu_ref, n_ref, out_ref, q32, k32):
    step = pl.program_id(0)
    chunks = log_ref.shape[1] // C

    @pl.when(step == 0)
    def _():
        q32[...] = q_ref[...].astype(F32)
        k32[...] = k_ref[...].astype(F32)

    row, col = iotas()
    eye = row == col
    within = row >= col
    for j in range(step_heads):
        head = step * step_heads + j
        for c in range(chunks):
            rows = pl.ds(c * C * heads + head, C, stride=heads)
            query, raw = q32[rows, :], k32[rows, :]
            column, decay = decay_parts(head_row(log_ref, head, c), within, eye)
            scale = inverse_scale(query)
            pairs = dot(query.astype(BF16), raw.astype(BF16), NT)
            pairs = pairs * decay * scale * to_row(inverse_scale(raw), eye)
            both = dot3(split(pairs), split(wu_ref[j * chunks + c]))
            reach = query * (scale * jnp.exp(column)) - both[:, :C]
            fresh = both[:, C:]
            if c > 0:
                earlier = dot3(split(reach), split(n_ref[j * chunks + c]))
                reach = earlier[:, :C]
                fresh = fresh + earlier[:, C:]
            out_ref[j, c * C : (c + 1) * C, :] = jnp.concatenate([reach, fresh], axis=1)


def row_maps(query, key, log_decay, wu, states, heads, step_heads):
    tokens = log_decay.shape[1]
    chunks = tokens // C
    whole = lambda shape: pl.BlockSpec(shape, lambda i: (0,) * len(shape))
    part = lambda shape: pl.BlockSpec(shape, lambda i: (i,) + (0,) * (len(shape) - 1))
    return pl.pallas_call(
        functools.partial(rows_kernel, heads, step_heads),
        grid=(heads // step_heads,),
        in_specs=[
            whole((tokens * heads, C)),
            whole((tokens * heads, C)),
            whole((heads, tokens)),
            part((step_heads * chunks, C, 2 * C)),
            part((step_heads * chunks, C, 2 * C)),
        ],
        out_specs=part((step_heads, tokens, 2 * C)),
        out_shape=jax.ShapeDtypeStruct((heads, tokens, 2 * C), F32),
        scratch_shapes=[pltpu.VMEM((tokens * heads, C), F32), pltpu.VMEM((tokens * heads, C), F32)],
        compiler_params=pltpu.CompilerParams(vmem_limit_bytes=24 * MIB),
        cost_estimate=pl.CostEstimate(flops=4000000000, bytes_accessed=10000000, transcendentals=0),
        name="row_maps",
    )(query, key, log_decay, wu, states)


def chain_kernel(blocks, *refs):
    sends, (out_ref, held) = refs[:blocks], refs[blocks:]
    me = lax.axis_index("seq")
    width = held.shape[1] - C
    for r in range(blocks):
        held[lax.rem(me + r, blocks)] = sends[r][...]
    state = jnp.zeros((width, C), F32)
    states = []
    for d in range(blocks):
        states.append(state)
        if d + 1 < blocks:
            added = held[d, C:, :].astype(F32)
            if d == 0:
                state = added
            else:
                both = dot(jnp.concatenate(split(state), axis=0), held[d, :C, :], NT)
                state = both[:width] + both[width:] + added
    for d in range(blocks):
        out_ref[d] = states[d].astype(BF16)


def chain(sent):
    blocks = len(sent)
    tall = sent[0].shape[0]
    return pl.pallas_call(
        functools.partial(chain_kernel, blocks),
        out_shape=jax.ShapeDtypeStruct((blocks, tall - C, C), BF16),
        scratch_shapes=[pltpu.VMEM((blocks, tall, C), BF16)],
        compiler_params=pltpu.CompilerParams(vmem_limit_bytes=4 * MIB),
        name="chain",
    )(*sent)


def apply_kernel(heads, rows_ref, st_ref, keep_ref, send_ref):
    step = pl.program_id(0)
    attended = []
    for h in range(heads):
        reach, fresh = rows_ref[h, :, :C], rows_ref[h, :, C:]
        high, low = split(reach)
        state = st_ref[h]
        attended.append((fresh + dot(high, state, NT) + dot(low, state, NT)).astype(BF16))
    attended = jnp.concatenate(attended, axis=1)
    mine = lax.rem(step, 2) == lax.rem(lax.axis_index("head"), 2)

    @pl.when(mine)
    def _():
        keep_ref[step // 2] = attended

    @pl.when(jnp.logical_not(mine))
    def _():
        send_ref[step // 2] = attended


def apply(rows, states_t, groups):
    heads, tokens, _ = rows.shape
    block = tokens // groups
    out = jax.ShapeDtypeStruct((groups // 2, block, heads * C), BF16)
    return pl.pallas_call(
        functools.partial(apply_kernel, heads),
        grid=(groups,),
        in_specs=[
            pl.BlockSpec((heads, block, 2 * C), lambda i: (0, i, 0)),
            pl.BlockSpec(states_t.shape, lambda i: (0, 0, 0)),
        ],
        out_specs=[pl.BlockSpec(out.shape, lambda i: (0, 0, 0))] * 2,
        out_shape=[out, out],
        compiler_params=pltpu.CompilerParams(vmem_limit_bytes=14 * MIB),
        name="apply",
    )(rows, states_t)


def project_kernel(other, keep_ref, got_ref, w_ref, w2_ref, out_ref):
    pair = lax.axis_index("head") // 2
    index = 1 - pair if other else pair
    out_ref[...] = (dot(keep_ref[index], w_ref[...]) + dot(got_ref[index], w2_ref[...])).astype(out_ref.dtype)


def project(other, keep, got, weight, weight2):
    _, block, depth = keep.shape
    width = weight.shape[1]
    return pl.pallas_call(
        functools.partial(project_kernel, other),
        out_shape=jax.ShapeDtypeStruct((block, width), BF16 if other else F32),
        compiler_params=pltpu.CompilerParams(vmem_limit_bytes=20 * MIB),
        cost_estimate=pl.CostEstimate(
            flops=4 * block * depth * width, bytes_accessed=4 * depth * width, transcendentals=0
        ),
        name="project",
    )(keep, got, weight, weight2)


def swap(x, axis, bit):
    count = lax.axis_size(axis)
    return lax.ppermute(x, axis, [(i, i ^ bit) for i in range(count)])


def shift(x, axis, amount):
    count = lax.axis_size(axis)
    return lax.ppermute(x, axis, [(i, (i + amount) % count) for i in range(count)])


def prefix(moved, added):
    me = lax.axis_index("seq")
    moved, added = lax.all_gather(moved, "seq"), lax.all_gather(added, "seq")

    def step(d, state):
        both = jnp.stack(split(state))
        both = jnp.einsum("phwk,hik->phwi", both, moved[d], preferred_element_type=F32)
        return jnp.where(d < me, both[0] + both[1] + added[d].astype(F32), state)

    start = jnp.zeros(added.shape[1:], F32)
    return lax.fori_loop(0, moved.shape[0] - 1, step, start).astype(BF16)


def body(query, key, value, beta, log_decay, out_weight):
    tokens, heads, _ = key.shape
    blocks = lax.axis_size("seq")
    groups = lax.axis_size("head")
    flat = lambda x: x.reshape(tokens * heads, C)
    q2, k2, v2 = flat(query), flat(key), flat(value)
    weight2 = swap(out_weight, "head", 1)
    direct = blocks % heads == 0 and C * heads // blocks >= 64
    wu, states, moved, added, *sends = local_maps(k2, v2, beta, log_decay, heads, 2, blocks if direct else 0)
    rows = row_maps(q2, k2, log_decay, wu, states, heads, 1)
    if direct:
        sent = [x if r == 0 else shift(x, "seq", -r) for r, x in enumerate(sends)]
        sent, rows = lax.optimization_barrier((sent, rows))
        entering = lax.all_to_all(chain(sent), "seq", 0, 0, tiled=True).reshape(heads, C, C)
    else:
        entering = prefix(moved, added)
    keep, away = apply(rows, entering, groups)
    got = swap(away, "head", 1)
    theirs = swap(project(True, keep, got, out_weight, weight2), "head", 2)
    mine = project(False, keep, got, out_weight, weight2)
    return (mine + theirs.astype(F32)).astype(BF16)


def solution(mesh):
    in_specs = (
        P("seq", "head", None),
        P("seq", "head", None),
        P("seq", "head", None),
        P("head", "seq"),
        P("head", "seq"),
        P("head", None),
    )
    out_specs = P(("seq", "head"), None)
    return jax.shard_map(body, mesh=mesh, in_specs=in_specs, out_specs=out_specs, check_vma=False)
```

```python
import functools

import jax
import jax.numpy as jnp
from jax import lax
from jax.experimental import pallas as pl
from jax.experimental.pallas import tpu as pltpu
from jax.sharding import PartitionSpec as P

C = 128
B = 16
F32 = jnp.float32
BF16 = jnp.bfloat16
NN = (((1,), (0,)), ((), ()))
NT = (((1,), (1,)), ((), ()))
TN = (((0,), (0,)), ((), ()))
MIB = 1024 * 1024


def dot(a, b, dims=NN):
    return lax.dot_general(a, b, dims, preferred_element_type=F32)


def split(x):
    high = x.astype(BF16)
    return high, (x - high.astype(F32)).astype(BF16)


def twice(x):
    return jnp.concatenate([x, x], axis=0)


def dot3(a, b):
    (ah, al), (bh, bl) = a, b
    width = bh.shape[1]
    left = jnp.concatenate([ah, al], axis=1)
    if width > C:
        return dot(left, twice(bh)) + dot(ah, bl)
    both = dot(left, twice(jnp.concatenate([bh, bl], axis=1)))
    return both[:, :width] + both[:, width:]


def iotas():
    return (
        lax.broadcasted_iota(jnp.int32, (C, C), 0),
        lax.broadcasted_iota(jnp.int32, (C, C), 1),
    )


def to_column(row, eye):
    return jnp.sum(jnp.where(eye, row, 0.0), axis=1, keepdims=True)


def to_row(column, eye):
    return jnp.sum(jnp.where(eye, column, 0.0), axis=0, keepdims=True)


def inverse_scale(rows):
    return lax.rsqrt(jnp.sum(rows * rows, axis=1, keepdims=True) + 1e-06)


def decay_parts(log_row, within, eye):
    column = jnp.sum(jnp.where(within, log_row, 0.0), axis=1, keepdims=True)
    row = to_row(column, eye)
    decay = jnp.where(within, jnp.exp(jnp.where(within, column - row, 0.0)), 0.0)
    return column, decay


def base_inverse(lower, row, col):
    on_block = (row // B) == (col // B)
    blocks = jnp.where(on_block, lower, 0.0)
    packed = sum(blocks[i * B : (i + 1) * B] for i in range(1, C // B)) + blocks[:B]
    r, c = row[:B], col[:B]
    found = jnp.where(r == c % B, 1.0, 0.0)
    first = (c // B) * B
    for j in range(B - 1):
        factor = jnp.take_along_axis(packed, first + j, axis=1)
        found = found - factor * found[j : j + 1]
    return jnp.where(on_block, jnp.concatenate([found] * (C // B), axis=0), 0.0)


def odd_rows(x, size):
    return jnp.concatenate([x[i : i + size] for i in range(size, C, 2 * size)], axis=0)


def weave(even, odd, size):
    parts = []
    for i in range(0, C // 2, size):
        parts += [even[i : i + size], odd[i : i + size]]
    return jnp.concatenate(parts, axis=0)


def even_rows(x, size):
    return jnp.concatenate([x[i : i + size] for i in range(0, C, 2 * size)], axis=0)


def inverses(lowers, row, col):
    found = [base_inverse(a, row, col) for a in lowers]
    parts = [split(a) for a in lowers]
    size = B
    while size < C:
        r, c = odd_rows(row, size), odd_rows(col, size)
        mask = ((r // (2 * size)) == (c // (2 * size))) & ((r // size) != (c // size))
        nothing = jnp.zeros((C // 2, C), BF16)
        joins = [tuple(jnp.where(mask, odd_rows(x, size), nothing) for x in part) for part in parts]
        halves = [split(x) for x in found]
        middle = [split(dot3(a, x)) for a, x in zip(joins, halves)]
        middle = [tuple(weave(nothing, x, size) for x in part) for part in middle]
        lows = [dot3(tuple(odd_rows(x, size) for x in h), y) for h, y in zip(halves, middle)]
        found = [weave(even_rows(x, size), odd_rows(x, size) - y, size) for x, y in zip(found, lows)]
        size *= 2
    return found


def first_heads(heads, phase):
    return (phase, phase + heads // 2)


def fetch(pairs, sems):
    copies = [pltpu.make_async_copy(x, y, sems.at[i]) for i, (x, y) in enumerate(pairs)]
    for copy in copies:
        copy.start()
    for copy in copies:
        copy.wait()


def in_hbm(*arrays):
    return [pltpu.with_memory_space_constraint(x, pltpu.HBM) for x in arrays]


def chunk_rows(heads, head, c):
    return pl.ds(c * C * heads + head, C, stride=heads)


def tokens_of(ref, head, c):
    return ref[head : head + 1, c * C : (c + 1) * C]


def local_body(heads, phase, k32, v32, beta_ref, log_ref, wu_ref, n_ref, own_ref, send_ref):
    chunks = beta_ref.shape[1] // C
    row, col = iotas()
    eye = row == col
    within = row >= col
    strict = row > col
    pair = first_heads(heads, phase)
    jobs = [(head, c) for head in pair for c in range(chunks)]
    lowers, sides, fades, ends = [], [], [], []
    for head, c in jobs:
        raw = k32[chunk_rows(heads, head, c), :]
        value = v32[chunk_rows(heads, head, c), :]
        beta = to_column(tokens_of(beta_ref, head, c), eye)
        column, decay = decay_parts(tokens_of(log_ref, head, c), within, eye)
        scale = inverse_scale(raw)
        raw16 = raw.astype(BF16)
        gram = dot(raw16, raw16, NT)
        lowers.append(jnp.where(strict, gram * decay * (beta * scale) * to_row(scale, eye), 0.0))
        unit = raw * scale
        last = column[C - 1 : C, :]
        sides.append(jnp.concatenate([unit * (beta * jnp.exp(column)), value * beta], axis=1))
        fades.append((unit * jnp.exp(last - column)).T)
        ends.append(jnp.exp(last))
    solved = [dot3(split(x), split(s)) for x, s in zip(inverses(lowers, row, col), sides)]
    maps = []
    for i in range(len(jobs)):
        wu_ref[i] = solved[i]
        both = dot3(split(fades[i]), split(solved[i]))
        maps.append((jnp.where(eye, ends[i], 0.0) - both[:, :C], both[:, C:]))
    totals = []
    for j in range(2):
        state = jnp.concatenate(maps[j * chunks], axis=1)
        for c in range(1, chunks):
            n_ref[j * chunks + c] = state
            moved, fresh = maps[j * chunks + c]
            state = dot3(split(moved), split(state))
            state = jnp.concatenate([state[:, :C], state[:, C:] + fresh], axis=1)
        totals.append(state)
    even = lax.rem(lax.axis_index("seq"), 2) == 0
    own_ref[...] = jnp.where(even, totals[0], totals[1])
    send_ref[...] = jnp.where(even, totals[1], totals[0]).astype(BF16)


def first_kernel(heads, k_hbm, v_hbm, beta_hbm, log_hbm, k32, v32, beta_ref, log_ref, wu, n, own, send, k16, v16, sems):
    fetch(((k_hbm, k16), (log_hbm, log_ref), (beta_hbm, beta_ref), (v_hbm, v16)), sems)
    k32[...] = k16[...].astype(F32)
    v32[...] = v16[...].astype(F32)
    local_body(heads, 0, k32, v32, beta_ref, log_ref, wu, n, own, send)


def local_shapes(tokens):
    chunks = tokens // C
    return [
        jax.ShapeDtypeStruct((2 * chunks, C, 2 * C), F32),
        jax.ShapeDtypeStruct((2 * chunks, C, 2 * C), F32),
        jax.ShapeDtypeStruct((C, 2 * C), F32),
        jax.ShapeDtypeStruct((C, 2 * C), BF16),
    ]


def first_maps(key, value, beta, log_decay):
    heads, tokens = beta.shape
    here = pl.BlockSpec(memory_space=pltpu.VMEM)
    wide = jax.ShapeDtypeStruct(key.shape, F32)
    small = jax.ShapeDtypeStruct(beta.shape, F32)
    return pl.pallas_call(
        functools.partial(first_kernel, heads),
        in_specs=[pl.BlockSpec(memory_space=pltpu.HBM)] * 4,
        out_specs=[here] * 8,
        out_shape=[wide, wide, small, small] + local_shapes(tokens),
        scratch_shapes=[
            pltpu.VMEM(key.shape, BF16),
            pltpu.VMEM(key.shape, BF16),
            pltpu.SemaphoreType.DMA((4,)),
        ],
        compiler_params=pltpu.CompilerParams(vmem_limit_bytes=24 * MIB),
        name="first_maps",
    )(*in_hbm(key, value, beta, log_decay))


def more_maps(phase, key, value, beta, log_decay):
    heads, tokens = beta.shape
    here = pl.BlockSpec(memory_space=pltpu.VMEM)
    return pl.pallas_call(
        functools.partial(local_body, heads, phase),
        in_specs=[here] * 4,
        out_specs=[here] * 4,
        out_shape=local_shapes(tokens),
        compiler_params=pltpu.CompilerParams(vmem_limit_bytes=24 * MIB),
        cost_estimate=pl.CostEstimate(flops=4000000000, bytes_accessed=10000000, transcendentals=0),
        name="more_maps",
    )(key, value, beta, log_decay)


def rows_kernel(heads, phase, q_hbm, k32, log_ref, wu_ref, n_ref, out_ref, q16, q32, sems):
    fetch(((q_hbm, q16),), sems)
    q32[...] = q16[...].astype(F32)
    chunks = log_ref.shape[1] // C
    row, col = iotas()
    eye = row == col
    within = row >= col
    for j, head in enumerate(first_heads(heads, phase)):
        for c in range(chunks):
            query, raw = q32[chunk_rows(heads, head, c), :], k32[chunk_rows(heads, head, c), :]
            column, decay = decay_parts(tokens_of(log_ref, head, c), within, eye)
            scale = inverse_scale(query)
            pairs = dot(query.astype(BF16), raw.astype(BF16), NT)
            pairs = pairs * decay * scale * to_row(inverse_scale(raw), eye)
            both = dot3(split(pairs), split(wu_ref[j * chunks + c]))
            reach = query * (scale * jnp.exp(column)) - both[:, :C]
            fresh = both[:, C:]
            if c > 0:
                earlier = dot3(split(reach), split(n_ref[j * chunks + c]))
                reach = earlier[:, :C]
                fresh = fresh + earlier[:, C:]
            out_ref[j, c * C : (c + 1) * C, :] = jnp.concatenate([reach, fresh], axis=1)


def row_maps(phase, query, k32, log_decay, wu, states):
    heads, tokens = log_decay.shape
    here = pl.BlockSpec(memory_space=pltpu.VMEM)
    return pl.pallas_call(
        functools.partial(rows_kernel, heads, phase),
        in_specs=[pl.BlockSpec(memory_space=pltpu.HBM)] + [here] * 4,
        out_specs=here,
        out_shape=jax.ShapeDtypeStruct((2, tokens, 2 * C), F32),
        scratch_shapes=[
            pltpu.VMEM(query.shape, BF16),
            pltpu.VMEM(query.shape, F32),
            pltpu.SemaphoreType.DMA((1,)),
        ],
        compiler_params=pltpu.CompilerParams(vmem_limit_bytes=16 * MIB),
        cost_estimate=pl.CostEstimate(flops=2000000000, bytes_accessed=8000000, transcendentals=0),
        name="row_maps",
    )(*in_hbm(query), k32, log_decay, wu, states)


def on_pairs(kernel, out_shape, *args):
    here = pl.BlockSpec(memory_space=pltpu.VMEM)
    return pl.pallas_call(
        kernel,
        in_specs=[here] * len(args),
        out_specs=[here] * len(out_shape),
        out_shape=out_shape,
        compiler_params=pltpu.CompilerParams(vmem_limit_bytes=8 * MIB),
        name=kernel.__name__,
    )(*args)


def pair_total(own0, own1, got0, got1, first_ref, total_ref, m_ref, u_ref):
    even = lax.rem(lax.axis_index("seq"), 2) == 0
    for i, (own_ref, got_ref) in enumerate(((own0, got0), (own1, got1))):
        own, got = own_ref[...], got_ref[...].astype(F32)
        first = jnp.where(even, own, got)
        second = jnp.where(even, got, own)
        first_ref[i] = first
        total = dot3(split(second[:, :C]), split(first))
        total = jnp.concatenate([total[:, :C], total[:, C:] + second[:, C:]], axis=1)
        total_ref[i] = total
        m_ref[i] = total[:, :C].astype(BF16)
        u_ref[i] = total[:, C:].astype(BF16)


def moved_on(maps, state16, added):
    high, low = split(maps)
    return dot(jnp.concatenate([high, low], axis=1), twice(state16)) + added


def next_state(total_ref, u_ref, out_ref):
    for i in range(total_ref.shape[0]):
        out_ref[i] = moved_on(total_ref[i, :, :C], u_ref[i], total_ref[i, :, C:]).astype(BF16)


def both_states(entering, first, i, keep_ref, send_ref):
    middle = moved_on(first[:, :C], entering, first[:, C:]).astype(BF16)
    even = lax.rem(lax.axis_index("seq"), 2) == 0
    keep_ref[i] = jnp.where(even, entering, middle)
    send_ref[i] = jnp.where(even, middle, entering)


def entering_of_four(first_ref, u_ref, m_ref, near_ref, far_ref, keep_ref, send_ref):
    place = lax.axis_index("seq") // 2
    for i in range(first_ref.shape[0]):
        last = (dot(m_ref[i], far_ref[i]) + u_ref[i].astype(F32)).astype(BF16)
        entering = jnp.where(place == 1, u_ref[i], jnp.where(place == 2, near_ref[i], last))
        entering = jnp.where(place == 0, jnp.zeros_like(entering), entering)
        both_states(entering, first_ref[i], i, keep_ref, send_ref)


def entering_given(first_ref, entering_ref, keep_ref, send_ref):
    for i in range(first_ref.shape[0]):
        both_states(entering_ref[i], first_ref[i], i, keep_ref, send_ref)


def prefix(maps, added):
    count = lax.axis_size("seq")
    groups = [list(range(i, count, 2)) for i in range(2)]
    me = lax.axis_index("seq") // 2
    maps, added = (lax.all_gather(x, "seq", axis_index_groups=groups) for x in (maps, added))

    def step(d, state):
        longer = jnp.einsum("hik,phkw->hiw", maps[d], jnp.stack(split(state)), preferred_element_type=F32)
        return jnp.where(d < me, longer + added[d].astype(F32), state)

    start = jnp.zeros(added.shape[1:], F32)
    return lax.fori_loop(0, count // 2 - 1, step, start).astype(BF16)


def apply_kernel(heads, rows0_ref, rows1_ref, keep_st, got_st, keep_ref, send_ref):
    step = pl.program_id(0)
    even = lax.rem(lax.axis_index("seq"), 2) == 0
    attended = []
    for h in range(heads):
        phase, side = h % 2, h // 2
        rows_ref = (rows0_ref, rows1_ref)[phase]
        reach, fresh = rows_ref[side, :, :C], rows_ref[side, :, C:]
        mine = even if side == 0 else jnp.logical_not(even)
        state = jnp.where(mine, keep_st[phase], got_st[phase])
        attended.append(moved_on(reach, state, fresh).astype(BF16))
    attended = jnp.concatenate(attended, axis=1)
    mine = lax.rem(step, 2) == lax.rem(lax.axis_index("head"), 2)

    @pl.when(mine)
    def _():
        keep_ref[step // 2] = attended

    @pl.when(jnp.logical_not(mine))
    def _():
        send_ref[step // 2] = attended


def apply(rows, keep_st, got_st, groups):
    _, tokens, _ = rows[0].shape
    heads = 2 * len(rows)
    block = tokens // groups
    out = jax.ShapeDtypeStruct((groups // 2, block, heads * C), BF16)
    states = pl.BlockSpec(keep_st.shape, lambda i: (0, 0, 0))
    return pl.pallas_call(
        functools.partial(apply_kernel, heads),
        grid=(groups,),
        in_specs=[pl.BlockSpec((2, block, 2 * C), lambda i: (0, i, 0))] * 2 + [states] * 2,
        out_specs=[pl.BlockSpec(out.shape, lambda i: (0, 0, 0))] * 2,
        out_shape=[out, out],
        compiler_params=pltpu.CompilerParams(vmem_limit_bytes=14 * MIB),
        name="apply",
    )(*rows, keep_st, got_st)


def project_kernel(other, keep_ref, got_ref, w_ref, w2_ref, out_ref):
    pair = lax.axis_index("head") // 2
    index = 1 - pair if other else pair
    out_ref[...] = (dot(keep_ref[index], w_ref[...]) + dot(got_ref[index], w2_ref[...])).astype(out_ref.dtype)


def project(other, keep, got, weight, weight2):
    _, block, depth = keep.shape
    width = weight.shape[1]
    return pl.pallas_call(
        functools.partial(project_kernel, other),
        out_shape=jax.ShapeDtypeStruct((block, width), BF16 if other else F32),
        compiler_params=pltpu.CompilerParams(vmem_limit_bytes=20 * MIB),
        cost_estimate=pl.CostEstimate(
            flops=4 * block * depth * width, bytes_accessed=4 * depth * width, transcendentals=0
        ),
        name="project",
    )(keep, got, weight, weight2)


def swap(x, axis, bit):
    count = lax.axis_size(axis)
    return lax.ppermute(x, axis, [(i, i ^ bit) for i in range(count)])


def body(query, key, value, beta, log_decay, out_weight):
    tokens, heads, _ = key.shape
    count = lax.axis_size("seq")
    flat = lambda x: x.reshape(tokens * heads, C)
    weight2 = swap(out_weight, "head", 1)
    k32, v32, beta, log_decay, wu0, n0, own0, send0 = first_maps(flat(key), flat(value), beta, log_decay)
    got0 = swap(send0, "seq", 1)
    wu1, n1, own1, send1 = more_maps(1, k32, v32, beta, log_decay)
    got1 = swap(send1, "seq", 1)
    rows = [row_maps(p, flat(query), k32, log_decay, *x) for p, x in enumerate(((wu0, n0), (wu1, n1)))]
    wide = jax.ShapeDtypeStruct((2, C, 2 * C), F32)
    square = jax.ShapeDtypeStruct((2, C, C), BF16)
    first, total, maps, added = on_pairs(pair_total, [wide, wide, square, square], own0, own1, got0, got1)
    if count == 8:
        added = swap(added, "seq", 2)
        maps = swap(maps, "seq", 2)
        (state,) = on_pairs(next_state, [square], total, added)
        near = lax.ppermute(state, "seq", [(2, 4), (3, 5)])
        far = lax.ppermute(state, "seq", [(2, 6), (3, 7)])
        keep, send = on_pairs(entering_of_four, [square, square], first, added, maps, near, far)
    else:
        keep, send = on_pairs(entering_given, [square, square], first, prefix(maps, added))
    got = swap(send, "seq", 1)
    keep, away = apply(rows, keep, got, lax.axis_size("head"))
    got = swap(away, "head", 1)
    theirs = swap(project(True, keep, got, out_weight, weight2), "head", 2)
    mine = project(False, keep, got, out_weight, weight2)
    return (mine + theirs.astype(F32)).astype(BF16)


def solution(mesh):
    in_specs = (
        P("seq", "head", None),
        P("seq", "head", None),
        P("seq", "head", None),
        P("head", "seq"),
        P("head", "seq"),
        P("head", None),
    )
    out_specs = P(("seq", "head"), None)
    return jax.shard_map(body, mesh=mesh, in_specs=in_specs, out_specs=out_specs, check_vma=False)
```

```python
import functools

import jax
import jax.numpy as jnp
from jax import lax
from jax.experimental import pallas as pl
from jax.experimental.pallas import tpu as pltpu
from jax.sharding import PartitionSpec as P

C = 128
B = 16
F32 = jnp.float32
BF16 = jnp.bfloat16
NN = (((1,), (0,)), ((), ()))
NT = (((1,), (1,)), ((), ()))
TN = (((0,), (0,)), ((), ()))
MIB = 1024 * 1024


def dot(a, b, dims=NN):
    return lax.dot_general(a, b, dims, preferred_element_type=F32)


def split(x):
    high = x.astype(BF16)
    return high, (x - high.astype(F32)).astype(BF16)


def twice(x):
    return jnp.concatenate([x, x], axis=0)


def dot3(a, b):
    (ah, al), (bh, bl) = a, b
    width = bh.shape[1]
    left = jnp.concatenate([ah, al], axis=1)
    if width > C:
        return dot(left, twice(bh)) + dot(ah, bl)
    both = dot(left, twice(jnp.concatenate([bh, bl], axis=1)))
    return both[:, :width] + both[:, width:]


def iotas():
    return (
        lax.broadcasted_iota(jnp.int32, (C, C), 0),
        lax.broadcasted_iota(jnp.int32, (C, C), 1),
    )


def to_column(row, eye):
    return jnp.sum(jnp.where(eye, row, 0.0), axis=1, keepdims=True)


def to_row(column, eye):
    return jnp.sum(jnp.where(eye, column, 0.0), axis=0, keepdims=True)


def inverse_scale(rows):
    return lax.rsqrt(jnp.sum(rows * rows, axis=1, keepdims=True) + 1e-06)


def decay_parts(log_row, within, eye):
    column = jnp.sum(jnp.where(within, log_row, 0.0), axis=1, keepdims=True)
    row = to_row(column, eye)
    decay = jnp.where(within, jnp.exp(jnp.where(within, column - row, 0.0)), 0.0)
    return column, decay


def base_inverse(lower, row, col):
    on_block = (row // B) == (col // B)
    blocks = jnp.where(on_block, lower, 0.0)
    packed = sum(blocks[i * B : (i + 1) * B] for i in range(1, C // B)) + blocks[:B]
    r, c = row[:B], col[:B]
    found = jnp.where(r == c % B, 1.0, 0.0)
    first = (c // B) * B
    for j in range(B - 1):
        factor = jnp.take_along_axis(packed, first + j, axis=1)
        found = found - factor * found[j : j + 1]
    return jnp.where(on_block, jnp.concatenate([found] * (C // B), axis=0), 0.0)


def odd_rows(x, size):
    return jnp.concatenate([x[i : i + size] for i in range(size, C, 2 * size)], axis=0)


def weave(even, odd, size):
    parts = []
    for i in range(0, C // 2, size):
        parts += [even[i : i + size], odd[i : i + size]]
    return jnp.concatenate(parts, axis=0)


def even_rows(x, size):
    return jnp.concatenate([x[i : i + size] for i in range(0, C, 2 * size)], axis=0)


def inverses(lowers, row, col):
    found = [base_inverse(a, row, col) for a in lowers]
    parts = [split(a) for a in lowers]
    size = B
    while size < C:
        r, c = odd_rows(row, size), odd_rows(col, size)
        mask = ((r // (2 * size)) == (c // (2 * size))) & ((r // size) != (c // size))
        nothing = jnp.zeros((C // 2, C), BF16)
        joins = [tuple(jnp.where(mask, odd_rows(x, size), nothing) for x in part) for part in parts]
        halves = [split(x) for x in found]
        middle = [split(dot3(a, x)) for a, x in zip(joins, halves)]
        middle = [tuple(weave(nothing, x, size) for x in part) for part in middle]
        lows = [dot3(tuple(odd_rows(x, size) for x in h), y) for h, y in zip(halves, middle)]
        found = [weave(even_rows(x, size), odd_rows(x, size) - y, size) for x, y in zip(found, lows)]
        size *= 2
    return found


def first_heads(heads, phase):
    return (phase, phase + heads // 2)


def fetch(pairs, sems):
    copies = [pltpu.make_async_copy(x, y, sems.at[i]) for i, (x, y) in enumerate(pairs)]
    for copy in copies:
        copy.start()
    for copy in copies:
        copy.wait()


def in_hbm(*arrays):
    return [pltpu.with_memory_space_constraint(x, pltpu.HBM) for x in arrays]


def chunk_rows(heads, head, c):
    return pl.ds(c * C * heads + head, C, stride=heads)


def tokens_of(ref, head, c):
    return ref[head : head + 1, c * C : (c + 1) * C]


def local_body(heads, phase, k32, v32, beta_ref, log_ref, wu_ref, n_ref, own_ref, send_ref):
    chunks = beta_ref.shape[1] // C
    row, col = iotas()
    eye = row == col
    within = row >= col
    strict = row > col
    pair = first_heads(heads, phase)
    jobs = [(head, c) for head in pair for c in range(chunks)]
    lowers, sides, fades, ends = [], [], [], []
    for head, c in jobs:
        raw = k32[chunk_rows(heads, head, c), :]
        value = v32[chunk_rows(heads, head, c), :]
        beta = to_column(tokens_of(beta_ref, head, c), eye)
        column, decay = decay_parts(tokens_of(log_ref, head, c), within, eye)
        scale = inverse_scale(raw)
        raw16 = raw.astype(BF16)
        gram = dot(raw16, raw16, NT)
        lowers.append(jnp.where(strict, gram * decay * (beta * scale) * to_row(scale, eye), 0.0))
        unit = raw * scale
        last = column[C - 1 : C, :]
        sides.append(jnp.concatenate([unit * (beta * jnp.exp(column)), value * beta], axis=1))
        fades.append((unit * jnp.exp(last - column)).T)
        ends.append(jnp.exp(last))
    solved = [dot3(split(x), split(s)) for x, s in zip(inverses(lowers, row, col), sides)]
    maps = []
    for i in range(len(jobs)):
        wu_ref[i] = solved[i]
        both = dot3(split(fades[i]), split(solved[i]))
        maps.append((jnp.where(eye, ends[i], 0.0) - both[:, :C], both[:, C:]))
    totals = []
    for j in range(2):
        state = jnp.concatenate(maps[j * chunks], axis=1)
        for c in range(1, chunks):
            n_ref[j * chunks + c] = state
            moved, fresh = maps[j * chunks + c]
            state = dot3(split(moved), split(state))
            state = jnp.concatenate([state[:, :C], state[:, C:] + fresh], axis=1)
        totals.append(state)
    even = lax.rem(lax.axis_index("seq"), 2) == 0
    own_ref[...] = jnp.where(even, totals[0], totals[1])
    send_ref[...] = jnp.where(even, totals[1], totals[0]).astype(BF16)


def first_kernel(heads, k_hbm, v_hbm, beta_hbm, log_hbm, k32, v32, beta_ref, log_ref, wu, n, own, send, k16, v16, sems):
    fetch(((k_hbm, k16), (log_hbm, log_ref), (beta_hbm, beta_ref), (v_hbm, v16)), sems)
    k32[...] = k16[...].astype(F32)
    v32[...] = v16[...].astype(F32)
    local_body(heads, 0, k32, v32, beta_ref, log_ref, wu, n, own, send)


def local_shapes(tokens):
    chunks = tokens // C
    return [
        jax.ShapeDtypeStruct((2 * chunks, C, 2 * C), F32),
        jax.ShapeDtypeStruct((2 * chunks, C, 2 * C), F32),
        jax.ShapeDtypeStruct((C, 2 * C), F32),
        jax.ShapeDtypeStruct((C, 2 * C), BF16),
    ]


def first_maps(key, value, beta, log_decay):
    heads, tokens = beta.shape
    here = pl.BlockSpec(memory_space=pltpu.VMEM)
    wide = jax.ShapeDtypeStruct(key.shape, F32)
    small = jax.ShapeDtypeStruct(beta.shape, F32)
    return pl.pallas_call(
        functools.partial(first_kernel, heads),
        in_specs=[pl.BlockSpec(memory_space=pltpu.HBM)] * 4,
        out_specs=[here] * 8,
        out_shape=[wide, wide, small, small] + local_shapes(tokens),
        scratch_shapes=[
            pltpu.VMEM(key.shape, BF16),
            pltpu.VMEM(key.shape, BF16),
            pltpu.SemaphoreType.DMA((4,)),
        ],
        compiler_params=pltpu.CompilerParams(vmem_limit_bytes=24 * MIB),
        name="first_maps",
    )(*in_hbm(key, value, beta, log_decay))


def more_maps(phase, key, value, beta, log_decay):
    heads, tokens = beta.shape
    here = pl.BlockSpec(memory_space=pltpu.VMEM)
    return pl.pallas_call(
        functools.partial(local_body, heads, phase),
        in_specs=[here] * 4,
        out_specs=[here] * 4,
        out_shape=local_shapes(tokens),
        compiler_params=pltpu.CompilerParams(vmem_limit_bytes=24 * MIB),
        cost_estimate=pl.CostEstimate(flops=4000000000, bytes_accessed=10000000, transcendentals=0),
        name="more_maps",
    )(key, value, beta, log_decay)


def rows_kernel(heads, phase, q_hbm, k32, log_ref, wu_ref, n_ref, out_ref, q16, q32, sems):
    fetch(((q_hbm, q16),), sems)
    q32[...] = q16[...].astype(F32)
    chunks = log_ref.shape[1] // C
    row, col = iotas()
    eye = row == col
    within = row >= col
    for j, head in enumerate(first_heads(heads, phase)):
        for c in range(chunks):
            query, raw = q32[chunk_rows(heads, head, c), :], k32[chunk_rows(heads, head, c), :]
            column, decay = decay_parts(tokens_of(log_ref, head, c), within, eye)
            scale = inverse_scale(query)
            pairs = dot(query.astype(BF16), raw.astype(BF16), NT)
            pairs = pairs * decay * scale * to_row(inverse_scale(raw), eye)
            both = dot3(split(pairs), split(wu_ref[j * chunks + c]))
            reach = query * (scale * jnp.exp(column)) - both[:, :C]
            fresh = both[:, C:]
            if c > 0:
                earlier = dot3(split(reach), split(n_ref[j * chunks + c]))
                reach = earlier[:, :C]
                fresh = fresh + earlier[:, C:]
            out_ref[j, c * C : (c + 1) * C, :] = jnp.concatenate([reach, fresh], axis=1)


def row_maps(phase, query, k32, log_decay, wu, states):
    heads, tokens = log_decay.shape
    here = pl.BlockSpec(memory_space=pltpu.VMEM)
    return pl.pallas_call(
        functools.partial(rows_kernel, heads, phase),
        in_specs=[pl.BlockSpec(memory_space=pltpu.HBM)] + [here] * 4,
        out_specs=here,
        out_shape=jax.ShapeDtypeStruct((2, tokens, 2 * C), F32),
        scratch_shapes=[
            pltpu.VMEM(query.shape, BF16),
            pltpu.VMEM(query.shape, F32),
            pltpu.SemaphoreType.DMA((1,)),
        ],
        compiler_params=pltpu.CompilerParams(vmem_limit_bytes=16 * MIB),
        cost_estimate=pl.CostEstimate(flops=2000000000, bytes_accessed=8000000, transcendentals=0),
        name="row_maps",
    )(*in_hbm(query), k32, log_decay, wu, states)


def on_pairs(kernel, out_shape, *args):
    here = pl.BlockSpec(memory_space=pltpu.VMEM)
    return pl.pallas_call(
        kernel,
        in_specs=[here] * len(args),
        out_specs=[here] * len(out_shape),
        out_shape=out_shape,
        compiler_params=pltpu.CompilerParams(vmem_limit_bytes=8 * MIB),
        name=kernel.__name__,
    )(*args)


def pair_total(own0, own1, got0, got1, first_ref, total_ref, send_ref):
    even = lax.rem(lax.axis_index("seq"), 2) == 0
    for i, (own_ref, got_ref) in enumerate(((own0, got0), (own1, got1))):
        own, got = own_ref[...], got_ref[...].astype(F32)
        first = jnp.where(even, own, got)
        second = jnp.where(even, got, own)
        first_ref[i] = first
        total = dot3(split(second[:, :C]), split(first))
        total = jnp.concatenate([total[:, :C], total[:, C:] + second[:, C:]], axis=1)
        total_ref[i] = total
        send_ref[i] = total.astype(BF16)


def moved_on(maps, state16, added):
    high, low = split(maps)
    return dot(jnp.concatenate([high, low], axis=1), twice(state16)) + added


def next_state(total_ref, got_ref, out_ref):
    even = lax.rem(lax.axis_index("seq") // 2, 2) == 0
    for i in range(total_ref.shape[0]):
        own, got = total_ref[i], got_ref[i]
        later = jnp.where(even, got.astype(F32), own)
        state = jnp.where(even, own[:, C:].astype(BF16), got[:, C:])
        out_ref[i] = moved_on(later[:, :C], state, later[:, C:]).astype(BF16)


def both_states(entering, first, i, keep_ref, send_ref):
    middle = moved_on(first[:, :C], entering, first[:, C:]).astype(BF16)
    even = lax.rem(lax.axis_index("seq"), 2) == 0
    keep_ref[i] = jnp.where(even, entering, middle)
    send_ref[i] = jnp.where(even, middle, entering)


def entering_of_four(first_ref, got_ref, lower_ref, keep_ref, send_ref):
    place = lax.axis_index("seq") // 2
    for i in range(first_ref.shape[0]):
        got, lower = got_ref[i], lower_ref[i]
        last = (dot(got[:, :C], lower) + got[:, C:].astype(F32)).astype(BF16)
        entering = jnp.where(place == 1, got[:, C:], jnp.where(place == 2, lower, last))
        entering = jnp.where(place == 0, jnp.zeros_like(entering), entering)
        both_states(entering, first_ref[i], i, keep_ref, send_ref)


def entering_given(first_ref, entering_ref, keep_ref, send_ref):
    for i in range(first_ref.shape[0]):
        both_states(entering_ref[i], first_ref[i], i, keep_ref, send_ref)


def prefix(totals):
    count = lax.axis_size("seq")
    groups = [list(range(i, count, 2)) for i in range(2)]
    me = lax.axis_index("seq") // 2
    totals = lax.all_gather(totals, "seq", axis_index_groups=groups)
    maps, added = totals[..., :C], totals[..., C:]

    def step(d, state):
        longer = jnp.einsum("hik,phkw->hiw", maps[d], jnp.stack(split(state)), preferred_element_type=F32)
        return jnp.where(d < me, longer + added[d].astype(F32), state)

    start = jnp.zeros(added.shape[1:], F32)
    return lax.fori_loop(0, count // 2 - 1, step, start).astype(BF16)


def apply_kernel(heads, rows0_ref, rows1_ref, keep_st, got_st, keep_ref, send_ref):
    step = pl.program_id(0)
    even = lax.rem(lax.axis_index("seq"), 2) == 0
    attended = []
    for h in range(heads):
        phase, side = h % 2, h // 2
        rows_ref = (rows0_ref, rows1_ref)[phase]
        reach, fresh = rows_ref[side, :, :C], rows_ref[side, :, C:]
        mine = even if side == 0 else jnp.logical_not(even)
        state = jnp.where(mine, keep_st[phase], got_st[phase])
        attended.append(moved_on(reach, state, fresh).astype(BF16))
    attended = jnp.concatenate(attended, axis=1)
    mine = lax.rem(step, 2) == lax.rem(lax.axis_index("head"), 2)

    @pl.when(mine)
    def _():
        keep_ref[step // 2] = attended

    @pl.when(jnp.logical_not(mine))
    def _():
        send_ref[step // 2] = attended


def apply(rows, keep_st, got_st, groups):
    _, tokens, _ = rows[0].shape
    heads = 2 * len(rows)
    block = tokens // groups
    out = jax.ShapeDtypeStruct((groups // 2, block, heads * C), BF16)
    states = pl.BlockSpec(keep_st.shape, lambda i: (0, 0, 0))
    return pl.pallas_call(
        functools.partial(apply_kernel, heads),
        grid=(groups,),
        in_specs=[pl.BlockSpec((2, block, 2 * C), lambda i: (0, i, 0))] * 2 + [states] * 2,
        out_specs=[pl.BlockSpec(out.shape, lambda i: (0, 0, 0))] * 2,
        out_shape=[out, out],
        compiler_params=pltpu.CompilerParams(vmem_limit_bytes=14 * MIB),
        name="apply",
    )(*rows, keep_st, got_st)


def project_kernel(other, keep_ref, got_ref, w_ref, w2_ref, out_ref):
    pair = lax.axis_index("head") // 2
    index = 1 - pair if other else pair
    out_ref[...] = (dot(keep_ref[index], w_ref[...]) + dot(got_ref[index], w2_ref[...])).astype(out_ref.dtype)


def project(other, keep, got, weight, weight2):
    _, block, depth = keep.shape
    width = weight.shape[1]
    return pl.pallas_call(
        functools.partial(project_kernel, other),
        out_shape=jax.ShapeDtypeStruct((block, width), BF16 if other else F32),
        compiler_params=pltpu.CompilerParams(vmem_limit_bytes=20 * MIB),
        cost_estimate=pl.CostEstimate(
            flops=4 * block * depth * width, bytes_accessed=4 * depth * width, transcendentals=0
        ),
        name="project",
    )(keep, got, weight, weight2)


def swap(x, axis, bit):
    count = lax.axis_size(axis)
    return lax.ppermute(x, axis, [(i, i ^ bit) for i in range(count)])


def body(query, key, value, beta, log_decay, out_weight):
    tokens, heads, _ = key.shape
    count = lax.axis_size("seq")
    flat = lambda x: x.reshape(tokens * heads, C)
    weight2 = swap(out_weight, "head", 1)
    k32, v32, beta, log_decay, wu0, n0, own0, send0 = first_maps(flat(key), flat(value), beta, log_decay)
    got0 = swap(send0, "seq", 1)
    wu1, n1, own1, send1 = more_maps(1, k32, v32, beta, log_decay)
    got1 = swap(send1, "seq", 1)
    wu0, got0 = lax.optimization_barrier((wu0, got0))
    rows0 = row_maps(0, flat(query), k32, log_decay, wu0, n0)
    rows1 = row_maps(1, flat(query), k32, log_decay, wu1, n1)
    rows0, got1 = lax.optimization_barrier((rows0, got1))
    wide = jax.ShapeDtypeStruct((2, C, 2 * C), F32)
    narrow = jax.ShapeDtypeStruct((2, C, 2 * C), BF16)
    square = jax.ShapeDtypeStruct((2, C, C), BF16)
    first, total, total16 = on_pairs(pair_total, [wide, wide, narrow], own0, own1, got0, got1)
    if count == 8:
        other = swap(total16, "seq", 2)
        (state,) = on_pairs(next_state, [square], total, other)
        lower = swap(state, "seq", 4)
        rows1, lower = lax.optimization_barrier((rows1, lower))
        keep, send = on_pairs(entering_of_four, [square, square], first, other, lower)
    else:
        keep, send = on_pairs(entering_given, [square, square], first, prefix(total16))
    got = swap(send, "seq", 1)
    keep, away = apply((rows0, rows1), keep, got, lax.axis_size("head"))
    got = swap(away, "head", 1)
    theirs = swap(project(True, keep, got, out_weight, weight2), "head", 2)
    mine = project(False, keep, got, out_weight, weight2)
    return (mine + theirs.astype(F32)).astype(BF16)


def solution(mesh):
    in_specs = (
        P("seq", "head", None),
        P("seq", "head", None),
        P("seq", "head", None),
        P("head", "seq"),
        P("head", "seq"),
        P("head", None),
    )
    out_specs = P(("seq", "head"), None)
    return jax.shard_map(body, mesh=mesh, in_specs=in_specs, out_specs=out_specs, check_vma=False)
```

```python
import functools

import jax
import jax.numpy as jnp
from jax import lax
from jax.experimental import pallas as pl
from jax.experimental.pallas import tpu as pltpu
from jax.sharding import PartitionSpec as P

C = 128
B = 16
F32 = jnp.float32
BF16 = jnp.bfloat16
NN = (((1,), (0,)), ((), ()))
NT = (((1,), (1,)), ((), ()))
TN = (((0,), (0,)), ((), ()))
MIB = 1024 * 1024


def dot(a, b, dims=NN):
    return lax.dot_general(a, b, dims, preferred_element_type=F32)


def split(x):
    high = x.astype(BF16)
    return high, (x - high.astype(F32)).astype(BF16)


def twice(x):
    return jnp.concatenate([x, x], axis=0)


def dot3(a, b):
    (ah, al), (bh, bl) = a, b
    width = bh.shape[1]
    left = jnp.concatenate([ah, al], axis=1)
    if width > C:
        return dot(left, twice(bh)) + dot(ah, bl)
    both = dot(left, twice(jnp.concatenate([bh, bl], axis=1)))
    return both[:, :width] + both[:, width:]


def iotas():
    return (
        lax.broadcasted_iota(jnp.int32, (C, C), 0),
        lax.broadcasted_iota(jnp.int32, (C, C), 1),
    )


def to_column(row, eye):
    return jnp.sum(jnp.where(eye, row, 0.0), axis=1, keepdims=True)


def to_row(column, eye):
    return jnp.sum(jnp.where(eye, column, 0.0), axis=0, keepdims=True)


def inverse_scale(rows):
    return lax.rsqrt(jnp.sum(rows * rows, axis=1, keepdims=True) + 1e-06)


def decay_parts(log_row, within, eye):
    column = jnp.sum(jnp.where(within, log_row, 0.0), axis=1, keepdims=True)
    row = to_row(column, eye)
    decay = jnp.where(within, jnp.exp(jnp.where(within, column - row, 0.0)), 0.0)
    return column, decay


def base_inverse(lower, row, col):
    on_block = (row // B) == (col // B)
    blocks = jnp.where(on_block, lower, 0.0)
    packed = sum(blocks[i * B : (i + 1) * B] for i in range(1, C // B)) + blocks[:B]
    r, c = row[:B], col[:B]
    found = jnp.where(r == c % B, 1.0, 0.0)
    first = (c // B) * B
    for j in range(B - 1):
        factor = jnp.take_along_axis(packed, first + j, axis=1)
        found = found - factor * found[j : j + 1]
    return jnp.where(on_block, jnp.concatenate([found] * (C // B), axis=0), 0.0)


def odd_rows(x, size):
    return jnp.concatenate([x[i : i + size] for i in range(size, C, 2 * size)], axis=0)


def weave(even, odd, size):
    parts = []
    for i in range(0, C // 2, size):
        parts += [even[i : i + size], odd[i : i + size]]
    return jnp.concatenate(parts, axis=0)


def even_rows(x, size):
    return jnp.concatenate([x[i : i + size] for i in range(0, C, 2 * size)], axis=0)


def inverses(lowers, row, col):
    found = [base_inverse(a, row, col) for a in lowers]
    parts = [split(a) for a in lowers]
    size = B
    while size < C:
        r, c = odd_rows(row, size), odd_rows(col, size)
        mask = ((r // (2 * size)) == (c // (2 * size))) & ((r // size) != (c // size))
        nothing = jnp.zeros((C // 2, C), BF16)
        joins = [tuple(jnp.where(mask, odd_rows(x, size), nothing) for x in part) for part in parts]
        halves = [split(x) for x in found]
        middle = [split(dot3(a, x)) for a, x in zip(joins, halves)]
        middle = [tuple(weave(nothing, x, size) for x in part) for part in middle]
        lows = [dot3(tuple(odd_rows(x, size) for x in h), y) for h, y in zip(halves, middle)]
        found = [weave(even_rows(x, size), odd_rows(x, size) - y, size) for x, y in zip(found, lows)]
        size *= 2
    return found


def fetch(pairs, sems):
    copies = [pltpu.make_async_copy(x, y, sems.at[i]) for i, (x, y) in enumerate(pairs)]
    for copy in copies:
        copy.start()
    for copy in copies:
        copy.wait()


def in_hbm(*arrays):
    return [pltpu.with_memory_space_constraint(x, pltpu.HBM) for x in arrays]


def chunk_rows(heads, head, c):
    return pl.ds(c * C * heads + head, C, stride=heads)


def tokens_of(ref, head, c):
    return ref[head : head + 1, c * C : (c + 1) * C]


def local_maps_kernel(heads, batch, k_hbm, v_hbm, beta_hbm, log_hbm, k32, log_ref, wu_ref, n_ref, own_ref, *rest):
    sends, (k16, v16, v32, beta_ref, all_ref, sems) = rest[: heads - 1], rest[heads - 1 :]
    fetch(((k_hbm, k16), (log_hbm, log_ref), (beta_hbm, beta_ref), (v_hbm, v16)), sems)
    k32[...] = k16[...].astype(F32)
    v32[...] = v16[...].astype(F32)
    chunks = beta_ref.shape[1] // C
    row, col = iotas()
    eye = row == col
    within = row >= col
    strict = row > col
    for start in range(0, heads, batch):
        jobs = [(head, c) for head in range(start, start + batch) for c in range(chunks)]
        lowers, sides, fades, ends = [], [], [], []
        for head, c in jobs:
            raw = k32[chunk_rows(heads, head, c), :]
            value = v32[chunk_rows(heads, head, c), :]
            beta = to_column(tokens_of(beta_ref, head, c), eye)
            column, decay = decay_parts(tokens_of(log_ref, head, c), within, eye)
            scale = inverse_scale(raw)
            raw16 = raw.astype(BF16)
            gram = dot(raw16, raw16, NT)
            lowers.append(jnp.where(strict, gram * decay * (beta * scale) * to_row(scale, eye), 0.0))
            unit = raw * scale
            last = column[C - 1 : C, :]
            sides.append(jnp.concatenate([unit * (beta * jnp.exp(column)), value * beta], axis=1))
            fades.append((unit * jnp.exp(last - column)).T)
            ends.append(jnp.exp(last))
        solved = [dot3(split(x), split(s)) for x, s in zip(inverses(lowers, row, col), sides)]
        maps = []
        for i, (head, c) in enumerate(jobs):
            wu_ref[head * chunks + c] = solved[i]
            both = dot3(split(fades[i]), split(solved[i]))
            maps.append((jnp.where(eye, ends[i], 0.0) - both[:, :C], both[:, C:]))
        for j in range(batch):
            state = jnp.concatenate(maps[j * chunks], axis=1)
            for c in range(1, chunks):
                n_ref[(start + j) * chunks + c] = state
                moved, fresh = maps[j * chunks + c]
                state = dot3(split(moved), split(state))
                state = jnp.concatenate([state[:, :C], state[:, C:] + fresh], axis=1)
            all_ref[start + j] = state
    place = lax.rem(lax.axis_index("seq"), heads)
    own_ref[...] = all_ref[place]
    for r in range(1, heads):
        sends[r - 1][...] = all_ref[other_place(place, r, heads)].astype(BF16)


def other_place(place, r, heads):
    result = place
    for i in range(heads):
        result = jnp.where(place == i, i ^ r, result)
    return result


def local_maps(key, value, beta, log_decay, batch):
    heads, tokens = beta.shape
    chunks = tokens // C
    here = pl.BlockSpec(memory_space=pltpu.VMEM)
    return pl.pallas_call(
        functools.partial(local_maps_kernel, heads, batch),
        in_specs=[pl.BlockSpec(memory_space=pltpu.HBM)] * 4,
        out_specs=[here] * (4 + heads),
        out_shape=[
            jax.ShapeDtypeStruct(key.shape, F32),
            jax.ShapeDtypeStruct(beta.shape, F32),
            jax.ShapeDtypeStruct((heads * chunks, C, 2 * C), F32),
            jax.ShapeDtypeStruct((heads * chunks, C, 2 * C), F32),
            jax.ShapeDtypeStruct((C, 2 * C), F32),
        ]
        + [jax.ShapeDtypeStruct((C, 2 * C), BF16)] * (heads - 1),
        scratch_shapes=[
            pltpu.VMEM(key.shape, BF16),
            pltpu.VMEM(key.shape, BF16),
            pltpu.VMEM(key.shape, F32),
            pltpu.VMEM(beta.shape, F32),
            pltpu.VMEM((heads, C, 2 * C), F32),
            pltpu.SemaphoreType.DMA((4,)),
        ],
        compiler_params=pltpu.CompilerParams(vmem_limit_bytes=32 * MIB),
        name="local_maps",
    )(*in_hbm(key, value, beta, log_decay))


def rows_kernel(heads, mine, q_hbm, k32, log_ref, wu_ref, n_ref, out_ref, q16, q32, sems):
    fetch(((q_hbm, q16),), sems)
    q32[...] = q16[...].astype(F32)
    chunks = log_ref.shape[1] // C
    row, col = iotas()
    eye = row == col
    within = row >= col
    for j, head in enumerate(mine):
        for c in range(chunks):
            query, raw = q32[chunk_rows(heads, head, c), :], k32[chunk_rows(heads, head, c), :]
            column, decay = decay_parts(tokens_of(log_ref, head, c), within, eye)
            scale = inverse_scale(query)
            pairs = dot(query.astype(BF16), raw.astype(BF16), NT)
            pairs = pairs * decay * scale * to_row(inverse_scale(raw), eye)
            both = dot3(split(pairs), split(wu_ref[head * chunks + c]))
            reach = query * (scale * jnp.exp(column)) - both[:, :C]
            fresh = both[:, C:]
            if c > 0:
                earlier = dot3(split(reach), split(n_ref[head * chunks + c]))
                reach = earlier[:, :C]
                fresh = fresh + earlier[:, C:]
            out_ref[j, c * C : (c + 1) * C, :] = jnp.concatenate([reach, fresh], axis=1)


def row_maps(mine, query, k32, log_decay, wu, states):
    heads, tokens = log_decay.shape
    here = pl.BlockSpec(memory_space=pltpu.VMEM)
    return pl.pallas_call(
        functools.partial(rows_kernel, heads, mine),
        in_specs=[pl.BlockSpec(memory_space=pltpu.HBM)] + [here] * 4,
        out_specs=here,
        out_shape=jax.ShapeDtypeStruct((len(mine), tokens, 2 * C), F32),
        scratch_shapes=[
            pltpu.VMEM(query.shape, BF16),
            pltpu.VMEM(query.shape, F32),
            pltpu.SemaphoreType.DMA((1,)),
        ],
        compiler_params=pltpu.CompilerParams(vmem_limit_bytes=16 * MIB),
        cost_estimate=pl.CostEstimate(flops=2000000000, bytes_accessed=8000000, transcendentals=0),
        name="row_maps",
    )(*in_hbm(query), k32, log_decay, wu, states)


def small_call(kernel, out_shape, *args):
    here = pl.BlockSpec(memory_space=pltpu.VMEM)
    return pl.pallas_call(
        kernel,
        in_specs=[here] * len(args),
        out_specs=[here] * len(out_shape),
        out_shape=out_shape,
        compiler_params=pltpu.CompilerParams(vmem_limit_bytes=8 * MIB),
        name=kernel.__name__,
    )(*args)


def moved_on(maps, state16, added):
    high, low = split(maps)
    return dot(jnp.concatenate([high, low], axis=1), twice(state16)) + added


def in_order(own_ref, got_refs, held):
    heads = held.shape[0]
    place = lax.rem(lax.axis_index("seq"), heads)
    held[place] = own_ref[...]
    for r, got in enumerate(got_refs, 1):
        held[other_place(place, r, heads)] = got[...].astype(F32)
    return place


def group_state(own_ref, *refs):
    got_refs, (held, out_ref) = refs[:-2], refs[-2:]
    in_order(own_ref, got_refs, held)
    state = held[0, :, C:].astype(BF16)
    for i in range(1, held.shape[0]):
        state = moved_on(held[i, :, :C], state, held[i, :, C:]).astype(BF16)
    out_ref[...] = state


def group_total(own_ref, *refs):
    got_refs, (held, out_ref) = refs[:-2], refs[-2:]
    in_order(own_ref, got_refs, held)
    total = held[0]
    for i in range(1, held.shape[0]):
        later = held[i]
        total = dot3(split(later[:, :C]), split(total))
        total = jnp.concatenate([total[:, :C], total[:, C:] + later[:, C:]], axis=1)
    out_ref[...] = total.astype(BF16)


def group_states(held, state, keep_ref, send_refs, states):
    heads = held.shape[0]
    for i in range(heads):
        states[i] = state
        if i + 1 < heads:
            state = moved_on(held[i, :, :C], state, held[i, :, C:]).astype(BF16)
    place = lax.rem(lax.axis_index("seq"), heads)
    keep_ref[...] = states[place]
    for r, send in enumerate(send_refs, 1):
        send[...] = states[other_place(place, r, heads)]


def states_of_upper(held, lower_ref, keep_ref, *refs):
    lower = lower_ref[...]
    state = jnp.where(lax.axis_index("seq") < held.shape[0], jnp.zeros_like(lower), lower)
    group_states(held, state, keep_ref, refs[:-1], refs[-1])


def states_given(held, state_ref, keep_ref, *refs):
    group_states(held, state_ref[...], keep_ref, refs[:-1], refs[-1])


def prefix(total, heads):
    count = lax.axis_size("seq")
    groups = [list(range(i, count, heads)) for i in range(heads)]
    me = lax.axis_index("seq") // heads
    totals = lax.all_gather(total, "seq", axis_index_groups=groups)

    def step(d, state):
        longer = jnp.einsum("ik,pkw->iw", totals[d, :, :C], jnp.stack(split(state)), preferred_element_type=F32)
        return jnp.where(d < me, longer + totals[d, :, C:].astype(F32), state)

    start = jnp.zeros((C, C), F32)
    return lax.fori_loop(0, count // heads - 1, step, start).astype(BF16)


def apply_kernel(heads, rows0_ref, rows1_ref, *refs):
    states, (keep_ref, send_ref, held) = refs[:heads], refs[heads:]
    step = pl.program_id(0)

    @pl.when(step == 0)
    def _():
        place = lax.rem(lax.axis_index("seq"), heads)
        for r in range(heads):
            held[other_place(place, r, heads)] = states[r][...]

    attended = []
    for h in range(heads):
        rows_ref = (rows0_ref, rows1_ref)[h // (heads // 2)]
        reach, fresh = rows_ref[h % (heads // 2), :, :C], rows_ref[h % (heads // 2), :, C:]
        attended.append(moved_on(reach, held[h], fresh).astype(BF16))
    attended = jnp.concatenate(attended, axis=1)
    mine = lax.rem(step, 2) == lax.rem(lax.axis_index("head"), 2)

    @pl.when(mine)
    def _():
        keep_ref[step // 2] = attended

    @pl.when(jnp.logical_not(mine))
    def _():
        send_ref[step // 2] = attended


def apply(rows, states, groups):
    _, tokens, _ = rows[0].shape
    heads = len(states)
    block = tokens // groups
    out = jax.ShapeDtypeStruct((groups // 2, block, heads * C), BF16)
    return pl.pallas_call(
        functools.partial(apply_kernel, heads),
        grid=(groups,),
        in_specs=[pl.BlockSpec((heads // 2, block, 2 * C), lambda i: (0, i, 0))] * 2
        + [pl.BlockSpec((C, C), lambda i: (0, 0))] * heads,
        out_specs=[pl.BlockSpec(out.shape, lambda i: (0, 0, 0))] * 2,
        out_shape=[out, out],
        scratch_shapes=[pltpu.VMEM((heads, C, C), BF16)],
        compiler_params=pltpu.CompilerParams(vmem_limit_bytes=14 * MIB),
        name="apply",
    )(*rows, *states)


def project_kernel(other, keep_ref, got_ref, w_ref, w2_ref, out_ref):
    pair = lax.axis_index("head") // 2
    index = 1 - pair if other else pair
    out_ref[...] = (dot(keep_ref[index], w_ref[...]) + dot(got_ref[index], w2_ref[...])).astype(out_ref.dtype)


def project(other, keep, got, weight, weight2):
    _, block, depth = keep.shape
    width = weight.shape[1]
    return pl.pallas_call(
        functools.partial(project_kernel, other),
        out_shape=jax.ShapeDtypeStruct((block, width), BF16 if other else F32),
        compiler_params=pltpu.CompilerParams(vmem_limit_bytes=20 * MIB),
        cost_estimate=pl.CostEstimate(
            flops=4 * block * depth * width, bytes_accessed=4 * depth * width, transcendentals=0
        ),
        name="project",
    )(keep, got, weight, weight2)


def swap(x, axis, bit):
    count = lax.axis_size(axis)
    return lax.ppermute(x, axis, [(i, i ^ bit) for i in range(count)])


def body(query, key, value, beta, log_decay, out_weight):
    tokens, heads, _ = key.shape
    count = lax.axis_size("seq")
    flat = lambda x: x.reshape(tokens * heads, C)
    weight2 = swap(out_weight, "head", 1)
    k32, logs, wu, states, own, *sends = local_maps(flat(key), flat(value), beta, log_decay, 2)
    got = [swap(x, "seq", r) for r, x in enumerate(sends, 1)]
    half = heads // 2
    rows0 = row_maps(range(half), flat(query), k32, logs, wu, states)
    rows1 = row_maps(range(half, heads), flat(query), k32, logs, wu, states)
    rows0, got = lax.optimization_barrier((rows0, got))
    wide = jax.ShapeDtypeStruct((heads, C, 2 * C), F32)
    square = jax.ShapeDtypeStruct((C, C), BF16)
    outs = [square] * heads + [jax.ShapeDtypeStruct((heads, C, C), BF16)]
    if count == 2 * heads:
        held, state = small_call(group_state, [wide, square], own, *got)
        lower = swap(state, "seq", heads)
        rows1, lower = lax.optimization_barrier((rows1, lower))
        keep, *sends = small_call(states_of_upper, outs, held, lower)
    else:
        total16 = jax.ShapeDtypeStruct((C, 2 * C), BF16)
        held, total = small_call(group_total, [wide, total16], own, *got)
        keep, *sends = small_call(states_given, outs, held, prefix(total, heads))
    entering = [keep] + [swap(x, "seq", r) for r, x in enumerate(sends[: heads - 1], 1)]
    keep, away = apply((rows0, rows1), entering, lax.axis_size("head"))
    got = swap(away, "head", 1)
    theirs = swap(project(True, keep, got, out_weight, weight2), "head", 2)
    mine = project(False, keep, got, out_weight, weight2)
    return (mine + theirs.astype(F32)).astype(BF16)


def solution(mesh):
    in_specs = (
        P("seq", "head", None),
        P("seq", "head", None),
        P("seq", "head", None),
        P("head", "seq"),
        P("head", "seq"),
        P("head", None),
    )
    out_specs = P(("seq", "head"), None)
    return jax.shard_map(body, mesh=mesh, in_specs=in_specs, out_specs=out_specs, check_vma=False)
```

```python
import functools

import jax
import jax.numpy as jnp
from jax import lax
from jax.experimental import pallas as pl
from jax.experimental.pallas import tpu as pltpu
from jax.sharding import PartitionSpec as P

C = 128
B = 16
F32 = jnp.float32
BF16 = jnp.bfloat16
NN = (((1,), (0,)), ((), ()))
NT = (((1,), (1,)), ((), ()))
TN = (((0,), (0,)), ((), ()))
MIB = 1024 * 1024


def dot(a, b, dims=NN):
    return lax.dot_general(a, b, dims, preferred_element_type=F32)


def split(x):
    high = x.astype(BF16)
    return high, (x - high.astype(F32)).astype(BF16)


def twice(x):
    return jnp.concatenate([x, x], axis=0)


def dot3(a, b):
    (ah, al), (bh, bl) = a, b
    width = bh.shape[1]
    left = jnp.concatenate([ah, al], axis=1)
    if width > C:
        return dot(left, twice(bh)) + dot(ah, bl)
    both = dot(left, twice(jnp.concatenate([bh, bl], axis=1)))
    return both[:, :width] + both[:, width:]


def iotas():
    return (
        lax.broadcasted_iota(jnp.int32, (C, C), 0),
        lax.broadcasted_iota(jnp.int32, (C, C), 1),
    )


def to_column(row, eye):
    return jnp.sum(jnp.where(eye, row, 0.0), axis=1, keepdims=True)


def to_row(column, eye):
    return jnp.sum(jnp.where(eye, column, 0.0), axis=0, keepdims=True)


def inverse_scale(rows):
    return lax.rsqrt(jnp.sum(rows * rows, axis=1, keepdims=True) + 1e-06)


def three(x):
    high, rest = x.astype(BF16), x
    rest = rest - high.astype(F32)
    return (high,) + split(rest)


def running_sums(rows, upper):
    return sum(dot(x, upper) for x in reversed(three(rows)))


def spread_columns(row, eye, ones):
    parts = three(jnp.broadcast_to(row, (16, C)))
    high, middle, low = (
        jnp.where(eye, jnp.concatenate([x] * (C // 16), axis=0), jnp.zeros((), BF16)) for x in parts
    )
    return dot(jnp.concatenate([high, middle], axis=1), twice(ones)) + dot(low, ones)


def base_inverse(lower, row, col):
    on_block = (row // B) == (col // B)
    blocks = jnp.where(on_block, lower, 0.0)
    packed = sum(blocks[i * B : (i + 1) * B] for i in range(1, C // B)) + blocks[:B]
    r, c = row[:B], col[:B]
    found = jnp.where(r == c % B, 1.0, 0.0)
    first = (c // B) * B
    for j in range(B - 1):
        factor = jnp.take_along_axis(packed, first + j, axis=1)
        found = found - factor * found[j : j + 1]
    return jnp.where(on_block, jnp.concatenate([found] * (C // B), axis=0), 0.0)


def odd_rows(x, size):
    return jnp.concatenate([x[i : i + size] for i in range(size, C, 2 * size)], axis=0)


def weave(even, odd, size):
    parts = []
    for i in range(0, C // 2, size):
        parts += [even[i : i + size], odd[i : i + size]]
    return jnp.concatenate(parts, axis=0)


def even_rows(x, size):
    return jnp.concatenate([x[i : i + size] for i in range(0, C, 2 * size)], axis=0)


def inverses(lowers, row, col):
    found = [base_inverse(a, row, col) for a in lowers]
    parts = [split(a) for a in lowers]
    size = B
    while size < C:
        r, c = odd_rows(row, size), odd_rows(col, size)
        mask = ((r // (2 * size)) == (c // (2 * size))) & ((r // size) != (c // size))
        nothing = jnp.zeros((C // 2, C), BF16)
        joins = [tuple(jnp.where(mask, odd_rows(x, size), nothing) for x in part) for part in parts]
        halves = [split(x) for x in found]
        middle = [split(dot3(a, x)) for a, x in zip(joins, halves)]
        middle = [tuple(weave(nothing, x, size) for x in part) for part in middle]
        lows = [dot3(tuple(odd_rows(x, size) for x in h), y) for h, y in zip(halves, middle)]
        found = [weave(even_rows(x, size), odd_rows(x, size) - y, size) for x, y in zip(found, lows)]
        size *= 2
    return found


def fetch(pairs, sems):
    copies = [pltpu.make_async_copy(x, y, sems.at[i]) for i, (x, y) in enumerate(pairs)]
    for copy in copies:
        copy.start()
    for copy in copies:
        copy.wait()


def in_hbm(*arrays):
    return [pltpu.with_memory_space_constraint(x, pltpu.HBM) for x in arrays]


def chunk_rows(heads, head, c):
    return pl.ds(c * C * heads + head, C, stride=heads)


def tokens_of(ref, head, c):
    return ref[head : head + 1, c * C : (c + 1) * C]


def per_chunk(ref):
    return jnp.concatenate([ref[:, i : i + C] for i in range(0, ref.shape[1], C)], axis=0)


def local_maps_kernel(heads, batch, k_hbm, v_hbm, beta_hbm, log_hbm, k32, sums_ref, mix_ref, wu_ref, n_ref, own_ref, *rest):
    sends, (k16, v16, v32, beta_ref, log_ref, all_ref, sems) = rest[: heads - 1], rest[heads - 1 :]
    fetch(((k_hbm, k16), (log_hbm, log_ref), (beta_hbm, beta_ref), (v_hbm, v16)), sems)
    k32[...] = k16[...].astype(F32)
    v32[...] = v16[...].astype(F32)
    chunks = beta_ref.shape[1] // C
    row, col = iotas()
    eye = row == col
    within = row >= col
    strict = row > col
    one = jnp.ones((C, C), BF16)
    eye16 = jnp.where(eye, one, jnp.zeros((), BF16))
    sums = running_sums(per_chunk(log_ref), jnp.where(row <= col, one, jnp.zeros((), BF16)))
    sums_ref[...] = sums
    grown = jnp.exp(sums)
    faded = jnp.exp(sums[:, C - 1 :] - sums)
    betas = per_chunk(beta_ref)
    for start in range(0, heads, batch):
        jobs = [(head, c) for head in range(start, start + batch) for c in range(chunks)]
        lowers, raws, values, fades, lengths = [], [], [], [], []
        for head, c in jobs:
            at = slice(c * heads + head, c * heads + head + 1)
            raw = k32[chunk_rows(heads, head, c), :].astype(BF16)
            raws.append(raw)
            values.append(v32[chunk_rows(heads, head, c), :].astype(BF16))
            both = dot(jnp.concatenate([raw, eye16], axis=0), raw, NT)
            gram, turned = both[:C], both[C:]
            square = to_row(gram, eye) + 1e-06
            scale = lax.rsqrt(square)
            lengths.append(square * scale)
            strength = betas[at] * (scale * scale)
            span = spread_columns(sums[at], eye, one) - sums[at]
            mix = jnp.where(within, jnp.exp(span), 0.0) * strength
            mix_ref[head * chunks + c] = mix
            lowers.append(jnp.where(strict, gram * mix, 0.0))
            fades.append(turned * (strength * faded[at]))
        solved = []
        for i, found in enumerate(inverses(lowers, row, col)):
            at = slice(jobs[i][1] * heads + jobs[i][0], jobs[i][1] * heads + jobs[i][0] + 1)
            kept = dot(jnp.concatenate(split(found * grown[at]), axis=1), twice(raws[i]))
            fresh = dot(jnp.concatenate(split(found * lengths[i]), axis=1), twice(values[i]))
            solved.append(jnp.concatenate([kept, fresh], axis=1))
        maps = []
        for i, (head, c) in enumerate(jobs):
            wu_ref[head * chunks + c] = solved[i]
            both = dot3(split(fades[i]), split(solved[i]))
            end = grown[c * heads + head : c * heads + head + 1, C - 1 :]
            maps.append((jnp.where(eye, end, 0.0) - both[:, :C], both[:, C:]))
        for j in range(batch):
            state = jnp.concatenate(maps[j * chunks], axis=1)
            for c in range(1, chunks):
                n_ref[(start + j) * chunks + c] = state
                moved, fresh = maps[j * chunks + c]
                state = dot3(split(moved), split(state))
                state = jnp.concatenate([state[:, :C], state[:, C:] + fresh], axis=1)
            all_ref[start + j] = state
    place = lax.rem(lax.axis_index("seq"), heads)
    own_ref[...] = all_ref[place]
    for r in range(1, heads):
        sends[r - 1][...] = all_ref[other_place(place, r, heads)].astype(BF16)


def other_place(place, r, heads):
    result = place
    for i in range(heads):
        result = jnp.where(place == i, i ^ r, result)
    return result


def local_maps(key, value, beta, log_decay, batch):
    heads, tokens = beta.shape
    count = heads * (tokens // C)
    here = pl.BlockSpec(memory_space=pltpu.VMEM)
    return pl.pallas_call(
        functools.partial(local_maps_kernel, heads, batch),
        in_specs=[pl.BlockSpec(memory_space=pltpu.HBM)] * 4,
        out_specs=[here] * (5 + heads),
        out_shape=[
            jax.ShapeDtypeStruct(key.shape, F32),
            jax.ShapeDtypeStruct((count, C), F32),
            jax.ShapeDtypeStruct((count, C, C), F32),
            jax.ShapeDtypeStruct((count, C, 2 * C), F32),
            jax.ShapeDtypeStruct((count, C, 2 * C), F32),
            jax.ShapeDtypeStruct((C, 2 * C), F32),
        ]
        + [jax.ShapeDtypeStruct((C, 2 * C), BF16)] * (heads - 1),
        scratch_shapes=[
            pltpu.VMEM(key.shape, BF16),
            pltpu.VMEM(key.shape, BF16),
            pltpu.VMEM(key.shape, F32),
            pltpu.VMEM(beta.shape, F32),
            pltpu.VMEM(beta.shape, F32),
            pltpu.VMEM((heads, C, 2 * C), F32),
            pltpu.SemaphoreType.DMA((4,)),
        ],
        compiler_params=pltpu.CompilerParams(vmem_limit_bytes=32 * MIB),
        name="local_maps",
    )(*in_hbm(key, value, beta, log_decay))


def rows_kernel(heads, mine, q_hbm, k32, sums_ref, mix_ref, wu_ref, n_ref, out_ref, q16, q32, sems):
    fetch(((q_hbm, q16),), sems)
    q32[...] = q16[...].astype(F32)
    chunks = q16.shape[0] // (heads * C)
    row, col = iotas()
    eye = row == col
    for j, head in enumerate(mine):
        for c in range(chunks):
            i = head * chunks + c
            query, raw = q32[chunk_rows(heads, head, c), :], k32[chunk_rows(heads, head, c), :]
            grown = to_column(jnp.exp(sums_ref[c * heads + head : c * heads + head + 1, :]), eye)
            pairs = dot(query.astype(BF16), raw.astype(BF16), NT) * mix_ref[i]
            both = dot3(split(pairs), split(wu_ref[i]))
            scale = inverse_scale(query)
            reach = (query * grown - both[:, :C]) * scale
            fresh = both[:, C:] * scale
            if c > 0:
                earlier = dot3(split(reach), split(n_ref[i]))
                reach = earlier[:, :C]
                fresh = fresh + earlier[:, C:]
            out_ref[j, c * C : (c + 1) * C, :] = jnp.concatenate([reach, fresh], axis=1)


def row_maps(heads, mine, query, k32, sums, mix, wu, states):
    tokens = query.shape[0] // heads
    here = pl.BlockSpec(memory_space=pltpu.VMEM)
    return pl.pallas_call(
        functools.partial(rows_kernel, heads, mine),
        in_specs=[pl.BlockSpec(memory_space=pltpu.HBM)] + [here] * 5,
        out_specs=here,
        out_shape=jax.ShapeDtypeStruct((len(mine), tokens, 2 * C), F32),
        scratch_shapes=[
            pltpu.VMEM(query.shape, BF16),
            pltpu.VMEM(query.shape, F32),
            pltpu.SemaphoreType.DMA((1,)),
        ],
        compiler_params=pltpu.CompilerParams(vmem_limit_bytes=16 * MIB),
        cost_estimate=pl.CostEstimate(flops=2000000000, bytes_accessed=8000000, transcendentals=0),
        name="row_maps",
    )(*in_hbm(query), k32, sums, mix, wu, states)


def small_call(kernel, out_shape, *args):
    here = pl.BlockSpec(memory_space=pltpu.VMEM)
    return pl.pallas_call(
        kernel,
        in_specs=[here] * len(args),
        out_specs=[here] * len(out_shape),
        out_shape=out_shape,
        compiler_params=pltpu.CompilerParams(vmem_limit_bytes=8 * MIB),
        name=kernel.__name__,
    )(*args)


def moved_on(maps, state16, added):
    high, low = split(maps)
    return dot(jnp.concatenate([high, low], axis=1), twice(state16)) + added


def in_order(own_ref, got_refs, held):
    heads = held.shape[0]
    place = lax.rem(lax.axis_index("seq"), heads)
    held[place] = own_ref[...]
    for r, got in enumerate(got_refs, 1):
        held[other_place(place, r, heads)] = got[...].astype(F32)
    return place


def group_state(own_ref, *refs):
    got_refs, (held, out_ref) = refs[:-2], refs[-2:]
    in_order(own_ref, got_refs, held)
    state = held[0, :, C:].astype(BF16)
    for i in range(1, held.shape[0]):
        state = moved_on(held[i, :, :C], state, held[i, :, C:]).astype(BF16)
    out_ref[...] = state


def group_total(own_ref, *refs):
    got_refs, (held, out_ref) = refs[:-2], refs[-2:]
    in_order(own_ref, got_refs, held)
    total = held[0]
    for i in range(1, held.shape[0]):
        later = held[i]
        total = dot3(split(later[:, :C]), split(total))
        total = jnp.concatenate([total[:, :C], total[:, C:] + later[:, C:]], axis=1)
    out_ref[...] = total.astype(BF16)


def group_states(held, state, keep_ref, send_refs, states):
    heads = held.shape[0]
    for i in range(heads):
        states[i] = state
        if i + 1 < heads:
            state = moved_on(held[i, :, :C], state, held[i, :, C:]).astype(BF16)
    place = lax.rem(lax.axis_index("seq"), heads)
    keep_ref[...] = states[place]
    for r, send in enumerate(send_refs, 1):
        send[...] = states[other_place(place, r, heads)]


def states_of_upper(held, lower_ref, keep_ref, *refs):
    lower = lower_ref[...]
    state = jnp.where(lax.axis_index("seq") < held.shape[0], jnp.zeros_like(lower), lower)
    group_states(held, state, keep_ref, refs[:-1], refs[-1])


def states_given(held, state_ref, keep_ref, *refs):
    group_states(held, state_ref[...], keep_ref, refs[:-1], refs[-1])


def prefix(total, heads):
    count = lax.axis_size("seq")
    groups = [list(range(i, count, heads)) for i in range(heads)]
    me = lax.axis_index("seq") // heads
    totals = lax.all_gather(total, "seq", axis_index_groups=groups)

    def step(d, state):
        longer = jnp.einsum("ik,pkw->iw", totals[d, :, :C], jnp.stack(split(state)), preferred_element_type=F32)
        return jnp.where(d < me, longer + totals[d, :, C:].astype(F32), state)

    start = jnp.zeros((C, C), F32)
    return lax.fori_loop(0, count // heads - 1, step, start).astype(BF16)


def apply_kernel(heads, rows0_ref, rows1_ref, *refs):
    states, (keep_ref, send_ref, held) = refs[:heads], refs[heads:]
    step = pl.program_id(0)

    @pl.when(step == 0)
    def _():
        place = lax.rem(lax.axis_index("seq"), heads)
        for r in range(heads):
            held[other_place(place, r, heads)] = states[r][...]

    attended = []
    for h in range(heads):
        rows_ref = (rows0_ref, rows1_ref)[h // (heads // 2)]
        reach, fresh = rows_ref[h % (heads // 2), :, :C], rows_ref[h % (heads // 2), :, C:]
        attended.append(moved_on(reach, held[h], fresh).astype(BF16))
    attended = jnp.concatenate(attended, axis=1)
    mine = lax.rem(step, 2) == lax.rem(lax.axis_index("head"), 2)

    @pl.when(mine)
    def _():
        keep_ref[step // 2] = attended

    @pl.when(jnp.logical_not(mine))
    def _():
        send_ref[step // 2] = attended


def apply(rows, states, groups):
    _, tokens, _ = rows[0].shape
    heads = len(states)
    block = tokens // groups
    out = jax.ShapeDtypeStruct((groups // 2, block, heads * C), BF16)
    return pl.pallas_call(
        functools.partial(apply_kernel, heads),
        grid=(groups,),
        in_specs=[pl.BlockSpec((heads // 2, block, 2 * C), lambda i: (0, i, 0))] * 2
        + [pl.BlockSpec((C, C), lambda i: (0, 0))] * heads,
        out_specs=[pl.BlockSpec(out.shape, lambda i: (0, 0, 0))] * 2,
        out_shape=[out, out],
        scratch_shapes=[pltpu.VMEM((heads, C, C), BF16)],
        compiler_params=pltpu.CompilerParams(vmem_limit_bytes=14 * MIB),
        name="apply",
    )(*rows, *states)


def project_kernel(other, keep_ref, got_ref, w_ref, w2_ref, out_ref):
    pair = lax.axis_index("head") // 2
    index = 1 - pair if other else pair
    out_ref[...] = (dot(keep_ref[index], w_ref[...]) + dot(got_ref[index], w2_ref[...])).astype(out_ref.dtype)


def project(other, keep, got, weight, weight2):
    _, block, depth = keep.shape
    width = weight.shape[1]
    return pl.pallas_call(
        functools.partial(project_kernel, other),
        out_shape=jax.ShapeDtypeStruct((block, width), BF16 if other else F32),
        compiler_params=pltpu.CompilerParams(vmem_limit_bytes=20 * MIB),
        cost_estimate=pl.CostEstimate(
            flops=4 * block * depth * width, bytes_accessed=4 * depth * width, transcendentals=0
        ),
        name="project",
    )(keep, got, weight, weight2)


def swap(x, axis, bit):
    count = lax.axis_size(axis)
    return lax.ppermute(x, axis, [(i, i ^ bit) for i in range(count)])


def body(query, key, value, beta, log_decay, out_weight):
    tokens, heads, _ = key.shape
    count = lax.axis_size("seq")
    flat = lambda x: x.reshape(tokens * heads, C)
    weight2 = swap(out_weight, "head", 1)
    k32, *chunk_maps, own, send1, send2, send3 = local_maps(flat(key), flat(value), beta, log_decay, 2)
    got = [swap(x, "seq", r) for r, x in enumerate((send1, send2, send3), 1)]
    half = heads // 2
    rows0 = row_maps(heads, range(half), flat(query), k32, *chunk_maps)
    rows1 = row_maps(heads, range(half, heads), flat(query), k32, *chunk_maps)
    rows0, got = lax.optimization_barrier((rows0, got))
    wide = jax.ShapeDtypeStruct((heads, C, 2 * C), F32)
    square = jax.ShapeDtypeStruct((C, C), BF16)
    outs = [square] * heads + [jax.ShapeDtypeStruct((heads, C, C), BF16)]
    if count == 2 * heads:
        held, state = small_call(group_state, [wide, square], own, *got)
        lower = swap(state, "seq", heads)
        keep, *sends = small_call(states_of_upper, outs, held, lower)
    else:
        total16 = jax.ShapeDtypeStruct((C, 2 * C), BF16)
        held, total = small_call(group_total, [wide, total16], own, *got)
        keep, *sends = small_call(states_given, outs, held, prefix(total, heads))
    entering = [keep] + [swap(x, "seq", r) for r, x in enumerate(sends[: heads - 1], 1)]
    keep, away = apply((rows0, rows1), entering, lax.axis_size("head"))
    got = swap(away, "head", 1)
    theirs = swap(project(True, keep, got, out_weight, weight2), "head", 2)
    mine = project(False, keep, got, out_weight, weight2)
    return (mine + theirs.astype(F32)).astype(BF16)


def solution(mesh):
    in_specs = (
        P("seq", "head", None),
        P("seq", "head", None),
        P("seq", "head", None),
        P("head", "seq"),
        P("head", "seq"),
        P("head", None),
    )
    out_specs = P(("seq", "head"), None)
    return jax.shard_map(body, mesh=mesh, in_specs=in_specs, out_specs=out_specs, check_vma=False)
```

```python
import functools

import jax
import jax.numpy as jnp
from jax import lax
from jax.experimental import pallas as pl
from jax.experimental.pallas import tpu as pltpu
from jax.sharding import PartitionSpec as P

C = 128
B = 16
F32 = jnp.float32
BF16 = jnp.bfloat16
NN = (((1,), (0,)), ((), ()))
NT = (((1,), (1,)), ((), ()))
TN = (((0,), (0,)), ((), ()))
MIB = 1024 * 1024


def dot(a, b, dims=NN):
    return lax.dot_general(a, b, dims, preferred_element_type=F32)


def split(x):
    high = x.astype(BF16)
    return high, (x - high.astype(F32)).astype(BF16)


def twice(x):
    return jnp.concatenate([x, x], axis=0)


def dot3(a, b):
    (ah, al), (bh, bl) = a, b
    width = bh.shape[1]
    left = jnp.concatenate([ah, al], axis=1)
    if width > C:
        return dot(left, twice(bh)) + dot(ah, bl)
    both = dot(left, twice(jnp.concatenate([bh, bl], axis=1)))
    return both[:, :width] + both[:, width:]


def iotas():
    return (
        lax.broadcasted_iota(jnp.int32, (C, C), 0),
        lax.broadcasted_iota(jnp.int32, (C, C), 1),
    )


def to_column(row, eye):
    return jnp.sum(jnp.where(eye, row, 0.0), axis=1, keepdims=True)


def to_row(column, eye):
    return jnp.sum(jnp.where(eye, column, 0.0), axis=0, keepdims=True)


def inverse_scale(rows):
    return lax.rsqrt(jnp.sum(rows * rows, axis=1, keepdims=True) + 1e-06)


def three(x):
    high, rest = x.astype(BF16), x
    rest = rest - high.astype(F32)
    return (high,) + split(rest)


def running_sums(rows, upper):
    return sum(dot(x, upper) for x in reversed(three(rows)))


def spread_columns(row, eye, ones):
    parts = three(jnp.broadcast_to(row, (16, C)))
    high, middle, low = (
        jnp.where(eye, jnp.concatenate([x] * (C // 16), axis=0), jnp.zeros((), BF16)) for x in parts
    )
    return dot(jnp.concatenate([high, middle], axis=1), twice(ones)) + dot(low, ones)


def base_inverse(lower, row, col):
    on_block = (row // B) == (col // B)
    blocks = jnp.where(on_block, lower, 0.0)
    packed = sum(blocks[i * B : (i + 1) * B] for i in range(1, C // B)) + blocks[:B]
    r, c = row[:B], col[:B]
    found = jnp.where(r == c % B, 1.0, 0.0)
    first = (c // B) * B
    for j in range(B - 1):
        factor = jnp.take_along_axis(packed, first + j, axis=1)
        found = found - factor * found[j : j + 1]
    return jnp.where(on_block, jnp.concatenate([found] * (C // B), axis=0), 0.0)


def odd_rows(x, size):
    return jnp.concatenate([x[i : i + size] for i in range(size, C, 2 * size)], axis=0)


def weave(even, odd, size):
    parts = []
    for i in range(0, C // 2, size):
        parts += [even[i : i + size], odd[i : i + size]]
    return jnp.concatenate(parts, axis=0)


def even_rows(x, size):
    return jnp.concatenate([x[i : i + size] for i in range(0, C, 2 * size)], axis=0)


def inverses(lowers, row, col):
    found = [base_inverse(a, row, col) for a in lowers]
    parts = [split(a) for a in lowers]
    size = B
    while size < C:
        r, c = odd_rows(row, size), odd_rows(col, size)
        mask = ((r // (2 * size)) == (c // (2 * size))) & ((r // size) != (c // size))
        nothing = jnp.zeros((C // 2, C), BF16)
        joins = [tuple(jnp.where(mask, odd_rows(x, size), nothing) for x in part) for part in parts]
        halves = [split(x) for x in found]
        middle = [split(dot3(a, x)) for a, x in zip(joins, halves)]
        middle = [tuple(weave(nothing, x, size) for x in part) for part in middle]
        lows = [dot3(tuple(odd_rows(x, size) for x in h), y) for h, y in zip(halves, middle)]
        found = [weave(even_rows(x, size), odd_rows(x, size) - y, size) for x, y in zip(found, lows)]
        size *= 2
    return found


def fetch(pairs, sems, late):
    copies = [pltpu.make_async_copy(x, y, sems.at[i]) for i, (x, y) in enumerate(pairs)]
    for copy in copies:
        copy.start()
    late.start()
    for copy in copies:
        copy.wait()


def in_hbm(*arrays):
    return [pltpu.with_memory_space_constraint(x, pltpu.HBM) for x in arrays]


def chunk_rows(heads, head, c):
    return pl.ds(c * C * heads + head, C, stride=heads)


def tokens_of(ref, head, c):
    return ref[head : head + 1, c * C : (c + 1) * C]


def per_chunk(ref):
    return jnp.concatenate([ref[:, i : i + C] for i in range(0, ref.shape[1], C)], axis=0)


def local_maps_kernel(heads, batch, k_hbm, v_hbm, beta_hbm, log_hbm, q_hbm, q16, k32, sums_ref, mix_ref, wu_ref, n_ref, own_ref, *rest):
    sends, (k16, v16, v32, beta_ref, log_ref, all_ref, sems) = rest[: heads - 1], rest[heads - 1 :]
    late = pltpu.make_async_copy(q_hbm, q16, sems.at[4])
    fetch(((k_hbm, k16), (log_hbm, log_ref), (beta_hbm, beta_ref), (v_hbm, v16)), sems, late)
    k32[...] = k16[...].astype(F32)
    v32[...] = v16[...].astype(F32)
    chunks = beta_ref.shape[1] // C
    row, col = iotas()
    eye = row == col
    within = row >= col
    strict = row > col
    one = jnp.ones((C, C), BF16)
    eye16 = jnp.where(eye, one, jnp.zeros((), BF16))
    sums = running_sums(per_chunk(log_ref), jnp.where(row <= col, one, jnp.zeros((), BF16)))
    sums_ref[...] = sums
    grown = jnp.exp(sums)
    faded = jnp.exp(sums[:, C - 1 :] - sums)
    betas = per_chunk(beta_ref)
    for start in range(0, heads, batch):
        jobs = [(head, c) for head in range(start, start + batch) for c in range(chunks)]
        lowers, raws, values, fades, lengths = [], [], [], [], []
        for head, c in jobs:
            at = slice(c * heads + head, c * heads + head + 1)
            raw = k32[chunk_rows(heads, head, c), :].astype(BF16)
            raws.append(raw)
            values.append(v32[chunk_rows(heads, head, c), :].astype(BF16))
            both = dot(jnp.concatenate([raw, eye16], axis=0), raw, NT)
            gram, turned = both[:C], both[C:]
            square = to_row(gram, eye) + 1e-06
            scale = lax.rsqrt(square)
            lengths.append(square * scale)
            strength = betas[at] * (scale * scale)
            span = spread_columns(sums[at], eye, one) - sums[at]
            mix = jnp.where(within, jnp.exp(span), 0.0) * strength
            mix_ref[head * chunks + c] = mix
            lowers.append(jnp.where(strict, gram * mix, 0.0))
            fades.append(turned * (strength * faded[at]))
        solved = []
        for i, found in enumerate(inverses(lowers, row, col)):
            at = slice(jobs[i][1] * heads + jobs[i][0], jobs[i][1] * heads + jobs[i][0] + 1)
            kept = dot(jnp.concatenate(split(found * grown[at]), axis=1), twice(raws[i]))
            fresh = dot(jnp.concatenate(split(found * lengths[i]), axis=1), twice(values[i]))
            solved.append(jnp.concatenate([kept, fresh], axis=1))
        maps = []
        for i, (head, c) in enumerate(jobs):
            wu_ref[head * chunks + c] = solved[i]
            both = dot3(split(fades[i]), split(solved[i]))
            end = grown[c * heads + head : c * heads + head + 1, C - 1 :]
            maps.append((jnp.where(eye, end, 0.0) - both[:, :C], both[:, C:]))
        for j in range(batch):
            state = jnp.concatenate(maps[j * chunks], axis=1)
            for c in range(1, chunks):
                n_ref[(start + j) * chunks + c] = state
                moved, fresh = maps[j * chunks + c]
                state = dot3(split(moved), split(state))
                state = jnp.concatenate([state[:, :C], state[:, C:] + fresh], axis=1)
            all_ref[start + j] = state
    place = lax.rem(lax.axis_index("seq"), heads)
    own_ref[...] = all_ref[place]
    for r in range(1, heads):
        sends[r - 1][...] = all_ref[other_place(place, r, heads)].astype(BF16)
    late.wait()


def other_place(place, r, heads):
    result = place
    for i in range(heads):
        result = jnp.where(place == i, i ^ r, result)
    return result


def local_maps(key, value, beta, log_decay, query, batch):
    heads, tokens = beta.shape
    count = heads * (tokens // C)
    here = pl.BlockSpec(memory_space=pltpu.VMEM)
    return pl.pallas_call(
        functools.partial(local_maps_kernel, heads, batch),
        in_specs=[pl.BlockSpec(memory_space=pltpu.HBM)] * 5,
        out_specs=[here] * (6 + heads),
        out_shape=[
            jax.ShapeDtypeStruct(query.shape, BF16),
            jax.ShapeDtypeStruct(key.shape, F32),
            jax.ShapeDtypeStruct((count, C), F32),
            jax.ShapeDtypeStruct((count, C, C), F32),
            jax.ShapeDtypeStruct((count, C, 2 * C), F32),
            jax.ShapeDtypeStruct((count, C, 2 * C), F32),
            jax.ShapeDtypeStruct((C, 2 * C), F32),
        ]
        + [jax.ShapeDtypeStruct((C, 2 * C), BF16)] * (heads - 1),
        scratch_shapes=[
            pltpu.VMEM(key.shape, BF16),
            pltpu.VMEM(key.shape, BF16),
            pltpu.VMEM(key.shape, F32),
            pltpu.VMEM(beta.shape, F32),
            pltpu.VMEM(beta.shape, F32),
            pltpu.VMEM((heads, C, 2 * C), F32),
            pltpu.SemaphoreType.DMA((5,)),
        ],
        compiler_params=pltpu.CompilerParams(vmem_limit_bytes=32 * MIB),
        name="local_maps",
    )(*in_hbm(key, value, beta, log_decay, query))


def rows_kernel(heads, mine, q16, k32, sums_ref, mix_ref, wu_ref, n_ref, out_ref, q32):
    q32[...] = q16[...].astype(F32)
    chunks = q16.shape[0] // (heads * C)
    row, col = iotas()
    eye = row == col
    for j, head in enumerate(mine):
        for c in range(chunks):
            i = head * chunks + c
            query, raw = q32[chunk_rows(heads, head, c), :], k32[chunk_rows(heads, head, c), :]
            grown = to_column(jnp.exp(sums_ref[c * heads + head : c * heads + head + 1, :]), eye)
            pairs = dot(query.astype(BF16), raw.astype(BF16), NT) * mix_ref[i]
            both = dot3(split(pairs), split(wu_ref[i]))
            scale = inverse_scale(query)
            reach = (query * grown - both[:, :C]) * scale
            fresh = both[:, C:] * scale
            if c > 0:
                earlier = dot3(split(reach), split(n_ref[i]))
                reach = earlier[:, :C]
                fresh = fresh + earlier[:, C:]
            out_ref[j, c * C : (c + 1) * C, :] = jnp.concatenate([reach, fresh], axis=1)


def row_maps(heads, mine, query, k32, sums, mix, wu, states):
    tokens = query.shape[0] // heads
    here = pl.BlockSpec(memory_space=pltpu.VMEM)
    return pl.pallas_call(
        functools.partial(rows_kernel, heads, mine),
        in_specs=[here] * 6,
        out_specs=here,
        out_shape=jax.ShapeDtypeStruct((len(mine), tokens, 2 * C), F32),
        scratch_shapes=[pltpu.VMEM(query.shape, F32)],
        compiler_params=pltpu.CompilerParams(vmem_limit_bytes=16 * MIB),
        cost_estimate=pl.CostEstimate(flops=2000000000, bytes_accessed=8000000, transcendentals=0),
        name="row_maps",
    )(query, k32, sums, mix, wu, states)


def small_call(kernel, out_shape, *args):
    here = pl.BlockSpec(memory_space=pltpu.VMEM)
    return pl.pallas_call(
        kernel,
        in_specs=[here] * len(args),
        out_specs=[here] * len(out_shape),
        out_shape=out_shape,
        compiler_params=pltpu.CompilerParams(vmem_limit_bytes=8 * MIB),
        name=kernel.__name__,
    )(*args)


def moved_on(maps, state16, added):
    high, low = split(maps)
    return dot(jnp.concatenate([high, low], axis=1), twice(state16)) + added


def in_order(own_ref, got_refs, held):
    heads = held.shape[0]
    place = lax.rem(lax.axis_index("seq"), heads)
    held[place] = own_ref[...]
    for r, got in enumerate(got_refs, 1):
        held[other_place(place, r, heads)] = got[...].astype(F32)
    return place


def group_state(own_ref, *refs):
    got_refs, (held, out_ref) = refs[:-2], refs[-2:]
    in_order(own_ref, got_refs, held)
    state = held[0, :, C:].astype(BF16)
    for i in range(1, held.shape[0]):
        state = moved_on(held[i, :, :C], state, held[i, :, C:]).astype(BF16)
    out_ref[...] = state


def group_prefix(held, high_ref, low_ref, added_ref, total_ref):
    row, col = iotas()
    eye = jnp.where(row == col, 1.0, 0.0)
    total = jnp.concatenate([eye, jnp.zeros((C, C), F32)], axis=1)
    for i in range(held.shape[0]):
        high_ref[i], low_ref[i] = split(total[:, :C])
        added_ref[i] = total[:, C:]
        later = held[i]
        if i == 0:
            total = later
        else:
            total = dot3(split(later[:, :C]), split(total))
            total = jnp.concatenate([total[:, :C], total[:, C:] + later[:, C:]], axis=1)
    total_ref[...] = total.astype(BF16)


def group_states(upper_only, high_ref, low_ref, added_ref, state_ref, keep_ref, *refs):
    sends, states = refs[:-1], refs[-1]
    heads = added_ref.shape[0]
    state = state_ref[...]
    if upper_only:
        state = jnp.where(lax.axis_index("seq") < heads, jnp.zeros_like(state), state)
    both = twice(state)
    for i in range(heads):
        maps = jnp.concatenate([high_ref[i], low_ref[i]], axis=1)
        states[i] = (dot(maps, both) + added_ref[i]).astype(BF16)
    place = lax.rem(lax.axis_index("seq"), heads)
    keep_ref[...] = states[place]
    for r, send in enumerate(sends, 1):
        send[...] = states[other_place(place, r, heads)]


def states_of_upper(*refs):
    group_states(True, *refs)


def states_given(*refs):
    group_states(False, *refs)


def prefix(total, heads):
    count = lax.axis_size("seq")
    groups = [list(range(i, count, heads)) for i in range(heads)]
    me = lax.axis_index("seq") // heads
    totals = lax.all_gather(total, "seq", axis_index_groups=groups)

    def step(d, state):
        longer = jnp.einsum("ik,pkw->iw", totals[d, :, :C], jnp.stack(split(state)), preferred_element_type=F32)
        return jnp.where(d < me, longer + totals[d, :, C:].astype(F32), state)

    start = jnp.zeros((C, C), F32)
    return lax.fori_loop(0, count // heads - 1, step, start).astype(BF16)


def apply_kernel(groups, rows0_ref, rows1_ref, *refs):
    states, (keep_ref, send_ref, held) = refs[:-3], refs[-3:]
    heads = len(states)
    half, tokens, _ = rows0_ref.shape
    block = tokens // groups
    place = lax.rem(lax.axis_index("seq"), heads)
    for r in range(heads):
        held[other_place(place, r, heads)] = states[r][...]
    core = lax.rem(lax.axis_index("head"), 2)
    for out_ref, parity in ((send_ref, 1 - core), (keep_ref, core)):
        for i in range(groups // 2):
            rows = pl.ds(pl.multiple_of((2 * i + parity) * block, block), block)
            for h in range(heads):
                ref = (rows0_ref, rows1_ref)[h // half]
                attended = moved_on(ref[h % half, rows, :C], held[h], ref[h % half, rows, C:])
                out_ref[i, :, h * C : (h + 1) * C] = attended.astype(BF16)


def apply(rows, states, groups):
    _, tokens, _ = rows[0].shape
    heads = len(states)
    here = pl.BlockSpec(memory_space=pltpu.VMEM)
    out = jax.ShapeDtypeStruct((groups // 2, tokens // groups, heads * C), BF16)
    return pl.pallas_call(
        functools.partial(apply_kernel, groups),
        in_specs=[here] * (2 + heads),
        out_specs=[here] * 2,
        out_shape=[out, out],
        scratch_shapes=[pltpu.VMEM((heads, C, C), BF16)],
        compiler_params=pltpu.CompilerParams(vmem_limit_bytes=8 * MIB),
        name="apply",
    )(*rows, *states)


def project_kernel(other, keep_ref, got_ref, w_ref, w2_ref, out_ref):
    pair = lax.axis_index("head") // 2
    index = 1 - pair if other else pair
    out_ref[...] = (dot(keep_ref[index], w_ref[...]) + dot(got_ref[index], w2_ref[...])).astype(out_ref.dtype)


def project(other, keep, got, weight, weight2):
    _, block, depth = keep.shape
    width = weight.shape[1]
    return pl.pallas_call(
        functools.partial(project_kernel, other),
        out_shape=jax.ShapeDtypeStruct((block, width), BF16 if other else F32),
        compiler_params=pltpu.CompilerParams(vmem_limit_bytes=20 * MIB),
        cost_estimate=pl.CostEstimate(
            flops=4 * block * depth * width, bytes_accessed=4 * depth * width, transcendentals=0
        ),
        name="project",
    )(keep, got, weight, weight2)


def swap(x, axis, bit):
    count = lax.axis_size(axis)
    return lax.ppermute(x, axis, [(i, i ^ bit) for i in range(count)])


def body(query, key, value, beta, log_decay, out_weight):
    tokens, heads, _ = key.shape
    count = lax.axis_size("seq")
    flat = lambda x: x.reshape(tokens * heads, C)
    weight2 = swap(out_weight, "head", 1)
    q16, k32, *chunk_maps, own, send1, send2, send3 = local_maps(
        flat(key), flat(value), beta, log_decay, flat(query), heads
    )
    got = [swap(x, "seq", r) for r, x in enumerate((send1, send2, send3), 1)]
    half = heads // 2
    rows0 = row_maps(heads, range(half), q16, k32, *chunk_maps)
    rows1 = row_maps(heads, range(half, heads), q16, k32, *chunk_maps)
    rows0, got = lax.optimization_barrier((rows0, got))
    wide = jax.ShapeDtypeStruct((heads, C, 2 * C), F32)
    square = jax.ShapeDtypeStruct((C, C), BF16)
    squares = jax.ShapeDtypeStruct((heads, C, C), BF16)
    added = jax.ShapeDtypeStruct((heads, C, C), F32)
    held, state = small_call(group_state, [wide, square], own, *got)
    *maps, total = small_call(
        group_prefix, [squares, squares, added, jax.ShapeDtypeStruct((C, 2 * C), BF16)], held
    )
    outs = [square] * heads + [squares]
    if count == 2 * heads:
        lower = swap(state, "seq", heads)
        maps, lower = lax.optimization_barrier((maps, lower))
        keep, *sends = small_call(states_of_upper, outs, *maps, lower)
    else:
        keep, *sends = small_call(states_given, outs, *maps, prefix(total, heads))
    entering = [keep] + [swap(x, "seq", r) for r, x in enumerate(sends[: heads - 1], 1)]
    keep, away = apply((rows0, rows1), entering, lax.axis_size("head"))
    got = swap(away, "head", 1)
    theirs = swap(project(True, keep, got, out_weight, weight2), "head", 2)
    mine = project(False, keep, got, out_weight, weight2)
    return (mine + theirs.astype(F32)).astype(BF16)


def solution(mesh):
    in_specs = (
        P("seq", "head", None),
        P("seq", "head", None),
        P("seq", "head", None),
        P("head", "seq"),
        P("head", "seq"),
        P("head", None),
    )
    out_specs = P(("seq", "head"), None)
    return jax.shard_map(body, mesh=mesh, in_specs=in_specs, out_specs=out_specs, check_vma=False)
```

```python
import functools

import jax
import jax.numpy as jnp
from jax import lax
from jax.experimental import pallas as pl
from jax.experimental.pallas import tpu as pltpu
from jax.sharding import PartitionSpec as P

C = 128
B = 16
F32 = jnp.float32
BF16 = jnp.bfloat16
NN = (((1,), (0,)), ((), ()))
NT = (((1,), (1,)), ((), ()))
TN = (((0,), (0,)), ((), ()))
MIB = 1024 * 1024


def dot(a, b, dims=NN):
    return lax.dot_general(a, b, dims, preferred_element_type=F32)


def split(x):
    high = x.astype(BF16)
    return high, (x - high.astype(F32)).astype(BF16)


def twice(x):
    return jnp.concatenate([x, x], axis=0)


def dot3(a, b):
    (ah, al), (bh, bl) = a, b
    width = bh.shape[1]
    left = jnp.concatenate([ah, al], axis=1)
    if width > C:
        return dot(left, twice(bh)) + dot(ah, bl)
    both = dot(left, twice(jnp.concatenate([bh, bl], axis=1)))
    return both[:, :width] + both[:, width:]


def iotas():
    return (
        lax.broadcasted_iota(jnp.int32, (C, C), 0),
        lax.broadcasted_iota(jnp.int32, (C, C), 1),
    )


def to_column(row, eye):
    return jnp.sum(jnp.where(eye, row, 0.0), axis=1, keepdims=True)


def to_row(column, eye):
    return jnp.sum(jnp.where(eye, column, 0.0), axis=0, keepdims=True)


def inverse_scale(rows):
    return lax.rsqrt(jnp.sum(rows * rows, axis=1, keepdims=True) + 1e-06)


def three(x):
    high, rest = x.astype(BF16), x
    rest = rest - high.astype(F32)
    return (high,) + split(rest)


def running_sums(rows, upper):
    return sum(dot(x, upper) for x in reversed(three(rows)))


def spread_columns(row, eye, ones):
    parts = three(jnp.broadcast_to(row, (16, C)))
    high, middle, low = (
        jnp.where(eye, jnp.concatenate([x] * (C // 16), axis=0), jnp.zeros((), BF16)) for x in parts
    )
    return dot(jnp.concatenate([high, middle], axis=1), twice(ones)) + dot(low, ones)


def base_inverse(lower, row, col):
    on_block = (row // B) == (col // B)
    blocks = jnp.where(on_block, lower, 0.0)
    packed = sum(blocks[i * B : (i + 1) * B] for i in range(1, C // B)) + blocks[:B]
    r, c = row[:B], col[:B]
    found = jnp.where(r == c % B, 1.0, 0.0)
    first = (c // B) * B
    for j in range(B - 1):
        factor = jnp.take_along_axis(packed, first + j, axis=1)
        found = found - factor * found[j : j + 1]
    return jnp.where(on_block, jnp.concatenate([found] * (C // B), axis=0), 0.0)


def odd_rows(x, size):
    return jnp.concatenate([x[i : i + size] for i in range(size, C, 2 * size)], axis=0)


def weave(even, odd, size):
    parts = []
    for i in range(0, C // 2, size):
        parts += [even[i : i + size], odd[i : i + size]]
    return jnp.concatenate(parts, axis=0)


def even_rows(x, size):
    return jnp.concatenate([x[i : i + size] for i in range(0, C, 2 * size)], axis=0)


def inverses(lowers, row, col):
    found = [base_inverse(a, row, col) for a in lowers]
    parts = [split(a) for a in lowers]
    size = B
    while size < C:
        r, c = odd_rows(row, size), odd_rows(col, size)
        mask = ((r // (2 * size)) == (c // (2 * size))) & ((r // size) != (c // size))
        nothing = jnp.zeros((C // 2, C), BF16)
        joins = [tuple(jnp.where(mask, odd_rows(x, size), nothing) for x in part) for part in parts]
        halves = [split(x) for x in found]
        middle = [split(dot3(a, x)) for a, x in zip(joins, halves)]
        middle = [tuple(weave(nothing, x, size) for x in part) for part in middle]
        lows = [dot3(tuple(odd_rows(x, size) for x in h), y) for h, y in zip(halves, middle)]
        found = [weave(even_rows(x, size), odd_rows(x, size) - y, size) for x, y in zip(found, lows)]
        size *= 2
    return found


def fetch(pairs, sems, late):
    copies = [pltpu.make_async_copy(x, y, sems.at[i]) for i, (x, y) in enumerate(pairs)]
    for copy in copies:
        copy.start()
    late.start()
    for copy in copies:
        copy.wait()


def in_hbm(*arrays):
    return [pltpu.with_memory_space_constraint(x, pltpu.HBM) for x in arrays]


def chunk_rows(heads, head, c):
    return pl.ds(c * C * heads + head, C, stride=heads)


def tokens_of(ref, head, c):
    return ref[head : head + 1, c * C : (c + 1) * C]


def per_chunk(ref):
    return jnp.concatenate([ref[:, i : i + C] for i in range(0, ref.shape[1], C)], axis=0)


def local_maps_kernel(heads, batch, k_hbm, v_hbm, beta_hbm, log_hbm, q_hbm, q16, k32, sums_ref, mix_ref, wu_ref, n_ref, own_ref, send_ref, k16, v16, v32, beta_ref, log_ref, all_ref, sems):
    late = pltpu.make_async_copy(q_hbm, q16, sems.at[4])
    fetch(((k_hbm, k16), (log_hbm, log_ref), (beta_hbm, beta_ref), (v_hbm, v16)), sems, late)
    k32[...] = k16[...].astype(F32)
    v32[...] = v16[...].astype(F32)
    chunks = beta_ref.shape[1] // C
    row, col = iotas()
    eye = row == col
    within = row >= col
    strict = row > col
    one = jnp.ones((C, C), BF16)
    eye16 = jnp.where(eye, one, jnp.zeros((), BF16))
    sums = running_sums(per_chunk(log_ref), jnp.where(row <= col, one, jnp.zeros((), BF16)))
    sums_ref[...] = sums
    grown = jnp.exp(sums)
    faded = jnp.exp(sums[:, C - 1 :] - sums)
    betas = per_chunk(beta_ref)
    for start in range(0, heads, batch):
        jobs = [(head, c) for head in range(start, start + batch) for c in range(chunks)]
        lowers, raws, values, fades, lengths = [], [], [], [], []
        for head, c in jobs:
            at = slice(c * heads + head, c * heads + head + 1)
            raw = k32[chunk_rows(heads, head, c), :].astype(BF16)
            raws.append(raw)
            values.append(v32[chunk_rows(heads, head, c), :].astype(BF16))
            both = dot(jnp.concatenate([raw, eye16], axis=0), raw, NT)
            gram, turned = both[:C], both[C:]
            square = to_row(gram, eye) + 1e-06
            scale = lax.rsqrt(square)
            lengths.append(square * scale)
            strength = betas[at] * (scale * scale)
            span = spread_columns(sums[at], eye, one) - sums[at]
            mix = jnp.where(within, jnp.exp(span), 0.0) * strength
            mix_ref[head * chunks + c] = mix
            lowers.append(jnp.where(strict, gram * mix, 0.0))
            fades.append(turned * (strength * faded[at]))
        solved = []
        for i, found in enumerate(inverses(lowers, row, col)):
            at = slice(jobs[i][1] * heads + jobs[i][0], jobs[i][1] * heads + jobs[i][0] + 1)
            kept = dot(jnp.concatenate(split(found * grown[at]), axis=1), twice(raws[i]))
            fresh = dot(jnp.concatenate(split(found * lengths[i]), axis=1), twice(values[i]))
            solved.append(jnp.concatenate([kept, fresh], axis=1))
        maps = []
        for i, (head, c) in enumerate(jobs):
            wu_ref[head * chunks + c] = solved[i]
            both = dot3(split(fades[i]), split(solved[i]))
            end = grown[c * heads + head : c * heads + head + 1, C - 1 :]
            maps.append((jnp.where(eye, end, 0.0) - both[:, :C], both[:, C:]))
        for j in range(batch):
            state = jnp.concatenate(maps[j * chunks], axis=1)
            for c in range(1, chunks):
                n_ref[(start + j) * chunks + c] = state
                moved, fresh = maps[j * chunks + c]
                state = dot3(split(moved), split(state))
                state = jnp.concatenate([state[:, :C], state[:, C:] + fresh], axis=1)
            all_ref[start + j] = state
            send_ref[start + j] = state.astype(BF16)
    place = lax.rem(lax.axis_index("seq"), heads)
    own_ref[...] = all_ref[place]
    late.wait()


def local_maps(key, value, beta, log_decay, query, batch):
    heads, tokens = beta.shape
    count = heads * (tokens // C)
    here = pl.BlockSpec(memory_space=pltpu.VMEM)
    return pl.pallas_call(
        functools.partial(local_maps_kernel, heads, batch),
        in_specs=[pl.BlockSpec(memory_space=pltpu.HBM)] * 5,
        out_specs=[here] * 8,
        out_shape=[
            jax.ShapeDtypeStruct(query.shape, BF16),
            jax.ShapeDtypeStruct(key.shape, F32),
            jax.ShapeDtypeStruct((count, C), F32),
            jax.ShapeDtypeStruct((count, C, C), F32),
            jax.ShapeDtypeStruct((count, C, 2 * C), F32),
            jax.ShapeDtypeStruct((count, C, 2 * C), F32),
            jax.ShapeDtypeStruct((C, 2 * C), F32),
            jax.ShapeDtypeStruct((heads, C, 2 * C), BF16),
        ],
        scratch_shapes=[
            pltpu.VMEM(key.shape, BF16),
            pltpu.VMEM(key.shape, BF16),
            pltpu.VMEM(key.shape, F32),
            pltpu.VMEM(beta.shape, F32),
            pltpu.VMEM(beta.shape, F32),
            pltpu.VMEM((heads, C, 2 * C), F32),
            pltpu.SemaphoreType.DMA((5,)),
        ],
        compiler_params=pltpu.CompilerParams(vmem_limit_bytes=32 * MIB),
        name="local_maps",
    )(*in_hbm(key, value, beta, log_decay, query))


def rows_kernel(heads, mine, q16, k32, sums_ref, mix_ref, wu_ref, n_ref, out_ref, q32):
    q32[...] = q16[...].astype(F32)
    chunks = q16.shape[0] // (heads * C)
    row, col = iotas()
    eye = row == col
    for j, head in enumerate(mine):
        for c in range(chunks):
            i = head * chunks + c
            query, raw = q32[chunk_rows(heads, head, c), :], k32[chunk_rows(heads, head, c), :]
            grown = to_column(jnp.exp(sums_ref[c * heads + head : c * heads + head + 1, :]), eye)
            pairs = dot(query.astype(BF16), raw.astype(BF16), NT) * mix_ref[i]
            both = dot3(split(pairs), split(wu_ref[i]))
            scale = inverse_scale(query)
            reach = (query * grown - both[:, :C]) * scale
            fresh = both[:, C:] * scale
            if c > 0:
                earlier = dot3(split(reach), split(n_ref[i]))
                reach = earlier[:, :C]
                fresh = fresh + earlier[:, C:]
            out_ref[j, c * C : (c + 1) * C, :] = jnp.concatenate([reach, fresh], axis=1)


def row_maps(heads, mine, query, k32, sums, mix, wu, states):
    tokens = query.shape[0] // heads
    here = pl.BlockSpec(memory_space=pltpu.VMEM)
    return pl.pallas_call(
        functools.partial(rows_kernel, heads, mine),
        in_specs=[here] * 6,
        out_specs=here,
        out_shape=jax.ShapeDtypeStruct((len(mine), tokens, 2 * C), F32),
        scratch_shapes=[pltpu.VMEM(query.shape, F32)],
        compiler_params=pltpu.CompilerParams(vmem_limit_bytes=16 * MIB),
        cost_estimate=pl.CostEstimate(flops=2000000000, bytes_accessed=8000000, transcendentals=0),
        name="row_maps",
    )(query, k32, sums, mix, wu, states)


def small_call(kernel, out_shape, *args):
    here = pl.BlockSpec(memory_space=pltpu.VMEM)
    return pl.pallas_call(
        kernel,
        in_specs=[here] * len(args),
        out_specs=[here] * len(out_shape),
        out_shape=out_shape,
        compiler_params=pltpu.CompilerParams(vmem_limit_bytes=8 * MIB),
        name=kernel.__name__,
    )(*args)


def moved_on(maps, state16, added):
    high, low = split(maps)
    return dot(jnp.concatenate([high, low], axis=1), twice(state16)) + added


def group_state(own_ref, got_ref, held, out_ref):
    heads = held.shape[0]
    held[...] = got_ref[...].astype(F32)
    held[lax.rem(lax.axis_index("seq"), heads)] = own_ref[...]
    state = held[0, :, C:].astype(BF16)
    for i in range(1, heads):
        state = moved_on(held[i, :, :C], state, held[i, :, C:]).astype(BF16)
    out_ref[...] = state


def group_prefix(held, high_ref, low_ref, added_ref, total_ref):
    row, col = iotas()
    eye = jnp.where(row == col, 1.0, 0.0)
    total = jnp.concatenate([eye, jnp.zeros((C, C), F32)], axis=1)
    for i in range(held.shape[0]):
        high_ref[i], low_ref[i] = split(total[:, :C])
        added_ref[i] = total[:, C:]
        later = held[i]
        if i == 0:
            total = later
        else:
            total = dot3(split(later[:, :C]), split(total))
            total = jnp.concatenate([total[:, :C], total[:, C:] + later[:, C:]], axis=1)
    total_ref[...] = total.astype(BF16)


def group_states(upper_only, high_ref, low_ref, added_ref, state_ref, out_ref):
    heads = added_ref.shape[0]
    state = state_ref[...]
    if upper_only:
        state = jnp.where(lax.axis_index("seq") < heads, jnp.zeros_like(state), state)
    both = twice(state)
    for i in range(heads):
        maps = jnp.concatenate([high_ref[i], low_ref[i]], axis=1)
        out_ref[i] = (dot(maps, both) + added_ref[i]).astype(BF16)


def states_of_upper(*refs):
    group_states(True, *refs)


def states_given(*refs):
    group_states(False, *refs)


def prefix(total, heads):
    count = lax.axis_size("seq")
    groups = [list(range(i, count, heads)) for i in range(heads)]
    me = lax.axis_index("seq") // heads
    totals = lax.all_gather(total, "seq", axis_index_groups=groups)

    def step(d, state):
        longer = jnp.einsum("ik,pkw->iw", totals[d, :, :C], jnp.stack(split(state)), preferred_element_type=F32)
        return jnp.where(d < me, longer + totals[d, :, C:].astype(F32), state)

    start = jnp.zeros((C, C), F32)
    return lax.fori_loop(0, count // heads - 1, step, start).astype(BF16)


def apply_kernel(groups, rows0_ref, rows1_ref, held, keep_ref, send_ref):
    heads = held.shape[0]
    half, tokens, _ = rows0_ref.shape
    block = tokens // groups
    core = lax.rem(lax.axis_index("head"), 2)
    for out_ref, parity in ((send_ref, 1 - core), (keep_ref, core)):
        for i in range(groups // 2):
            rows = pl.ds(pl.multiple_of((2 * i + parity) * block, block), block)
            for h in range(heads):
                ref = (rows0_ref, rows1_ref)[h // half]
                attended = moved_on(ref[h % half, rows, :C], held[h], ref[h % half, rows, C:])
                out_ref[i, :, h * C : (h + 1) * C] = attended.astype(BF16)


def apply(rows, states, groups):
    _, tokens, _ = rows[0].shape
    heads = states.shape[0]
    here = pl.BlockSpec(memory_space=pltpu.VMEM)
    out = jax.ShapeDtypeStruct((groups // 2, tokens // groups, heads * C), BF16)
    return pl.pallas_call(
        functools.partial(apply_kernel, groups),
        in_specs=[here] * 3,
        out_specs=[here] * 2,
        out_shape=[out, out],
        compiler_params=pltpu.CompilerParams(vmem_limit_bytes=8 * MIB),
        name="apply",
    )(*rows, states)


def project_kernel(other, keep_ref, got_ref, w_ref, w2_ref, out_ref):
    pair = lax.axis_index("head") // 2
    index = 1 - pair if other else pair
    out_ref[...] = (dot(keep_ref[index], w_ref[...]) + dot(got_ref[index], w2_ref[...])).astype(out_ref.dtype)


def project(other, keep, got, weight, weight2):
    _, block, depth = keep.shape
    width = weight.shape[1]
    return pl.pallas_call(
        functools.partial(project_kernel, other),
        out_shape=jax.ShapeDtypeStruct((block, width), BF16 if other else F32),
        compiler_params=pltpu.CompilerParams(vmem_limit_bytes=20 * MIB),
        cost_estimate=pl.CostEstimate(
            flops=4 * block * depth * width, bytes_accessed=4 * depth * width, transcendentals=0
        ),
        name="project",
    )(keep, got, weight, weight2)


def swap(x, axis, bit):
    count = lax.axis_size(axis)
    return lax.ppermute(x, axis, [(i, i ^ bit) for i in range(count)])


def share_out(parts):
    size, count = parts.shape[0], lax.axis_size("seq")
    groups = [list(range(i, i + size)) for i in range(0, count, size)]
    return lax.all_to_all(parts, "seq", 0, 0, axis_index_groups=groups, tiled=True)


def body(query, key, value, beta, log_decay, out_weight):
    tokens, heads, _ = key.shape
    count = lax.axis_size("seq")
    flat = lambda x: x.reshape(tokens * heads, C)
    weight2 = swap(out_weight, "head", 1)
    q16, k32, *chunk_maps, own, send = local_maps(
        flat(key), flat(value), beta, log_decay, flat(query), heads
    )
    got = share_out(send)
    half = heads // 2
    rows0 = row_maps(heads, range(half), q16, k32, *chunk_maps)
    rows1 = row_maps(heads, range(half, heads), q16, k32, *chunk_maps)
    wide = jax.ShapeDtypeStruct((heads, C, 2 * C), F32)
    square = jax.ShapeDtypeStruct((C, C), BF16)
    squares = jax.ShapeDtypeStruct((heads, C, C), BF16)
    added = jax.ShapeDtypeStruct((heads, C, C), F32)
    held, state = small_call(group_state, [wide, square], own, got)
    *maps, total = small_call(
        group_prefix, [squares, squares, added, jax.ShapeDtypeStruct((C, 2 * C), BF16)], held
    )
    if count == 2 * heads:
        lower = swap(state, "seq", heads)
        maps, lower = lax.optimization_barrier((maps, lower))
        (states,) = small_call(states_of_upper, [squares], *maps, lower)
    else:
        (states,) = small_call(states_given, [squares], *maps, prefix(total, heads))
    keep, away = apply((rows0, rows1), share_out(states), lax.axis_size("head"))
    got = swap(away, "head", 1)
    theirs = swap(project(True, keep, got, out_weight, weight2), "head", 2)
    mine = project(False, keep, got, out_weight, weight2)
    return (mine + theirs.astype(F32)).astype(BF16)


def solution(mesh):
    in_specs = (
        P("seq", "head", None),
        P("seq", "head", None),
        P("seq", "head", None),
        P("head", "seq"),
        P("head", "seq"),
        P("head", None),
    )
    out_specs = P(("seq", "head"), None)
    return jax.shard_map(body, mesh=mesh, in_specs=in_specs, out_specs=out_specs, check_vma=False)
```

```python
import functools

import jax
import jax.numpy as jnp
from jax import lax
from jax.experimental import pallas as pl
from jax.experimental.pallas import tpu as pltpu
from jax.sharding import PartitionSpec as P

C = 128
B = 16
F32 = jnp.float32
BF16 = jnp.bfloat16
NN = (((1,), (0,)), ((), ()))
NT = (((1,), (1,)), ((), ()))
TN = (((0,), (0,)), ((), ()))
MIB = 1024 * 1024


def dot(a, b, dims=NN):
    return lax.dot_general(a, b, dims, preferred_element_type=F32)


def split(x):
    high = x.astype(BF16)
    return high, (x - high.astype(F32)).astype(BF16)


def twice(x):
    return jnp.concatenate([x, x], axis=0)


def dot3(a, b):
    (ah, al), (bh, bl) = a, b
    return dot(jnp.concatenate([ah, al, ah], axis=1), jnp.concatenate([bh, bh, bl], axis=0))


def iotas():
    return (
        lax.broadcasted_iota(jnp.int32, (C, C), 0),
        lax.broadcasted_iota(jnp.int32, (C, C), 1),
    )


def to_column(row, eye):
    return jnp.sum(jnp.where(eye, row, 0.0), axis=1, keepdims=True)


def to_row(column, eye):
    return jnp.sum(jnp.where(eye, column, 0.0), axis=0, keepdims=True)


def inverse_scale(rows):
    return lax.rsqrt(jnp.sum(rows * rows, axis=1, keepdims=True) + 1e-06)


def three(x):
    high, rest = x.astype(BF16), x
    rest = rest - high.astype(F32)
    return (high,) + split(rest)


def running_sums(rows, upper):
    return sum(dot(x, upper) for x in reversed(three(rows)))


def spread_columns(row, eye, ones):
    parts = three(jnp.broadcast_to(row, (16, C)))
    high, middle, low = (
        jnp.where(eye, jnp.concatenate([x] * (C // 16), axis=0), jnp.zeros((), BF16)) for x in parts
    )
    return dot(jnp.concatenate([high, middle, low], axis=1), jnp.concatenate([ones] * 3, axis=0))


def base_inverse(lower, row, col):
    on_block = (row // B) == (col // B)
    blocks = jnp.where(on_block, lower, 0.0)
    packed = sum(blocks[i * B : (i + 1) * B] for i in range(1, C // B)) + blocks[:B]
    r, c = row[:B], col[:B]
    found = jnp.where(r == c % B, 1.0, 0.0)
    first = (c // B) * B
    for j in range(B - 1):
        factor = jnp.take_along_axis(packed, first + j, axis=1)
        found = found - factor * found[j : j + 1]
    return jnp.where(on_block, jnp.concatenate([found] * (C // B), axis=0), 0.0)


def odd_rows(x, size):
    return jnp.concatenate([x[i : i + size] for i in range(size, C, 2 * size)], axis=0)


def weave(even, odd, size):
    parts = []
    for i in range(0, C // 2, size):
        parts += [even[i : i + size], odd[i : i + size]]
    return jnp.concatenate(parts, axis=0)


def even_rows(x, size):
    return jnp.concatenate([x[i : i + size] for i in range(0, C, 2 * size)], axis=0)


def inverses(lowers, row, col):
    found = [base_inverse(a, row, col) for a in lowers]
    parts = [split(a) for a in lowers]
    halves = [split(x) for x in found]
    size = B
    while size < C:
        r, c = odd_rows(row, size), odd_rows(col, size)
        mask = ((r // (2 * size)) == (c // (2 * size))) & ((r // size) != (c // size))
        nothing = jnp.zeros((C // 2, C), BF16)
        joins = [tuple(jnp.where(mask, odd_rows(x, size), nothing) for x in part) for part in parts]
        middle = [split(dot3(a, x)) for a, x in zip(joins, halves)]
        middle = [tuple(weave(nothing, x, size) for x in part) for part in middle]
        lows = [dot3(tuple(odd_rows(x, size) for x in h), y) for h, y in zip(halves, middle)]
        lows = [odd_rows(x, size) - y for x, y in zip(found, lows)]
        found = [weave(even_rows(x, size), y, size) for x, y in zip(found, lows)]
        if 2 * size < C:
            halves = [
                tuple(weave(even_rows(x, size), y, size) for x, y in zip(h, split(low)))
                for h, low in zip(halves, lows)
            ]
        size *= 2
    return found


def fetch(pairs, sems, late):
    copies = [pltpu.make_async_copy(x, y, sems.at[i]) for i, (x, y) in enumerate(pairs)]
    for copy in copies:
        copy.start()
    late.start()
    for copy in copies:
        copy.wait()


def in_hbm(*arrays):
    return [pltpu.with_memory_space_constraint(x, pltpu.HBM) for x in arrays]


def chunk_rows(heads, head, c):
    return pl.ds(c * C * heads + head, C, stride=heads)


def tokens_of(ref, head, c):
    return ref[head : head + 1, c * C : (c + 1) * C]


def per_chunk(ref):
    return jnp.concatenate([ref[:, i : i + C] for i in range(0, ref.shape[1], C)], axis=0)


def local_maps_kernel(heads, batch, k_hbm, v_hbm, beta_hbm, log_hbm, q_hbm, q16, k32, sums_ref, mix_ref, wu_ref, n_ref, own_ref, *rest):
    sends, (k16, v16, v32, beta_ref, log_ref, all_ref, sems) = rest[: heads - 1], rest[heads - 1 :]
    late = pltpu.make_async_copy(q_hbm, q16, sems.at[4])
    fetch(((k_hbm, k16), (log_hbm, log_ref), (beta_hbm, beta_ref), (v_hbm, v16)), sems, late)
    k32[...] = k16[...].astype(F32)
    v32[...] = v16[...].astype(F32)
    chunks = beta_ref.shape[1] // C
    row, col = iotas()
    eye = row == col
    within = row >= col
    strict = row > col
    one = jnp.ones((C, C), BF16)
    eye16 = jnp.where(eye, one, jnp.zeros((), BF16))
    sums = running_sums(per_chunk(log_ref), jnp.where(row <= col, one, jnp.zeros((), BF16)))
    sums_ref[...] = sums
    grown = jnp.exp(sums)
    faded = jnp.exp(sums[:, C - 1 :] - sums)
    betas = per_chunk(beta_ref)
    for start in range(0, heads, batch):
        jobs = [(head, c) for head in range(start, start + batch) for c in range(chunks)]
        lowers, raws, values, fades, lengths = [], [], [], [], []
        for head, c in jobs:
            at = slice(c * heads + head, c * heads + head + 1)
            raw = k32[chunk_rows(heads, head, c), :].astype(BF16)
            raws.append(raw)
            values.append(v32[chunk_rows(heads, head, c), :].astype(BF16))
            both = dot(jnp.concatenate([raw, eye16], axis=0), raw, NT)
            gram, turned = both[:C], both[C:]
            square = to_row(gram, eye) + 1e-06
            scale = lax.rsqrt(square)
            lengths.append(square * scale)
            strength = betas[at] * (scale * scale)
            span = spread_columns(sums[at], eye, one) - sums[at]
            mix = jnp.where(within, jnp.exp(span), 0.0) * strength
            mix_ref[head * chunks + c] = mix
            lowers.append(jnp.where(strict, gram * mix, 0.0))
            fades.append(turned * (strength * faded[at]))
        solved = []
        for i, found in enumerate(inverses(lowers, row, col)):
            at = slice(jobs[i][1] * heads + jobs[i][0], jobs[i][1] * heads + jobs[i][0] + 1)
            kept = dot(jnp.concatenate(split(found * grown[at]), axis=1), twice(raws[i]))
            fresh = dot(jnp.concatenate(split(found * lengths[i]), axis=1), twice(values[i]))
            solved.append(jnp.concatenate([kept, fresh], axis=1))
        maps = []
        for i, (head, c) in enumerate(jobs):
            wu_ref[head * chunks + c] = solved[i]
            both = dot3(split(fades[i]), split(solved[i]))
            end = grown[c * heads + head : c * heads + head + 1, C - 1 :]
            maps.append((jnp.where(eye, end, 0.0) - both[:, :C], both[:, C:]))
        for j in range(batch):
            state = jnp.concatenate(maps[j * chunks], axis=1)
            for c in range(1, chunks):
                n_ref[(start + j) * chunks + c] = state
                moved, fresh = maps[j * chunks + c]
                state = dot3(split(moved), split(state))
                state = jnp.concatenate([state[:, :C], state[:, C:] + fresh], axis=1)
            all_ref[start + j] = state
    place = lax.rem(lax.axis_index("seq"), heads)
    own_ref[...] = all_ref[place]
    for r in range(1, heads):
        sends[r - 1][...] = all_ref[other_place(place, r, heads)].astype(BF16)
    late.wait()


def other_place(place, r, heads):
    result = place
    for i in range(heads):
        result = jnp.where(place == i, i ^ r, result)
    return result


def local_maps(key, value, beta, log_decay, query, batch):
    heads, tokens = beta.shape
    count = heads * (tokens // C)
    here = pl.BlockSpec(memory_space=pltpu.VMEM)
    return pl.pallas_call(
        functools.partial(local_maps_kernel, heads, batch),
        in_specs=[pl.BlockSpec(memory_space=pltpu.HBM)] * 5,
        out_specs=[here] * (6 + heads),
        out_shape=[
            jax.ShapeDtypeStruct(query.shape, BF16),
            jax.ShapeDtypeStruct(key.shape, F32),
            jax.ShapeDtypeStruct((count, C), F32),
            jax.ShapeDtypeStruct((count, C, C), F32),
            jax.ShapeDtypeStruct((count, C, 2 * C), F32),
            jax.ShapeDtypeStruct((count, C, 2 * C), F32),
            jax.ShapeDtypeStruct((C, 2 * C), F32),
        ]
        + [jax.ShapeDtypeStruct((C, 2 * C), BF16)] * (heads - 1),
        scratch_shapes=[
            pltpu.VMEM(key.shape, BF16),
            pltpu.VMEM(key.shape, BF16),
            pltpu.VMEM(key.shape, F32),
            pltpu.VMEM(beta.shape, F32),
            pltpu.VMEM(beta.shape, F32),
            pltpu.VMEM((heads, C, 2 * C), F32),
            pltpu.SemaphoreType.DMA((5,)),
        ],
        compiler_params=pltpu.CompilerParams(vmem_limit_bytes=32 * MIB),
        name="local_maps",
    )(*in_hbm(key, value, beta, log_decay, query))


def rows_kernel(heads, mine, q16, k32, sums_ref, mix_ref, wu_ref, n_ref, out_ref, q32):
    q32[...] = q16[...].astype(F32)
    chunks = q16.shape[0] // (heads * C)
    row, col = iotas()
    eye = row == col
    for j, head in enumerate(mine):
        for c in range(chunks):
            i = head * chunks + c
            query, raw = q32[chunk_rows(heads, head, c), :], k32[chunk_rows(heads, head, c), :]
            grown = to_column(jnp.exp(sums_ref[c * heads + head : c * heads + head + 1, :]), eye)
            pairs = dot(query.astype(BF16), raw.astype(BF16), NT) * mix_ref[i]
            both = dot3(split(pairs), split(wu_ref[i]))
            scale = inverse_scale(query)
            reach = (query * grown - both[:, :C]) * scale
            fresh = both[:, C:] * scale
            if c > 0:
                earlier = dot3(split(reach), split(n_ref[i]))
                reach = earlier[:, :C]
                fresh = fresh + earlier[:, C:]
            out_ref[j, c * C : (c + 1) * C, :] = jnp.concatenate([reach, fresh], axis=1)


def row_maps(heads, mine, query, k32, sums, mix, wu, states):
    tokens = query.shape[0] // heads
    here = pl.BlockSpec(memory_space=pltpu.VMEM)
    return pl.pallas_call(
        functools.partial(rows_kernel, heads, mine),
        in_specs=[here] * 6,
        out_specs=here,
        out_shape=jax.ShapeDtypeStruct((len(mine), tokens, 2 * C), F32),
        scratch_shapes=[pltpu.VMEM(query.shape, F32)],
        compiler_params=pltpu.CompilerParams(vmem_limit_bytes=16 * MIB),
        cost_estimate=pl.CostEstimate(flops=2000000000, bytes_accessed=8000000, transcendentals=0),
        name="row_maps",
    )(query, k32, sums, mix, wu, states)


def small_call(kernel, out_shape, *args):
    here = pl.BlockSpec(memory_space=pltpu.VMEM)
    return pl.pallas_call(
        kernel,
        in_specs=[here] * len(args),
        out_specs=[here] * len(out_shape),
        out_shape=out_shape,
        compiler_params=pltpu.CompilerParams(vmem_limit_bytes=8 * MIB),
        name=kernel.__name__,
    )(*args)


def moved_on(maps, state16, added):
    high, low = split(maps)
    return dot(jnp.concatenate([high, low], axis=1), twice(state16)) + added


def in_order(own_ref, got_refs, held):
    heads = held.shape[0]
    place = lax.rem(lax.axis_index("seq"), heads)
    held[place] = own_ref[...]
    for r, got in enumerate(got_refs, 1):
        held[other_place(place, r, heads)] = got[...].astype(F32)
    return place


def group_state(own_ref, *refs):
    got_refs, (held, out_ref) = refs[:-2], refs[-2:]
    in_order(own_ref, got_refs, held)
    state = held[0, :, C:].astype(BF16)
    for i in range(1, held.shape[0]):
        state = moved_on(held[i, :, :C], state, held[i, :, C:]).astype(BF16)
    out_ref[...] = state


def group_prefix(held, high_ref, low_ref, added_ref, total_ref):
    row, col = iotas()
    eye = jnp.where(row == col, 1.0, 0.0)
    total = jnp.concatenate([eye, jnp.zeros((C, C), F32)], axis=1)
    for i in range(held.shape[0]):
        high_ref[i], low_ref[i] = split(total[:, :C])
        added_ref[i] = total[:, C:]
        later = held[i]
        if i == 0:
            total = later
        else:
            total = dot3(split(later[:, :C]), split(total))
            total = jnp.concatenate([total[:, :C], total[:, C:] + later[:, C:]], axis=1)
    total_ref[...] = total.astype(BF16)


def group_states(upper_only, high_ref, low_ref, added_ref, state_ref, keep_ref, *refs):
    sends, states = refs[:-1], refs[-1]
    heads = added_ref.shape[0]
    state = state_ref[...]
    if upper_only:
        state = jnp.where(lax.axis_index("seq") < heads, jnp.zeros_like(state), state)
    both = twice(state)
    for i in range(heads):
        maps = jnp.concatenate([high_ref[i], low_ref[i]], axis=1)
        states[i] = (dot(maps, both) + added_ref[i]).astype(BF16)
    place = lax.rem(lax.axis_index("seq"), heads)
    keep_ref[...] = states[place]
    for r, send in enumerate(sends, 1):
        send[...] = states[other_place(place, r, heads)]


def states_of_upper(*refs):
    group_states(True, *refs)


def states_given(*refs):
    group_states(False, *refs)


def prefix(total, heads):
    count = lax.axis_size("seq")
    groups = [list(range(i, count, heads)) for i in range(heads)]
    me = lax.axis_index("seq") // heads
    totals = lax.all_gather(total, "seq", axis_index_groups=groups)

    def step(d, state):
        longer = jnp.einsum("ik,pkw->iw", totals[d, :, :C], jnp.stack(split(state)), preferred_element_type=F32)
        return jnp.where(d < me, longer + totals[d, :, C:].astype(F32), state)

    start = jnp.zeros((C, C), F32)
    return lax.fori_loop(0, count // heads - 1, step, start).astype(BF16)


def apply_kernel(groups, rows0_ref, rows1_ref, *refs):
    states, (keep_ref, send_ref, held) = refs[:-3], refs[-3:]
    heads = len(states)
    half, tokens, _ = rows0_ref.shape
    block = tokens // groups
    place = lax.rem(lax.axis_index("seq"), heads)
    for r in range(heads):
        held[other_place(place, r, heads)] = states[r][...]
    core = lax.rem(lax.axis_index("head"), 2)
    for out_ref, parity in ((send_ref, 1 - core), (keep_ref, core)):
        for i in range(groups // 2):
            rows = pl.ds(pl.multiple_of((2 * i + parity) * block, block), block)
            for h in range(heads):
                ref = (rows0_ref, rows1_ref)[h // half]
                attended = moved_on(ref[h % half, rows, :C], held[h], ref[h % half, rows, C:])
                out_ref[i, :, h * C : (h + 1) * C] = attended.astype(BF16)


def apply(rows, states, groups):
    _, tokens, _ = rows[0].shape
    heads = len(states)
    here = pl.BlockSpec(memory_space=pltpu.VMEM)
    out = jax.ShapeDtypeStruct((groups // 2, tokens // groups, heads * C), BF16)
    return pl.pallas_call(
        functools.partial(apply_kernel, groups),
        in_specs=[here] * (2 + heads),
        out_specs=[here] * 2,
        out_shape=[out, out],
        scratch_shapes=[pltpu.VMEM((heads, C, C), BF16)],
        compiler_params=pltpu.CompilerParams(vmem_limit_bytes=8 * MIB),
        name="apply",
    )(*rows, *states)


def project_kernel(other, start, keep_ref, got_ref, w_ref, w2_ref, out_ref):
    pair = lax.axis_index("head") // 2
    index = 1 - pair if other else pair
    columns = slice(start, start + out_ref.shape[1])
    shares = dot(keep_ref[index], w_ref[:, columns]) + dot(got_ref[index], w2_ref[:, columns])
    out_ref[...] = shares.astype(out_ref.dtype)


def project(other, start, width, keep, got, weight, weight2):
    _, block, depth = keep.shape
    return pl.pallas_call(
        functools.partial(project_kernel, other, start),
        out_shape=jax.ShapeDtypeStruct((block, width), BF16 if other else F32),
        compiler_params=pltpu.CompilerParams(vmem_limit_bytes=20 * MIB),
        cost_estimate=pl.CostEstimate(
            flops=4 * block * depth * width, bytes_accessed=4 * depth * width, transcendentals=0
        ),
        name="project",
    )(keep, got, weight, weight2)


def add_kernel(mine_ref, theirs_ref, *refs):
    refs[-1][...] = (mine_ref[...] + theirs_ref[...].astype(F32)).astype(BF16)


def add_part(index, parts, mine, theirs, earlier):
    block, width = mine.shape
    here = pl.BlockSpec(memory_space=pltpu.VMEM)
    return pl.pallas_call(
        add_kernel,
        grid=(1,),
        in_specs=[here, here] + [pl.BlockSpec(memory_space=pl.ANY)] * len(earlier),
        out_specs=pl.BlockSpec((block, width), lambda i: (0, index)),
        out_shape=jax.ShapeDtypeStruct((block, width * parts), BF16),
        input_output_aliases={2: 0} if earlier else {},
        compiler_params=pltpu.CompilerParams(vmem_limit_bytes=8 * MIB),
        name="add_part",
    )(mine, theirs, *earlier)


def swap(x, axis, bit):
    count = lax.axis_size(axis)
    return lax.ppermute(x, axis, [(i, i ^ bit) for i in range(count)])


def body(query, key, value, beta, log_decay, out_weight):
    tokens, heads, _ = key.shape
    count = lax.axis_size("seq")
    flat = lambda x: x.reshape(tokens * heads, C)
    weight2 = swap(out_weight, "head", 1)
    q16, k32, *chunk_maps, own, send1, send2, send3 = local_maps(
        flat(key), flat(value), beta, log_decay, flat(query), heads
    )
    got = [swap(x, "seq", r) for r, x in enumerate((send1, send2, send3), 1)]
    half = heads // 2
    rows0 = row_maps(heads, range(half), q16, k32, *chunk_maps)
    rows1 = row_maps(heads, range(half, heads), q16, k32, *chunk_maps)
    rows0, got = lax.optimization_barrier((rows0, got))
    wide = jax.ShapeDtypeStruct((heads, C, 2 * C), F32)
    square = jax.ShapeDtypeStruct((C, C), BF16)
    squares = jax.ShapeDtypeStruct((heads, C, C), BF16)
    added = jax.ShapeDtypeStruct((heads, C, C), F32)
    held, state = small_call(group_state, [wide, square], own, *got)
    *maps, total = small_call(
        group_prefix, [squares, squares, added, jax.ShapeDtypeStruct((C, 2 * C), BF16)], held
    )
    outs = [square] * heads + [squares]
    if count == 2 * heads:
        lower = swap(state, "seq", heads)
        maps, lower = lax.optimization_barrier((maps, lower))
        keep, *sends = small_call(states_of_upper, outs, *maps, lower)
    else:
        keep, *sends = small_call(states_given, outs, *maps, prefix(total, heads))
    entering = [keep] + [swap(x, "seq", r) for r, x in enumerate(sends[: heads - 1], 1)]
    keep, away = apply((rows0, rows1), entering, lax.axis_size("head"))
    got = swap(away, "head", 1)
    parts = 2
    width = out_weight.shape[1] // parts
    ranges = [(i * width, width) for i in range(parts)]
    args = (keep, got, out_weight, weight2)
    theirs = [swap(project(True, *x, *args), "head", 2) for x in ranges]
    mine = [project(False, *x, *args) for x in ranges]
    mixed = []
    for i in range(parts):
        mixed = [add_part(i, parts, mine[i], theirs[i], mixed)]
    return mixed[0]


def solution(mesh):
    in_specs = (
        P("seq", "head", None),
        P("seq", "head", None),
        P("seq", "head", None),
        P("head", "seq"),
        P("head", "seq"),
        P("head", None),
    )
    out_specs = P(("seq", "head"), None)
    return jax.shard_map(body, mesh=mesh, in_specs=in_specs, out_specs=out_specs, check_vma=False)
```

```python
import functools

import jax
import jax.numpy as jnp
from jax import lax
from jax.experimental import pallas as pl
from jax.experimental.pallas import tpu as pltpu
from jax.sharding import PartitionSpec as P

C = 128
B = 16
F32 = jnp.float32
BF16 = jnp.bfloat16
NN = (((1,), (0,)), ((), ()))
NT = (((1,), (1,)), ((), ()))
TN = (((0,), (0,)), ((), ()))
MIB = 1024 * 1024


def dot(a, b, dims=NN):
    return lax.dot_general(a, b, dims, preferred_element_type=F32)


def split(x):
    high = x.astype(BF16)
    return high, (x - high.astype(F32)).astype(BF16)


def twice(x):
    return jnp.concatenate([x, x], axis=0)


def dot3(a, b):
    (ah, al), (bh, bl) = a, b
    width = bh.shape[1]
    left = jnp.concatenate([ah, al], axis=1)
    if width > C:
        return dot(left, twice(bh)) + dot(ah, bl)
    both = dot(left, twice(jnp.concatenate([bh, bl], axis=1)))
    return both[:, :width] + both[:, width:]


def iotas():
    return (
        lax.broadcasted_iota(jnp.int32, (C, C), 0),
        lax.broadcasted_iota(jnp.int32, (C, C), 1),
    )


def to_column(row, eye):
    return jnp.sum(jnp.where(eye, row, 0.0), axis=1, keepdims=True)


def to_row(column, eye):
    return jnp.sum(jnp.where(eye, column, 0.0), axis=0, keepdims=True)


def inverse_scale(rows):
    return lax.rsqrt(jnp.sum(rows * rows, axis=1, keepdims=True) + 1e-06)


def three(x):
    high, rest = x.astype(BF16), x
    rest = rest - high.astype(F32)
    return (high,) + split(rest)


def running_sums(rows, upper):
    return sum(dot(x, upper) for x in reversed(three(rows)))


def spread_columns(row, eye, ones):
    parts = three(jnp.broadcast_to(row, (16, C)))
    high, middle, low = (
        jnp.where(eye, jnp.concatenate([x] * (C // 16), axis=0), jnp.zeros((), BF16)) for x in parts
    )
    return dot(jnp.concatenate([high, middle], axis=1), twice(ones)) + dot(low, ones)


def base_inverse(lower, row, col):
    on_block = (row // B) == (col // B)
    blocks = jnp.where(on_block, lower, 0.0)
    packed = sum(blocks[i * B : (i + 1) * B] for i in range(1, C // B)) + blocks[:B]
    r, c = row[:B], col[:B]
    found = jnp.where(r == c % B, 1.0, 0.0)
    first = (c // B) * B
    for j in range(B - 1):
        factor = jnp.take_along_axis(packed, first + j, axis=1)
        found = found - factor * found[j : j + 1]
    return jnp.where(on_block, jnp.concatenate([found] * (C // B), axis=0), 0.0)


def odd_rows(x, size):
    return jnp.concatenate([x[i : i + size] for i in range(size, C, 2 * size)], axis=0)


def weave(even, odd, size):
    parts = []
    for i in range(0, C // 2, size):
        parts += [even[i : i + size], odd[i : i + size]]
    return jnp.concatenate(parts, axis=0)


def even_rows(x, size):
    return jnp.concatenate([x[i : i + size] for i in range(0, C, 2 * size)], axis=0)


def inverses(lowers, row, col):
    found = [base_inverse(a, row, col) for a in lowers]
    parts = [split(a) for a in lowers]
    halves = [split(x) for x in found]
    size = B
    while size < C:
        r, c = odd_rows(row, size), odd_rows(col, size)
        mask = ((r // (2 * size)) == (c // (2 * size))) & ((r // size) != (c // size))
        nothing = jnp.zeros((C // 2, C), BF16)
        joins = [tuple(jnp.where(mask, odd_rows(x, size), nothing) for x in part) for part in parts]
        middle = [split(dot3(a, x)) for a, x in zip(joins, halves)]
        middle = [tuple(weave(nothing, x, size) for x in part) for part in middle]
        lows = [dot3(tuple(odd_rows(x, size) for x in h), y) for h, y in zip(halves, middle)]
        lows = [odd_rows(x, size) - y for x, y in zip(found, lows)]
        found = [weave(even_rows(x, size), y, size) for x, y in zip(found, lows)]
        if 2 * size < C:
            halves = [
                tuple(weave(even_rows(x, size), y, size) for x, y in zip(h, split(low)))
                for h, low in zip(halves, lows)
            ]
        size *= 2
    return found


def fetch(pairs, sems, late):
    copies = [pltpu.make_async_copy(x, y, sems.at[i]) for i, (x, y) in enumerate(pairs)]
    for copy in copies:
        copy.start()
    late.start()
    for copy in copies:
        copy.wait()


def in_hbm(*arrays):
    return [pltpu.with_memory_space_constraint(x, pltpu.HBM) for x in arrays]


def chunk_rows(heads, head, c):
    return pl.ds(c * C * heads + head, C, stride=heads)


def tokens_of(ref, head, c):
    return ref[head : head + 1, c * C : (c + 1) * C]


def per_chunk(ref):
    return jnp.concatenate([ref[:, i : i + C] for i in range(0, ref.shape[1], C)], axis=0)


def local_maps_kernel(
    heads, k_hbm, v_hbm, beta_hbm, log_hbm, q_hbm, q16, k32, sums_ref, mix_ref, wu_ref, n_ref, send_ref,
    k16, v16, v32, beta_ref, log_ref, sems,
):
    late = pltpu.make_async_copy(q_hbm, q16, sems.at[4])
    fetch(((k_hbm, k16), (log_hbm, log_ref), (beta_hbm, beta_ref), (v_hbm, v16)), sems, late)
    k32[...] = k16[...].astype(F32)
    v32[...] = v16[...].astype(F32)
    chunks = beta_ref.shape[1] // C
    row, col = iotas()
    eye = row == col
    within = row >= col
    strict = row > col
    one = jnp.ones((C, C), BF16)
    eye16 = jnp.where(eye, one, jnp.zeros((), BF16))
    sums = running_sums(per_chunk(log_ref), jnp.where(row <= col, one, jnp.zeros((), BF16)))
    sums_ref[...] = sums
    grown = jnp.exp(sums)
    faded = jnp.exp(sums[:, C - 1 :] - sums)
    betas = per_chunk(beta_ref)
    jobs = [(head, c) for head in range(heads) for c in range(chunks)]
    spots = [slice(c * heads + head, c * heads + head + 1) for head, c in jobs]
    lowers, raws, values, fades, lengths = [], [], [], [], []
    for i, (head, c) in enumerate(jobs):
        raw = k32[chunk_rows(heads, head, c), :].astype(BF16)
        raws.append(raw)
        values.append(v32[chunk_rows(heads, head, c), :].astype(BF16))
        both = dot(jnp.concatenate([raw, eye16], axis=0), raw, NT)
        gram, turned = both[:C], both[C:]
        square = to_row(gram, eye) + 1e-06
        scale = lax.rsqrt(square)
        lengths.append(square * scale)
        strength = betas[spots[i]] * (scale * scale)
        span = spread_columns(sums[spots[i]], eye, one) - sums[spots[i]]
        mix = jnp.where(within, jnp.exp(span), 0.0) * strength
        mix_ref[i] = mix
        lowers.append(jnp.where(strict, gram * mix, 0.0))
        fades.append(turned * (strength * faded[spots[i]]))
    solved = []
    for i, found in enumerate(inverses(lowers, row, col)):
        kept = dot(jnp.concatenate(split(found * grown[spots[i]]), axis=1), twice(raws[i]))
        fresh = dot(jnp.concatenate(split(found * lengths[i]), axis=1), twice(values[i]))
        solved.append(jnp.concatenate([kept, fresh], axis=1))
    maps = []
    for i in range(len(jobs)):
        wu_ref[i] = solved[i]
        both = dot3(split(fades[i]), split(solved[i]))
        maps.append((jnp.where(eye, grown[spots[i], C - 1 :], 0.0) - both[:, :C], both[:, C:]))
    place = lax.rem(lax.axis_index("seq"), heads)
    for head in range(heads):
        state = jnp.concatenate(maps[head * chunks], axis=1)
        for c in range(1, chunks):
            n_ref[head * chunks + c] = state
            moved, fresh = maps[head * chunks + c]
            state = dot3(split(moved), split(state))
            state = jnp.concatenate([state[:, :C], state[:, C:] + fresh], axis=1)
        send_ref[other_place(place, head, heads)] = state.astype(BF16)
    late.wait()


def other_place(place, r, heads):
    result = place
    for i in range(heads):
        result = jnp.where(place == i, i ^ r, result)
    return result


def local_maps(key, value, beta, log_decay, query):
    heads, tokens = beta.shape
    count = heads * (tokens // C)
    here = pl.BlockSpec(memory_space=pltpu.VMEM)
    return pl.pallas_call(
        functools.partial(local_maps_kernel, heads),
        in_specs=[pl.BlockSpec(memory_space=pltpu.HBM)] * 5,
        out_specs=[here] * 7,
        out_shape=[
            jax.ShapeDtypeStruct(query.shape, BF16),
            jax.ShapeDtypeStruct(key.shape, F32),
            jax.ShapeDtypeStruct((count, C), F32),
            jax.ShapeDtypeStruct((count, C, C), F32),
            jax.ShapeDtypeStruct((count, C, 2 * C), F32),
            jax.ShapeDtypeStruct((count, C, 2 * C), F32),
            jax.ShapeDtypeStruct((heads, C, 2 * C), BF16),
        ],
        scratch_shapes=[
            pltpu.VMEM(key.shape, BF16),
            pltpu.VMEM(key.shape, BF16),
            pltpu.VMEM(key.shape, F32),
            pltpu.VMEM(beta.shape, F32),
            pltpu.VMEM(beta.shape, F32),
            pltpu.SemaphoreType.DMA((5,)),
        ],
        compiler_params=pltpu.CompilerParams(vmem_limit_bytes=32 * MIB),
        name="local_maps",
    )(*in_hbm(key, value, beta, log_decay, query))


def on_core(core):
    return lax.rem(lax.axis_index("head"), 2) == core


def rows_kernel(heads, mine, q16, k32, sums_ref, mix_ref, wu_ref, n_ref, keep_ref, send_ref, q32):
    q32[...] = q16[...].astype(F32)
    chunks = q16.shape[0] // (heads * C)
    row, col = iotas()
    eye = row == col
    for j, head in enumerate(mine):
        for c in range(chunks):
            i = head * chunks + c
            query, raw = q32[chunk_rows(heads, head, c), :], k32[chunk_rows(heads, head, c), :]
            grown = to_column(jnp.exp(sums_ref[c * heads + head : c * heads + head + 1, :]), eye)
            pairs = dot(query.astype(BF16), raw.astype(BF16), NT) * mix_ref[i]
            both = dot3(split(pairs), split(wu_ref[i]))
            scale = inverse_scale(query)
            reach = (query * grown - both[:, :C]) * scale
            fresh = both[:, C:] * scale
            if c > 0:
                earlier = dot3(split(reach), split(n_ref[i]))
                reach = earlier[:, :C]
                fresh = fresh + earlier[:, C:]
            for ref, core in ((keep_ref, c % 2), (send_ref, 1 - c % 2)):

                @pl.when(on_core(core))
                def _(ref=ref, reach=reach, fresh=fresh):
                    ref[c // 2, j, :, :C] = reach
                    ref[c // 2, j, :, C:] = fresh


def row_maps(heads, mine, query, k32, sums, mix, wu, states):
    chunks = query.shape[0] // (heads * C)
    here = pl.BlockSpec(memory_space=pltpu.VMEM)
    out = jax.ShapeDtypeStruct((chunks // 2, len(mine), C, 2 * C), F32)
    return pl.pallas_call(
        functools.partial(rows_kernel, heads, mine),
        in_specs=[here] * 6,
        out_specs=[here] * 2,
        out_shape=[out, out],
        scratch_shapes=[pltpu.VMEM(query.shape, F32)],
        compiler_params=pltpu.CompilerParams(vmem_limit_bytes=16 * MIB),
        cost_estimate=pl.CostEstimate(flops=2000000000, bytes_accessed=8000000, transcendentals=0),
        name="row_maps",
    )(query, k32, sums, mix, wu, states)


def small_call(kernel, out_shape, *args):
    here = pl.BlockSpec(memory_space=pltpu.VMEM)
    return pl.pallas_call(
        kernel,
        in_specs=[here] * len(args),
        out_specs=[here] * len(out_shape),
        out_shape=out_shape,
        compiler_params=pltpu.CompilerParams(vmem_limit_bytes=8 * MIB),
        name=kernel.__name__,
    )(*args)


def moved_on(maps, state16, added):
    high, low = split(maps)
    return dot(jnp.concatenate([high, low], axis=1), twice(state16)) + added


def gather_cores(mine_ref, other_ref, *out_refs):
    for first, second, core in ((mine_ref, other_ref, 0), (other_ref, mine_ref, 1)):

        @pl.when(on_core(core))
        def _(first=first, second=second):
            for r, out_ref in enumerate(out_refs):
                out_ref[0] = first[r]
                out_ref[1] = second[r]


def times_parts(maps16, x):
    width = x.shape[1]
    both = dot(maps16, jnp.concatenate(split(x), axis=1))
    return both[:, :width] + both[:, width:]


def group_state(*refs):
    parts, (held, out_ref) = refs[:-2], refs[-2:]
    heads = len(parts)
    place = lax.rem(lax.axis_index("seq"), heads)
    for r, part in enumerate(parts):
        member = other_place(place, r, heads)
        for g in range(2):
            held[g * heads + member] = part[g]
    for g in range(2):
        state = held[g * heads, :, C:].astype(F32)
        for i in range(g * heads + 1, (g + 1) * heads):
            state = times_parts(held[i, :, :C], state) + held[i, :, C:].astype(F32)
        out_ref[g] = state.astype(BF16)


def group_prefix(held, high_ref, low_ref, added_ref, total_ref):
    heads = held.shape[0] // 2
    row, col = iotas()
    eye = jnp.where(row == col, 1.0, 0.0)
    for g in range(2):
        total = jnp.concatenate([eye, jnp.zeros((C, C), F32)], axis=1)
        for i in range(g * heads, (g + 1) * heads):
            high_ref[i], low_ref[i] = split(total[:, :C])
            added_ref[i] = total[:, C:]
            if i == g * heads:
                total = held[i].astype(F32)
            else:
                total = times_parts(held[i, :, :C], total)
                total = jnp.concatenate([total[:, :C], total[:, C:] + held[i, :, C:].astype(F32)], axis=1)
        total_ref[g] = total.astype(BF16)


def group_states(upper_only, high_ref, low_ref, added_ref, state_ref, *refs):
    outs, states = refs[:-1], refs[-1]
    heads = len(outs)
    for g in range(2):
        state = state_ref[g]
        if upper_only:
            state = jnp.where(lax.axis_index("seq") < heads, jnp.zeros_like(state), state)
        both = twice(state)
        for i in range(g * heads, (g + 1) * heads):
            maps = jnp.concatenate([high_ref[i], low_ref[i]], axis=1)
            states[i] = (dot(maps, both) + added_ref[i]).astype(BF16)
    place = lax.rem(lax.axis_index("seq"), heads)
    for r, out_ref in enumerate(outs):
        member = other_place(place, r, heads)
        for g in range(2):
            out_ref[g] = states[g * heads + member]


def states_of_upper(*refs):
    group_states(True, *refs)


def states_given(*refs):
    group_states(False, *refs)


def gather_heads(*refs):
    parts, out_ref = refs[:-1], refs[-1]
    heads = len(parts)
    place = lax.rem(lax.axis_index("seq"), heads)
    for r, part in enumerate(parts):
        head = other_place(place, r, heads)
        for g in range(2):
            out_ref[g * heads + head] = part[g]


def prefix(total, heads):
    count = lax.axis_size("seq")
    groups = [list(range(i, count, heads)) for i in range(heads)]
    me = lax.axis_index("seq") // heads
    totals = lax.all_gather(total, "seq", axis_index_groups=groups)

    def step(d, state):
        parts = jnp.stack(split(state))
        longer = jnp.einsum("gik,pgkw->giw", totals[d, :, :, :C], parts, preferred_element_type=F32)
        return jnp.where(d < me, longer + totals[d, :, :, C:].astype(F32), state)

    start = jnp.zeros((2, C, C), F32)
    return lax.fori_loop(0, count // heads - 1, step, start).astype(BF16)


def share_of(block, rows, st_ref, w_ref, w2_ref):
    heads = st_ref.shape[0] // 2
    core = lax.rem(lax.axis_index("head"), 2)
    sums = []
    for refs, first, weight in ((rows[:2], core, w_ref), (rows[2:], 1 - core, w2_ref)):
        attended = []
        for h in range(heads):
            ref = refs[h // (heads // 2)]
            state = st_ref[first * heads + h]
            j = h % (heads // 2)
            attended.append(moved_on(ref[block, j, :, :C], state, ref[block, j, :, C:]).astype(BF16))
        sums.append(dot(jnp.concatenate(attended, axis=1), weight[...]))
    return sums[0] + sums[1]


def share_out_kernel(core, rows0, rows1, rows2, rows3, st_ref, w_ref, w2_ref, *refs):
    @pl.when(on_core(core))
    def _():
        block = 1 - lax.axis_index("head") // 2
        refs[-1][...] = share_of(block, (rows0, rows1, rows2, rows3), st_ref, w_ref, w2_ref).astype(BF16)

    if len(refs) > 1:

        @pl.when(on_core(1 - core))
        def _():
            refs[-1][...] = refs[0][...]


def share_out(core, rows, states, weight, weight2, earlier):
    here = pl.BlockSpec(memory_space=pltpu.VMEM)
    width = weight.shape[1]
    return pl.pallas_call(
        functools.partial(share_out_kernel, core),
        in_specs=[here] * (7 + len(earlier)),
        out_specs=here,
        out_shape=jax.ShapeDtypeStruct((C, width), BF16),
        compiler_params=pltpu.CompilerParams(vmem_limit_bytes=16 * MIB),
        cost_estimate=pl.CostEstimate(
            flops=4 * C * weight.size, bytes_accessed=4 * weight.size, transcendentals=0
        ),
        name="share_out",
    )(*rows, states, weight, weight2, *earlier)


def share_here_kernel(rows0, rows1, rows2, rows3, st0_ref, st1_ref, w_ref, w2_ref, out_ref):
    for core, st_ref in ((0, st0_ref), (1, st1_ref)):

        @pl.when(on_core(core))
        def _(st_ref=st_ref):
            block = lax.axis_index("head") // 2
            out_ref[...] = share_of(block, (rows0, rows1, rows2, rows3), st_ref, w_ref, w2_ref)


def share_here(rows, states0, states1, weight, weight2):
    here = pl.BlockSpec(memory_space=pltpu.VMEM)
    return pl.pallas_call(
        share_here_kernel,
        in_specs=[here] * 8,
        out_specs=here,
        out_shape=jax.ShapeDtypeStruct((C, weight.shape[1]), F32),
        compiler_params=pltpu.CompilerParams(vmem_limit_bytes=16 * MIB),
        cost_estimate=pl.CostEstimate(
            flops=4 * C * weight.size, bytes_accessed=4 * weight.size, transcendentals=0
        ),
        name="share_here",
    )(*rows, states0, states1, weight, weight2)


def swap(x, axis, bit):
    count = lax.axis_size(axis)
    return lax.ppermute(x, axis, [(i, i ^ bit) for i in range(count)])


def swap_odd(x, bit):
    count, groups = lax.axis_size("seq"), lax.axis_size("head")
    pairs = [(i * groups + g, (i ^ bit) * groups + g) for i in range(count) for g in range(1, groups, 2)]
    return lax.ppermute(x, ("seq", "head"), pairs)


def hand_back(x):
    return lax.ppermute(x, "head", [(g, g - 1) for g in range(1, lax.axis_size("head"), 2)])


def body(query, key, value, beta, log_decay, out_weight):
    tokens, heads, _ = key.shape
    count = lax.axis_size("seq")
    flat = lambda x: x.reshape(tokens * heads, C)
    weight2 = swap(out_weight, "head", 1)
    q16, k32, *chunk_maps, send = local_maps(flat(key), flat(value), beta, log_decay, flat(query))
    other = swap(send, "head", 1)
    part = jax.ShapeDtypeStruct((2, C, 2 * C), BF16)
    square = jax.ShapeDtypeStruct((2, C, C), BF16)
    squares = jax.ShapeDtypeStruct((2 * heads, C, C), BF16)
    both = jax.ShapeDtypeStruct((2 * heads, C, 2 * C), BF16)
    parts = small_call(gather_cores, [part] * heads, send, other)
    got = [parts[0]] + [swap_odd(x, r) for r, x in enumerate(parts[1:], 1)]
    half = heads // 2
    keep0, away0 = row_maps(heads, range(half), q16, k32, *chunk_maps)
    keep1, away1 = row_maps(heads, range(half, heads), q16, k32, *chunk_maps)
    keep0, got = lax.optimization_barrier((keep0, got))
    held, state = small_call(group_state, [both, square], *got)
    *maps, total = small_call(
        group_prefix, [squares, squares, jax.ShapeDtypeStruct((2 * heads, C, C), F32), part], held
    )
    rows = (keep0, keep1, swap(away0, "head", 1), swap(away1, "head", 1))
    if count == 2 * heads:
        lower = swap_odd(state, heads)
        maps, lower, rows, weight2 = lax.optimization_barrier((maps, lower, rows, weight2))
        sends = small_call(states_of_upper, [square] * heads + [squares], *maps, lower)
    else:
        sends = small_call(states_given, [square] * heads + [squares], *maps, prefix(total, heads))
    got = [sends[0]] + [swap_odd(x, r) for r, x in enumerate(sends[1:heads], 1)]
    (states1,) = small_call(gather_heads, [squares], *got)
    states0 = hand_back(states1)
    theirs = share_out(1, rows, states1, out_weight, weight2, [])
    theirs = share_out(0, rows, states0, out_weight, weight2, [theirs])
    theirs = swap(theirs, "head", 2)
    mine = share_here(rows, states0, states1, out_weight, weight2)
    return (mine + theirs.astype(F32)).astype(BF16)


def solution(mesh):
    in_specs = (
        P("seq", "head", None),
        P("seq", "head", None),
        P("seq", "head", None),
        P("head", "seq"),
        P("head", "seq"),
        P("head", None),
    )
    out_specs = P(("seq", "head"), None)
    return jax.shard_map(body, mesh=mesh, in_specs=in_specs, out_specs=out_specs, check_vma=False)
```

```python
import functools

import jax
import jax.numpy as jnp
from jax import lax
from jax.experimental import pallas as pl
from jax.experimental.pallas import tpu as pltpu
from jax.sharding import PartitionSpec as P

C = 128
B = 16
F32 = jnp.float32
BF16 = jnp.bfloat16
NN = (((1,), (0,)), ((), ()))
NT = (((1,), (1,)), ((), ()))
TN = (((0,), (0,)), ((), ()))
MIB = 1024 * 1024


def dot(a, b, dims=NN):
    return lax.dot_general(a, b, dims, preferred_element_type=F32)


def split(x):
    high = x.astype(BF16)
    return high, (x - high.astype(F32)).astype(BF16)


def twice(x):
    return jnp.concatenate([x, x], axis=0)


def dot3(a, b):
    (ah, al), (bh, bl) = a, b
    width = bh.shape[1]
    left = jnp.concatenate([ah, al], axis=1)
    if width > C:
        return dot(left, twice(bh)) + dot(ah, bl)
    both = dot(left, twice(jnp.concatenate([bh, bl], axis=1)))
    return both[:, :width] + both[:, width:]


def iotas():
    return (
        lax.broadcasted_iota(jnp.int32, (C, C), 0),
        lax.broadcasted_iota(jnp.int32, (C, C), 1),
    )


def to_column(row, eye):
    return jnp.sum(jnp.where(eye, row, 0.0), axis=1, keepdims=True)


def to_row(column, eye):
    return jnp.sum(jnp.where(eye, column, 0.0), axis=0, keepdims=True)


def inverse_scale(rows):
    return lax.rsqrt(jnp.sum(rows * rows, axis=1, keepdims=True) + 1e-06)


def three(x):
    high, rest = x.astype(BF16), x
    rest = rest - high.astype(F32)
    return (high,) + split(rest)


def running_sums(rows, upper):
    return sum(dot(x, upper) for x in reversed(three(rows)))


def base_inverse(lower, row, col):
    on_block = (row // B) == (col // B)
    blocks = jnp.where(on_block, lower, 0.0)
    packed = sum(blocks[i * B : (i + 1) * B] for i in range(1, C // B)) + blocks[:B]
    r, c = row[:B], col[:B]
    found = jnp.where(r == c % B, 1.0, 0.0)
    first = (c // B) * B
    for j in range(B - 1):
        factor = jnp.take_along_axis(packed, first + j, axis=1)
        found = found - factor * found[j : j + 1]
    return jnp.where(on_block, jnp.concatenate([found] * (C // B), axis=0), 0.0)


def odd_rows(x, size):
    return jnp.concatenate([x[i : i + size] for i in range(size, C, 2 * size)], axis=0)


def weave(even, odd, size):
    parts = []
    for i in range(0, C // 2, size):
        parts += [even[i : i + size], odd[i : i + size]]
    return jnp.concatenate(parts, axis=0)


def even_rows(x, size):
    return jnp.concatenate([x[i : i + size] for i in range(0, C, 2 * size)], axis=0)


def inverses(lowers, row, col):
    found = [base_inverse(a, row, col) for a in lowers]
    parts = [split(a) for a in lowers]
    halves = [split(x) for x in found]
    size = B
    while size < C:
        r, c = odd_rows(row, size), odd_rows(col, size)
        mask = ((r // (2 * size)) == (c // (2 * size))) & ((r // size) != (c // size))
        nothing = jnp.zeros((C // 2, C), BF16)
        mask = jnp.where(mask, 1.0, 0.0).astype(BF16)
        joins = [tuple(odd_rows(x, size) * mask for x in part) for part in parts]
        middle = [split(dot3(a, x)) for a, x in zip(joins, halves)]
        middle = [tuple(weave(nothing, x, size) for x in part) for part in middle]
        lows = [dot3(tuple(odd_rows(x, size) for x in h), y) for h, y in zip(halves, middle)]
        lows = [odd_rows(x, size) - y for x, y in zip(found, lows)]
        found = [weave(even_rows(x, size), y, size) for x, y in zip(found, lows)]
        if 2 * size < C:
            halves = [
                tuple(weave(even_rows(x, size), y, size) for x, y in zip(h, split(low)))
                for h, low in zip(halves, lows)
            ]
        size *= 2
    return found


def fetch(pairs, sems, late):
    copies = [pltpu.make_async_copy(x, y, sems.at[i]) for i, (x, y) in enumerate(pairs)]
    for copy in copies:
        copy.start()
    late.start()
    for copy in copies:
        copy.wait()


def in_hbm(*arrays):
    return [pltpu.with_memory_space_constraint(x, pltpu.HBM) for x in arrays]


def chunk_rows(heads, head, c):
    return pl.ds(c * C * heads + head, C, stride=heads)


def tokens_of(ref, head, c):
    return ref[head : head + 1, c * C : (c + 1) * C]


def join(moved, added):
    return jnp.concatenate([moved, added], axis=1)


def after(later, earlier):
    total = dot3(split(later[:, :C]), split(earlier))
    return join(total[:, :C], total[:, C:] + later[:, C:])


def per_chunk(ref):
    return jnp.concatenate([ref[:, i : i + C] for i in range(0, ref.shape[1], C)], axis=0)


def local_maps_kernel(heads, batch, k_hbm, v_hbm, beta_hbm, log_hbm, q_hbm, q16, k32, sums_ref, mix_ref, wu_ref, n_ref, own_ref, *rest):
    sends, (k16, v16, v32, beta_ref, log_ref, all_ref, sems) = rest[: heads - 1], rest[heads - 1 :]
    late = pltpu.make_async_copy(q_hbm, q16, sems.at[4])
    fetch(((k_hbm, k16), (log_hbm, log_ref), (beta_hbm, beta_ref), (v_hbm, v16)), sems, late)
    k32[...] = k16[...].astype(F32)
    v32[...] = v16[...].astype(F32)
    chunks = beta_ref.shape[1] // C
    row, col = iotas()
    eye = row == col
    within = row >= col
    strict = row > col
    one = jnp.ones((C, C), BF16)
    eye16 = jnp.where(eye, one, jnp.zeros((), BF16))
    sums = running_sums(per_chunk(log_ref), jnp.where(row <= col, one, jnp.zeros((), BF16)))
    sums_ref[...] = sums
    columns = jnp.concatenate([sums] * (C // sums.shape[0]), axis=0).T
    grown = jnp.exp(sums)
    faded = jnp.exp(sums[:, C - 1 :] - sums)
    betas = per_chunk(beta_ref)
    for start in range(0, heads, batch):
        jobs = [(head, c) for head in range(start, start + batch) for c in range(chunks)]
        lowers, raws, values, fades, lengths = [], [], [], [], []
        for head, c in jobs:
            at = slice(c * heads + head, c * heads + head + 1)
            raw = k32[chunk_rows(heads, head, c), :].astype(BF16)
            raws.append(raw)
            values.append(v32[chunk_rows(heads, head, c), :].astype(BF16))
            both = dot(jnp.concatenate([raw, eye16], axis=0), raw, NT)
            gram, turned = both[:C], both[C:]
            square = to_row(gram, eye) + 1e-06
            scale = lax.rsqrt(square)
            lengths.append(square * scale)
            strength = betas[at] * (scale * scale)
            span = columns[:, c * heads + head : c * heads + head + 1] - sums[at]
            mix = jnp.where(within, jnp.exp(span), 0.0) * strength
            mix_ref[head * chunks + c] = mix
            lowers.append(jnp.where(strict, gram * mix, 0.0))
            fades.append(turned * (strength * faded[at]))
        solved = []
        for i, found in enumerate(inverses(lowers, row, col)):
            at = slice(jobs[i][1] * heads + jobs[i][0], jobs[i][1] * heads + jobs[i][0] + 1)
            kept = dot(jnp.concatenate(split(found * grown[at]), axis=1), twice(raws[i]))
            fresh = dot(jnp.concatenate(split(found * lengths[i]), axis=1), twice(values[i]))
            solved.append(jnp.concatenate([kept, fresh], axis=1))
        maps = []
        for i, (head, c) in enumerate(jobs):
            wu_ref[head * chunks + c] = solved[i]
            both = dot3(split(fades[i]), split(solved[i]))
            end = grown[c * heads + head : c * heads + head + 1, C - 1 :]
            maps.append((jnp.where(eye, end, 0.0) - both[:, :C], both[:, C:]))
        for j in range(batch):
            first, second, third, last = (join(*x) for x in maps[j * chunks : (j + 1) * chunks])
            early = after(second, first)
            n_ref[(start + j) * chunks + 1] = first
            n_ref[(start + j) * chunks + 2] = early
            n_ref[(start + j) * chunks + 3] = after(third, early)
            all_ref[start + j] = after(after(last, third), early)
    place = lax.rem(lax.axis_index("seq"), heads)
    own_ref[...] = all_ref[place]
    for r in range(1, heads):
        sends[r - 1][...] = all_ref[other_place(place, r, heads)].astype(BF16)
    late.wait()


def other_place(place, r, heads):
    result = place
    for i in range(heads):
        result = jnp.where(place == i, i ^ r, result)
    return result


def local_maps(key, value, beta, log_decay, query, batch):
    heads, tokens = beta.shape
    count = heads * (tokens // C)
    here = pl.BlockSpec(memory_space=pltpu.VMEM)
    return pl.pallas_call(
        functools.partial(local_maps_kernel, heads, batch),
        in_specs=[pl.BlockSpec(memory_space=pltpu.HBM)] * 5,
        out_specs=[here] * (6 + heads),
        out_shape=[
            jax.ShapeDtypeStruct(query.shape, BF16),
            jax.ShapeDtypeStruct(key.shape, F32),
            jax.ShapeDtypeStruct((count, C), F32),
            jax.ShapeDtypeStruct((count, C, C), F32),
            jax.ShapeDtypeStruct((count, C, 2 * C), F32),
            jax.ShapeDtypeStruct((count, C, 2 * C), F32),
            jax.ShapeDtypeStruct((C, 2 * C), F32),
        ]
        + [jax.ShapeDtypeStruct((C, 2 * C), BF16)] * (heads - 1),
        scratch_shapes=[
            pltpu.VMEM(key.shape, BF16),
            pltpu.VMEM(key.shape, BF16),
            pltpu.VMEM(key.shape, F32),
            pltpu.VMEM(beta.shape, F32),
            pltpu.VMEM(beta.shape, F32),
            pltpu.VMEM((heads, C, 2 * C), F32),
            pltpu.SemaphoreType.DMA((5,)),
        ],
        compiler_params=pltpu.CompilerParams(vmem_limit_bytes=32 * MIB),
        name="local_maps",
    )(*in_hbm(key, value, beta, log_decay, query))


def rows_kernel(heads, mine, q16, k32, sums_ref, mix_ref, wu_ref, n_ref, out_ref, q32):
    q32[...] = q16[...].astype(F32)
    chunks = q16.shape[0] // (heads * C)
    row, col = iotas()
    eye = row == col
    for j, head in enumerate(mine):
        for c in range(chunks):
            i = head * chunks + c
            query, raw = q32[chunk_rows(heads, head, c), :], k32[chunk_rows(heads, head, c), :]
            grown = to_column(jnp.exp(sums_ref[c * heads + head : c * heads + head + 1, :]), eye)
            pairs = dot(query.astype(BF16), raw.astype(BF16), NT) * mix_ref[i]
            both = dot3(split(pairs), split(wu_ref[i]))
            scale = inverse_scale(query)
            reach = (query * grown - both[:, :C]) * scale
            fresh = both[:, C:] * scale
            if c > 0:
                earlier = dot3(split(reach), split(n_ref[i]))
                reach = earlier[:, :C]
                fresh = fresh + earlier[:, C:]
            out_ref[j, c * C : (c + 1) * C, :] = jnp.concatenate([reach, fresh], axis=1)


def row_maps(heads, mine, query, k32, sums, mix, wu, states):
    tokens = query.shape[0] // heads
    here = pl.BlockSpec(memory_space=pltpu.VMEM)
    return pl.pallas_call(
        functools.partial(rows_kernel, heads, mine),
        in_specs=[here] * 6,
        out_specs=here,
        out_shape=jax.ShapeDtypeStruct((len(mine), tokens, 2 * C), F32),
        scratch_shapes=[pltpu.VMEM(query.shape, F32)],
        compiler_params=pltpu.CompilerParams(vmem_limit_bytes=16 * MIB),
        cost_estimate=pl.CostEstimate(flops=2000000000, bytes_accessed=8000000, transcendentals=0),
        name="row_maps",
    )(query, k32, sums, mix, wu, states)


def small_call(kernel, out_shape, *args):
    here = pl.BlockSpec(memory_space=pltpu.VMEM)
    return pl.pallas_call(
        kernel,
        in_specs=[here] * len(args),
        out_specs=[here] * len(out_shape),
        out_shape=out_shape,
        compiler_params=pltpu.CompilerParams(vmem_limit_bytes=8 * MIB),
        name=kernel.__name__,
    )(*args)


def moved_on(maps, state16, added):
    high, low = split(maps)
    return dot(jnp.concatenate([high, low], axis=1), twice(state16)) + added


def in_order(own_ref, got_refs, held):
    heads = held.shape[0]
    place = lax.rem(lax.axis_index("seq"), heads)
    held[place] = own_ref[...]
    for r, got in enumerate(got_refs, 1):
        held[other_place(place, r, heads)] = got[...].astype(F32)
    return place


def group_state(own_ref, *refs):
    got_refs, (held, out_ref) = refs[:-2], refs[-2:]
    in_order(own_ref, got_refs, held)
    state = held[0, :, C:].astype(BF16)
    for i in range(1, held.shape[0]):
        state = moved_on(held[i, :, :C], state, held[i, :, C:]).astype(BF16)
    out_ref[...] = state


def group_prefix(held, high_ref, low_ref, added_ref, total_ref):
    row, col = iotas()
    eye = jnp.where(row == col, 1.0, 0.0)
    total = jnp.concatenate([eye, jnp.zeros((C, C), F32)], axis=1)
    for i in range(held.shape[0]):
        high_ref[i], low_ref[i] = split(total[:, :C])
        added_ref[i] = total[:, C:]
        later = held[i]
        if i == 0:
            total = later
        else:
            total = dot3(split(later[:, :C]), split(total))
            total = jnp.concatenate([total[:, :C], total[:, C:] + later[:, C:]], axis=1)
    total_ref[...] = total.astype(BF16)


def group_states(upper_only, high_ref, low_ref, added_ref, state_ref, keep_ref, *refs):
    sends, states = refs[:-1], refs[-1]
    heads = added_ref.shape[0]
    state = state_ref[...]
    if upper_only:
        state = jnp.where(lax.axis_index("seq") < heads, jnp.zeros_like(state), state)
    both = twice(state)
    for i in range(heads):
        maps = jnp.concatenate([high_ref[i], low_ref[i]], axis=1)
        states[i] = (dot(maps, both) + added_ref[i]).astype(BF16)
    place = lax.rem(lax.axis_index("seq"), heads)
    keep_ref[...] = states[place]
    for r, send in enumerate(sends, 1):
        send[...] = states[other_place(place, r, heads)]


def states_of_upper(*refs):
    group_states(True, *refs)


def states_given(*refs):
    group_states(False, *refs)


def prefix(total, heads):
    count = lax.axis_size("seq")
    groups = [list(range(i, count, heads)) for i in range(heads)]
    me = lax.axis_index("seq") // heads
    totals = lax.all_gather(total, "seq", axis_index_groups=groups)

    def step(d, state):
        longer = jnp.einsum("ik,pkw->iw", totals[d, :, :C], jnp.stack(split(state)), preferred_element_type=F32)
        return jnp.where(d < me, longer + totals[d, :, C:].astype(F32), state)

    start = jnp.zeros((C, C), F32)
    return lax.fori_loop(0, count // heads - 1, step, start).astype(BF16)


def apply_kernel(groups, rows0_ref, rows1_ref, *refs):
    states, (keep_ref, send_ref, held) = refs[:-3], refs[-3:]
    heads = len(states)
    half, tokens, _ = rows0_ref.shape
    block = tokens // groups
    place = lax.rem(lax.axis_index("seq"), heads)
    for r in range(heads):
        held[other_place(place, r, heads)] = states[r][...]
    core = lax.rem(lax.axis_index("head"), 2)
    for out_ref, parity in ((send_ref, 1 - core), (keep_ref, core)):
        for i in range(groups // 2):
            rows = pl.ds(pl.multiple_of((2 * i + parity) * block, block), block)
            for h in range(heads):
                ref = (rows0_ref, rows1_ref)[h // half]
                attended = moved_on(ref[h % half, rows, :C], held[h], ref[h % half, rows, C:])
                out_ref[i, :, h * C : (h + 1) * C] = attended.astype(BF16)


def apply(rows, states, groups):
    _, tokens, _ = rows[0].shape
    heads = len(states)
    here = pl.BlockSpec(memory_space=pltpu.VMEM)
    out = jax.ShapeDtypeStruct((groups // 2, tokens // groups, heads * C), BF16)
    return pl.pallas_call(
        functools.partial(apply_kernel, groups),
        in_specs=[here] * (2 + heads),
        out_specs=[here] * 2,
        out_shape=[out, out],
        scratch_shapes=[pltpu.VMEM((heads, C, C), BF16)],
        compiler_params=pltpu.CompilerParams(vmem_limit_bytes=8 * MIB),
        name="apply",
    )(*rows, *states)


def project_kernel(other, start, keep_ref, got_ref, w_ref, w2_ref, out_ref):
    pair = lax.axis_index("head") // 2
    index = 1 - pair if other else pair
    columns = slice(start, start + out_ref.shape[1])
    shares = dot(keep_ref[index], w_ref[:, columns]) + dot(got_ref[index], w2_ref[:, columns])
    out_ref[...] = shares.astype(out_ref.dtype)


def project(other, start, width, keep, got, weight, weight2):
    _, block, depth = keep.shape
    return pl.pallas_call(
        functools.partial(project_kernel, other, start),
        out_shape=jax.ShapeDtypeStruct((block, width), BF16 if other else F32),
        compiler_params=pltpu.CompilerParams(vmem_limit_bytes=20 * MIB),
        cost_estimate=pl.CostEstimate(
            flops=4 * block * depth * width, bytes_accessed=4 * depth * width, transcendentals=0
        ),
        name="project",
    )(keep, got, weight, weight2)


def add_kernel(mine_ref, theirs_ref, *refs):
    refs[-1][...] = (mine_ref[...] + theirs_ref[...].astype(F32)).astype(BF16)


def add_part(index, parts, mine, theirs, earlier):
    block, width = mine.shape
    here = pl.BlockSpec(memory_space=pltpu.VMEM)
    return pl.pallas_call(
        add_kernel,
        grid=(1,),
        in_specs=[here, here] + [pl.BlockSpec(memory_space=pl.ANY)] * len(earlier),
        out_specs=pl.BlockSpec((block, width), lambda i: (0, index)),
        out_shape=jax.ShapeDtypeStruct((block, width * parts), BF16),
        input_output_aliases={2: 0} if earlier else {},
        compiler_params=pltpu.CompilerParams(vmem_limit_bytes=8 * MIB),
        name="add_part",
    )(mine, theirs, *earlier)


def swap(x, axis, bit):
    count = lax.axis_size(axis)
    return lax.ppermute(x, axis, [(i, i ^ bit) for i in range(count)])


def body(query, key, value, beta, log_decay, out_weight):
    tokens, heads, _ = key.shape
    count = lax.axis_size("seq")
    flat = lambda x: x.reshape(tokens * heads, C)
    weight2 = swap(out_weight, "head", 1)
    q16, k32, *chunk_maps, own, send1, send2, send3 = local_maps(
        flat(key), flat(value), beta, log_decay, flat(query), heads
    )
    got = [swap(x, "seq", r) for r, x in enumerate((send1, send2, send3), 1)]
    half = heads // 2
    rows0 = row_maps(heads, range(half), q16, k32, *chunk_maps)
    rows1 = row_maps(heads, range(half, heads), q16, k32, *chunk_maps)
    rows0, got = lax.optimization_barrier((rows0, got))
    wide = jax.ShapeDtypeStruct((heads, C, 2 * C), F32)
    square = jax.ShapeDtypeStruct((C, C), BF16)
    squares = jax.ShapeDtypeStruct((heads, C, C), BF16)
    added = jax.ShapeDtypeStruct((heads, C, C), F32)
    held, state = small_call(group_state, [wide, square], own, *got)
    *maps, total = small_call(
        group_prefix, [squares, squares, added, jax.ShapeDtypeStruct((C, 2 * C), BF16)], held
    )
    outs = [square] * heads + [squares]
    if count == 2 * heads:
        lower = swap(state, "seq", heads)
        maps, lower = lax.optimization_barrier((maps, lower))
        keep, *sends = small_call(states_of_upper, outs, *maps, lower)
    else:
        keep, *sends = small_call(states_given, outs, *maps, prefix(total, heads))
    entering = [keep] + [swap(x, "seq", r) for r, x in enumerate(sends[: heads - 1], 1)]
    keep, away = apply((rows0, rows1), entering, lax.axis_size("head"))
    got = swap(away, "head", 1)
    parts = 2
    width = out_weight.shape[1] // parts
    ranges = [(i * width, width) for i in range(parts)]
    args = (keep, got, out_weight, weight2)
    theirs = [swap(project(True, *x, *args), "head", 2) for x in ranges]
    mine = [project(False, *x, *args) for x in ranges]
    mixed = []
    for i in range(parts):
        mixed = [add_part(i, parts, mine[i], theirs[i], mixed)]
    return mixed[0]


def solution(mesh):
    in_specs = (
        P("seq", "head", None),
        P("seq", "head", None),
        P("seq", "head", None),
        P("head", "seq"),
        P("head", "seq"),
        P("head", None),
    )
    out_specs = P(("seq", "head"), None)
    return jax.shard_map(body, mesh=mesh, in_specs=in_specs, out_specs=out_specs, check_vma=False)
```

```python
import functools

import jax
import jax.numpy as jnp
from jax import lax
from jax.experimental import pallas as pl
from jax.experimental.pallas import tpu as pltpu
from jax.sharding import PartitionSpec as P

C = 128
B = 16
F32 = jnp.float32
BF16 = jnp.bfloat16
NN = (((1,), (0,)), ((), ()))
NT = (((1,), (1,)), ((), ()))
TN = (((0,), (0,)), ((), ()))
MIB = 1024 * 1024


def dot(a, b, dims=NN):
    return lax.dot_general(a, b, dims, preferred_element_type=F32)


def split(x):
    high = x.astype(BF16)
    return high, (x - high.astype(F32)).astype(BF16)


def twice(x):
    return jnp.concatenate([x, x], axis=0)


def dot3(a, b):
    (ah, al), (bh, bl) = a, b
    width = bh.shape[1]
    if width > C:
        return dot(jnp.concatenate([ah, al], axis=1), twice(bh)) + dot(ah, bl)
    rows = ah.shape[0]
    both = dot(jnp.concatenate([ah, al], axis=0), jnp.concatenate([bh, bl], axis=1))
    return both[:rows, :width] + (both[:rows, width:] + both[rows:, :width])


def iotas():
    return (
        lax.broadcasted_iota(jnp.int32, (C, C), 0),
        lax.broadcasted_iota(jnp.int32, (C, C), 1),
    )


def to_column(row, eye):
    return jnp.sum(jnp.where(eye, row, 0.0), axis=1, keepdims=True)


def to_row(column, eye):
    return jnp.sum(jnp.where(eye, column, 0.0), axis=0, keepdims=True)


def inverse_scale(rows):
    return lax.rsqrt(jnp.sum(rows * rows, axis=1, keepdims=True) + 1e-06)


def three(x):
    high, rest = x.astype(BF16), x
    rest = rest - high.astype(F32)
    return (high,) + split(rest)


def running_sums(rows, upper):
    return sum(dot(x, upper) for x in reversed(three(rows)))


def base_inverse(lower, row, col):
    on_block = (row // B) == (col // B)
    blocks = jnp.where(on_block, lower, 0.0)
    packed = sum(blocks[i * B : (i + 1) * B] for i in range(1, C // B)) + blocks[:B]
    r, c = row[:B], col[:B]
    found = jnp.where(r == c % B, 1.0, 0.0)
    first = (c // B) * B
    for j in range(B - 1):
        factor = jnp.take_along_axis(packed, first + j, axis=1)
        found = found - factor * found[j : j + 1]
    return jnp.where(on_block, jnp.concatenate([found] * (C // B), axis=0), 0.0)


def odd_rows(x, size):
    return jnp.concatenate([x[i : i + size] for i in range(size, C, 2 * size)], axis=0)


def weave(even, odd, size):
    parts = []
    for i in range(0, C // 2, size):
        parts += [even[i : i + size], odd[i : i + size]]
    return jnp.concatenate(parts, axis=0)


def even_rows(x, size):
    return jnp.concatenate([x[i : i + size] for i in range(0, C, 2 * size)], axis=0)


def inverses(lowers, row, col):
    found = [base_inverse(a, row, col) for a in lowers]
    parts = [split(a) for a in lowers]
    halves = [split(x) for x in found]
    size = B
    while size < C:
        r, c = odd_rows(row, size), odd_rows(col, size)
        mask = ((r // (2 * size)) == (c // (2 * size))) & ((r // size) != (c // size))
        nothing = jnp.zeros((C // 2, C), BF16)
        mask = jnp.where(mask, 1.0, 0.0).astype(BF16)
        joins = [tuple(odd_rows(x, size) * mask for x in part) for part in parts]
        middle = [split(dot3(a, x)) for a, x in zip(joins, halves)]
        middle = [tuple(weave(nothing, x, size) for x in part) for part in middle]
        lows = [dot3(tuple(odd_rows(x, size) for x in h), y) for h, y in zip(halves, middle)]
        lows = [odd_rows(x, size) - y for x, y in zip(found, lows)]
        found = [weave(even_rows(x, size), y, size) for x, y in zip(found, lows)]
        if 2 * size < C:
            halves = [
                tuple(weave(even_rows(x, size), y, size) for x, y in zip(h, split(low)))
                for h, low in zip(halves, lows)
            ]
        size *= 2
    return found


def fetch(pairs, sems, late):
    copies = [pltpu.make_async_copy(x, y, sems.at[i]) for i, (x, y) in enumerate(pairs)]
    for copy in copies:
        copy.start()
    late.start()
    for copy in copies:
        copy.wait()


def in_hbm(*arrays):
    return [pltpu.with_memory_space_constraint(x, pltpu.HBM) for x in arrays]


def chunk_rows(heads, head, c):
    return pl.ds(c * C * heads + head, C, stride=heads)


def tokens_of(ref, head, c):
    return ref[head : head + 1, c * C : (c + 1) * C]


def join(moved, added):
    return jnp.concatenate([moved, added], axis=1)


def after(later, earlier):
    total = dot3(split(later[:, :C]), split(earlier))
    return join(total[:, :C], total[:, C:] + later[:, C:])


def per_chunk(ref):
    return jnp.concatenate([ref[:, i : i + C] for i in range(0, ref.shape[1], C)], axis=0)


def local_maps_kernel(heads, batch, k_hbm, v_hbm, beta_hbm, log_hbm, q_hbm, q16, k32, sums_ref, mix_ref, wu_ref, n_ref, own_ref, *rest):
    sends, (k16, v16, v32, beta_ref, log_ref, all_ref, sems) = rest[: heads - 1], rest[heads - 1 :]
    late = pltpu.make_async_copy(q_hbm, q16, sems.at[4])
    fetch(((k_hbm, k16), (log_hbm, log_ref), (beta_hbm, beta_ref), (v_hbm, v16)), sems, late)
    k32[...] = k16[...].astype(F32)
    v32[...] = v16[...].astype(F32)
    chunks = beta_ref.shape[1] // C
    row, col = iotas()
    eye = row == col
    within = row >= col
    strict = row > col
    one = jnp.ones((C, C), BF16)
    eye16 = jnp.where(eye, one, jnp.zeros((), BF16))
    sums = running_sums(per_chunk(log_ref), jnp.where(row <= col, one, jnp.zeros((), BF16)))
    sums_ref[...] = sums
    columns = jnp.concatenate([sums] * (C // sums.shape[0]), axis=0).T
    grown = jnp.exp(sums)
    faded = jnp.exp(sums[:, C - 1 :] - sums)
    betas = per_chunk(beta_ref)
    for start in range(0, heads, batch):
        jobs = [(head, c) for head in range(start, start + batch) for c in range(chunks)]
        lowers, raws, values, fades, lengths = [], [], [], [], []
        for head, c in jobs:
            at = slice(c * heads + head, c * heads + head + 1)
            raw = k32[chunk_rows(heads, head, c), :].astype(BF16)
            raws.append(raw)
            values.append(v32[chunk_rows(heads, head, c), :].astype(BF16))
            both = dot(jnp.concatenate([raw, eye16], axis=0), raw, NT)
            gram, turned = both[:C], both[C:]
            square = to_row(gram, eye) + 1e-06
            scale = lax.rsqrt(square)
            lengths.append(square * scale)
            strength = betas[at] * (scale * scale)
            span = columns[:, c * heads + head : c * heads + head + 1] - sums[at]
            mix = jnp.where(within, jnp.exp(span), 0.0) * strength
            mix_ref[head * chunks + c] = mix
            lowers.append(jnp.where(strict, gram * mix, 0.0))
            fades.append(turned * (strength * faded[at]))
        solved = []
        for i, found in enumerate(inverses(lowers, row, col)):
            at = slice(jobs[i][1] * heads + jobs[i][0], jobs[i][1] * heads + jobs[i][0] + 1)
            kept = dot(jnp.concatenate(split(found * grown[at]), axis=1), twice(raws[i]))
            fresh = dot(jnp.concatenate(split(found * lengths[i]), axis=1), twice(values[i]))
            solved.append(jnp.concatenate([kept, fresh], axis=1))
        maps = []
        for i, (head, c) in enumerate(jobs):
            wu_ref[head * chunks + c] = solved[i]
            both = dot3(split(fades[i]), split(solved[i]))
            end = grown[c * heads + head : c * heads + head + 1, C - 1 :]
            maps.append((jnp.where(eye, end, 0.0) - both[:, :C], both[:, C:]))
        for j in range(batch):
            first, second, third, last = (join(*x) for x in maps[j * chunks : (j + 1) * chunks])
            early = after(second, first)
            n_ref[(start + j) * chunks + 1] = first
            n_ref[(start + j) * chunks + 2] = early
            n_ref[(start + j) * chunks + 3] = after(third, early)
            all_ref[start + j] = after(after(last, third), early)
    place = lax.rem(lax.axis_index("seq"), heads)
    own_ref[...] = all_ref[place]
    for r in range(1, heads):
        sends[r - 1][...] = all_ref[other_place(place, r)].astype(BF16)
    late.wait()


def other_place(place, r):
    return lax.bitwise_xor(place, r)


def local_maps(key, value, beta, log_decay, query, batch):
    heads, tokens = beta.shape
    count = heads * (tokens // C)
    here = pl.BlockSpec(memory_space=pltpu.VMEM)
    return pl.pallas_call(
        functools.partial(local_maps_kernel, heads, batch),
        in_specs=[pl.BlockSpec(memory_space=pltpu.HBM)] * 5,
        out_specs=[here] * (6 + heads),
        out_shape=[
            jax.ShapeDtypeStruct(query.shape, BF16),
            jax.ShapeDtypeStruct(key.shape, F32),
            jax.ShapeDtypeStruct((count, C), F32),
            jax.ShapeDtypeStruct((count, C, C), F32),
            jax.ShapeDtypeStruct((count, C, 2 * C), F32),
            jax.ShapeDtypeStruct((count, C, 2 * C), F32),
            jax.ShapeDtypeStruct((C, 2 * C), F32),
        ]
        + [jax.ShapeDtypeStruct((C, 2 * C), BF16)] * (heads - 1),
        scratch_shapes=[
            pltpu.VMEM(key.shape, BF16),
            pltpu.VMEM(key.shape, BF16),
            pltpu.VMEM(key.shape, F32),
            pltpu.VMEM(beta.shape, F32),
            pltpu.VMEM(beta.shape, F32),
            pltpu.VMEM((heads, C, 2 * C), F32),
            pltpu.SemaphoreType.DMA((5,)),
        ],
        compiler_params=pltpu.CompilerParams(vmem_limit_bytes=32 * MIB),
        name="local_maps",
    )(*in_hbm(key, value, beta, log_decay, query))


def rows_kernel(heads, mine, q16, k32, sums_ref, mix_ref, wu_ref, n_ref, out_ref, q32):
    q32[...] = q16[...].astype(F32)
    chunks = q16.shape[0] // (heads * C)
    row, col = iotas()
    eye = row == col
    for j, head in enumerate(mine):
        for c in range(chunks):
            i = head * chunks + c
            query, raw = q32[chunk_rows(heads, head, c), :], k32[chunk_rows(heads, head, c), :]
            grown = to_column(jnp.exp(sums_ref[c * heads + head : c * heads + head + 1, :]), eye)
            pairs = dot(query.astype(BF16), raw.astype(BF16), NT) * mix_ref[i]
            both = dot3(split(pairs), split(wu_ref[i]))
            scale = inverse_scale(query)
            reach = (query * grown - both[:, :C]) * scale
            fresh = both[:, C:] * scale
            if c > 0:
                earlier = dot3(split(reach), split(n_ref[i]))
                reach = earlier[:, :C]
                fresh = fresh + earlier[:, C:]
            out_ref[j, c * C : (c + 1) * C, :] = jnp.concatenate([reach, fresh], axis=1)


def row_maps(heads, mine, query, k32, sums, mix, wu, states):
    tokens = query.shape[0] // heads
    here = pl.BlockSpec(memory_space=pltpu.VMEM)
    return pl.pallas_call(
        functools.partial(rows_kernel, heads, mine),
        in_specs=[here] * 6,
        out_specs=here,
        out_shape=jax.ShapeDtypeStruct((len(mine), tokens, 2 * C), F32),
        scratch_shapes=[pltpu.VMEM(query.shape, F32)],
        compiler_params=pltpu.CompilerParams(vmem_limit_bytes=16 * MIB),
        cost_estimate=pl.CostEstimate(flops=2000000000, bytes_accessed=8000000, transcendentals=0),
        name="row_maps",
    )(query, k32, sums, mix, wu, states)


def small_call(kernel, out_shape, *args):
    here = pl.BlockSpec(memory_space=pltpu.VMEM)
    return pl.pallas_call(
        kernel,
        in_specs=[here] * len(args),
        out_specs=[here] * len(out_shape),
        out_shape=out_shape,
        compiler_params=pltpu.CompilerParams(vmem_limit_bytes=8 * MIB),
        name=kernel.__name__,
    )(*args)


def moved_on(maps, state16, added):
    high, low = split(maps)
    return dot(jnp.concatenate([high, low], axis=1), twice(state16)) + added


def in_order(own_ref, got_refs, held):
    heads = held.shape[0]
    place = lax.rem(lax.axis_index("seq"), heads)
    held[place] = own_ref[...]
    for r, got in zip(range(heads - 1, 0, -1), got_refs):
        held[other_place(place, r)] = got[...].astype(F32)
    return place


def group_state(own_ref, *refs):
    got_refs, (held, out_ref) = refs[:-2], refs[-2:]
    in_order(own_ref, got_refs, held)
    state = held[0, :, C:].astype(BF16)
    for i in range(1, held.shape[0]):
        state = moved_on(held[i, :, :C], state, held[i, :, C:]).astype(BF16)
    out_ref[...] = state


def group_prefix(held, high_ref, low_ref, added_ref, total_ref):
    row, col = iotas()
    eye = jnp.where(row == col, 1.0, 0.0)
    total = jnp.concatenate([eye, jnp.zeros((C, C), F32)], axis=1)
    for i in range(held.shape[0]):
        high_ref[i], low_ref[i] = split(total[:, :C])
        added_ref[i] = total[:, C:]
        later = held[i]
        if i == 0:
            total = later
        else:
            total = dot3(split(later[:, :C]), split(total))
            total = jnp.concatenate([total[:, :C], total[:, C:] + later[:, C:]], axis=1)
    total_ref[...] = total.astype(BF16)


def group_states(upper_only, high_ref, low_ref, added_ref, state_ref, keep_ref, *refs):
    sends, states = refs[:-1], refs[-1]
    heads = added_ref.shape[0]
    state = state_ref[...]
    if upper_only:
        state = jnp.where(lax.axis_index("seq") < heads, jnp.zeros_like(state), state)
    both = twice(state)
    for i in range(heads):
        maps = jnp.concatenate([high_ref[i], low_ref[i]], axis=1)
        states[i] = (dot(maps, both) + added_ref[i]).astype(BF16)
    place = lax.rem(lax.axis_index("seq"), heads)
    keep_ref[...] = states[place]
    for r, send in enumerate(sends, 1):
        send[...] = states[other_place(place, r)]


def states_of_upper(*refs):
    group_states(True, *refs)


def states_given(*refs):
    group_states(False, *refs)


def prefix(total, heads):
    count = lax.axis_size("seq")
    groups = [list(range(i, count, heads)) for i in range(heads)]
    me = lax.axis_index("seq") // heads
    totals = lax.all_gather(total, "seq", axis_index_groups=groups)

    def step(d, state):
        longer = jnp.einsum("ik,pkw->iw", totals[d, :, :C], jnp.stack(split(state)), preferred_element_type=F32)
        return jnp.where(d < me, longer + totals[d, :, C:].astype(F32), state)

    start = jnp.zeros((C, C), F32)
    return lax.fori_loop(0, count // heads - 1, step, start).astype(BF16)


def apply_kernel(groups, rows0_ref, rows1_ref, *refs):
    states, (keep_ref, send_ref, held) = refs[:-3], refs[-3:]
    heads = len(states)
    half, tokens, _ = rows0_ref.shape
    block = tokens // groups
    place = lax.rem(lax.axis_index("seq"), heads)
    for r, state in zip(range(heads - 1, -1, -1), states):
        held[other_place(place, r)] = state[...]
    core = lax.rem(lax.axis_index("head"), 2)
    for out_ref, parity in ((send_ref, 1 - core), (keep_ref, core)):
        for i in range(groups // 2):
            rows = pl.ds(pl.multiple_of((2 * i + parity) * block, block), block)
            for h in range(heads):
                ref = (rows0_ref, rows1_ref)[h // half]
                attended = moved_on(ref[h % half, rows, :C], held[h], ref[h % half, rows, C:])
                out_ref[i, :, h * C : (h + 1) * C] = attended.astype(BF16)


def apply(rows, states, groups):
    _, tokens, _ = rows[0].shape
    heads = len(states)
    here = pl.BlockSpec(memory_space=pltpu.VMEM)
    out = jax.ShapeDtypeStruct((groups // 2, tokens // groups, heads * C), BF16)
    return pl.pallas_call(
        functools.partial(apply_kernel, groups),
        in_specs=[here] * (2 + heads),
        out_specs=[here] * 2,
        out_shape=[out, out],
        scratch_shapes=[pltpu.VMEM((heads, C, C), BF16)],
        compiler_params=pltpu.CompilerParams(vmem_limit_bytes=8 * MIB),
        name="apply",
    )(*rows, *states)


def project_kernel(other, start, keep_ref, got_ref, w_ref, w2_ref, out_ref):
    pair = lax.axis_index("head") // 2
    index = 1 - pair if other else pair
    columns = slice(start, start + out_ref.shape[1])
    shares = dot(keep_ref[index], w_ref[:, columns]) + dot(got_ref[index], w2_ref[:, columns])
    out_ref[...] = shares.astype(out_ref.dtype)


def project(other, start, width, keep, got, weight, weight2):
    _, block, depth = keep.shape
    return pl.pallas_call(
        functools.partial(project_kernel, other, start),
        out_shape=jax.ShapeDtypeStruct((block, width), BF16 if other else F32),
        compiler_params=pltpu.CompilerParams(vmem_limit_bytes=20 * MIB),
        cost_estimate=pl.CostEstimate(
            flops=4 * block * depth * width, bytes_accessed=4 * depth * width, transcendentals=0
        ),
        name="project",
    )(keep, got, weight, weight2)


def add_kernel(mine_ref, theirs_ref, *refs):
    refs[-1][...] = (mine_ref[...] + theirs_ref[...].astype(F32)).astype(BF16)


def add_part(index, parts, mine, theirs, earlier):
    block, width = mine.shape
    here = pl.BlockSpec(memory_space=pltpu.VMEM)
    return pl.pallas_call(
        add_kernel,
        grid=(1,),
        in_specs=[here, here] + [pl.BlockSpec(memory_space=pl.ANY)] * len(earlier),
        out_specs=pl.BlockSpec((block, width), lambda i: (0, index)),
        out_shape=jax.ShapeDtypeStruct((block, width * parts), BF16),
        input_output_aliases={2: 0} if earlier else {},
        compiler_params=pltpu.CompilerParams(vmem_limit_bytes=8 * MIB),
        name="add_part",
    )(mine, theirs, *earlier)


def swap(x, axis, bit):
    count = lax.axis_size(axis)
    return lax.ppermute(x, axis, [(i, i ^ bit) for i in range(count)])


def swap_all(parts):
    return [swap(parts[r - 1], "seq", r) for r in range(len(parts), 0, -1)]


def body(query, key, value, beta, log_decay, out_weight):
    tokens, heads, _ = key.shape
    count = lax.axis_size("seq")
    flat = lambda x: x.reshape(tokens * heads, C)
    weight2 = swap(out_weight, "head", 1)
    q16, k32, *chunk_maps, own, send1, send2, send3 = local_maps(
        flat(key), flat(value), beta, log_decay, flat(query), heads
    )
    got = swap_all([send1, send2, send3])
    half = heads // 2
    rows0 = row_maps(heads, range(half), q16, k32, *chunk_maps)
    rows1 = row_maps(heads, range(half, heads), q16, k32, *chunk_maps)
    rows0, got = lax.optimization_barrier((rows0, got))
    wide = jax.ShapeDtypeStruct((heads, C, 2 * C), F32)
    square = jax.ShapeDtypeStruct((C, C), BF16)
    squares = jax.ShapeDtypeStruct((heads, C, C), BF16)
    added = jax.ShapeDtypeStruct((heads, C, C), F32)
    held, state = small_call(group_state, [wide, square], own, *got)
    *maps, total = small_call(
        group_prefix, [squares, squares, added, jax.ShapeDtypeStruct((C, 2 * C), BF16)], held
    )
    outs = [square] * heads + [squares]
    if count == 2 * heads:
        lower = swap(state, "seq", heads)
        maps, lower = lax.optimization_barrier((maps, lower))
        keep, *sends = small_call(states_of_upper, outs, *maps, lower)
    else:
        keep, *sends = small_call(states_given, outs, *maps, prefix(total, heads))
    entering = swap_all(sends[: heads - 1]) + [keep]
    keep, away = apply((rows0, rows1), entering, lax.axis_size("head"))
    got = swap(away, "head", 1)
    parts = 2
    width = out_weight.shape[1] // parts
    ranges = [(i * width, width) for i in range(parts)]
    args = (keep, got, out_weight, weight2)
    theirs = [swap(project(True, *x, *args), "head", 2) for x in ranges]
    mine = [project(False, *x, *args) for x in ranges]
    mixed = []
    for i in range(parts):
        mixed = [add_part(i, parts, mine[i], theirs[i], mixed)]
    return mixed[0]


def solution(mesh):
    in_specs = (
        P("seq", "head", None),
        P("seq", "head", None),
        P("seq", "head", None),
        P("head", "seq"),
        P("head", "seq"),
        P("head", None),
    )
    out_specs = P(("seq", "head"), None)
    return jax.shard_map(body, mesh=mesh, in_specs=in_specs, out_specs=out_specs, check_vma=False)
```

```python
import functools

import jax
import jax.numpy as jnp
from jax import lax
from jax.experimental import pallas as pl
from jax.experimental.pallas import tpu as pltpu
from jax.sharding import PartitionSpec as P

C = 128
B = 16
F32 = jnp.float32
BF16 = jnp.bfloat16
NN = (((1,), (0,)), ((), ()))
NT = (((1,), (1,)), ((), ()))
TN = (((0,), (0,)), ((), ()))
MIB = 1024 * 1024


def dot(a, b, dims=NN):
    return lax.dot_general(a, b, dims, preferred_element_type=F32)


def split(x):
    high = x.astype(BF16)
    return high, (x - high.astype(F32)).astype(BF16)


def twice(x):
    return jnp.concatenate([x, x], axis=0)


def dot3(a, b):
    (ah, al), (bh, bl) = a, b
    width = bh.shape[1]
    if width > C:
        return dot(jnp.concatenate([ah, al], axis=1), twice(bh)) + dot(ah, bl)
    rows = ah.shape[0]
    both = dot(jnp.concatenate([ah, al], axis=0), jnp.concatenate([bh, bl], axis=1))
    return both[:rows, :width] + (both[:rows, width:] + both[rows:, :width])


def iotas():
    return (
        lax.broadcasted_iota(jnp.int32, (C, C), 0),
        lax.broadcasted_iota(jnp.int32, (C, C), 1),
    )


def to_column(row, eye):
    return jnp.sum(jnp.where(eye, row, 0.0), axis=1, keepdims=True)


def to_row(column, eye):
    return jnp.sum(jnp.where(eye, column, 0.0), axis=0, keepdims=True)


def inverse_scale(rows):
    return lax.rsqrt(jnp.sum(rows * rows, axis=1, keepdims=True) + 1e-06)


def three(x):
    high, rest = x.astype(BF16), x
    rest = rest - high.astype(F32)
    return (high,) + split(rest)


def running_sums(rows, upper):
    return sum(dot(x, upper) for x in reversed(three(rows)))


def base_inverse(lower, row, col):
    on_block = (row // B) == (col // B)
    blocks = jnp.where(on_block, lower, 0.0)
    packed = sum(blocks[i * B : (i + 1) * B] for i in range(1, C // B)) + blocks[:B]
    r, c = row[:B], col[:B]
    found = jnp.where(r == c % B, 1.0, 0.0)
    first = (c // B) * B
    for j in range(B - 1):
        factor = jnp.take_along_axis(packed, first + j, axis=1)
        found = found - factor * found[j : j + 1]
    return jnp.where(on_block, jnp.concatenate([found] * (C // B), axis=0), 0.0)


def odd_rows(x, size):
    return jnp.concatenate([x[i : i + size] for i in range(size, C, 2 * size)], axis=0)


def weave(even, odd, size):
    parts = []
    for i in range(0, C // 2, size):
        parts += [even[i : i + size], odd[i : i + size]]
    return jnp.concatenate(parts, axis=0)


def even_rows(x, size):
    return jnp.concatenate([x[i : i + size] for i in range(0, C, 2 * size)], axis=0)


def inverses(lowers, row, col):
    found = [base_inverse(a, row, col) for a in lowers]
    parts = [split(a) for a in lowers]
    halves = [split(x) for x in found]
    size = B
    while size < C:
        r, c = odd_rows(row, size), odd_rows(col, size)
        mask = ((r // (2 * size)) == (c // (2 * size))) & ((r // size) != (c // size))
        nothing = jnp.zeros((C // 2, C), BF16)
        mask = jnp.where(mask, 1.0, 0.0).astype(BF16)
        joins = [tuple(odd_rows(x, size) * mask for x in part) for part in parts]
        middle = [split(dot3(a, x)) for a, x in zip(joins, halves)]
        middle = [tuple(weave(nothing, x, size) for x in part) for part in middle]
        lows = [dot3(tuple(odd_rows(x, size) for x in h), y) for h, y in zip(halves, middle)]
        lows = [odd_rows(x, size) - y for x, y in zip(found, lows)]
        found = [weave(even_rows(x, size), y, size) for x, y in zip(found, lows)]
        if 2 * size < C:
            halves = [
                tuple(weave(even_rows(x, size), y, size) for x, y in zip(h, split(low)))
                for h, low in zip(halves, lows)
            ]
        size *= 2
    return found


def fetch(pairs, sems):
    copies = [pltpu.make_async_copy(x, y, sems.at[i]) for i, (x, y) in enumerate(pairs)]
    for copy in copies:
        copy.start()
    return copies


def in_hbm(*arrays):
    return [pltpu.with_memory_space_constraint(x, pltpu.HBM) for x in arrays]


def join(moved, added):
    return jnp.concatenate([moved, added], axis=1)


def after(later, earlier):
    total = dot3(split(later[:, :C]), split(earlier))
    return join(total[:, :C], total[:, C:] + later[:, C:])


def per_chunk(ref):
    return jnp.concatenate([ref[:, i : i + C] for i in range(0, ref.shape[1], C)], axis=0)


def chunk_rows(heads, head, c):
    return pl.ds(c * C * heads + head, C, stride=heads)


def places(heads):
    place = lax.rem(lax.axis_index("seq"), heads)
    return place, [lax.bitwise_xor(place, r) for r in range(heads - 1, -1, -1)]


def local_heads(heads, mine, k32, v32, sums_ref, betas_ref, mix_ref, wu_ref, n_ref):
    chunks = sums_ref.shape[0] // heads
    row, col = iotas()
    eye = row == col
    within = row >= col
    strict = row > col
    eye16 = jnp.where(eye, 1.0, 0.0).astype(BF16)
    jobs = [(head, c) for head in mine for c in range(chunks)]
    sums = jnp.concatenate([sums_ref[pl.ds(head, chunks, stride=heads), :] for head in mine], axis=0)
    betas = jnp.concatenate([betas_ref[pl.ds(head, chunks, stride=heads), :] for head in mine], axis=0)
    filled = jnp.concatenate([sums, jnp.zeros((C - sums.shape[0], C), F32)], axis=0)
    columns = filled.T
    grown = jnp.exp(sums)
    faded = jnp.exp(sums[:, C - 1 :] - sums)
    lowers, raws, values, fades, lengths = [], [], [], [], []
    for i, (head, c) in enumerate(jobs):
        at = slice(i, i + 1)
        raw = k32[chunk_rows(heads, head, c), :].astype(BF16)
        raws.append(raw)
        values.append(v32[chunk_rows(heads, head, c), :].astype(BF16))
        both = dot(jnp.concatenate([raw, eye16], axis=0), raw, NT)
        gram, turned = both[:C], both[C:]
        square = to_row(gram, eye) + 1e-06
        scale = lax.rsqrt(square)
        lengths.append(square * scale)
        strength = betas[at] * (scale * scale)
        mix = jnp.where(within, jnp.exp(columns[:, at] - sums[at]), 0.0) * strength
        mix_ref[i] = mix
        lowers.append(jnp.where(strict, gram * mix, 0.0))
        fades.append(turned * (strength * faded[at]))
    solved = []
    for i, found in enumerate(inverses(lowers, row, col)):
        at = slice(i, i + 1)
        kept = dot(jnp.concatenate(split(found * grown[at]), axis=1), twice(raws[i]))
        fresh = dot(jnp.concatenate(split(found * lengths[i]), axis=1), twice(values[i]))
        solved.append(join(kept, fresh))
    maps = []
    for i in range(len(jobs)):
        wu_ref[i] = solved[i]
        both = dot3(split(fades[i]), split(solved[i]))
        maps.append(join(jnp.where(eye, grown[i : i + 1, C - 1 :], 0.0) - both[:, :C], both[:, C:]))
    totals = []
    for j in range(len(mine)):
        first, second, third, last = maps[j * chunks : (j + 1) * chunks]
        early = after(second, first)
        n_ref[j * chunks + 1] = first
        n_ref[j * chunks + 2] = early
        n_ref[j * chunks + 3] = after(third, early)
        totals.append(after(after(last, third), early))
    return totals


def first_kernel(
    heads, k_hbm, v_hbm, beta_hbm, log_hbm, q_hbm, q16, k32, v32, sums_ref, betas_ref, mix_ref, wu_ref, n_ref, *refs
):
    sends, (k16, v16, beta_ref, log_ref, sems) = refs[: heads - 1], refs[heads - 1 :]
    pairs = ((k_hbm, k16), (log_hbm, log_ref), (beta_hbm, beta_ref), (v_hbm, v16), (q_hbm, q16))
    *copies, late = fetch(pairs, sems)
    for copy in copies:
        copy.wait()
    k32[...] = k16[...].astype(F32)
    v32[...] = v16[...].astype(F32)
    row, col = iotas()
    sums_ref[...] = running_sums(per_chunk(log_ref), jnp.where(row <= col, 1.0, 0.0).astype(BF16))
    betas_ref[...] = per_chunk(beta_ref)
    mine = places(heads)[1][: heads - 1]
    totals = local_heads(heads, mine, k32, v32, sums_ref, betas_ref, mix_ref, wu_ref, n_ref)
    for send, total in zip(sends, totals):
        send[...] = total.astype(BF16)
    late.wait()


def maps_shapes(heads, chunks):
    return [
        jax.ShapeDtypeStruct((heads * chunks, C, C), F32),
        jax.ShapeDtypeStruct((heads * chunks, C, 2 * C), F32),
        jax.ShapeDtypeStruct((heads * chunks, C, 2 * C), F32),
    ] + [jax.ShapeDtypeStruct((C, 2 * C), BF16)] * heads


def first_maps(key, value, beta, log_decay, query):
    heads, tokens = beta.shape
    chunks = tokens // C
    here = pl.BlockSpec(memory_space=pltpu.VMEM)
    rows = jax.ShapeDtypeStruct((chunks * heads, C), F32)
    wide = jax.ShapeDtypeStruct(key.shape, F32)
    out_shape = [jax.ShapeDtypeStruct(query.shape, BF16), wide, wide, rows, rows] + maps_shapes(heads - 1, chunks)
    return pl.pallas_call(
        functools.partial(first_kernel, heads),
        in_specs=[pl.BlockSpec(memory_space=pltpu.HBM)] * 5,
        out_specs=[here] * len(out_shape),
        out_shape=out_shape,
        scratch_shapes=[
            pltpu.VMEM(key.shape, BF16),
            pltpu.VMEM(key.shape, BF16),
            pltpu.VMEM(beta.shape, F32),
            pltpu.VMEM(beta.shape, F32),
            pltpu.SemaphoreType.DMA((5,)),
        ],
        compiler_params=pltpu.CompilerParams(vmem_limit_bytes=32 * MIB),
        name="first_maps",
    )(*in_hbm(key, value, beta, log_decay, query))


def own_kernel(heads, k32, v32, sums_ref, betas_ref, mix_ref, wu_ref, n_ref, own_ref):
    mine = places(heads)[1][heads - 1 :]
    (total,) = local_heads(heads, mine, k32, v32, sums_ref, betas_ref, mix_ref, wu_ref, n_ref)
    own_ref[...] = total.astype(BF16)


def own_maps(heads, k32, v32, sums, betas):
    here = pl.BlockSpec(memory_space=pltpu.VMEM)
    out_shape = maps_shapes(1, sums.shape[0] // heads)
    return pl.pallas_call(
        functools.partial(own_kernel, heads),
        in_specs=[here] * 4,
        out_specs=[here] * len(out_shape),
        out_shape=out_shape,
        compiler_params=pltpu.CompilerParams(vmem_limit_bytes=16 * MIB),
        cost_estimate=pl.CostEstimate(flops=2000000000, bytes_accessed=8000000, transcendentals=0),
        name="own_maps",
    )(k32, v32, sums, betas)


def rows_kernel(heads, work, q16, k32, sums_ref, *refs):
    *maps, out_ref, q32 = refs
    q32[...] = q16[...].astype(F32)
    chunks = sums_ref.shape[0] // heads
    row, col = iotas()
    eye = row == col
    order = places(heads)[1]
    for j, (spot, source, slot) in enumerate(work):
        mix_ref, wu_ref, n_ref = maps[3 * source : 3 * source + 3]
        head = order[spot]
        grown = jnp.exp(sums_ref[pl.ds(head, chunks, stride=heads), :])
        for c in range(chunks):
            i = slot * chunks + c
            query, raw = q32[chunk_rows(heads, head, c), :], k32[chunk_rows(heads, head, c), :]
            pairs = dot(query.astype(BF16), raw.astype(BF16), NT) * mix_ref[i]
            both = dot3(split(pairs), split(wu_ref[i]))
            scale = inverse_scale(query)
            reach = (query * to_column(grown[c : c + 1], eye) - both[:, :C]) * scale
            fresh = both[:, C:] * scale
            if c > 0:
                earlier = dot3(split(reach), split(n_ref[i]))
                reach = earlier[:, :C]
                fresh = fresh + earlier[:, C:]
            out_ref[j, c * C : (c + 1) * C, :] = join(reach, fresh)


def row_maps(heads, work, query, k32, sums, *maps):
    tokens = query.shape[0] // heads
    here = pl.BlockSpec(memory_space=pltpu.VMEM)
    return pl.pallas_call(
        functools.partial(rows_kernel, heads, work),
        in_specs=[here] * (3 + len(maps)),
        out_specs=here,
        out_shape=jax.ShapeDtypeStruct((len(work), tokens, 2 * C), F32),
        scratch_shapes=[pltpu.VMEM(query.shape, F32)],
        compiler_params=pltpu.CompilerParams(vmem_limit_bytes=16 * MIB),
        cost_estimate=pl.CostEstimate(flops=2000000000, bytes_accessed=8000000, transcendentals=0),
        name="row_maps",
    )(query, k32, sums, *maps)


def small_call(kernel, out_shape, *args):
    here = pl.BlockSpec(memory_space=pltpu.VMEM)
    return pl.pallas_call(
        kernel,
        in_specs=[here] * len(args),
        out_specs=[here] * len(out_shape),
        out_shape=out_shape,
        compiler_params=pltpu.CompilerParams(vmem_limit_bytes=8 * MIB),
        name=kernel.__name__,
    )(*args)


def moved_on(maps, state16, added):
    high, low = split(maps)
    return dot(jnp.concatenate([high, low], axis=1), twice(state16)) + added


def times_parts(maps16, x):
    width = x.shape[1]
    both = dot(maps16, jnp.concatenate(split(x), axis=1))
    return both[:, :width] + both[:, width:]


def by_place(parts, work):
    heads = len(parts)
    place = places(heads)[0]
    for p in range(heads):

        @pl.when(place == p)
        def _(p=p):
            members = [i ^ p for i in range(heads)]
            work([parts[heads - 1 - r] for r in members], members)


def group_state(*refs):
    out_ref = refs[-1]

    def work(parts, _):
        state = parts[0][:, C:].astype(F32)
        for part in parts[1:]:
            state = times_parts(part[:, :C], state) + part[:, C:].astype(F32)
        out_ref[...] = state.astype(BF16)

    by_place(refs[:-1], work)


def group_prefix(*refs):
    parts, (maps_ref, added_ref, total_ref) = refs[:-3], refs[-3:]
    row, col = iotas()

    def work(parts, members):
        total = join(jnp.where(row == col, 1.0, 0.0), jnp.zeros((C, C), F32))
        for i, (part, r) in enumerate(zip(parts, members)):
            maps_ref[r] = jnp.concatenate(split(total[:, :C]), axis=1)
            added_ref[r] = total[:, C:]
            if i == 0:
                total = part[...].astype(F32)
            else:
                total = times_parts(part[:, :C], total)
                total = join(total[:, :C], total[:, C:] + part[:, C:].astype(F32))
        total_ref[...] = total.astype(BF16)

    by_place(parts, work)


def group_states(upper_only, maps_ref, added_ref, state_ref, *outs):
    state = state_ref[...]
    if upper_only:
        state = jnp.where(lax.axis_index("seq") < len(outs), jnp.zeros_like(state), state)
    both = twice(state)
    for r, out_ref in enumerate(outs):
        out_ref[...] = (dot(maps_ref[r], both) + added_ref[r]).astype(BF16)


def states_of_upper(*refs):
    group_states(True, *refs)


def states_given(*refs):
    group_states(False, *refs)


def prefix(total, heads):
    count = lax.axis_size("seq")
    groups = [list(range(i, count, heads)) for i in range(heads)]
    me = lax.axis_index("seq") // heads
    totals = lax.all_gather(total, "seq", axis_index_groups=groups)

    def step(d, state):
        longer = jnp.einsum("ik,pkw->iw", totals[d, :, :C], jnp.stack(split(state)), preferred_element_type=F32)
        return jnp.where(d < me, longer + totals[d, :, C:].astype(F32), state)

    start = jnp.zeros((C, C), F32)
    return lax.fori_loop(0, count // heads - 1, step, start).astype(BF16)


def apply_kernel(groups, rows0_ref, rows1_ref, *refs):
    states, (keep_ref, send_ref) = refs[:-2], refs[-2:]
    heads = len(states)
    half, tokens, _ = rows0_ref.shape
    block = tokens // groups
    order = places(heads)[1]
    core = lax.rem(lax.axis_index("head"), 2)
    for out_ref, parity in ((send_ref, 1 - core), (keep_ref, core)):
        for i in range(groups // 2):
            rows = pl.ds(pl.multiple_of((2 * i + parity) * block, block), block)
            for spot, state in enumerate(states):
                ref, j = (rows0_ref, rows1_ref)[spot // half], spot % half
                attended = moved_on(ref[j, rows, :C], state[...], ref[j, rows, C:])
                columns = pl.ds(pl.multiple_of(order[spot] * C, C), C)
                out_ref[i, :, columns] = attended.astype(BF16)


def apply(rows, states, groups):
    _, tokens, _ = rows[0].shape
    heads = len(states)
    here = pl.BlockSpec(memory_space=pltpu.VMEM)
    out = jax.ShapeDtypeStruct((groups // 2, tokens // groups, heads * C), BF16)
    return pl.pallas_call(
        functools.partial(apply_kernel, groups),
        in_specs=[here] * (2 + heads),
        out_specs=[here] * 2,
        out_shape=[out, out],
        compiler_params=pltpu.CompilerParams(vmem_limit_bytes=8 * MIB),
        name="apply",
    )(*rows, *states)


def project_kernel(other, start, keep_ref, got_ref, w_ref, w2_ref, out_ref):
    pair = lax.axis_index("head") // 2
    index = 1 - pair if other else pair
    columns = slice(start, start + out_ref.shape[1])
    shares = dot(keep_ref[index], w_ref[:, columns]) + dot(got_ref[index], w2_ref[:, columns])
    out_ref[...] = shares.astype(out_ref.dtype)


def project(other, start, width, keep, got, weight, weight2):
    _, block, depth = keep.shape
    return pl.pallas_call(
        functools.partial(project_kernel, other, start),
        out_shape=jax.ShapeDtypeStruct((block, width), BF16 if other else F32),
        compiler_params=pltpu.CompilerParams(vmem_limit_bytes=20 * MIB),
        cost_estimate=pl.CostEstimate(
            flops=4 * block * depth * width, bytes_accessed=4 * depth * width, transcendentals=0
        ),
        name="project",
    )(keep, got, weight, weight2)


def add_kernel(mine_ref, theirs_ref, *refs):
    refs[-1][...] = (mine_ref[...] + theirs_ref[...].astype(F32)).astype(BF16)


def add_part(index, parts, mine, theirs, earlier):
    block, width = mine.shape
    here = pl.BlockSpec(memory_space=pltpu.VMEM)
    return pl.pallas_call(
        add_kernel,
        grid=(1,),
        in_specs=[here, here] + [pl.BlockSpec(memory_space=pl.ANY)] * len(earlier),
        out_specs=pl.BlockSpec((block, width), lambda i: (0, index)),
        out_shape=jax.ShapeDtypeStruct((block, width * parts), BF16),
        input_output_aliases={2: 0} if earlier else {},
        compiler_params=pltpu.CompilerParams(vmem_limit_bytes=8 * MIB),
        name="add_part",
    )(mine, theirs, *earlier)


def swap(x, axis, bit):
    count = lax.axis_size(axis)
    return lax.ppermute(x, axis, [(i, i ^ bit) for i in range(count)])


def body(query, key, value, beta, log_decay, out_weight):
    tokens, heads, _ = key.shape
    count = lax.axis_size("seq")
    flat = lambda x: x.reshape(tokens * heads, C)
    weight2 = swap(out_weight, "head", 1)
    q16, k32, v32, sums, betas, mix, wu, states, *sends = first_maps(
        flat(key), flat(value), beta, log_decay, flat(query)
    )
    away = range(heads - 1, 0, -1)
    parts = [swap(x, "seq", r) for r, x in zip(away, sends)]
    *own_chunks, own = own_maps(heads, k32, v32, sums, betas)
    parts = lax.optimization_barrier(parts + [own])
    first = (mix, wu, states)
    rows0 = row_maps(heads, ((0, 0, 0), (1, 0, 1)), q16, k32, sums, *first)
    rows1 = row_maps(heads, ((2, 0, 2), (3, 1, 0)), q16, k32, sums, *first, *own_chunks)
    square = jax.ShapeDtypeStruct((C, C), BF16)
    both = jax.ShapeDtypeStruct((heads, C, 2 * C), BF16)
    added = jax.ShapeDtypeStruct((heads, C, C), F32)
    (state,) = small_call(group_state, [square], *parts)
    *maps, total = small_call(group_prefix, [both, added, jax.ShapeDtypeStruct((C, 2 * C), BF16)], *parts)
    if count == 2 * heads:
        lower = swap(state, "seq", heads)
        rows0, maps, lower = lax.optimization_barrier((rows0, maps, lower))
        keep, *sends = small_call(states_of_upper, [square] * heads, *maps, lower)
    else:
        keep, *sends = small_call(states_given, [square] * heads, *maps, prefix(total, heads))
    entering = [swap(sends[r - 1], "seq", r) for r in away] + [keep]
    keep, away = apply((rows0, rows1), entering, lax.axis_size("head"))
    got = swap(away, "head", 1)
    parts = 2
    width = out_weight.shape[1] // parts
    ranges = [(i * width, width) for i in range(parts)]
    args = (keep, got, out_weight, weight2)
    theirs = [swap(project(True, *x, *args), "head", 2) for x in ranges]
    mine = [project(False, *x, *args) for x in ranges]
    mixed = []
    for i in range(parts):
        mixed = [add_part(i, parts, mine[i], theirs[i], mixed)]
    return mixed[0]


def solution(mesh):
    in_specs = (
        P("seq", "head", None),
        P("seq", "head", None),
        P("seq", "head", None),
        P("head", "seq"),
        P("head", "seq"),
        P("head", None),
    )
    out_specs = P(("seq", "head"), None)
    return jax.shard_map(body, mesh=mesh, in_specs=in_specs, out_specs=out_specs, check_vma=False)
```

```python
import functools

import jax
import jax.numpy as jnp
from jax import lax
from jax.experimental import pallas as pl
from jax.experimental.pallas import tpu as pltpu
from jax.sharding import PartitionSpec as P

C = 128
B = 16
F32 = jnp.float32
BF16 = jnp.bfloat16
NN = (((1,), (0,)), ((), ()))
NT = (((1,), (1,)), ((), ()))
TN = (((0,), (0,)), ((), ()))
MIB = 1024 * 1024


def dot(a, b, dims=NN):
    return lax.dot_general(a, b, dims, preferred_element_type=F32)


def split(x):
    high = x.astype(BF16)
    return high, (x - high.astype(F32)).astype(BF16)


def twice(x):
    return jnp.concatenate([x, x], axis=0)


def dot3(a, b):
    (ah, al), (bh, bl) = a, b
    width = bh.shape[1]
    if width > C:
        return dot(jnp.concatenate([ah, al], axis=1), twice(bh)) + dot(ah, bl)
    rows = ah.shape[0]
    both = dot(jnp.concatenate([ah, al], axis=0), jnp.concatenate([bh, bl], axis=1))
    return both[:rows, :width] + (both[:rows, width:] + both[rows:, :width])


def iotas():
    return (
        lax.broadcasted_iota(jnp.int32, (C, C), 0),
        lax.broadcasted_iota(jnp.int32, (C, C), 1),
    )


def to_column(row, eye):
    return jnp.sum(jnp.where(eye, row, 0.0), axis=1, keepdims=True)


def to_row(column, eye):
    return jnp.sum(jnp.where(eye, column, 0.0), axis=0, keepdims=True)


def inverse_scale(rows):
    return lax.rsqrt(jnp.sum(rows * rows, axis=1, keepdims=True) + 1e-06)


def three(x):
    high, rest = x.astype(BF16), x
    rest = rest - high.astype(F32)
    return (high,) + split(rest)


def running_sums(rows, upper):
    return sum(dot(x, upper) for x in reversed(three(rows)))


def base_inverse(lower, row, col):
    on_block = (row // B) == (col // B)
    blocks = jnp.where(on_block, lower, 0.0)
    packed = sum(blocks[i * B : (i + 1) * B] for i in range(1, C // B)) + blocks[:B]
    r, c = row[:B], col[:B]
    found = jnp.where(r == c % B, 1.0, 0.0)
    first = (c // B) * B
    for j in range(B - 1):
        factor = jnp.take_along_axis(packed, first + j, axis=1)
        found = found - factor * found[j : j + 1]
    return jnp.where(on_block, jnp.concatenate([found] * (C // B), axis=0), 0.0)


def odd_rows(x, size):
    return jnp.concatenate([x[i : i + size] for i in range(size, C, 2 * size)], axis=0)


def weave(even, odd, size):
    parts = []
    for i in range(0, C // 2, size):
        parts += [even[i : i + size], odd[i : i + size]]
    return jnp.concatenate(parts, axis=0)


def even_rows(x, size):
    return jnp.concatenate([x[i : i + size] for i in range(0, C, 2 * size)], axis=0)


def inverses(lowers, row, col):
    found = [base_inverse(a, row, col) for a in lowers]
    parts = [split(a) for a in lowers]
    halves = [split(x) for x in found]
    size = B
    while size < C:
        r, c = odd_rows(row, size), odd_rows(col, size)
        mask = ((r // (2 * size)) == (c // (2 * size))) & ((r // size) != (c // size))
        nothing = jnp.zeros((C // 2, C), BF16)
        mask = jnp.where(mask, 1.0, 0.0).astype(BF16)
        joins = [tuple(odd_rows(x, size) * mask for x in part) for part in parts]
        middle = [split(dot3(a, x)) for a, x in zip(joins, halves)]
        middle = [tuple(weave(nothing, x, size) for x in part) for part in middle]
        lows = [dot3(tuple(odd_rows(x, size) for x in h), y) for h, y in zip(halves, middle)]
        lows = [odd_rows(x, size) - y for x, y in zip(found, lows)]
        found = [weave(even_rows(x, size), y, size) for x, y in zip(found, lows)]
        if 2 * size < C:
            halves = [
                tuple(weave(even_rows(x, size), y, size) for x, y in zip(h, split(low)))
                for h, low in zip(halves, lows)
            ]
        size *= 2
    return found


def in_hbm(*arrays):
    return [pltpu.with_memory_space_constraint(x, pltpu.HBM) for x in arrays]


def join(moved, added):
    return jnp.concatenate([moved, added], axis=1)


def after(later, earlier):
    total = dot3(split(later[:, :C]), split(earlier))
    return join(total[:, :C], total[:, C:] + later[:, C:])


def per_chunk(ref):
    return jnp.concatenate([ref[:, i : i + C] for i in range(0, ref.shape[1], C)], axis=0)


def chunk_rows(heads, head, c):
    return pl.ds(c * C * heads + head, C, stride=heads)


def places(heads):
    place = lax.rem(lax.axis_index("seq"), heads)
    return place, [lax.bitwise_xor(place, r) for r in range(heads - 1, -1, -1)]


def local_heads(heads, mine, k32, v32, sums_ref, betas_ref, mix_ref, wu_ref, n_ref):
    chunks = sums_ref.shape[0] // heads
    row, col = iotas()
    eye = row == col
    within = row >= col
    strict = row > col
    eye16 = jnp.where(eye, 1.0, 0.0).astype(BF16)
    jobs = [(head, c) for head in mine for c in range(chunks)]
    sums = jnp.concatenate([sums_ref[pl.ds(head, chunks, stride=heads), :] for head in mine], axis=0)
    betas = jnp.concatenate([betas_ref[pl.ds(head, chunks, stride=heads), :] for head in mine], axis=0)
    filled = jnp.concatenate([sums, jnp.zeros((C - sums.shape[0], C), F32)], axis=0)
    columns = filled.T
    grown = jnp.exp(sums)
    faded = jnp.exp(sums[:, C - 1 :] - sums)
    lowers, raws, values, fades, lengths = [], [], [], [], []
    for i, (head, c) in enumerate(jobs):
        at = slice(i, i + 1)
        raw = k32[chunk_rows(heads, head, c), :].astype(BF16)
        raws.append(raw)
        values.append(v32[chunk_rows(heads, head, c), :].astype(BF16))
        both = dot(jnp.concatenate([raw, eye16], axis=0), raw, NT)
        gram, turned = both[:C], both[C:]
        square = to_row(gram, eye) + 1e-06
        scale = lax.rsqrt(square)
        lengths.append(square * scale)
        strength = betas[at] * (scale * scale)
        mix = jnp.where(within, jnp.exp(columns[:, at] - sums[at]), 0.0) * strength
        mix_ref[i] = mix
        lowers.append(jnp.where(strict, gram * mix, 0.0))
        fades.append(turned * (strength * faded[at]))
    solved = []
    for i, found in enumerate(inverses(lowers, row, col)):
        at = slice(i, i + 1)
        kept = dot(jnp.concatenate(split(found * grown[at]), axis=1), twice(raws[i]))
        fresh = dot(jnp.concatenate(split(found * lengths[i]), axis=1), twice(values[i]))
        solved.append(join(kept, fresh))
    maps = []
    for i in range(len(jobs)):
        wu_ref[i] = solved[i]
        both = dot3(split(fades[i]), split(solved[i]))
        maps.append(join(jnp.where(eye, grown[i : i + 1, C - 1 :], 0.0) - both[:, :C], both[:, C:]))
    totals = []
    for j in range(len(mine)):
        first, second, third, last = maps[j * chunks : (j + 1) * chunks]
        early = after(second, first)
        n_ref[j * chunks + 1] = first
        n_ref[j * chunks + 2] = early
        n_ref[j * chunks + 3] = after(third, early)
        totals.append(after(after(last, third), early))
    return totals


def first_kernel(
    heads, k_hbm, v_hbm, beta_hbm, log_hbm, q_hbm, q16, k32, v32, sums_ref, betas_ref, mix_ref, wu_ref, n_ref, *refs
):
    sends, (k16, v16, beta_ref, log_ref, sems) = refs[: heads - 1], refs[heads - 1 :]
    pairs = ((log_hbm, log_ref), (beta_hbm, beta_ref), (k_hbm, k16), (v_hbm, v16), (q_hbm, q16))
    copies = [pltpu.make_async_copy(x, y, sems.at[i]) for i, (x, y) in enumerate(pairs)]
    *early, late = copies
    for copy in early:
        copy.start()
    for copy in early[:2]:
        copy.wait()
    row, col = iotas()
    sums_ref[...] = running_sums(per_chunk(log_ref), jnp.where(row <= col, 1.0, 0.0).astype(BF16))
    betas_ref[...] = per_chunk(beta_ref)
    early[2].wait()
    k32[...] = k16[...].astype(F32)
    early[3].wait()
    late.start()
    v32[...] = v16[...].astype(F32)
    mine = places(heads)[1][: heads - 1]
    totals = local_heads(heads, mine, k32, v32, sums_ref, betas_ref, mix_ref, wu_ref, n_ref)
    for send, total in zip(sends, totals):
        send[...] = total.astype(BF16)
    late.wait()


def maps_shapes(heads, chunks):
    return [
        jax.ShapeDtypeStruct((heads * chunks, C, C), F32),
        jax.ShapeDtypeStruct((heads * chunks, C, 2 * C), F32),
        jax.ShapeDtypeStruct((heads * chunks, C, 2 * C), F32),
    ] + [jax.ShapeDtypeStruct((C, 2 * C), BF16)] * heads


def first_maps(key, value, beta, log_decay, query):
    heads, tokens = beta.shape
    chunks = tokens // C
    here = pl.BlockSpec(memory_space=pltpu.VMEM)
    rows = jax.ShapeDtypeStruct((chunks * heads, C), F32)
    wide = jax.ShapeDtypeStruct(key.shape, F32)
    out_shape = [jax.ShapeDtypeStruct(query.shape, BF16), wide, wide, rows, rows] + maps_shapes(heads - 1, chunks)
    return pl.pallas_call(
        functools.partial(first_kernel, heads),
        in_specs=[pl.BlockSpec(memory_space=pltpu.HBM)] * 5,
        out_specs=[here] * len(out_shape),
        out_shape=out_shape,
        scratch_shapes=[
            pltpu.VMEM(key.shape, BF16),
            pltpu.VMEM(key.shape, BF16),
            pltpu.VMEM(beta.shape, F32),
            pltpu.VMEM(beta.shape, F32),
            pltpu.SemaphoreType.DMA((5,)),
        ],
        compiler_params=pltpu.CompilerParams(vmem_limit_bytes=32 * MIB),
        name="first_maps",
    )(*in_hbm(key, value, beta, log_decay, query))


def own_kernel(heads, k32, v32, sums_ref, betas_ref, mix_ref, wu_ref, n_ref, own_ref):
    mine = places(heads)[1][heads - 1 :]
    (total,) = local_heads(heads, mine, k32, v32, sums_ref, betas_ref, mix_ref, wu_ref, n_ref)
    own_ref[...] = total.astype(BF16)


def own_maps(heads, k32, v32, sums, betas):
    here = pl.BlockSpec(memory_space=pltpu.VMEM)
    out_shape = maps_shapes(1, sums.shape[0] // heads)
    return pl.pallas_call(
        functools.partial(own_kernel, heads),
        in_specs=[here] * 4,
        out_specs=[here] * len(out_shape),
        out_shape=out_shape,
        compiler_params=pltpu.CompilerParams(vmem_limit_bytes=16 * MIB),
        cost_estimate=pl.CostEstimate(flops=2000000000, bytes_accessed=8000000, transcendentals=0),
        name="own_maps",
    )(k32, v32, sums, betas)


def rows_kernel(heads, spot, slot, q_ref, k32, sums_ref, mix_ref, wu_ref, n_ref, out_ref, *wide):
    if wide:
        wide[0][...] = q_ref[...].astype(F32)
    q32 = wide[0] if wide else q_ref
    chunks = sums_ref.shape[0] // heads
    row, col = iotas()
    eye = row == col
    head = places(heads)[1][spot]
    grown = jnp.exp(sums_ref[pl.ds(head, chunks, stride=heads), :])
    for c in range(chunks):
        i = slot * chunks + c
        query, raw = q32[chunk_rows(heads, head, c), :], k32[chunk_rows(heads, head, c), :]
        pairs = dot(query.astype(BF16), raw.astype(BF16), NT) * mix_ref[i]
        both = dot3(split(pairs), split(wu_ref[i]))
        scale = inverse_scale(query)
        reach = (query * to_column(grown[c : c + 1], eye) - both[:, :C]) * scale
        fresh = both[:, C:] * scale
        if c > 0:
            earlier = dot3(split(reach), split(n_ref[i]))
            reach = earlier[:, :C]
            fresh = fresh + earlier[:, C:]
        out_ref[c * C : (c + 1) * C, :] = join(reach, fresh)


def row_maps(heads, spot, slot, query, *maps):
    tokens = query.shape[0] // heads
    here = pl.BlockSpec(memory_space=pltpu.VMEM)
    out_shape = [jax.ShapeDtypeStruct((tokens, 2 * C), F32)]
    if query.dtype == BF16:
        out_shape.append(jax.ShapeDtypeStruct(query.shape, F32))
    return pl.pallas_call(
        functools.partial(rows_kernel, heads, spot, slot),
        in_specs=[here] * (1 + len(maps)),
        out_specs=[here] * len(out_shape),
        out_shape=out_shape,
        compiler_params=pltpu.CompilerParams(vmem_limit_bytes=16 * MIB),
        cost_estimate=pl.CostEstimate(flops=1000000000, bytes_accessed=4000000, transcendentals=0),
        name="row_maps",
    )(query, *maps)


def small_call(kernel, out_shape, *args):
    here = pl.BlockSpec(memory_space=pltpu.VMEM)
    return pl.pallas_call(
        kernel,
        in_specs=[here] * len(args),
        out_specs=[here] * len(out_shape),
        out_shape=out_shape,
        compiler_params=pltpu.CompilerParams(vmem_limit_bytes=8 * MIB),
        name=kernel.__name__,
    )(*args)


def moved_on(maps, state16, added):
    high, low = split(maps)
    return dot(jnp.concatenate([high, low], axis=1), twice(state16)) + added


def times_parts(maps16, x):
    width = x.shape[1]
    both = dot(maps16, jnp.concatenate(split(x), axis=1))
    return both[:, :width] + both[:, width:]


def by_place(parts, work):
    heads = len(parts)
    place = places(heads)[0]
    for p in range(heads):

        @pl.when(place == p)
        def _(p=p):
            members = [i ^ p for i in range(heads)]
            work([parts[heads - 1 - r] for r in members], members)


def group_state(*refs):
    out_ref = refs[-1]

    def work(parts, _):
        state = parts[0][:, C:].astype(F32)
        for part in parts[1:]:
            state = times_parts(part[:, :C], state) + part[:, C:].astype(F32)
        out_ref[...] = state.astype(BF16)

    by_place(refs[:-1], work)


def group_prefix(*refs):
    parts, (maps_ref, added_ref, total_ref) = refs[:-3], refs[-3:]
    row, col = iotas()

    def work(parts, members):
        total = join(jnp.where(row == col, 1.0, 0.0), jnp.zeros((C, C), F32))
        for i, (part, r) in enumerate(zip(parts, members)):
            maps_ref[r] = jnp.concatenate(split(total[:, :C]), axis=1)
            added_ref[r] = total[:, C:]
            if i == 0:
                total = part[...].astype(F32)
            else:
                total = times_parts(part[:, :C], total)
                total = join(total[:, :C], total[:, C:] + part[:, C:].astype(F32))
        total_ref[...] = total.astype(BF16)

    by_place(parts, work)


def group_states(upper_only, maps_ref, added_ref, state_ref, *outs):
    state = state_ref[...]
    if upper_only:
        state = jnp.where(lax.axis_index("seq") < len(outs), jnp.zeros_like(state), state)
    both = twice(state)
    for r, out_ref in enumerate(outs):
        out_ref[...] = (dot(maps_ref[r], both) + added_ref[r]).astype(BF16)


def states_of_upper(*refs):
    group_states(True, *refs)


def states_given(*refs):
    group_states(False, *refs)


def prefix(total, heads):
    count = lax.axis_size("seq")
    groups = [list(range(i, count, heads)) for i in range(heads)]
    me = lax.axis_index("seq") // heads
    totals = lax.all_gather(total, "seq", axis_index_groups=groups)

    def step(d, state):
        longer = jnp.einsum("ik,pkw->iw", totals[d, :, :C], jnp.stack(split(state)), preferred_element_type=F32)
        return jnp.where(d < me, longer + totals[d, :, C:].astype(F32), state)

    start = jnp.zeros((C, C), F32)
    return lax.fori_loop(0, count // heads - 1, step, start).astype(BF16)


def apply_kernel(groups, other, *refs):
    heads = (len(refs) - 2) // 2
    rows_refs, states, (keep_ref, send_ref) = refs[:heads], refs[heads : 2 * heads], refs[2 * heads :]
    block = rows_refs[0].shape[0] // groups
    order = places(heads)[1]
    member = lax.axis_index("head")
    pair, core = member // 2, lax.rem(member, 2)
    pair = 1 - pair if other else pair
    for out_ref, parity in ((send_ref, 1 - core), (keep_ref, core)):
        rows = pl.ds(pl.multiple_of((2 * pair + parity) * block, block), block)
        for head, rows_ref, state in zip(order, rows_refs, states):
            attended = moved_on(rows_ref[rows, :C], state[...], rows_ref[rows, C:])
            out_ref[:, pl.ds(pl.multiple_of(head * C, C), C)] = attended.astype(BF16)


def apply(other, rows, states, groups):
    heads = len(states)
    here = pl.BlockSpec(memory_space=pltpu.VMEM)
    out = jax.ShapeDtypeStruct((rows[0].shape[0] // groups, heads * C), BF16)
    return pl.pallas_call(
        functools.partial(apply_kernel, groups, other),
        in_specs=[here] * (2 * heads),
        out_specs=[here] * 2,
        out_shape=[out, out],
        compiler_params=pltpu.CompilerParams(vmem_limit_bytes=8 * MIB),
        cost_estimate=pl.CostEstimate(flops=200000000, bytes_accessed=1000000, transcendentals=0),
        name="apply",
    )(*rows, *states)


def project_kernel(start, keep_ref, got_ref, w_ref, w2_ref, out_ref):
    columns = slice(start, start + out_ref.shape[1])
    shares = dot(keep_ref[...], w_ref[:, columns]) + dot(got_ref[...], w2_ref[:, columns])
    out_ref[...] = shares.astype(out_ref.dtype)


def project(dtype, start, width, keep, got, weight, weight2):
    block, depth = keep.shape
    return pl.pallas_call(
        functools.partial(project_kernel, start),
        out_shape=jax.ShapeDtypeStruct((block, width), dtype),
        compiler_params=pltpu.CompilerParams(vmem_limit_bytes=20 * MIB),
        cost_estimate=pl.CostEstimate(
            flops=4 * block * depth * width, bytes_accessed=4 * depth * width, transcendentals=0
        ),
        name="project",
    )(keep, got, weight, weight2)


def add_kernel(mine_ref, theirs_ref, *refs):
    refs[-1][...] = (mine_ref[...] + theirs_ref[...].astype(F32)).astype(BF16)


def add_part(index, parts, mine, theirs, earlier):
    block, width = mine.shape
    here = pl.BlockSpec(memory_space=pltpu.VMEM)
    return pl.pallas_call(
        add_kernel,
        grid=(1,),
        in_specs=[here, here] + [pl.BlockSpec(memory_space=pl.ANY)] * len(earlier),
        out_specs=pl.BlockSpec((block, width), lambda i: (0, index)),
        out_shape=jax.ShapeDtypeStruct((block, width * parts), BF16),
        input_output_aliases={2: 0} if earlier else {},
        compiler_params=pltpu.CompilerParams(vmem_limit_bytes=8 * MIB),
        name="add_part",
    )(mine, theirs, *earlier)


def swap(x, axis, bit):
    count = lax.axis_size(axis)
    return lax.ppermute(x, axis, [(i, i ^ bit) for i in range(count)])


def body(query, key, value, beta, log_decay, out_weight):
    tokens, heads, _ = key.shape
    count = lax.axis_size("seq")
    flat = lambda x: x.reshape(tokens * heads, C)
    weight2 = swap(out_weight, "head", 1)
    q16, k32, v32, sums, betas, mix, wu, states, *sends = first_maps(
        flat(key), flat(value), beta, log_decay, flat(query)
    )
    away = range(heads - 1, 0, -1)
    parts = [swap(x, "seq", r) for r, x in zip(away, sends)]
    *own_chunks, own = own_maps(heads, k32, v32, sums, betas)
    first = (k32, sums, mix, wu, states)
    own_maps_here = (k32, sums, *own_chunks)
    rows3, q32 = row_maps(heads, 0, 0, q16, *first)
    rows3, *parts = lax.optimization_barrier([rows3] + parts + [own])
    square = jax.ShapeDtypeStruct((C, C), BF16)
    both = jax.ShapeDtypeStruct((heads, C, 2 * C), BF16)
    added = jax.ShapeDtypeStruct((heads, C, C), F32)
    (state,) = small_call(group_state, [square], *parts)
    state, q32 = lax.optimization_barrier((state, q32))
    (rows2,) = row_maps(heads, 1, 1, q32, *first)
    *maps, total = small_call(group_prefix, [both, added, jax.ShapeDtypeStruct((C, 2 * C), BF16)], *parts)
    if count == 2 * heads:
        lower = swap(state, "seq", heads)
        rows2, maps, lower = lax.optimization_barrier((rows2, maps, lower))
        keep, *sends = small_call(states_of_upper, [square] * heads, *maps, lower)
    else:
        keep, *sends = small_call(states_given, [square] * heads, *maps, prefix(total, heads))
    keep, q32 = lax.optimization_barrier((keep, q32))
    (rows1,) = row_maps(heads, 2, 2, q32, *first)
    (rows0,) = row_maps(heads, 3, 0, q32, *own_maps_here)
    entering = [swap(sends[r - 1], "seq", r) for r in away] + [keep]
    rows = (rows3, rows2, rows1, rows0)
    groups = lax.axis_size("head")
    keep, send = apply(True, rows, entering, groups)
    across = (keep, swap(send, "head", 1), out_weight, weight2)
    keep, send = apply(False, rows, entering, groups)
    here = (keep, swap(send, "head", 1), out_weight, weight2)
    parts = 2
    width = out_weight.shape[1] // parts
    ranges = [(i * width, width) for i in range(parts)]
    theirs = [swap(project(BF16, *x, *across), "head", 2) for x in ranges]
    mine = [project(F32, *x, *here) for x in ranges]
    mixed = []
    for i in range(parts):
        mixed = [add_part(i, parts, mine[i], theirs[i], mixed)]
    return mixed[0]


def solution(mesh):
    in_specs = (
        P("seq", "head", None),
        P("seq", "head", None),
        P("seq", "head", None),
        P("head", "seq"),
        P("head", "seq"),
        P("head", None),
    )
    out_specs = P(("seq", "head"), None)
    return jax.shard_map(body, mesh=mesh, in_specs=in_specs, out_specs=out_specs, check_vma=False)
```

```python
import functools

import jax
import jax.numpy as jnp
from jax import lax
from jax.experimental import pallas as pl
from jax.experimental.pallas import tpu as pltpu
from jax.sharding import PartitionSpec as P

C = 128
B = 16
F32 = jnp.float32
BF16 = jnp.bfloat16
NN = (((1,), (0,)), ((), ()))
NT = (((1,), (1,)), ((), ()))
TN = (((0,), (0,)), ((), ()))
MIB = 1024 * 1024


def dot(a, b, dims=NN):
    return lax.dot_general(a, b, dims, preferred_element_type=F32)


def split(x):
    high = x.astype(BF16)
    return high, (x - high.astype(F32)).astype(BF16)


def twice(x):
    return jnp.concatenate([x, x], axis=0)


def dot3(a, b):
    (ah, al), (bh, bl) = a, b
    width = bh.shape[1]
    if width > C:
        return dot(jnp.concatenate([ah, al], axis=1), twice(bh)) + dot(ah, bl)
    rows = ah.shape[0]
    both = dot(jnp.concatenate([ah, al], axis=0), jnp.concatenate([bh, bl], axis=1))
    return both[:rows, :width] + (both[:rows, width:] + both[rows:, :width])


def iotas():
    return (
        lax.broadcasted_iota(jnp.int32, (C, C), 0),
        lax.broadcasted_iota(jnp.int32, (C, C), 1),
    )


def to_column(row, eye):
    return jnp.sum(jnp.where(eye, row, 0.0), axis=1, keepdims=True)


def to_row(column, eye):
    return jnp.sum(jnp.where(eye, column, 0.0), axis=0, keepdims=True)


def inverse_scale(rows):
    return lax.rsqrt(jnp.sum(rows * rows, axis=1, keepdims=True) + 1e-06)


def three(x):
    high, rest = x.astype(BF16), x
    rest = rest - high.astype(F32)
    return (high,) + split(rest)


def running_sums(rows, upper):
    return sum(dot(x, upper) for x in reversed(three(rows)))


def base_inverse(lower, row, col):
    on_block = (row // B) == (col // B)
    blocks = jnp.where(on_block, lower, 0.0)
    packed = sum(blocks[i * B : (i + 1) * B] for i in range(1, C // B)) + blocks[:B]
    r, c = row[:B], col[:B]
    found = jnp.where(r == c % B, 1.0, 0.0)
    first = (c // B) * B
    for j in range(B - 1):
        factor = jnp.take_along_axis(packed, first + j, axis=1)
        found = found - factor * found[j : j + 1]
    return jnp.where(on_block, jnp.concatenate([found] * (C // B), axis=0), 0.0)


def odd_rows(x, size):
    return jnp.concatenate([x[i : i + size] for i in range(size, C, 2 * size)], axis=0)


def weave(even, odd, size):
    parts = []
    for i in range(0, C // 2, size):
        parts += [even[i : i + size], odd[i : i + size]]
    return jnp.concatenate(parts, axis=0)


def even_rows(x, size):
    return jnp.concatenate([x[i : i + size] for i in range(0, C, 2 * size)], axis=0)


def inverses(lowers, row, col):
    found = [base_inverse(a, row, col) for a in lowers]
    parts = [split(a) for a in lowers]
    halves = [split(x) for x in found]
    size = B
    while size < C:
        r, c = odd_rows(row, size), odd_rows(col, size)
        mask = ((r // (2 * size)) == (c // (2 * size))) & ((r // size) != (c // size))
        nothing = jnp.zeros((C // 2, C), BF16)
        mask = jnp.where(mask, 1.0, 0.0).astype(BF16)
        joins = [tuple(odd_rows(x, size) * mask for x in part) for part in parts]
        middle = [split(dot3(a, x)) for a, x in zip(joins, halves)]
        middle = [tuple(weave(nothing, x, size) for x in part) for part in middle]
        lows = [dot3(tuple(odd_rows(x, size) for x in h), y) for h, y in zip(halves, middle)]
        lows = [odd_rows(x, size) - y for x, y in zip(found, lows)]
        found = [weave(even_rows(x, size), y, size) for x, y in zip(found, lows)]
        if 2 * size < C:
            halves = [
                tuple(weave(even_rows(x, size), y, size) for x, y in zip(h, split(low)))
                for h, low in zip(halves, lows)
            ]
        size *= 2
    return found


def in_hbm(*arrays):
    return [pltpu.with_memory_space_constraint(x, pltpu.HBM) for x in arrays]


def join(moved, added):
    return jnp.concatenate([moved, added], axis=1)


def after(later, earlier):
    total = dot3(split(later[:, :C]), split(earlier))
    return join(total[:, :C], total[:, C:] + later[:, C:])


def per_chunk(ref):
    return jnp.concatenate([ref[:, i : i + C] for i in range(0, ref.shape[1], C)], axis=0)


def chunk_rows(heads, head, c):
    return pl.ds(c * C * heads + head, C, stride=heads)


def places(heads):
    place = lax.rem(lax.axis_index("seq"), heads)
    return place, [lax.bitwise_xor(place, r) for r in range(heads - 1, -1, -1)]


def local_heads(heads, mine, k32, v32, sums_ref, betas_ref, mix_ref, wu_ref, n_ref, fetch_values=lambda: None):
    chunks = sums_ref.shape[0] // heads
    row, col = iotas()
    eye = row == col
    within = row >= col
    strict = row > col
    eye16 = jnp.where(eye, 1.0, 0.0).astype(BF16)
    jobs = [(head, c) for head in mine for c in range(chunks)]
    sums = jnp.concatenate([sums_ref[pl.ds(head, chunks, stride=heads), :] for head in mine], axis=0)
    betas = jnp.concatenate([betas_ref[pl.ds(head, chunks, stride=heads), :] for head in mine], axis=0)
    filled = jnp.concatenate([sums, jnp.zeros((C - sums.shape[0], C), F32)], axis=0)
    columns = filled.T
    grown = jnp.exp(sums)
    faded = jnp.exp(sums[:, C - 1 :] - sums)
    lowers, raws, fades, lengths = [], [], [], []
    for i, (head, c) in enumerate(jobs):
        at = slice(i, i + 1)
        raw = k32[chunk_rows(heads, head, c), :].astype(BF16)
        raws.append(raw)
        both = dot(jnp.concatenate([raw, eye16], axis=0), raw, NT)
        gram, turned = both[:C], both[C:]
        square = to_row(gram, eye) + 1e-06
        scale = lax.rsqrt(square)
        lengths.append(square * scale)
        strength = betas[at] * (scale * scale)
        mix = jnp.where(within, jnp.exp(columns[:, at] - sums[at]), 0.0) * strength
        mix_ref[i] = mix
        lowers.append(jnp.where(strict, gram * mix, 0.0))
        fades.append(turned * (strength * faded[at]))
    solved = []
    inverted = inverses(lowers, row, col)
    fetch_values()
    for i, found in enumerate(inverted):
        at = slice(i, i + 1)
        value = v32[chunk_rows(heads, jobs[i][0], jobs[i][1]), :].astype(BF16)
        kept = dot(jnp.concatenate(split(found * grown[at]), axis=1), twice(raws[i]))
        fresh = dot(jnp.concatenate(split(found * lengths[i]), axis=1), twice(value))
        solved.append(join(kept, fresh))
    maps = []
    for i in range(len(jobs)):
        wu_ref[i] = solved[i]
        both = dot3(split(fades[i]), split(solved[i]))
        maps.append(join(jnp.where(eye, grown[i : i + 1, C - 1 :], 0.0) - both[:, :C], both[:, C:]))
    totals = []
    for j in range(len(mine)):
        first, second, third, last = maps[j * chunks : (j + 1) * chunks]
        early = after(second, first)
        n_ref[j * chunks + 1] = first
        n_ref[j * chunks + 2] = early
        n_ref[j * chunks + 3] = after(third, early)
        totals.append(after(after(last, third), early))
    return totals


def first_kernel(
    heads, k_hbm, v_hbm, beta_hbm, log_hbm, q_hbm, q16, k32, v32, sums_ref, betas_ref, mix_ref, wu_ref, n_ref, *refs
):
    sends, (k16, v16, beta_ref, log_ref, sems) = refs[: heads - 1], refs[heads - 1 :]
    pairs = ((log_hbm, log_ref), (beta_hbm, beta_ref), (k_hbm, k16), (v_hbm, v16), (q_hbm, q16))
    copies = [pltpu.make_async_copy(x, y, sems.at[i]) for i, (x, y) in enumerate(pairs)]
    *early, late = copies
    for copy in early:
        copy.start()
    for copy in early[:2]:
        copy.wait()
    row, col = iotas()
    sums_ref[...] = running_sums(per_chunk(log_ref), jnp.where(row <= col, 1.0, 0.0).astype(BF16))
    betas_ref[...] = per_chunk(beta_ref)
    early[2].wait()
    k32[...] = k16[...].astype(F32)

    def fetch_values():
        early[3].wait()
        late.start()
        v32[...] = v16[...].astype(F32)

    mine = places(heads)[1][: heads - 1]
    totals = local_heads(heads, mine, k32, v32, sums_ref, betas_ref, mix_ref, wu_ref, n_ref, fetch_values)
    for send, total in zip(sends, totals):
        send[...] = total.astype(BF16)
    late.wait()


def maps_shapes(heads, chunks):
    return [
        jax.ShapeDtypeStruct((heads * chunks, C, C), F32),
        jax.ShapeDtypeStruct((heads * chunks, C, 2 * C), F32),
        jax.ShapeDtypeStruct((heads * chunks, C, 2 * C), F32),
    ] + [jax.ShapeDtypeStruct((C, 2 * C), BF16)] * heads


def first_maps(key, value, beta, log_decay, query):
    heads, tokens = beta.shape
    chunks = tokens // C
    here = pl.BlockSpec(memory_space=pltpu.VMEM)
    rows = jax.ShapeDtypeStruct((chunks * heads, C), F32)
    wide = jax.ShapeDtypeStruct(key.shape, F32)
    out_shape = [jax.ShapeDtypeStruct(query.shape, BF16), wide, wide, rows, rows] + maps_shapes(heads - 1, chunks)
    return pl.pallas_call(
        functools.partial(first_kernel, heads),
        in_specs=[pl.BlockSpec(memory_space=pltpu.HBM)] * 5,
        out_specs=[here] * len(out_shape),
        out_shape=out_shape,
        scratch_shapes=[
            pltpu.VMEM(key.shape, BF16),
            pltpu.VMEM(key.shape, BF16),
            pltpu.VMEM(beta.shape, F32),
            pltpu.VMEM(beta.shape, F32),
            pltpu.SemaphoreType.DMA((5,)),
        ],
        compiler_params=pltpu.CompilerParams(vmem_limit_bytes=32 * MIB),
        name="first_maps",
    )(*in_hbm(key, value, beta, log_decay, query))


def own_kernel(heads, k32, v32, sums_ref, betas_ref, mix_ref, wu_ref, n_ref, own_ref):
    mine = places(heads)[1][heads - 1 :]
    (total,) = local_heads(heads, mine, k32, v32, sums_ref, betas_ref, mix_ref, wu_ref, n_ref)
    own_ref[...] = total.astype(BF16)


def own_maps(heads, k32, v32, sums, betas):
    here = pl.BlockSpec(memory_space=pltpu.VMEM)
    out_shape = maps_shapes(1, sums.shape[0] // heads)
    return pl.pallas_call(
        functools.partial(own_kernel, heads),
        in_specs=[here] * 4,
        out_specs=[here] * len(out_shape),
        out_shape=out_shape,
        compiler_params=pltpu.CompilerParams(vmem_limit_bytes=16 * MIB),
        cost_estimate=pl.CostEstimate(flops=2000000000, bytes_accessed=8000000, transcendentals=0),
        name="own_maps",
    )(k32, v32, sums, betas)


def rows_kernel(heads, spot, slot, q_ref, k32, sums_ref, mix_ref, wu_ref, n_ref, out_ref, *wide):
    if wide:
        wide[0][...] = q_ref[...].astype(F32)
    q32 = wide[0] if wide else q_ref
    chunks = sums_ref.shape[0] // heads
    row, col = iotas()
    eye = row == col
    head = places(heads)[1][spot]
    grown = jnp.exp(sums_ref[pl.ds(head, chunks, stride=heads), :])
    for c in range(chunks):
        i = slot * chunks + c
        query, raw = q32[chunk_rows(heads, head, c), :], k32[chunk_rows(heads, head, c), :]
        pairs = dot(query.astype(BF16), raw.astype(BF16), NT) * mix_ref[i]
        both = dot3(split(pairs), split(wu_ref[i]))
        scale = inverse_scale(query)
        reach = (query * to_column(grown[c : c + 1], eye) - both[:, :C]) * scale
        fresh = both[:, C:] * scale
        if c > 0:
            earlier = dot3(split(reach), split(n_ref[i]))
            reach = earlier[:, :C]
            fresh = fresh + earlier[:, C:]
        out_ref[c * C : (c + 1) * C, :] = join(reach, fresh)


def row_maps(heads, spot, slot, query, *maps):
    tokens = query.shape[0] // heads
    here = pl.BlockSpec(memory_space=pltpu.VMEM)
    out_shape = [jax.ShapeDtypeStruct((tokens, 2 * C), F32)]
    if query.dtype == BF16:
        out_shape.append(jax.ShapeDtypeStruct(query.shape, F32))
    return pl.pallas_call(
        functools.partial(rows_kernel, heads, spot, slot),
        in_specs=[here] * (1 + len(maps)),
        out_specs=[here] * len(out_shape),
        out_shape=out_shape,
        compiler_params=pltpu.CompilerParams(vmem_limit_bytes=16 * MIB),
        cost_estimate=pl.CostEstimate(flops=1000000000, bytes_accessed=4000000, transcendentals=0),
        name="row_maps",
    )(query, *maps)


def small_call(kernel, out_shape, *args):
    here = pl.BlockSpec(memory_space=pltpu.VMEM)
    return pl.pallas_call(
        kernel,
        in_specs=[here] * len(args),
        out_specs=[here] * len(out_shape),
        out_shape=out_shape,
        compiler_params=pltpu.CompilerParams(vmem_limit_bytes=8 * MIB),
        name=kernel.__name__,
    )(*args)


def moved_on(maps, state16, added):
    high, low = split(maps)
    return dot(jnp.concatenate([high, low], axis=1), twice(state16)) + added


def times_parts(maps16, x):
    width = x.shape[1]
    both = dot(maps16, jnp.concatenate(split(x), axis=1))
    return both[:, :width] + both[:, width:]


def by_place(parts, work):
    heads = len(parts)
    place = places(heads)[0]
    for p in range(heads):

        @pl.when(place == p)
        def _(p=p):
            members = [i ^ p for i in range(heads)]
            work([parts[heads - 1 - r] for r in members], members)


def group_state(*refs):
    out_ref = refs[-1]

    def work(parts, _):
        state = parts[0][:, C:].astype(F32)
        for part in parts[1:]:
            state = times_parts(part[:, :C], state) + part[:, C:].astype(F32)
        out_ref[...] = state.astype(BF16)

    by_place(refs[:-1], work)


def group_prefix(*refs):
    parts, (maps_ref, added_ref, total_ref) = refs[:-3], refs[-3:]
    row, col = iotas()

    def work(parts, members):
        total = join(jnp.where(row == col, 1.0, 0.0), jnp.zeros((C, C), F32))
        for i, (part, r) in enumerate(zip(parts, members)):
            maps_ref[r] = jnp.concatenate(split(total[:, :C]), axis=1)
            added_ref[r] = total[:, C:]
            if i == 0:
                total = part[...].astype(F32)
            else:
                total = times_parts(part[:, :C], total)
                total = join(total[:, :C], total[:, C:] + part[:, C:].astype(F32))
        total_ref[...] = total.astype(BF16)

    by_place(parts, work)


def group_states(upper_only, maps_ref, added_ref, state_ref, *outs):
    state = state_ref[...]
    if upper_only:
        state = jnp.where(lax.axis_index("seq") < len(outs), jnp.zeros_like(state), state)
    both = twice(state)
    for r, out_ref in enumerate(outs):
        out_ref[...] = (dot(maps_ref[r], both) + added_ref[r]).astype(BF16)


def states_of_upper(*refs):
    group_states(True, *refs)


def states_given(*refs):
    group_states(False, *refs)


def prefix(total, heads):
    count = lax.axis_size("seq")
    groups = [list(range(i, count, heads)) for i in range(heads)]
    me = lax.axis_index("seq") // heads
    totals = lax.all_gather(total, "seq", axis_index_groups=groups)

    def step(d, state):
        longer = jnp.einsum("ik,pkw->iw", totals[d, :, :C], jnp.stack(split(state)), preferred_element_type=F32)
        return jnp.where(d < me, longer + totals[d, :, C:].astype(F32), state)

    start = jnp.zeros((C, C), F32)
    return lax.fori_loop(0, count // heads - 1, step, start).astype(BF16)


def apply_kernel(groups, other, *refs):
    heads = (len(refs) - 2) // 2
    rows_refs, states, (keep_ref, send_ref) = refs[:heads], refs[heads : 2 * heads], refs[2 * heads :]
    block = rows_refs[0].shape[0] // groups
    order = places(heads)[1]
    member = lax.axis_index("head")
    pair, core = member // 2, lax.rem(member, 2)
    pair = 1 - pair if other else pair
    for out_ref, parity in ((send_ref, 1 - core), (keep_ref, core)):
        rows = pl.ds(pl.multiple_of((2 * pair + parity) * block, block), block)
        for head, rows_ref, state in zip(order, rows_refs, states):
            attended = moved_on(rows_ref[rows, :C], state[...], rows_ref[rows, C:])
            out_ref[:, pl.ds(pl.multiple_of(head * C, C), C)] = attended.astype(BF16)


def apply(other, rows, states, groups):
    heads = len(states)
    here = pl.BlockSpec(memory_space=pltpu.VMEM)
    out = jax.ShapeDtypeStruct((rows[0].shape[0] // groups, heads * C), BF16)
    return pl.pallas_call(
        functools.partial(apply_kernel, groups, other),
        in_specs=[here] * (2 * heads),
        out_specs=[here] * 2,
        out_shape=[out, out],
        compiler_params=pltpu.CompilerParams(vmem_limit_bytes=8 * MIB),
        cost_estimate=pl.CostEstimate(flops=200000000, bytes_accessed=1000000, transcendentals=0),
        name="apply",
    )(*rows, *states)


def project_kernel(start, keep_ref, got_ref, w_ref, w2_ref, out_ref):
    columns = slice(start, start + out_ref.shape[1])
    shares = dot(keep_ref[...], w_ref[:, columns]) + dot(got_ref[...], w2_ref[:, columns])
    out_ref[...] = shares.astype(out_ref.dtype)


def project(dtype, start, width, keep, got, weight, weight2):
    block, depth = keep.shape
    return pl.pallas_call(
        functools.partial(project_kernel, start),
        out_shape=jax.ShapeDtypeStruct((block, width), dtype),
        compiler_params=pltpu.CompilerParams(vmem_limit_bytes=20 * MIB),
        cost_estimate=pl.CostEstimate(
            flops=4 * block * depth * width, bytes_accessed=4 * depth * width, transcendentals=0
        ),
        name="project",
    )(keep, got, weight, weight2)


def add_kernel(mine_ref, theirs_ref, *refs):
    refs[-1][...] = (mine_ref[...] + theirs_ref[...].astype(F32)).astype(BF16)


def add_part(index, parts, mine, theirs, earlier):
    block, width = mine.shape
    here = pl.BlockSpec(memory_space=pltpu.VMEM)
    return pl.pallas_call(
        add_kernel,
        grid=(1,),
        in_specs=[here, here] + [pl.BlockSpec(memory_space=pl.ANY)] * len(earlier),
        out_specs=pl.BlockSpec((block, width), lambda i: (0, index)),
        out_shape=jax.ShapeDtypeStruct((block, width * parts), BF16),
        input_output_aliases={2: 0} if earlier else {},
        compiler_params=pltpu.CompilerParams(vmem_limit_bytes=8 * MIB),
        name="add_part",
    )(mine, theirs, *earlier)


def swap(x, axis, bit):
    count = lax.axis_size(axis)
    return lax.ppermute(x, axis, [(i, i ^ bit) for i in range(count)])


def body(query, key, value, beta, log_decay, out_weight):
    tokens, heads, _ = key.shape
    count = lax.axis_size("seq")
    flat = lambda x: x.reshape(tokens * heads, C)
    weight2 = swap(out_weight, "head", 1)
    q16, k32, v32, sums, betas, mix, wu, states, *sends = first_maps(
        flat(key), flat(value), beta, log_decay, flat(query)
    )
    away = range(heads - 1, 0, -1)
    parts = [swap(x, "seq", r) for r, x in zip(away, sends)]
    *own_chunks, own = own_maps(heads, k32, v32, sums, betas)
    first = (k32, sums, mix, wu, states)
    own_maps_here = (k32, sums, *own_chunks)
    rows3, q32 = row_maps(heads, 0, 0, q16, *first)
    rows3, *parts = lax.optimization_barrier([rows3] + parts + [own])
    square = jax.ShapeDtypeStruct((C, C), BF16)
    both = jax.ShapeDtypeStruct((heads, C, 2 * C), BF16)
    added = jax.ShapeDtypeStruct((heads, C, C), F32)
    (state,) = small_call(group_state, [square], *parts)
    state, q32 = lax.optimization_barrier((state, q32))
    (rows2,) = row_maps(heads, 1, 1, q32, *first)
    *maps, total = small_call(group_prefix, [both, added, jax.ShapeDtypeStruct((C, 2 * C), BF16)], *parts)
    if count == 2 * heads:
        lower = swap(state, "seq", heads)
        rows2, maps, lower = lax.optimization_barrier((rows2, maps, lower))
        keep, *sends = small_call(states_of_upper, [square] * heads, *maps, lower)
    else:
        keep, *sends = small_call(states_given, [square] * heads, *maps, prefix(total, heads))
    keep, q32 = lax.optimization_barrier((keep, q32))
    (rows1,) = row_maps(heads, 2, 2, q32, *first)
    (rows0,) = row_maps(heads, 3, 0, q32, *own_maps_here)
    entering = [swap(sends[r - 1], "seq", r) for r in away] + [keep]
    rows = (rows3, rows2, rows1, rows0)
    groups = lax.axis_size("head")
    keep, send = apply(True, rows, entering, groups)
    across = (keep, swap(send, "head", 1), out_weight, weight2)
    keep, send = apply(False, rows, entering, groups)
    here = (keep, swap(send, "head", 1), out_weight, weight2)
    parts = 4
    width = out_weight.shape[1] // parts
    ranges = [(i * width, width) for i in range(parts)]
    theirs = [swap(project(BF16, *x, *across), "head", 2) for x in ranges]
    mine = [project(F32, *x, *here) for x in ranges]
    mixed = []
    for i in range(parts):
        mixed = [add_part(i, parts, mine[i], theirs[i], mixed)]
    return mixed[0]


def solution(mesh):
    in_specs = (
        P("seq", "head", None),
        P("seq", "head", None),
        P("seq", "head", None),
        P("head", "seq"),
        P("head", "seq"),
        P("head", None),
    )
    out_specs = P(("seq", "head"), None)
    return jax.shard_map(body, mesh=mesh, in_specs=in_specs, out_specs=out_specs, check_vma=False)
```

```python
import functools

import jax
import jax.numpy as jnp
from jax import lax
from jax.experimental import pallas as pl
from jax.experimental.pallas import tpu as pltpu
from jax.sharding import PartitionSpec as P

C = 128
B = 16
F32 = jnp.float32
BF16 = jnp.bfloat16
NN = (((1,), (0,)), ((), ()))
NT = (((1,), (1,)), ((), ()))
TN = (((0,), (0,)), ((), ()))
MIB = 1024 * 1024


def dot(a, b, dims=NN):
    return lax.dot_general(a, b, dims, preferred_element_type=F32)


def split(x):
    high = x.astype(BF16)
    return high, (x - high.astype(F32)).astype(BF16)


def twice(x):
    return jnp.concatenate([x, x], axis=0)


def dot3(a, b):
    (ah, al), (bh, bl) = a, b
    width = bh.shape[1]
    if width > C:
        return dot(jnp.concatenate([ah, al], axis=1), twice(bh)) + dot(ah, bl)
    rows = ah.shape[0]
    both = dot(jnp.concatenate([ah, al], axis=0), jnp.concatenate([bh, bl], axis=1))
    return both[:rows, :width] + (both[:rows, width:] + both[rows:, :width])


def iotas():
    return (
        lax.broadcasted_iota(jnp.int32, (C, C), 0),
        lax.broadcasted_iota(jnp.int32, (C, C), 1),
    )


def to_column(row, eye):
    return jnp.sum(jnp.where(eye, row, 0.0), axis=1, keepdims=True)


def to_row(column, eye):
    return jnp.sum(jnp.where(eye, column, 0.0), axis=0, keepdims=True)


def inverse_scale(rows):
    return lax.rsqrt(jnp.sum(rows * rows, axis=1, keepdims=True) + 1e-06)


def three(x):
    high, rest = x.astype(BF16), x
    rest = rest - high.astype(F32)
    return (high,) + split(rest)


def running_sums(rows, upper):
    return sum(dot(x, upper) for x in reversed(three(rows)))


def base_inverse(lower, row, col):
    on_block = (row // B) == (col // B)
    blocks = jnp.where(on_block, lower, 0.0)
    packed = sum(blocks[i * B : (i + 1) * B] for i in range(1, C // B)) + blocks[:B]
    r, c = row[:B], col[:B]
    found = jnp.where(r == c % B, 1.0, 0.0)
    first = (c // B) * B
    for j in range(B - 1):
        factor = jnp.take_along_axis(packed, first + j, axis=1)
        found = found - factor * found[j : j + 1]
    return jnp.where(on_block, jnp.concatenate([found] * (C // B), axis=0), 0.0)


def odd_rows(x, size):
    return jnp.concatenate([x[i : i + size] for i in range(size, C, 2 * size)], axis=0)


def weave(even, odd, size):
    parts = []
    for i in range(0, C // 2, size):
        parts += [even[i : i + size], odd[i : i + size]]
    return jnp.concatenate(parts, axis=0)


def even_rows(x, size):
    return jnp.concatenate([x[i : i + size] for i in range(0, C, 2 * size)], axis=0)


def inverses(lowers, row, col):
    found = [base_inverse(a, row, col) for a in lowers]
    parts = [split(a) for a in lowers]
    halves = [split(x) for x in found]
    size = B
    while size < C:
        r, c = odd_rows(row, size), odd_rows(col, size)
        mask = ((r // (2 * size)) == (c // (2 * size))) & ((r // size) != (c // size))
        nothing = jnp.zeros((C // 2, C), BF16)
        mask = jnp.where(mask, 1.0, 0.0).astype(BF16)
        joins = [tuple(odd_rows(x, size) * mask for x in part) for part in parts]
        middle = [split(dot3(a, x)) for a, x in zip(joins, halves)]
        middle = [tuple(weave(nothing, x, size) for x in part) for part in middle]
        lows = [dot3(tuple(odd_rows(x, size) for x in h), y) for h, y in zip(halves, middle)]
        lows = [odd_rows(x, size) - y for x, y in zip(found, lows)]
        found = [weave(even_rows(x, size), y, size) for x, y in zip(found, lows)]
        if 2 * size < C:
            halves = [
                tuple(weave(even_rows(x, size), y, size) for x, y in zip(h, split(low)))
                for h, low in zip(halves, lows)
            ]
        size *= 2
    return found


def in_hbm(*arrays):
    return [pltpu.with_memory_space_constraint(x, pltpu.HBM) for x in arrays]


def join(moved, added):
    return jnp.concatenate([moved, added], axis=1)


def after(later, earlier):
    total = dot3(split(later[:, :C]), split(earlier))
    return join(total[:, :C], total[:, C:] + later[:, C:])


def per_chunk(ref):
    return jnp.concatenate([ref[:, i : i + C] for i in range(0, ref.shape[1], C)], axis=0)


def chunk_rows(heads, head, c):
    return pl.ds(c * C * heads + head, C, stride=heads)


def places(heads):
    place = lax.rem(lax.axis_index("seq"), heads)
    return place, [lax.bitwise_xor(place, r) for r in range(heads - 1, -1, -1)]


def local_heads(heads, mine, k32, v32, sums_ref, betas_ref, mix_ref, wu_ref, n_ref):
    chunks = sums_ref.shape[0] // heads
    row, col = iotas()
    eye = row == col
    within = row >= col
    strict = row > col
    eye16 = jnp.where(eye, 1.0, 0.0).astype(BF16)
    jobs = [(head, c) for head in mine for c in range(chunks)]
    sums = jnp.concatenate([sums_ref[pl.ds(head, chunks, stride=heads), :] for head in mine], axis=0)
    betas = jnp.concatenate([betas_ref[pl.ds(head, chunks, stride=heads), :] for head in mine], axis=0)
    filled = jnp.concatenate([sums, jnp.zeros((C - sums.shape[0], C), F32)], axis=0)
    columns = filled.T
    grown = jnp.exp(sums)
    faded = jnp.exp(sums[:, C - 1 :] - sums)
    lowers, raws, values, turns, fades, lengths = [], [], [], [], [], []
    for i, (head, c) in enumerate(jobs):
        at = slice(i, i + 1)
        raw = k32[chunk_rows(heads, head, c), :].astype(BF16)
        raws.append(raw)
        values.append(v32[chunk_rows(heads, head, c), :].astype(BF16))
        both = dot(jnp.concatenate([raw, eye16], axis=0), raw, NT)
        gram, turned = both[:C], both[C:]
        square = to_row(gram, eye) + 1e-06
        scale = lax.rsqrt(square)
        lengths.append(square * scale)
        strength = betas[at] * (scale * scale)
        mix = jnp.where(within, jnp.exp(columns[:, at] - sums[at]), 0.0) * strength
        mix_ref[i] = mix
        lowers.append(jnp.where(strict, gram * mix, 0.0))
        turns.append(turned.astype(BF16))
        fades.append(strength * faded[at])
    solved = []
    for i, found in enumerate(inverses(lowers, row, col)):
        at = slice(i, i + 1)
        kept = dot(jnp.concatenate(split(found * grown[at]), axis=1), twice(raws[i]))
        fresh = dot(jnp.concatenate(split(found * lengths[i]), axis=1), twice(values[i]))
        solved.append(join(kept, fresh))
    weights = jnp.concatenate(fades + [jnp.zeros((C - len(jobs), C), F32)], axis=0).T
    maps = []
    for i in range(len(jobs)):
        wu_ref[i] = solved[i]
        both = times_parts(turns[i], solved[i] * weights[:, i : i + 1])
        maps.append(join(jnp.where(eye, grown[i : i + 1, C - 1 :], 0.0) - both[:, :C], both[:, C:]))
    totals = []
    for j in range(len(mine)):
        first, second, third, last = maps[j * chunks : (j + 1) * chunks]
        early = after(second, first)
        n_ref[j * chunks + 1] = first
        n_ref[j * chunks + 2] = early
        n_ref[j * chunks + 3] = after(third, early)
        totals.append(after(after(last, third), early))
    return totals


def first_kernel(
    heads, k_hbm, v_hbm, beta_hbm, log_hbm, q_hbm, q16, k32, v32, sums_ref, betas_ref, mix_ref, wu_ref, n_ref, *refs
):
    sends, (k16, v16, beta_ref, log_ref, sems) = refs[: heads - 1], refs[heads - 1 :]
    pairs = ((log_hbm, log_ref), (beta_hbm, beta_ref), (k_hbm, k16), (v_hbm, v16), (q_hbm, q16))
    copies = [pltpu.make_async_copy(x, y, sems.at[i]) for i, (x, y) in enumerate(pairs)]
    *early, late = copies
    for copy in early:
        copy.start()
    for copy in early[:2]:
        copy.wait()
    row, col = iotas()
    sums_ref[...] = running_sums(per_chunk(log_ref), jnp.where(row <= col, 1.0, 0.0).astype(BF16))
    betas_ref[...] = per_chunk(beta_ref)
    early[2].wait()
    k32[...] = k16[...].astype(F32)
    early[3].wait()
    late.start()
    v32[...] = v16[...].astype(F32)
    mine = places(heads)[1][: heads - 1]
    totals = local_heads(heads, mine, k32, v32, sums_ref, betas_ref, mix_ref, wu_ref, n_ref)
    for send, total in zip(sends, totals):
        send[...] = total.astype(BF16)
    late.wait()


def maps_shapes(heads, chunks):
    return [
        jax.ShapeDtypeStruct((heads * chunks, C, C), F32),
        jax.ShapeDtypeStruct((heads * chunks, C, 2 * C), F32),
        jax.ShapeDtypeStruct((heads * chunks, C, 2 * C), F32),
    ] + [jax.ShapeDtypeStruct((C, 2 * C), BF16)] * heads


def first_maps(key, value, beta, log_decay, query):
    heads, tokens = beta.shape
    chunks = tokens // C
    here = pl.BlockSpec(memory_space=pltpu.VMEM)
    rows = jax.ShapeDtypeStruct((chunks * heads, C), F32)
    wide = jax.ShapeDtypeStruct(key.shape, F32)
    out_shape = [jax.ShapeDtypeStruct(query.shape, BF16), wide, wide, rows, rows] + maps_shapes(heads - 1, chunks)
    return pl.pallas_call(
        functools.partial(first_kernel, heads),
        in_specs=[pl.BlockSpec(memory_space=pltpu.HBM)] * 5,
        out_specs=[here] * len(out_shape),
        out_shape=out_shape,
        scratch_shapes=[
            pltpu.VMEM(key.shape, BF16),
            pltpu.VMEM(key.shape, BF16),
            pltpu.VMEM(beta.shape, F32),
            pltpu.VMEM(beta.shape, F32),
            pltpu.SemaphoreType.DMA((5,)),
        ],
        compiler_params=pltpu.CompilerParams(vmem_limit_bytes=32 * MIB),
        name="first_maps",
    )(*in_hbm(key, value, beta, log_decay, query))


def own_kernel(heads, k32, v32, sums_ref, betas_ref, mix_ref, wu_ref, n_ref, own_ref):
    mine = places(heads)[1][heads - 1 :]
    (total,) = local_heads(heads, mine, k32, v32, sums_ref, betas_ref, mix_ref, wu_ref, n_ref)
    own_ref[...] = total.astype(BF16)


def own_maps(heads, k32, v32, sums, betas):
    here = pl.BlockSpec(memory_space=pltpu.VMEM)
    out_shape = maps_shapes(1, sums.shape[0] // heads)
    return pl.pallas_call(
        functools.partial(own_kernel, heads),
        in_specs=[here] * 4,
        out_specs=[here] * len(out_shape),
        out_shape=out_shape,
        compiler_params=pltpu.CompilerParams(vmem_limit_bytes=16 * MIB),
        cost_estimate=pl.CostEstimate(flops=2000000000, bytes_accessed=8000000, transcendentals=0),
        name="own_maps",
    )(k32, v32, sums, betas)


def rows_kernel(heads, spot, slot, q_ref, k32, sums_ref, mix_ref, wu_ref, n_ref, out_ref, *wide):
    if wide:
        wide[0][...] = q_ref[...].astype(F32)
    q32 = wide[0] if wide else q_ref
    chunks = sums_ref.shape[0] // heads
    row, col = iotas()
    eye = row == col
    head = places(heads)[1][spot]
    grown = jnp.exp(sums_ref[pl.ds(head, chunks, stride=heads), :])
    for c in range(chunks):
        i = slot * chunks + c
        query, raw = q32[chunk_rows(heads, head, c), :], k32[chunk_rows(heads, head, c), :]
        pairs = dot(query.astype(BF16), raw.astype(BF16), NT) * mix_ref[i]
        both = dot3(split(pairs), split(wu_ref[i]))
        scale = inverse_scale(query)
        reach = (query * to_column(grown[c : c + 1], eye) - both[:, :C]) * scale
        fresh = both[:, C:] * scale
        if c > 0:
            earlier = dot3(split(reach), split(n_ref[i]))
            reach = earlier[:, :C]
            fresh = fresh + earlier[:, C:]
        out_ref[c * C : (c + 1) * C, :] = join(reach, fresh)


def row_maps(heads, spot, slot, query, *maps):
    tokens = query.shape[0] // heads
    here = pl.BlockSpec(memory_space=pltpu.VMEM)
    out_shape = [jax.ShapeDtypeStruct((tokens, 2 * C), F32)]
    if query.dtype == BF16:
        out_shape.append(jax.ShapeDtypeStruct(query.shape, F32))
    return pl.pallas_call(
        functools.partial(rows_kernel, heads, spot, slot),
        in_specs=[here] * (1 + len(maps)),
        out_specs=[here] * len(out_shape),
        out_shape=out_shape,
        compiler_params=pltpu.CompilerParams(vmem_limit_bytes=16 * MIB),
        cost_estimate=pl.CostEstimate(flops=1000000000, bytes_accessed=4000000, transcendentals=0),
        name="row_maps",
    )(query, *maps)


def small_call(kernel, out_shape, *args):
    here = pl.BlockSpec(memory_space=pltpu.VMEM)
    return pl.pallas_call(
        kernel,
        in_specs=[here] * len(args),
        out_specs=[here] * len(out_shape),
        out_shape=out_shape,
        compiler_params=pltpu.CompilerParams(vmem_limit_bytes=8 * MIB),
        name=kernel.__name__,
    )(*args)


def moved_on(maps, state16, added):
    high, low = split(maps)
    return dot(jnp.concatenate([high, low], axis=1), twice(state16)) + added


def times_parts(maps16, x):
    width = x.shape[1]
    both = dot(maps16, jnp.concatenate(split(x), axis=1))
    return both[:, :width] + both[:, width:]


def by_place(parts, work):
    heads = len(parts)
    place = places(heads)[0]
    for p in range(heads):

        @pl.when(place == p)
        def _(p=p):
            members = [i ^ p for i in range(heads)]
            work([parts[heads - 1 - r] for r in members], members)


def group_state(*refs):
    out_ref = refs[-1]

    def work(parts, _):
        state = parts[0][:, C:].astype(F32)
        for part in parts[1:]:
            state = times_parts(part[:, :C], state) + part[:, C:].astype(F32)
        out_ref[...] = state.astype(BF16)

    by_place(refs[:-1], work)


def group_prefix(*refs):
    parts, (maps_ref, added_ref, total_ref) = refs[:-3], refs[-3:]
    row, col = iotas()

    def work(parts, members):
        total = join(jnp.where(row == col, 1.0, 0.0), jnp.zeros((C, C), F32))
        for i, (part, r) in enumerate(zip(parts, members)):
            maps_ref[r] = jnp.concatenate(split(total[:, :C]), axis=1)
            added_ref[r] = total[:, C:]
            if i == 0:
                total = part[...].astype(F32)
            else:
                total = times_parts(part[:, :C], total)
                total = join(total[:, :C], total[:, C:] + part[:, C:].astype(F32))
        total_ref[...] = total.astype(BF16)

    by_place(parts, work)


def group_states(upper_only, maps_ref, added_ref, state_ref, *outs):
    state = state_ref[...]
    if upper_only:
        state = jnp.where(lax.axis_index("seq") < len(outs), jnp.zeros_like(state), state)
    both = twice(state)
    for r, out_ref in enumerate(outs):
        out_ref[...] = (dot(maps_ref[r], both) + added_ref[r]).astype(BF16)


def states_of_upper(*refs):
    group_states(True, *refs)


def states_given(*refs):
    group_states(False, *refs)


def prefix(total, heads):
    count = lax.axis_size("seq")
    groups = [list(range(i, count, heads)) for i in range(heads)]
    me = lax.axis_index("seq") // heads
    totals = lax.all_gather(total, "seq", axis_index_groups=groups)

    def step(d, state):
        longer = jnp.einsum("ik,pkw->iw", totals[d, :, :C], jnp.stack(split(state)), preferred_element_type=F32)
        return jnp.where(d < me, longer + totals[d, :, C:].astype(F32), state)

    start = jnp.zeros((C, C), F32)
    return lax.fori_loop(0, count // heads - 1, step, start).astype(BF16)


def apply_kernel(groups, other, *refs):
    heads = (len(refs) - 2) // 2
    rows_refs, states, (keep_ref, send_ref) = refs[:heads], refs[heads : 2 * heads], refs[2 * heads :]
    block = rows_refs[0].shape[0] // groups
    order = places(heads)[1]
    member = lax.axis_index("head")
    pair, core = member // 2, lax.rem(member, 2)
    pair = 1 - pair if other else pair
    for out_ref, parity in ((send_ref, 1 - core), (keep_ref, core)):
        rows = pl.ds(pl.multiple_of((2 * pair + parity) * block, block), block)
        for head, rows_ref, state in zip(order, rows_refs, states):
            attended = moved_on(rows_ref[rows, :C], state[...], rows_ref[rows, C:])
            out_ref[:, pl.ds(pl.multiple_of(head * C, C), C)] = attended.astype(BF16)


def apply(other, rows, states, groups):
    heads = len(states)
    here = pl.BlockSpec(memory_space=pltpu.VMEM)
    out = jax.ShapeDtypeStruct((rows[0].shape[0] // groups, heads * C), BF16)
    return pl.pallas_call(
        functools.partial(apply_kernel, groups, other),
        in_specs=[here] * (2 * heads),
        out_specs=[here] * 2,
        out_shape=[out, out],
        compiler_params=pltpu.CompilerParams(vmem_limit_bytes=8 * MIB),
        cost_estimate=pl.CostEstimate(flops=200000000, bytes_accessed=1000000, transcendentals=0),
        name="apply",
    )(*rows, *states)


def project_kernel(start, keep_ref, got_ref, w_ref, w2_ref, out_ref):
    columns = slice(start, start + out_ref.shape[1])
    shares = dot(keep_ref[...], w_ref[:, columns]) + dot(got_ref[...], w2_ref[:, columns])
    out_ref[...] = shares.astype(out_ref.dtype)


def project(dtype, start, width, keep, got, weight, weight2):
    block, depth = keep.shape
    return pl.pallas_call(
        functools.partial(project_kernel, start),
        out_shape=jax.ShapeDtypeStruct((block, width), dtype),
        compiler_params=pltpu.CompilerParams(vmem_limit_bytes=20 * MIB),
        cost_estimate=pl.CostEstimate(
            flops=4 * block * depth * width, bytes_accessed=4 * depth * width, transcendentals=0
        ),
        name="project",
    )(keep, got, weight, weight2)


def add_kernel(mine_ref, theirs_ref, *refs):
    refs[-1][...] = (mine_ref[...] + theirs_ref[...].astype(F32)).astype(BF16)


def add_part(index, parts, mine, theirs, earlier):
    block, width = mine.shape
    here = pl.BlockSpec(memory_space=pltpu.VMEM)
    return pl.pallas_call(
        add_kernel,
        grid=(1,),
        in_specs=[here, here] + [pl.BlockSpec(memory_space=pl.ANY)] * len(earlier),
        out_specs=pl.BlockSpec((block, width), lambda i: (0, index)),
        out_shape=jax.ShapeDtypeStruct((block, width * parts), BF16),
        input_output_aliases={2: 0} if earlier else {},
        compiler_params=pltpu.CompilerParams(vmem_limit_bytes=8 * MIB),
        name="add_part",
    )(mine, theirs, *earlier)


def swap(x, axis, bit):
    count = lax.axis_size(axis)
    return lax.ppermute(x, axis, [(i, i ^ bit) for i in range(count)])


def body(query, key, value, beta, log_decay, out_weight):
    tokens, heads, _ = key.shape
    count = lax.axis_size("seq")
    flat = lambda x: x.reshape(tokens * heads, C)
    weight2 = swap(out_weight, "head", 1)
    q16, k32, v32, sums, betas, mix, wu, states, *sends = first_maps(
        flat(key), flat(value), beta, log_decay, flat(query)
    )
    away = range(heads - 1, 0, -1)
    parts = [swap(x, "seq", r) for r, x in zip(away, sends)]
    *own_chunks, own = own_maps(heads, k32, v32, sums, betas)
    first = (k32, sums, mix, wu, states)
    own_maps_here = (k32, sums, *own_chunks)
    rows3, q32 = row_maps(heads, 0, 0, q16, *first)
    rows3, *parts = lax.optimization_barrier([rows3] + parts + [own])
    square = jax.ShapeDtypeStruct((C, C), BF16)
    both = jax.ShapeDtypeStruct((heads, C, 2 * C), BF16)
    added = jax.ShapeDtypeStruct((heads, C, C), F32)
    (state,) = small_call(group_state, [square], *parts)
    state, q32 = lax.optimization_barrier((state, q32))
    (rows2,) = row_maps(heads, 1, 1, q32, *first)
    *maps, total = small_call(group_prefix, [both, added, jax.ShapeDtypeStruct((C, 2 * C), BF16)], *parts)
    if count == 2 * heads:
        lower = swap(state, "seq", heads)
        rows2, maps, lower = lax.optimization_barrier((rows2, maps, lower))
        keep, *sends = small_call(states_of_upper, [square] * heads, *maps, lower)
    else:
        keep, *sends = small_call(states_given, [square] * heads, *maps, prefix(total, heads))
    keep, q32 = lax.optimization_barrier((keep, q32))
    (rows1,) = row_maps(heads, 2, 2, q32, *first)
    (rows0,) = row_maps(heads, 3, 0, q32, *own_maps_here)
    entering = [swap(sends[r - 1], "seq", r) for r in away] + [keep]
    rows = (rows3, rows2, rows1, rows0)
    groups = lax.axis_size("head")
    keep, send = apply(True, rows, entering, groups)
    across = (keep, swap(send, "head", 1), out_weight, weight2)
    keep, send = apply(False, rows, entering, groups)
    here = (keep, swap(send, "head", 1), out_weight, weight2)
    parts = 4
    width = out_weight.shape[1] // parts
    ranges = [(i * width, width) for i in range(parts)]
    theirs = [swap(project(BF16, *x, *across), "head", 2) for x in ranges]
    mine = [project(F32, *x, *here) for x in ranges]
    mixed = []
    for i in range(parts):
        mixed = [add_part(i, parts, mine[i], theirs[i], mixed)]
    return mixed[0]


def solution(mesh):
    in_specs = (
        P("seq", "head", None),
        P("seq", "head", None),
        P("seq", "head", None),
        P("head", "seq"),
        P("head", "seq"),
        P("head", None),
    )
    out_specs = P(("seq", "head"), None)
    return jax.shard_map(body, mesh=mesh, in_specs=in_specs, out_specs=out_specs, check_vma=False)
```

```python
import functools

import jax
import jax.numpy as jnp
from jax import lax
from jax.experimental import pallas as pl
from jax.experimental.pallas import tpu as pltpu
from jax.sharding import PartitionSpec as P

C = 128
B = 16
F32 = jnp.float32
BF16 = jnp.bfloat16
NN = (((1,), (0,)), ((), ()))
NT = (((1,), (1,)), ((), ()))
TN = (((0,), (0,)), ((), ()))
MIB = 1024 * 1024


def dot(a, b, dims=NN):
    return lax.dot_general(a, b, dims, preferred_element_type=F32)


def split(x):
    high = x.astype(BF16)
    return high, (x - high.astype(F32)).astype(BF16)


def twice(x):
    return jnp.concatenate([x, x], axis=0)


def dot3(a, b):
    (ah, al), (bh, bl) = a, b
    width = bh.shape[1]
    if width > C:
        return dot(jnp.concatenate([ah, al], axis=1), twice(bh)) + dot(ah, bl)
    rows = ah.shape[0]
    both = dot(jnp.concatenate([ah, al], axis=0), jnp.concatenate([bh, bl], axis=1))
    return both[:rows, :width] + (both[:rows, width:] + both[rows:, :width])


def iotas():
    return (
        lax.broadcasted_iota(jnp.int32, (C, C), 0),
        lax.broadcasted_iota(jnp.int32, (C, C), 1),
    )


def to_column(row, eye):
    return jnp.sum(jnp.where(eye, row, 0.0), axis=1, keepdims=True)


def to_row(column, eye):
    return jnp.sum(jnp.where(eye, column, 0.0), axis=0, keepdims=True)


def inverse_scale(rows):
    return lax.rsqrt(jnp.sum(rows * rows, axis=1, keepdims=True) + 1e-06)


def three(x):
    high, rest = x.astype(BF16), x
    rest = rest - high.astype(F32)
    return (high,) + split(rest)


def running_sums(rows, upper):
    return sum(dot(x, upper) for x in reversed(three(rows)))


def base_inverse(lower, row, col):
    on_block = (row // B) == (col // B)
    blocks = jnp.where(on_block, lower, 0.0)
    packed = sum(blocks[i * B : (i + 1) * B] for i in range(1, C // B)) + blocks[:B]
    r, c = row[:B], col[:B]
    found = jnp.where(r == c % B, 1.0, 0.0)
    first = (c // B) * B
    for j in range(B - 1):
        factor = jnp.take_along_axis(packed, first + j, axis=1)
        found = found - factor * found[j : j + 1]
    return jnp.where(on_block, jnp.concatenate([found] * (C // B), axis=0), 0.0)


def odd_rows(x, size):
    return jnp.concatenate([x[i : i + size] for i in range(size, C, 2 * size)], axis=0)


def weave(even, odd, size):
    parts = []
    for i in range(0, C // 2, size):
        parts += [even[i : i + size], odd[i : i + size]]
    return jnp.concatenate(parts, axis=0)


def even_rows(x, size):
    return jnp.concatenate([x[i : i + size] for i in range(0, C, 2 * size)], axis=0)


def inverses(lowers, row, col):
    found = [base_inverse(a, row, col) for a in lowers]
    parts = [split(a) for a in lowers]
    halves = [split(x) for x in found]
    size = B
    while size < C:
        r, c = odd_rows(row, size), odd_rows(col, size)
        mask = ((r // (2 * size)) == (c // (2 * size))) & ((r // size) != (c // size))
        nothing = jnp.zeros((C // 2, C), BF16)
        mask = jnp.where(mask, 1.0, 0.0).astype(BF16)
        joins = [tuple(odd_rows(x, size) * mask for x in part) for part in parts]
        middle = [split(dot3(a, x)) for a, x in zip(joins, halves)]
        middle = [tuple(weave(nothing, x, size) for x in part) for part in middle]
        lows = [dot3(tuple(odd_rows(x, size) for x in h), y) for h, y in zip(halves, middle)]
        lows = [odd_rows(x, size) - y for x, y in zip(found, lows)]
        found = [weave(even_rows(x, size), y, size) for x, y in zip(found, lows)]
        if 2 * size < C:
            halves = [
                tuple(weave(even_rows(x, size), y, size) for x, y in zip(h, split(low)))
                for h, low in zip(halves, lows)
            ]
        size *= 2
    return found


def in_hbm(*arrays):
    return [pltpu.with_memory_space_constraint(x, pltpu.HBM) for x in arrays]


def join(moved, added):
    return jnp.concatenate([moved, added], axis=1)


def after(later, earlier):
    total = dot3(split(later[:, :C]), split(earlier))
    return join(total[:, :C], total[:, C:] + later[:, C:])


def per_chunk(ref):
    return jnp.concatenate([ref[:, i : i + C] for i in range(0, ref.shape[1], C)], axis=0)


def chunk_rows(heads, head, c):
    return pl.ds(c * C * heads + head, C, stride=heads)


def places(heads):
    place = lax.rem(lax.axis_index("seq"), heads)
    return place, [lax.bitwise_xor(place, r) for r in range(heads - 1, -1, -1)]


def local_heads(heads, mine, k32, v32, sums_ref, betas_ref, mix_ref, wu_ref, n_ref):
    chunks = sums_ref.shape[0] // heads
    row, col = iotas()
    eye = row == col
    within = row >= col
    strict = row > col
    eye16 = jnp.where(eye, 1.0, 0.0).astype(BF16)
    jobs = [(head, c) for head in mine for c in range(chunks)]
    sums = jnp.concatenate([sums_ref[pl.ds(head, chunks, stride=heads), :] for head in mine], axis=0)
    betas = jnp.concatenate([betas_ref[pl.ds(head, chunks, stride=heads), :] for head in mine], axis=0)
    filled = jnp.concatenate([sums, jnp.zeros((C - sums.shape[0], C), F32)], axis=0)
    columns = filled.T
    grown = jnp.exp(sums)
    faded = jnp.exp(sums[:, C - 1 :] - sums)
    lowers, raws, values, fades, lengths = [], [], [], [], []
    for i, (head, c) in enumerate(jobs):
        at = slice(i, i + 1)
        raw = k32[chunk_rows(heads, head, c), :].astype(BF16)
        raws.append(raw)
        values.append(v32[chunk_rows(heads, head, c), :].astype(BF16))
        both = dot(jnp.concatenate([raw, eye16], axis=0), raw, NT)
        gram, turned = both[:C], both[C:]
        square = to_row(gram, eye) + 1e-06
        scale = lax.rsqrt(square)
        lengths.append(square * scale)
        strength = betas[at] * (scale * scale)
        mix = jnp.where(within, jnp.exp(columns[:, at] - sums[at]), 0.0) * strength
        mix_ref[i] = mix
        lowers.append(jnp.where(strict, gram * mix, 0.0))
        fades.append(turned * (strength * faded[at]))
    solved = []
    for i, found in enumerate(inverses(lowers, row, col)):
        at = slice(i, i + 1)
        kept = dot(jnp.concatenate(split(found * grown[at]), axis=1), twice(raws[i]))
        fresh = dot(jnp.concatenate(split(found * lengths[i]), axis=1), twice(values[i]))
        solved.append(join(kept, fresh))
    maps = []
    for i in range(len(jobs)):
        wu_ref[i] = solved[i]
        both = dot3(split(fades[i]), split(solved[i]))
        maps.append(join(jnp.where(eye, grown[i : i + 1, C - 1 :], 0.0) - both[:, :C], both[:, C:]))
    totals = []
    for j in range(len(mine)):
        first, second, third, last = maps[j * chunks : (j + 1) * chunks]
        early = after(second, first)
        n_ref[j * chunks + 1] = first
        n_ref[j * chunks + 2] = early
        n_ref[j * chunks + 3] = after(third, early)
        totals.append(after(after(last, third), early))
    return totals


def first_kernel(
    heads, k_hbm, v_hbm, beta_hbm, log_hbm, q_hbm, q16, k32, v32, sums_ref, betas_ref, mix_ref, wu_ref, n_ref, *refs
):
    sends, (k16, v16, beta_ref, log_ref, sems) = refs[: heads - 1], refs[heads - 1 :]
    pairs = ((log_hbm, log_ref), (beta_hbm, beta_ref), (k_hbm, k16), (v_hbm, v16), (q_hbm, q16))
    copies = [pltpu.make_async_copy(x, y, sems.at[i]) for i, (x, y) in enumerate(pairs)]
    *early, late = copies
    for copy in early:
        copy.start()
    for copy in early[:2]:
        copy.wait()
    row, col = iotas()
    sums_ref[...] = running_sums(per_chunk(log_ref), jnp.where(row <= col, 1.0, 0.0).astype(BF16))
    betas_ref[...] = per_chunk(beta_ref)
    early[2].wait()
    k32[...] = k16[...].astype(F32)
    early[3].wait()
    late.start()
    v32[...] = v16[...].astype(F32)
    mine = places(heads)[1][: heads - 1]
    totals = local_heads(heads, mine, k32, v32, sums_ref, betas_ref, mix_ref, wu_ref, n_ref)
    for send, total in zip(sends, totals):
        send[...] = total.astype(BF16)
    late.wait()


def maps_shapes(heads, chunks):
    return [
        jax.ShapeDtypeStruct((heads * chunks, C, C), F32),
        jax.ShapeDtypeStruct((heads * chunks, C, 2 * C), F32),
        jax.ShapeDtypeStruct((heads * chunks, C, 2 * C), F32),
    ] + [jax.ShapeDtypeStruct((C, 2 * C), BF16)] * heads


def first_maps(key, value, beta, log_decay, query):
    heads, tokens = beta.shape
    chunks = tokens // C
    here = pl.BlockSpec(memory_space=pltpu.VMEM)
    rows = jax.ShapeDtypeStruct((chunks * heads, C), F32)
    wide = jax.ShapeDtypeStruct(key.shape, F32)
    out_shape = [jax.ShapeDtypeStruct(query.shape, BF16), wide, wide, rows, rows] + maps_shapes(heads - 1, chunks)
    return pl.pallas_call(
        functools.partial(first_kernel, heads),
        in_specs=[pl.BlockSpec(memory_space=pltpu.HBM)] * 5,
        out_specs=[here] * len(out_shape),
        out_shape=out_shape,
        scratch_shapes=[
            pltpu.VMEM(key.shape, BF16),
            pltpu.VMEM(key.shape, BF16),
            pltpu.VMEM(beta.shape, F32),
            pltpu.VMEM(beta.shape, F32),
            pltpu.SemaphoreType.DMA((5,)),
        ],
        compiler_params=pltpu.CompilerParams(vmem_limit_bytes=32 * MIB),
        name="first_maps",
    )(*in_hbm(key, value, beta, log_decay, query))


def own_kernel(heads, k32, v32, sums_ref, betas_ref, mix_ref, wu_ref, n_ref, own_ref):
    mine = places(heads)[1][heads - 1 :]
    (total,) = local_heads(heads, mine, k32, v32, sums_ref, betas_ref, mix_ref, wu_ref, n_ref)
    own_ref[...] = total.astype(BF16)


def own_maps(heads, k32, v32, sums, betas):
    here = pl.BlockSpec(memory_space=pltpu.VMEM)
    out_shape = maps_shapes(1, sums.shape[0] // heads)
    return pl.pallas_call(
        functools.partial(own_kernel, heads),
        in_specs=[here] * 4,
        out_specs=[here] * len(out_shape),
        out_shape=out_shape,
        compiler_params=pltpu.CompilerParams(vmem_limit_bytes=16 * MIB),
        cost_estimate=pl.CostEstimate(flops=2000000000, bytes_accessed=8000000, transcendentals=0),
        name="own_maps",
    )(k32, v32, sums, betas)


def rows_kernel(heads, spot, slot, q_ref, k32, sums_ref, mix_ref, wu_ref, n_ref, out_ref, *wide):
    if wide:
        wide[0][...] = q_ref[...].astype(F32)
    q32 = wide[0] if wide else q_ref
    chunks = sums_ref.shape[0] // heads
    row, col = iotas()
    eye = row == col
    head = places(heads)[1][spot]
    grown = jnp.exp(sums_ref[pl.ds(head, chunks, stride=heads), :])
    for c in range(chunks):
        i = slot * chunks + c
        query, raw = q32[chunk_rows(heads, head, c), :], k32[chunk_rows(heads, head, c), :]
        pairs = dot(query.astype(BF16), raw.astype(BF16), NT) * mix_ref[i]
        both = dot3(split(pairs), split(wu_ref[i]))
        scale = inverse_scale(query)
        reach = (query * to_column(grown[c : c + 1], eye) - both[:, :C]) * scale
        fresh = both[:, C:] * scale
        if c > 0:
            earlier = dot3(split(reach), split(n_ref[i]))
            reach = earlier[:, :C]
            fresh = fresh + earlier[:, C:]
        out_ref[c * C : (c + 1) * C, :] = join(reach, fresh)


def row_maps(heads, spot, slot, query, *maps):
    tokens = query.shape[0] // heads
    here = pl.BlockSpec(memory_space=pltpu.VMEM)
    out_shape = [jax.ShapeDtypeStruct((tokens, 2 * C), F32)]
    if query.dtype == BF16:
        out_shape.append(jax.ShapeDtypeStruct(query.shape, F32))
    return pl.pallas_call(
        functools.partial(rows_kernel, heads, spot, slot),
        in_specs=[here] * (1 + len(maps)),
        out_specs=[here] * len(out_shape),
        out_shape=out_shape,
        compiler_params=pltpu.CompilerParams(vmem_limit_bytes=16 * MIB),
        cost_estimate=pl.CostEstimate(flops=1000000000, bytes_accessed=4000000, transcendentals=0),
        name="row_maps",
    )(query, *maps)


def small_call(kernel, out_shape, *args):
    here = pl.BlockSpec(memory_space=pltpu.VMEM)
    return pl.pallas_call(
        kernel,
        in_specs=[here] * len(args),
        out_specs=[here] * len(out_shape),
        out_shape=out_shape,
        compiler_params=pltpu.CompilerParams(vmem_limit_bytes=8 * MIB),
        name=kernel.__name__,
    )(*args)


def moved_on(maps, state16, added):
    high, low = split(maps)
    return dot(jnp.concatenate([high, low], axis=1), twice(state16)) + added


def times_parts(maps16, x):
    width = x.shape[1]
    both = dot(maps16, jnp.concatenate(split(x), axis=1))
    return both[:, :width] + both[:, width:]


def by_place(parts, work):
    heads = len(parts)
    place = places(heads)[0]
    for p in range(heads):

        @pl.when(place == p)
        def _(p=p):
            members = [i ^ p for i in range(heads)]
            work([parts[heads - 1 - r] for r in members], members)


def group_state(*refs):
    out_ref = refs[-1]

    def work(parts, _):
        state = parts[0][:, C:].astype(F32)
        for part in parts[1:]:
            state = times_parts(part[:, :C], state) + part[:, C:].astype(F32)
        out_ref[...] = state.astype(BF16)

    by_place(refs[:-1], work)


def group_prefix(*refs):
    parts, (maps_ref, added_ref, total_ref) = refs[:-3], refs[-3:]
    row, col = iotas()

    def work(parts, members):
        total = join(jnp.where(row == col, 1.0, 0.0), jnp.zeros((C, C), F32))
        for i, (part, r) in enumerate(zip(parts, members)):
            maps_ref[r] = jnp.concatenate(split(total[:, :C]), axis=1)
            added_ref[r] = total[:, C:]
            if i == 0:
                total = part[...].astype(F32)
            else:
                total = times_parts(part[:, :C], total)
                total = join(total[:, :C], total[:, C:] + part[:, C:].astype(F32))
        total_ref[...] = total.astype(BF16)

    by_place(parts, work)


def group_states(upper_only, maps_ref, added_ref, state_ref, *outs):
    state = state_ref[...]
    if upper_only:
        state = jnp.where(lax.axis_index("seq") < len(outs), jnp.zeros_like(state), state)
    both = twice(state)
    for r, out_ref in enumerate(outs):
        out_ref[...] = (dot(maps_ref[r], both) + added_ref[r]).astype(BF16)


def states_of_upper(*refs):
    group_states(True, *refs)


def states_given(*refs):
    group_states(False, *refs)


def prefix(total, heads):
    count = lax.axis_size("seq")
    groups = [list(range(i, count, heads)) for i in range(heads)]
    me = lax.axis_index("seq") // heads
    totals = lax.all_gather(total, "seq", axis_index_groups=groups)

    def step(d, state):
        longer = jnp.einsum("ik,pkw->iw", totals[d, :, :C], jnp.stack(split(state)), preferred_element_type=F32)
        return jnp.where(d < me, longer + totals[d, :, C:].astype(F32), state)

    start = jnp.zeros((C, C), F32)
    return lax.fori_loop(0, count // heads - 1, step, start).astype(BF16)


def apply_kernel(groups, other, *refs):
    heads = (len(refs) - 2) // 2
    rows_refs, states, (keep_ref, send_ref) = refs[:heads], refs[heads : 2 * heads], refs[2 * heads :]
    block = rows_refs[0].shape[0] // groups
    order = places(heads)[1]
    member = lax.axis_index("head")
    pair, core = member // 2, lax.rem(member, 2)
    pair = 1 - pair if other else pair
    for out_ref, parity in ((send_ref, 1 - core), (keep_ref, core)):
        rows = pl.ds(pl.multiple_of((2 * pair + parity) * block, block), block)
        for head, rows_ref, state in zip(order, rows_refs, states):
            attended = moved_on(rows_ref[rows, :C], state[...], rows_ref[rows, C:])
            out_ref[:, pl.ds(pl.multiple_of(head * C, C), C)] = attended.astype(BF16)


def apply(other, rows, states, groups):
    heads = len(states)
    here = pl.BlockSpec(memory_space=pltpu.VMEM)
    out = jax.ShapeDtypeStruct((rows[0].shape[0] // groups, heads * C), BF16)
    return pl.pallas_call(
        functools.partial(apply_kernel, groups, other),
        in_specs=[here] * (2 * heads),
        out_specs=[here] * 2,
        out_shape=[out, out],
        compiler_params=pltpu.CompilerParams(vmem_limit_bytes=8 * MIB),
        cost_estimate=pl.CostEstimate(flops=200000000, bytes_accessed=1000000, transcendentals=0),
        name="apply",
    )(*rows, *states)


def project_kernel(start, keep_ref, got_ref, w_ref, w2_ref, out_ref):
    columns = slice(start, start + out_ref.shape[1])
    shares = dot(keep_ref[...], w_ref[:, columns]) + dot(got_ref[...], w2_ref[:, columns])
    out_ref[...] = shares.astype(out_ref.dtype)


def project(dtype, start, width, keep, got, weight, weight2):
    block, depth = keep.shape
    return pl.pallas_call(
        functools.partial(project_kernel, start),
        out_shape=jax.ShapeDtypeStruct((block, width), dtype),
        compiler_params=pltpu.CompilerParams(vmem_limit_bytes=20 * MIB),
        cost_estimate=pl.CostEstimate(
            flops=4 * block * depth * width, bytes_accessed=4 * depth * width, transcendentals=0
        ),
        name="project",
    )(keep, got, weight, weight2)


def add_kernel(mine_ref, theirs_ref, *refs):
    refs[-1][...] = (mine_ref[...] + theirs_ref[...].astype(F32)).astype(BF16)


def add_part(index, parts, mine, theirs, earlier):
    block, width = mine.shape
    here = pl.BlockSpec(memory_space=pltpu.VMEM)
    return pl.pallas_call(
        add_kernel,
        grid=(1,),
        in_specs=[here, here] + [pl.BlockSpec(memory_space=pl.ANY)] * len(earlier),
        out_specs=pl.BlockSpec((block, width), lambda i: (0, index)),
        out_shape=jax.ShapeDtypeStruct((block, width * parts), BF16),
        input_output_aliases={2: 0} if earlier else {},
        compiler_params=pltpu.CompilerParams(vmem_limit_bytes=8 * MIB),
        name="add_part",
    )(mine, theirs, *earlier)


def swap(x, axis, bit):
    count = lax.axis_size(axis)
    return lax.ppermute(x, axis, [(i, i ^ bit) for i in range(count)])


def body(query, key, value, beta, log_decay, out_weight):
    tokens, heads, _ = key.shape
    count = lax.axis_size("seq")
    flat = lambda x: x.reshape(tokens * heads, C)
    weight2 = swap(out_weight, "head", 1)
    q16, k32, v32, sums, betas, mix, wu, states, *sends = first_maps(
        flat(key), flat(value), beta, log_decay, flat(query)
    )
    away = range(heads - 1, 0, -1)
    parts = [swap(x, "seq", r) for r, x in zip(away, sends)]
    *own_chunks, own = own_maps(heads, k32, v32, sums, betas)
    first = (k32, sums, mix, wu, states)
    own_maps_here = (k32, sums, *own_chunks)
    rows3, q32 = row_maps(heads, 0, 0, q16, *first)
    rows3, *parts = lax.optimization_barrier([rows3] + parts + [own])
    square = jax.ShapeDtypeStruct((C, C), BF16)
    both = jax.ShapeDtypeStruct((heads, C, 2 * C), BF16)
    added = jax.ShapeDtypeStruct((heads, C, C), F32)
    (state,) = small_call(group_state, [square], *parts)
    state, q32 = lax.optimization_barrier((state, q32))
    (rows2,) = row_maps(heads, 1, 1, q32, *first)
    *maps, total = small_call(group_prefix, [both, added, jax.ShapeDtypeStruct((C, 2 * C), BF16)], *parts)
    if count == 2 * heads:
        lower = swap(state, "seq", heads)
        rows2, maps, lower = lax.optimization_barrier((rows2, maps, lower))
        keep, *sends = small_call(states_of_upper, [square] * heads, *maps, lower)
    else:
        keep, *sends = small_call(states_given, [square] * heads, *maps, prefix(total, heads))
    keep, q32 = lax.optimization_barrier((keep, q32))
    (rows1,) = row_maps(heads, 2, 2, q32, *first)
    (rows0,) = row_maps(heads, 3, 0, q32, *own_maps_here)
    entering = [swap(sends[r - 1], "seq", r) for r in away] + [keep]
    rows = (rows3, rows2, rows1, rows0)
    groups = lax.axis_size("head")
    keep, send = apply(True, rows, entering, groups)
    across = (keep, swap(send, "head", 1), out_weight, weight2)
    keep, send = apply(False, rows, entering, groups)
    here = (keep, swap(send, "head", 1), out_weight, weight2)
    parts = 4
    width = out_weight.shape[1] // parts
    ranges = [(i * width, width) for i in range(parts)]
    theirs = [swap(project(BF16, *x, *across), "head", 2) for x in ranges]
    mine = [project(F32, *x, *here) for x in ranges]
    mixed = []
    for i in range(parts):
        mixed = [add_part(i, parts, mine[i], theirs[i], mixed)]
    return mixed[0]


def solution(mesh):
    in_specs = (
        P("seq", "head", None),
        P("seq", "head", None),
        P("seq", "head", None),
        P("head", "seq"),
        P("head", "seq"),
        P("head", None),
    )
    out_specs = P(("seq", "head"), None)
    return jax.shard_map(body, mesh=mesh, in_specs=in_specs, out_specs=out_specs, check_vma=False)
```

```python
import functools

import jax
import jax.numpy as jnp
from jax import lax
from jax.experimental import pallas as pl
from jax.experimental.pallas import tpu as pltpu
from jax.sharding import PartitionSpec as P

C = 128
B = 16
F32 = jnp.float32
BF16 = jnp.bfloat16
NN = (((1,), (0,)), ((), ()))
NT = (((1,), (1,)), ((), ()))
TN = (((0,), (0,)), ((), ()))
MIB = 1024 * 1024


def dot(a, b, dims=NN):
    return lax.dot_general(a, b, dims, preferred_element_type=F32)


def split(x):
    high = x.astype(BF16)
    return high, (x - high.astype(F32)).astype(BF16)


def twice(x):
    return jnp.concatenate([x, x], axis=0)


def dot3(a, b):
    (ah, al), (bh, bl) = a, b
    width = bh.shape[1]
    if width > C:
        return dot(jnp.concatenate([ah, al], axis=1), twice(bh)) + dot(ah, bl)
    rows = ah.shape[0]
    both = dot(jnp.concatenate([ah, al], axis=0), jnp.concatenate([bh, bl], axis=1))
    return both[:rows, :width] + (both[:rows, width:] + both[rows:, :width])


def iotas():
    return (
        lax.broadcasted_iota(jnp.int32, (C, C), 0),
        lax.broadcasted_iota(jnp.int32, (C, C), 1),
    )


def to_column(row, eye):
    return jnp.sum(jnp.where(eye, row, 0.0), axis=1, keepdims=True)


def to_row(column, eye):
    return jnp.sum(jnp.where(eye, column, 0.0), axis=0, keepdims=True)


def inverse_scale(rows):
    return lax.rsqrt(jnp.sum(rows * rows, axis=1, keepdims=True) + 1e-06)


def three(x):
    high, rest = x.astype(BF16), x
    rest = rest - high.astype(F32)
    return (high,) + split(rest)


def running_sums(rows, upper):
    return sum(dot(x, upper) for x in reversed(three(rows)))


LANES = lax.GatherDimensionNumbers(
    offset_dims=(),
    collapsed_slice_dims=(1,),
    start_index_map=(1,),
    operand_batching_dims=(0,),
    start_indices_batching_dims=(0,),
)


def pick_lanes(x, index):
    return lax.gather(x, index, LANES, (1, 1), mode=lax.GatherScatterMode.PROMISE_IN_BOUNDS)


def base_inverses(lowers, row, col):
    on_block = (row // B) == (col // B)
    r, c = row[:B], col[:B]
    identity = jnp.where(r == c % B, 1.0, 0.0)
    columns = [((c // B) * B + j)[..., None] for j in range(B - 1)]
    inverses = []
    for lower in lowers:
        blocks = jnp.where(on_block, lower, 0.0)
        packed = sum(blocks[i * B : (i + 1) * B] for i in range(1, C // B)) + blocks[:B]
        found = identity
        for j, column in enumerate(columns):
            found = found - pick_lanes(packed, column) * found[j : j + 1]
        inverses.append(jnp.where(on_block, jnp.concatenate([found] * (C // B), axis=0), 0.0))
    return inverses


def odd_rows(x, size):
    return jnp.concatenate([x[i : i + size] for i in range(size, C, 2 * size)], axis=0)


def weave(even, odd, size):
    parts = []
    for i in range(0, C // 2, size):
        parts += [even[i : i + size], odd[i : i + size]]
    return jnp.concatenate(parts, axis=0)


def even_rows(x, size):
    return jnp.concatenate([x[i : i + size] for i in range(0, C, 2 * size)], axis=0)


def inverses(lowers, row, col):
    found = base_inverses(lowers, row, col)
    parts = [split(a) for a in lowers]
    halves = [split(x) for x in found]
    size = B
    while size < C:
        r, c = odd_rows(row, size), odd_rows(col, size)
        mask = ((r // (2 * size)) == (c // (2 * size))) & ((r // size) != (c // size))
        nothing = jnp.zeros((C // 2, C), BF16)
        mask = jnp.where(mask, 1.0, 0.0).astype(BF16)
        joins = [tuple(odd_rows(x, size) * mask for x in part) for part in parts]
        middle = [split(dot3(a, x)) for a, x in zip(joins, halves)]
        middle = [tuple(weave(nothing, x, size) for x in part) for part in middle]
        lows = [dot3(tuple(odd_rows(x, size) for x in h), y) for h, y in zip(halves, middle)]
        lows = [odd_rows(x, size) - y for x, y in zip(found, lows)]
        found = [weave(even_rows(x, size), y, size) for x, y in zip(found, lows)]
        if 2 * size < C:
            halves = [
                tuple(weave(even_rows(x, size), y, size) for x, y in zip(h, split(low)))
                for h, low in zip(halves, lows)
            ]
        size *= 2
    return found


def in_hbm(*arrays):
    return [pltpu.with_memory_space_constraint(x, pltpu.HBM) for x in arrays]


def join(moved, added):
    return jnp.concatenate([moved, added], axis=1)


def after(later, earlier):
    total = dot3(split(later[:, :C]), split(earlier))
    return join(total[:, :C], total[:, C:] + later[:, C:])


def per_chunk(ref):
    return jnp.concatenate([ref[:, i : i + C] for i in range(0, ref.shape[1], C)], axis=0)


def chunk_rows(heads, head, c):
    return pl.ds(c * C * heads + head, C, stride=heads)


def places(heads):
    place = lax.rem(lax.axis_index("seq"), heads)
    return place, [lax.bitwise_xor(place, r) for r in range(heads - 1, -1, -1)]


def local_heads(heads, mine, k32, v32, sums_ref, betas_ref, mix_ref, wu_ref, n_ref):
    chunks = sums_ref.shape[0] // heads
    row, col = iotas()
    eye = row == col
    within = row >= col
    strict = row > col
    eye16 = jnp.where(eye, 1.0, 0.0).astype(BF16)
    jobs = [(head, c) for head in mine for c in range(chunks)]
    sums = jnp.concatenate([sums_ref[pl.ds(head, chunks, stride=heads), :] for head in mine], axis=0)
    betas = jnp.concatenate([betas_ref[pl.ds(head, chunks, stride=heads), :] for head in mine], axis=0)
    filled = jnp.concatenate([sums, jnp.zeros((C - sums.shape[0], C), F32)], axis=0)
    columns = filled.T
    grown = jnp.exp(sums)
    faded = jnp.exp(sums[:, C - 1 :] - sums)
    lowers, raws, values, fades, lengths = [], [], [], [], []
    for i, (head, c) in enumerate(jobs):
        at = slice(i, i + 1)
        raw = k32[chunk_rows(heads, head, c), :].astype(BF16)
        raws.append(raw)
        values.append(v32[chunk_rows(heads, head, c), :].astype(BF16))
        both = dot(jnp.concatenate([raw, eye16], axis=0), raw, NT)
        gram, turned = both[:C], both[C:]
        square = to_row(gram, eye) + 1e-06
        scale = lax.rsqrt(square)
        lengths.append(square * scale)
        strength = betas[at] * (scale * scale)
        mix = jnp.where(within, jnp.exp(columns[:, at] - sums[at]), 0.0) * strength
        mix_ref[i] = mix
        lowers.append(jnp.where(strict, gram * mix, 0.0))
        fades.append(turned * (strength * faded[at]))
    solved = []
    for i, found in enumerate(inverses(lowers, row, col)):
        at = slice(i, i + 1)
        kept = dot(jnp.concatenate(split(found * grown[at]), axis=1), twice(raws[i]))
        fresh = dot(jnp.concatenate(split(found * lengths[i]), axis=1), twice(values[i]))
        solved.append(join(kept, fresh))
    maps = []
    for i in range(len(jobs)):
        wu_ref[i] = solved[i]
        both = dot3(split(fades[i]), split(solved[i]))
        maps.append(join(jnp.where(eye, grown[i : i + 1, C - 1 :], 0.0) - both[:, :C], both[:, C:]))
    totals = []
    for j in range(len(mine)):
        first, second, third, last = maps[j * chunks : (j + 1) * chunks]
        early = after(second, first)
        n_ref[j * chunks + 1] = first
        n_ref[j * chunks + 2] = early
        n_ref[j * chunks + 3] = after(third, early)
        totals.append(after(after(last, third), early))
    return totals


def first_kernel(
    heads, k_hbm, v_hbm, beta_hbm, log_hbm, q_hbm, q16, k32, v32, sums_ref, betas_ref, mix_ref, wu_ref, n_ref, *refs
):
    sends, (k16, v16, beta_ref, log_ref, sems) = refs[: heads - 1], refs[heads - 1 :]
    pairs = ((log_hbm, log_ref), (beta_hbm, beta_ref), (k_hbm, k16), (v_hbm, v16), (q_hbm, q16))
    copies = [pltpu.make_async_copy(x, y, sems.at[i]) for i, (x, y) in enumerate(pairs)]
    *early, late = copies
    for copy in early:
        copy.start()
    for copy in early[:2]:
        copy.wait()
    row, col = iotas()
    sums_ref[...] = running_sums(per_chunk(log_ref), jnp.where(row <= col, 1.0, 0.0).astype(BF16))
    betas_ref[...] = per_chunk(beta_ref)
    early[2].wait()
    k32[...] = k16[...].astype(F32)
    early[3].wait()
    late.start()
    v32[...] = v16[...].astype(F32)
    mine = places(heads)[1][: heads - 1]
    totals = local_heads(heads, mine, k32, v32, sums_ref, betas_ref, mix_ref, wu_ref, n_ref)
    for send, total in zip(sends, totals):
        send[...] = total.astype(BF16)
    late.wait()


def maps_shapes(heads, chunks):
    return [
        jax.ShapeDtypeStruct((heads * chunks, C, C), F32),
        jax.ShapeDtypeStruct((heads * chunks, C, 2 * C), F32),
        jax.ShapeDtypeStruct((heads * chunks, C, 2 * C), F32),
    ] + [jax.ShapeDtypeStruct((C, 2 * C), BF16)] * heads


def first_maps(key, value, beta, log_decay, query):
    heads, tokens = beta.shape
    chunks = tokens // C
    here = pl.BlockSpec(memory_space=pltpu.VMEM)
    rows = jax.ShapeDtypeStruct((chunks * heads, C), F32)
    wide = jax.ShapeDtypeStruct(key.shape, F32)
    out_shape = [jax.ShapeDtypeStruct(query.shape, BF16), wide, wide, rows, rows] + maps_shapes(heads - 1, chunks)
    return pl.pallas_call(
        functools.partial(first_kernel, heads),
        in_specs=[pl.BlockSpec(memory_space=pltpu.HBM)] * 5,
        out_specs=[here] * len(out_shape),
        out_shape=out_shape,
        scratch_shapes=[
            pltpu.VMEM(key.shape, BF16),
            pltpu.VMEM(key.shape, BF16),
            pltpu.VMEM(beta.shape, F32),
            pltpu.VMEM(beta.shape, F32),
            pltpu.SemaphoreType.DMA((5,)),
        ],
        compiler_params=pltpu.CompilerParams(vmem_limit_bytes=32 * MIB),
        name="first_maps",
    )(*in_hbm(key, value, beta, log_decay, query))


def own_kernel(heads, k32, v32, sums_ref, betas_ref, mix_ref, wu_ref, n_ref, own_ref):
    mine = places(heads)[1][heads - 1 :]
    (total,) = local_heads(heads, mine, k32, v32, sums_ref, betas_ref, mix_ref, wu_ref, n_ref)
    own_ref[...] = total.astype(BF16)


def own_maps(heads, k32, v32, sums, betas):
    here = pl.BlockSpec(memory_space=pltpu.VMEM)
    out_shape = maps_shapes(1, sums.shape[0] // heads)
    return pl.pallas_call(
        functools.partial(own_kernel, heads),
        in_specs=[here] * 4,
        out_specs=[here] * len(out_shape),
        out_shape=out_shape,
        compiler_params=pltpu.CompilerParams(vmem_limit_bytes=16 * MIB),
        cost_estimate=pl.CostEstimate(flops=2000000000, bytes_accessed=8000000, transcendentals=0),
        name="own_maps",
    )(k32, v32, sums, betas)


def rows_kernel(heads, spot, slot, q_ref, k32, sums_ref, mix_ref, wu_ref, n_ref, out_ref, *wide):
    if wide:
        wide[0][...] = q_ref[...].astype(F32)
    q32 = wide[0] if wide else q_ref
    chunks = sums_ref.shape[0] // heads
    row, col = iotas()
    eye = row == col
    head = places(heads)[1][spot]
    grown = jnp.exp(sums_ref[pl.ds(head, chunks, stride=heads), :])
    for c in range(chunks):
        i = slot * chunks + c
        query, raw = q32[chunk_rows(heads, head, c), :], k32[chunk_rows(heads, head, c), :]
        pairs = dot(query.astype(BF16), raw.astype(BF16), NT) * mix_ref[i]
        both = dot3(split(pairs), split(wu_ref[i]))
        scale = inverse_scale(query)
        reach = (query * to_column(grown[c : c + 1], eye) - both[:, :C]) * scale
        fresh = both[:, C:] * scale
        if c > 0:
            earlier = dot3(split(reach), split(n_ref[i]))
            reach = earlier[:, :C]
            fresh = fresh + earlier[:, C:]
        out_ref[c * C : (c + 1) * C, :] = join(reach, fresh)


def row_maps(heads, spot, slot, query, *maps):
    tokens = query.shape[0] // heads
    here = pl.BlockSpec(memory_space=pltpu.VMEM)
    out_shape = [jax.ShapeDtypeStruct((tokens, 2 * C), F32)]
    if query.dtype == BF16:
        out_shape.append(jax.ShapeDtypeStruct(query.shape, F32))
    return pl.pallas_call(
        functools.partial(rows_kernel, heads, spot, slot),
        in_specs=[here] * (1 + len(maps)),
        out_specs=[here] * len(out_shape),
        out_shape=out_shape,
        compiler_params=pltpu.CompilerParams(vmem_limit_bytes=16 * MIB),
        cost_estimate=pl.CostEstimate(flops=1000000000, bytes_accessed=4000000, transcendentals=0),
        name="row_maps",
    )(query, *maps)


def small_call(kernel, out_shape, *args):
    here = pl.BlockSpec(memory_space=pltpu.VMEM)
    return pl.pallas_call(
        kernel,
        in_specs=[here] * len(args),
        out_specs=[here] * len(out_shape),
        out_shape=out_shape,
        compiler_params=pltpu.CompilerParams(vmem_limit_bytes=8 * MIB),
        name=kernel.__name__,
    )(*args)


def moved_on(maps, state16, added):
    high, low = split(maps)
    return dot(jnp.concatenate([high, low], axis=1), twice(state16)) + added


def times_parts(maps16, x):
    width = x.shape[1]
    both = dot(maps16, jnp.concatenate(split(x), axis=1))
    return both[:, :width] + both[:, width:]


def by_place(parts, work):
    heads = len(parts)
    place = places(heads)[0]
    for p in range(heads):

        @pl.when(place == p)
        def _(p=p):
            members = [i ^ p for i in range(heads)]
            work([parts[heads - 1 - r] for r in members], members)


def group_state(*refs):
    out_ref = refs[-1]

    def work(parts, _):
        first, second, third, last = parts
        state = dot(second[:, :C], first[:, C:]) + second[:, C:].astype(F32)
        both = dot(last[:, :C], third[...])
        state = dot3(split(both[:, :C]), split(state)) + (both[:, C:] + last[:, C:].astype(F32))
        out_ref[...] = state.astype(BF16)

    by_place(refs[:-1], work)


def group_prefix(*refs):
    parts, (maps_ref, added_ref, total_ref) = refs[:-3], refs[-3:]
    row, col = iotas()

    def work(parts, members):
        total = join(jnp.where(row == col, 1.0, 0.0), jnp.zeros((C, C), F32))
        for i, (part, r) in enumerate(zip(parts, members)):
            maps_ref[r] = jnp.concatenate(split(total[:, :C]), axis=1)
            added_ref[r] = total[:, C:]
            if i == 0:
                total = part[...].astype(F32)
            else:
                total = times_parts(part[:, :C], total)
                total = join(total[:, :C], total[:, C:] + part[:, C:].astype(F32))
        total_ref[...] = total.astype(BF16)

    by_place(parts, work)


def group_states(upper_only, maps_ref, added_ref, state_ref, *outs):
    state = state_ref[...]
    if upper_only:
        state = jnp.where(lax.axis_index("seq") < len(outs), jnp.zeros_like(state), state)
    both = twice(state)
    for r, out_ref in enumerate(outs):
        out_ref[...] = (dot(maps_ref[r], both) + added_ref[r]).astype(BF16)


def states_of_upper(*refs):
    group_states(True, *refs)


def states_given(*refs):
    group_states(False, *refs)


def prefix(total, heads):
    count = lax.axis_size("seq")
    groups = [list(range(i, count, heads)) for i in range(heads)]
    me = lax.axis_index("seq") // heads
    totals = lax.all_gather(total, "seq", axis_index_groups=groups)

    def step(d, state):
        longer = jnp.einsum("ik,pkw->iw", totals[d, :, :C], jnp.stack(split(state)), preferred_element_type=F32)
        return jnp.where(d < me, longer + totals[d, :, C:].astype(F32), state)

    start = jnp.zeros((C, C), F32)
    return lax.fori_loop(0, count // heads - 1, step, start).astype(BF16)


def apply_kernel(groups, other, *refs):
    heads = (len(refs) - 2) // 2
    rows_refs, states, (keep_ref, send_ref) = refs[:heads], refs[heads : 2 * heads], refs[2 * heads :]
    block = rows_refs[0].shape[0] // groups
    order = places(heads)[1]
    member = lax.axis_index("head")
    pair, core = member // 2, lax.rem(member, 2)
    pair = 1 - pair if other else pair
    for out_ref, parity in ((send_ref, 1 - core), (keep_ref, core)):
        rows = pl.ds(pl.multiple_of((2 * pair + parity) * block, block), block)
        for head, rows_ref, state in zip(order, rows_refs, states):
            attended = moved_on(rows_ref[rows, :C], state[...], rows_ref[rows, C:])
            out_ref[:, pl.ds(pl.multiple_of(head * C, C), C)] = attended.astype(BF16)


def apply(other, rows, states, groups):
    heads = len(states)
    here = pl.BlockSpec(memory_space=pltpu.VMEM)
    out = jax.ShapeDtypeStruct((rows[0].shape[0] // groups, heads * C), BF16)
    return pl.pallas_call(
        functools.partial(apply_kernel, groups, other),
        in_specs=[here] * (2 * heads),
        out_specs=[here] * 2,
        out_shape=[out, out],
        compiler_params=pltpu.CompilerParams(vmem_limit_bytes=8 * MIB),
        cost_estimate=pl.CostEstimate(flops=200000000, bytes_accessed=1000000, transcendentals=0),
        name="apply",
    )(*rows, *states)


def project_kernel(start, keep_ref, got_ref, w_ref, w2_ref, out_ref):
    columns = slice(start, start + out_ref.shape[1])
    shares = dot(keep_ref[...], w_ref[:, columns]) + dot(got_ref[...], w2_ref[:, columns])
    out_ref[...] = shares.astype(out_ref.dtype)


def project(dtype, start, width, keep, got, weight, weight2):
    block, depth = keep.shape
    return pl.pallas_call(
        functools.partial(project_kernel, start),
        out_shape=jax.ShapeDtypeStruct((block, width), dtype),
        compiler_params=pltpu.CompilerParams(vmem_limit_bytes=20 * MIB),
        cost_estimate=pl.CostEstimate(
            flops=4 * block * depth * width, bytes_accessed=4 * depth * width, transcendentals=0
        ),
        name="project",
    )(keep, got, weight, weight2)


def add_kernel(mine_ref, theirs_ref, *refs):
    refs[-1][...] = (mine_ref[...] + theirs_ref[...].astype(F32)).astype(BF16)


def add_part(index, parts, mine, theirs, earlier):
    block, width = mine.shape
    here = pl.BlockSpec(memory_space=pltpu.VMEM)
    return pl.pallas_call(
        add_kernel,
        grid=(1,),
        in_specs=[here, here] + [pl.BlockSpec(memory_space=pl.ANY)] * len(earlier),
        out_specs=pl.BlockSpec((block, width), lambda i: (0, index)),
        out_shape=jax.ShapeDtypeStruct((block, width * parts), BF16),
        input_output_aliases={2: 0} if earlier else {},
        compiler_params=pltpu.CompilerParams(vmem_limit_bytes=8 * MIB),
        name="add_part",
    )(mine, theirs, *earlier)


def swap(x, axis, bit):
    count = lax.axis_size(axis)
    return lax.ppermute(x, axis, [(i, i ^ bit) for i in range(count)])


def body(query, key, value, beta, log_decay, out_weight):
    tokens, heads, _ = key.shape
    count = lax.axis_size("seq")
    flat = lambda x: x.reshape(tokens * heads, C)
    weight2 = swap(out_weight, "head", 1)
    q16, k32, v32, sums, betas, mix, wu, states, *sends = first_maps(
        flat(key), flat(value), beta, log_decay, flat(query)
    )
    away = range(heads - 1, 0, -1)
    parts = [swap(x, "seq", r) for r, x in zip(away, sends)]
    *own_chunks, own = own_maps(heads, k32, v32, sums, betas)
    first = (k32, sums, mix, wu, states)
    own_maps_here = (k32, sums, *own_chunks)
    rows3, q32 = row_maps(heads, 0, 0, q16, *first)
    rows3, *parts = lax.optimization_barrier([rows3] + parts + [own])
    square = jax.ShapeDtypeStruct((C, C), BF16)
    both = jax.ShapeDtypeStruct((heads, C, 2 * C), BF16)
    added = jax.ShapeDtypeStruct((heads, C, C), F32)
    (state,) = small_call(group_state, [square], *parts)
    state, q32 = lax.optimization_barrier((state, q32))
    (rows2,) = row_maps(heads, 1, 1, q32, *first)
    *maps, total = small_call(group_prefix, [both, added, jax.ShapeDtypeStruct((C, 2 * C), BF16)], *parts)
    if count == 2 * heads:
        lower = swap(state, "seq", heads)
        rows2, maps, lower = lax.optimization_barrier((rows2, maps, lower))
        keep, *sends = small_call(states_of_upper, [square] * heads, *maps, lower)
    else:
        keep, *sends = small_call(states_given, [square] * heads, *maps, prefix(total, heads))
    keep, q32 = lax.optimization_barrier((keep, q32))
    (rows1,) = row_maps(heads, 2, 2, q32, *first)
    (rows0,) = row_maps(heads, 3, 0, q32, *own_maps_here)
    entering = [swap(sends[r - 1], "seq", r) for r in away] + [keep]
    rows = (rows3, rows2, rows1, rows0)
    groups = lax.axis_size("head")
    keep, send = apply(True, rows, entering, groups)
    across = (keep, swap(send, "head", 1), out_weight, weight2)
    keep, send = apply(False, rows, entering, groups)
    here = (keep, swap(send, "head", 1), out_weight, weight2)
    parts = 4
    width = out_weight.shape[1] // parts
    ranges = [(i * width, width) for i in range(parts)]
    theirs = [swap(project(BF16, *x, *across), "head", 2) for x in ranges]
    mine = [project(F32, *x, *here) for x in ranges]
    mixed = []
    for i in range(parts):
        mixed = [add_part(i, parts, mine[i], theirs[i], mixed)]
    return mixed[0]


def solution(mesh):
    in_specs = (
        P("seq", "head", None),
        P("seq", "head", None),
        P("seq", "head", None),
        P("head", "seq"),
        P("head", "seq"),
        P("head", None),
    )
    out_specs = P(("seq", "head"), None)
    return jax.shard_map(body, mesh=mesh, in_specs=in_specs, out_specs=out_specs, check_vma=False)
```

```python
import functools

import jax
import jax.numpy as jnp
from jax import lax
from jax.experimental import pallas as pl
from jax.experimental.pallas import tpu as pltpu
from jax.sharding import PartitionSpec as P

C = 128
B = 16
F32 = jnp.float32
BF16 = jnp.bfloat16
NN = (((1,), (0,)), ((), ()))
NT = (((1,), (1,)), ((), ()))
TN = (((0,), (0,)), ((), ()))
MIB = 1024 * 1024


def dot(a, b, dims=NN):
    return lax.dot_general(a, b, dims, preferred_element_type=F32)


def split(x):
    high = x.astype(BF16)
    return high, (x - high.astype(F32)).astype(BF16)


def twice(x):
    return jnp.concatenate([x, x], axis=0)


def dot3(a, b):
    (ah, al), (bh, bl) = a, b
    width = bh.shape[1]
    if width > C:
        return dot(jnp.concatenate([ah, al], axis=1), twice(bh)) + dot(ah, bl)
    rows = ah.shape[0]
    both = dot(jnp.concatenate([ah, al], axis=0), jnp.concatenate([bh, bl], axis=1))
    return both[:rows, :width] + (both[:rows, width:] + both[rows:, :width])


def iotas():
    return (
        lax.broadcasted_iota(jnp.int32, (C, C), 0),
        lax.broadcasted_iota(jnp.int32, (C, C), 1),
    )


def to_column(row, eye):
    return jnp.sum(jnp.where(eye, row, 0.0), axis=1, keepdims=True)


def to_row(column, eye):
    return jnp.sum(jnp.where(eye, column, 0.0), axis=0, keepdims=True)


def inverse_scale(rows):
    return lax.rsqrt(jnp.sum(rows * rows, axis=1, keepdims=True) + 1e-06)


def three(x):
    high, rest = x.astype(BF16), x
    rest = rest - high.astype(F32)
    return (high,) + split(rest)


def running_sums(rows, upper):
    return sum(dot(x, upper) for x in reversed(three(rows)))


LANES = lax.GatherDimensionNumbers(
    offset_dims=(),
    collapsed_slice_dims=(1,),
    start_index_map=(1,),
    operand_batching_dims=(0,),
    start_indices_batching_dims=(0,),
)


def pick_lanes(x, index):
    return lax.gather(x, index, LANES, (1, 1), mode=lax.GatherScatterMode.PROMISE_IN_BOUNDS)


def base_inverse(lower, row, col):
    on_block = (row // B) == (col // B)
    blocks = jnp.where(on_block, lower, 0.0)
    packed = sum(blocks[i * B : (i + 1) * B] for i in range(1, C // B)) + blocks[:B]
    r, c = row[:B], col[:B]
    found = jnp.where(r == c % B, 1.0, 0.0)
    first = (c // B) * B
    for j in range(B - 1):
        found = found - pick_lanes(packed, (first + j)[..., None]) * found[j : j + 1]
    return jnp.where(on_block, jnp.concatenate([found] * (C // B), axis=0), 0.0)


def odd_rows(x, size):
    return jnp.concatenate([x[i : i + size] for i in range(size, C, 2 * size)], axis=0)


def weave(even, odd, size):
    parts = []
    for i in range(0, C // 2, size):
        parts += [even[i : i + size], odd[i : i + size]]
    return jnp.concatenate(parts, axis=0)


def even_rows(x, size):
    return jnp.concatenate([x[i : i + size] for i in range(0, C, 2 * size)], axis=0)


def inverses(lowers, row, col):
    found = [base_inverse(a, row, col) for a in lowers]
    parts = [split(a) for a in lowers]
    halves = [split(x) for x in found]
    size = B
    while size < C:
        r, c = odd_rows(row, size), odd_rows(col, size)
        mask = ((r // (2 * size)) == (c // (2 * size))) & ((r // size) != (c // size))
        nothing = jnp.zeros((C // 2, C), BF16)
        mask = jnp.where(mask, 1.0, 0.0).astype(BF16)
        joins = [tuple(odd_rows(x, size) * mask for x in part) for part in parts]
        middle = [split(dot3(a, x)) for a, x in zip(joins, halves)]
        middle = [tuple(weave(nothing, x, size) for x in part) for part in middle]
        lows = [dot3(tuple(odd_rows(x, size) for x in h), y) for h, y in zip(halves, middle)]
        lows = [odd_rows(x, size) - y for x, y in zip(found, lows)]
        found = [weave(even_rows(x, size), y, size) for x, y in zip(found, lows)]
        if 2 * size < C:
            halves = [
                tuple(weave(even_rows(x, size), y, size) for x, y in zip(h, split(low)))
                for h, low in zip(halves, lows)
            ]
        size *= 2
    return found


def in_hbm(*arrays):
    return [pltpu.with_memory_space_constraint(x, pltpu.HBM) for x in arrays]


def join(moved, added):
    return jnp.concatenate([moved, added], axis=1)


def after(later, earlier):
    total = dot3(split(later[:, :C]), split(earlier))
    return join(total[:, :C], total[:, C:] + later[:, C:])


def per_chunk(ref):
    return jnp.concatenate([ref[:, i : i + C] for i in range(0, ref.shape[1], C)], axis=0)


def chunk_rows(heads, head, c):
    return pl.ds(c * C * heads + head, C, stride=heads)


def places(heads):
    place = lax.rem(lax.axis_index("seq"), heads)
    return place, [lax.bitwise_xor(place, r) for r in range(heads - 1, -1, -1)]


def local_heads(heads, mine, k32, v32, sums_ref, betas_ref, mix_ref, wu_ref, n_ref):
    chunks = sums_ref.shape[0] // heads
    row, col = iotas()
    eye = row == col
    within = row >= col
    strict = row > col
    eye16 = jnp.where(eye, 1.0, 0.0).astype(BF16)
    jobs = [(head, c) for head in mine for c in range(chunks)]
    sums = jnp.concatenate([sums_ref[pl.ds(head, chunks, stride=heads), :] for head in mine], axis=0)
    betas = jnp.concatenate([betas_ref[pl.ds(head, chunks, stride=heads), :] for head in mine], axis=0)
    filled = jnp.concatenate([sums, jnp.zeros((C - sums.shape[0], C), F32)], axis=0)
    columns = filled.T
    grown = jnp.exp(sums)
    faded = jnp.exp(sums[:, C - 1 :] - sums)
    lowers, raws, values, fades, lengths = [], [], [], [], []
    for i, (head, c) in enumerate(jobs):
        at = slice(i, i + 1)
        raw = k32[chunk_rows(heads, head, c), :].astype(BF16)
        raws.append(raw)
        values.append(v32[chunk_rows(heads, head, c), :].astype(BF16))
        both = dot(jnp.concatenate([raw, eye16], axis=0), raw, NT)
        gram, turned = both[:C], both[C:]
        square = to_row(gram, eye) + 1e-06
        scale = lax.rsqrt(square)
        lengths.append(square * scale)
        strength = betas[at] * (scale * scale)
        mix = jnp.where(within, jnp.exp(columns[:, at] - sums[at]), 0.0) * strength
        mix_ref[i] = mix
        lowers.append(jnp.where(strict, gram * mix, 0.0))
        fades.append(turned * (strength * faded[at]))
    solved = []
    for i, found in enumerate(inverses(lowers, row, col)):
        at = slice(i, i + 1)
        kept = dot(jnp.concatenate(split(found * grown[at]), axis=1), twice(raws[i]))
        fresh = dot(jnp.concatenate(split(found * lengths[i]), axis=1), twice(values[i]))
        solved.append(join(kept, fresh))
    maps = []
    for i in range(len(jobs)):
        wu_ref[i] = solved[i]
        both = dot3(split(fades[i]), split(solved[i]))
        maps.append(join(jnp.where(eye, grown[i : i + 1, C - 1 :], 0.0) - both[:, :C], both[:, C:]))
    totals = []
    for j in range(len(mine)):
        first, second, third, last = maps[j * chunks : (j + 1) * chunks]
        early = after(second, first)
        n_ref[j * chunks + 1] = first
        n_ref[j * chunks + 2] = early
        n_ref[j * chunks + 3] = after(third, early)
        totals.append(after(after(last, third), early))
    return totals


def first_kernel(
    heads, k_hbm, v_hbm, beta_hbm, log_hbm, q_hbm, q16, k32, v32, sums_ref, betas_ref, mix_ref, wu_ref, n_ref, *refs
):
    sends, (k16, v16, beta_ref, log_ref, sems) = refs[: heads - 1], refs[heads - 1 :]
    pairs = ((log_hbm, log_ref), (beta_hbm, beta_ref), (k_hbm, k16), (v_hbm, v16), (q_hbm, q16))
    copies = [pltpu.make_async_copy(x, y, sems.at[i]) for i, (x, y) in enumerate(pairs)]
    *early, late = copies
    for copy in early:
        copy.start()
    for copy in early[:2]:
        copy.wait()
    row, col = iotas()
    sums_ref[...] = running_sums(per_chunk(log_ref), jnp.where(row <= col, 1.0, 0.0).astype(BF16))
    betas_ref[...] = per_chunk(beta_ref)
    early[2].wait()
    k32[...] = k16[...].astype(F32)
    early[3].wait()
    late.start()
    v32[...] = v16[...].astype(F32)
    mine = places(heads)[1][: heads - 1]
    totals = local_heads(heads, mine, k32, v32, sums_ref, betas_ref, mix_ref, wu_ref, n_ref)
    for send, total in zip(sends, totals):
        send[...] = total.astype(BF16)
    late.wait()


def maps_shapes(heads, chunks):
    return [
        jax.ShapeDtypeStruct((heads * chunks, C, C), F32),
        jax.ShapeDtypeStruct((heads * chunks, C, 2 * C), F32),
        jax.ShapeDtypeStruct((heads * chunks, C, 2 * C), F32),
    ] + [jax.ShapeDtypeStruct((C, 2 * C), BF16)] * heads


def first_maps(key, value, beta, log_decay, query):
    heads, tokens = beta.shape
    chunks = tokens // C
    here = pl.BlockSpec(memory_space=pltpu.VMEM)
    rows = jax.ShapeDtypeStruct((chunks * heads, C), F32)
    wide = jax.ShapeDtypeStruct(key.shape, F32)
    out_shape = [jax.ShapeDtypeStruct(query.shape, BF16), wide, wide, rows, rows] + maps_shapes(heads - 1, chunks)
    return pl.pallas_call(
        functools.partial(first_kernel, heads),
        in_specs=[pl.BlockSpec(memory_space=pltpu.HBM)] * 5,
        out_specs=[here] * len(out_shape),
        out_shape=out_shape,
        scratch_shapes=[
            pltpu.VMEM(key.shape, BF16),
            pltpu.VMEM(key.shape, BF16),
            pltpu.VMEM(beta.shape, F32),
            pltpu.VMEM(beta.shape, F32),
            pltpu.SemaphoreType.DMA((5,)),
        ],
        compiler_params=pltpu.CompilerParams(vmem_limit_bytes=32 * MIB),
        name="first_maps",
    )(*in_hbm(key, value, beta, log_decay, query))


def own_kernel(heads, k32, v32, sums_ref, betas_ref, mix_ref, wu_ref, n_ref, own_ref):
    mine = places(heads)[1][heads - 1 :]
    (total,) = local_heads(heads, mine, k32, v32, sums_ref, betas_ref, mix_ref, wu_ref, n_ref)
    own_ref[...] = total.astype(BF16)


def own_maps(heads, k32, v32, sums, betas):
    here = pl.BlockSpec(memory_space=pltpu.VMEM)
    out_shape = maps_shapes(1, sums.shape[0] // heads)
    return pl.pallas_call(
        functools.partial(own_kernel, heads),
        in_specs=[here] * 4,
        out_specs=[here] * len(out_shape),
        out_shape=out_shape,
        compiler_params=pltpu.CompilerParams(vmem_limit_bytes=16 * MIB),
        cost_estimate=pl.CostEstimate(flops=2000000000, bytes_accessed=8000000, transcendentals=0),
        name="own_maps",
    )(k32, v32, sums, betas)


def rows_kernel(heads, spot, slot, q_ref, k32, sums_ref, mix_ref, wu_ref, n_ref, out_ref, *wide):
    if wide:
        wide[0][...] = q_ref[...].astype(F32)
    q32 = wide[0] if wide else q_ref
    chunks = sums_ref.shape[0] // heads
    row, col = iotas()
    eye = row == col
    head = places(heads)[1][spot]
    grown = jnp.exp(sums_ref[pl.ds(head, chunks, stride=heads), :])
    for c in range(chunks):
        i = slot * chunks + c
        query, raw = q32[chunk_rows(heads, head, c), :], k32[chunk_rows(heads, head, c), :]
        pairs = dot(query.astype(BF16), raw.astype(BF16), NT) * mix_ref[i]
        both = dot3(split(pairs), split(wu_ref[i]))
        scale = inverse_scale(query)
        reach = (query * to_column(grown[c : c + 1], eye) - both[:, :C]) * scale
        fresh = both[:, C:] * scale
        if c > 0:
            earlier = dot3(split(reach), split(n_ref[i]))
            reach = earlier[:, :C]
            fresh = fresh + earlier[:, C:]
        out_ref[c * C : (c + 1) * C, :] = join(reach, fresh)


def row_maps(heads, spot, slot, query, *maps):
    tokens = query.shape[0] // heads
    here = pl.BlockSpec(memory_space=pltpu.VMEM)
    out_shape = [jax.ShapeDtypeStruct((tokens, 2 * C), F32)]
    if query.dtype == BF16:
        out_shape.append(jax.ShapeDtypeStruct(query.shape, F32))
    return pl.pallas_call(
        functools.partial(rows_kernel, heads, spot, slot),
        in_specs=[here] * (1 + len(maps)),
        out_specs=[here] * len(out_shape),
        out_shape=out_shape,
        compiler_params=pltpu.CompilerParams(vmem_limit_bytes=16 * MIB),
        cost_estimate=pl.CostEstimate(flops=1000000000, bytes_accessed=4000000, transcendentals=0),
        name="row_maps",
    )(query, *maps)


def small_call(kernel, out_shape, *args):
    here = pl.BlockSpec(memory_space=pltpu.VMEM)
    return pl.pallas_call(
        kernel,
        in_specs=[here] * len(args),
        out_specs=[here] * len(out_shape),
        out_shape=out_shape,
        compiler_params=pltpu.CompilerParams(vmem_limit_bytes=8 * MIB),
        name=kernel.__name__,
    )(*args)


def moved_on(maps, state16, added):
    high, low = split(maps)
    return dot(jnp.concatenate([high, low], axis=1), twice(state16)) + added


def times_parts(maps16, x):
    width = x.shape[1]
    both = dot(maps16, jnp.concatenate(split(x), axis=1))
    return both[:, :width] + both[:, width:]


def by_place(parts, work):
    heads = len(parts)
    place = places(heads)[0]
    for p in range(heads):

        @pl.when(place == p)
        def _(p=p):
            members = [i ^ p for i in range(heads)]
            work([parts[heads - 1 - r] for r in members], members)


def group_state(*refs):
    out_ref = refs[-1]

    def work(parts, _):
        first, second, third, last = parts
        state = dot(second[:, :C], first[:, C:]) + second[:, C:].astype(F32)
        both = dot(last[:, :C], third[...])
        state = dot3(split(both[:, :C]), split(state)) + (both[:, C:] + last[:, C:].astype(F32))
        out_ref[...] = state.astype(BF16)

    by_place(refs[:-1], work)


def group_prefix(*refs):
    parts, (maps_ref, added_ref, total_ref) = refs[:-3], refs[-3:]
    row, col = iotas()

    def work(parts, members):
        total = join(jnp.where(row == col, 1.0, 0.0), jnp.zeros((C, C), F32))
        for i, (part, r) in enumerate(zip(parts, members)):
            maps_ref[r] = jnp.concatenate(split(total[:, :C]), axis=1)
            added_ref[r] = total[:, C:]
            if i == 0:
                total = part[...].astype(F32)
            else:
                total = times_parts(part[:, :C], total)
                total = join(total[:, :C], total[:, C:] + part[:, C:].astype(F32))
        total_ref[...] = total.astype(BF16)

    by_place(parts, work)


def group_states(upper_only, maps_ref, added_ref, state_ref, *outs):
    state = state_ref[...]
    if upper_only:
        state = jnp.where(lax.axis_index("seq") < len(outs), jnp.zeros_like(state), state)
    both = twice(state)
    for r, out_ref in enumerate(outs):
        out_ref[...] = (dot(maps_ref[r], both) + added_ref[r]).astype(BF16)


def states_of_upper(*refs):
    group_states(True, *refs)


def states_given(*refs):
    group_states(False, *refs)


def prefix(total, heads):
    count = lax.axis_size("seq")
    groups = [list(range(i, count, heads)) for i in range(heads)]
    me = lax.axis_index("seq") // heads
    totals = lax.all_gather(total, "seq", axis_index_groups=groups)

    def step(d, state):
        longer = jnp.einsum("ik,pkw->iw", totals[d, :, :C], jnp.stack(split(state)), preferred_element_type=F32)
        return jnp.where(d < me, longer + totals[d, :, C:].astype(F32), state)

    start = jnp.zeros((C, C), F32)
    return lax.fori_loop(0, count // heads - 1, step, start).astype(BF16)


def apply_kernel(groups, other, *refs):
    heads = (len(refs) - 2) // 2
    rows_refs, states, (keep_ref, send_ref) = refs[:heads], refs[heads : 2 * heads], refs[2 * heads :]
    block = rows_refs[0].shape[0] // groups
    order = places(heads)[1]
    member = lax.axis_index("head")
    pair, core = member // 2, lax.rem(member, 2)
    pair = 1 - pair if other else pair
    for out_ref, parity in ((send_ref, 1 - core), (keep_ref, core)):
        rows = pl.ds(pl.multiple_of((2 * pair + parity) * block, block), block)
        for head, rows_ref, state in zip(order, rows_refs, states):
            attended = moved_on(rows_ref[rows, :C], state[...], rows_ref[rows, C:])
            out_ref[:, pl.ds(pl.multiple_of(head * C, C), C)] = attended.astype(BF16)


def apply(other, rows, states, groups):
    heads = len(states)
    here = pl.BlockSpec(memory_space=pltpu.VMEM)
    out = jax.ShapeDtypeStruct((rows[0].shape[0] // groups, heads * C), BF16)
    return pl.pallas_call(
        functools.partial(apply_kernel, groups, other),
        in_specs=[here] * (2 * heads),
        out_specs=[here] * 2,
        out_shape=[out, out],
        compiler_params=pltpu.CompilerParams(vmem_limit_bytes=8 * MIB),
        cost_estimate=pl.CostEstimate(flops=200000000, bytes_accessed=1000000, transcendentals=0),
        name="apply",
    )(*rows, *states)


def project_kernel(start, keep_ref, got_ref, w_ref, w2_ref, out_ref):
    columns = slice(start, start + out_ref.shape[1])
    shares = dot(keep_ref[...], w_ref[:, columns]) + dot(got_ref[...], w2_ref[:, columns])
    out_ref[...] = shares.astype(out_ref.dtype)


def project(dtype, start, width, keep, got, weight, weight2):
    block, depth = keep.shape
    return pl.pallas_call(
        functools.partial(project_kernel, start),
        out_shape=jax.ShapeDtypeStruct((block, width), dtype),
        compiler_params=pltpu.CompilerParams(vmem_limit_bytes=20 * MIB),
        cost_estimate=pl.CostEstimate(
            flops=4 * block * depth * width, bytes_accessed=4 * depth * width, transcendentals=0
        ),
        name="project",
    )(keep, got, weight, weight2)


def add_kernel(mine_ref, theirs_ref, *refs):
    refs[-1][...] = (mine_ref[...] + theirs_ref[...].astype(F32)).astype(BF16)


def add_part(index, parts, mine, theirs, earlier):
    block, width = mine.shape
    here = pl.BlockSpec(memory_space=pltpu.VMEM)
    return pl.pallas_call(
        add_kernel,
        grid=(1,),
        in_specs=[here, here] + [pl.BlockSpec(memory_space=pl.ANY)] * len(earlier),
        out_specs=pl.BlockSpec((block, width), lambda i: (0, index)),
        out_shape=jax.ShapeDtypeStruct((block, width * parts), BF16),
        input_output_aliases={2: 0} if earlier else {},
        compiler_params=pltpu.CompilerParams(vmem_limit_bytes=8 * MIB),
        name="add_part",
    )(mine, theirs, *earlier)


def swap(x, axis, bit):
    count = lax.axis_size(axis)
    return lax.ppermute(x, axis, [(i, i ^ bit) for i in range(count)])


def body(query, key, value, beta, log_decay, out_weight):
    tokens, heads, _ = key.shape
    count = lax.axis_size("seq")
    flat = lambda x: x.reshape(tokens * heads, C)
    weight2 = swap(out_weight, "head", 1)
    q16, k32, v32, sums, betas, mix, wu, states, *sends = first_maps(
        flat(key), flat(value), beta, log_decay, flat(query)
    )
    away = range(heads - 1, 0, -1)
    parts = [swap(x, "seq", r) for r, x in zip(away, sends)]
    *own_chunks, own = own_maps(heads, k32, v32, sums, betas)
    first = (k32, sums, mix, wu, states)
    own_maps_here = (k32, sums, *own_chunks)
    rows3, q32 = row_maps(heads, 0, 0, q16, *first)
    rows3, *parts = lax.optimization_barrier([rows3] + parts + [own])
    square = jax.ShapeDtypeStruct((C, C), BF16)
    both = jax.ShapeDtypeStruct((heads, C, 2 * C), BF16)
    added = jax.ShapeDtypeStruct((heads, C, C), F32)
    (state,) = small_call(group_state, [square], *parts)
    state, q32 = lax.optimization_barrier((state, q32))
    (rows2,) = row_maps(heads, 1, 1, q32, *first)
    *maps, total = small_call(group_prefix, [both, added, jax.ShapeDtypeStruct((C, 2 * C), BF16)], *parts)
    if count == 2 * heads:
        lower = swap(state, "seq", heads)
        rows2, maps, lower = lax.optimization_barrier((rows2, maps, lower))
        keep, *sends = small_call(states_of_upper, [square] * heads, *maps, lower)
    else:
        keep, *sends = small_call(states_given, [square] * heads, *maps, prefix(total, heads))
    keep, q32 = lax.optimization_barrier((keep, q32))
    (rows1,) = row_maps(heads, 2, 2, q32, *first)
    (rows0,) = row_maps(heads, 3, 0, q32, *own_maps_here)
    entering = [swap(sends[r - 1], "seq", r) for r in away] + [keep]
    rows = (rows3, rows2, rows1, rows0)
    groups = lax.axis_size("head")
    keep, send = apply(True, rows, entering, groups)
    across = (keep, swap(send, "head", 1), out_weight, weight2)
    keep, send = apply(False, rows, entering, groups)
    here = (keep, swap(send, "head", 1), out_weight, weight2)
    parts = 4
    width = out_weight.shape[1] // parts
    ranges = [(i * width, width) for i in range(parts)]
    theirs = [swap(project(BF16, *x, *across), "head", 2) for x in ranges]
    mine = [project(F32, *x, *here) for x in ranges]
    mixed = []
    for i in range(parts):
        mixed = [add_part(i, parts, mine[i], theirs[i], mixed)]
    return mixed[0]


def solution(mesh):
    in_specs = (
        P("seq", "head", None),
        P("seq", "head", None),
        P("seq", "head", None),
        P("head", "seq"),
        P("head", "seq"),
        P("head", None),
    )
    out_specs = P(("seq", "head"), None)
    return jax.shard_map(body, mesh=mesh, in_specs=in_specs, out_specs=out_specs, check_vma=False)
```

```python
import functools

import jax
import jax.numpy as jnp
from jax import lax
from jax.experimental import pallas as pl
from jax.experimental.pallas import tpu as pltpu
from jax.sharding import PartitionSpec as P

C = 128
B = 16
F32 = jnp.float32
BF16 = jnp.bfloat16
NN = (((1,), (0,)), ((), ()))
NT = (((1,), (1,)), ((), ()))
TN = (((0,), (0,)), ((), ()))
MIB = 1024 * 1024


def dot(a, b, dims=NN):
    return lax.dot_general(a, b, dims, preferred_element_type=F32)


def split(x):
    high = x.astype(BF16)
    return high, (x - high.astype(F32)).astype(BF16)


def twice(x):
    return jnp.concatenate([x, x], axis=0)


def dot3(a, b):
    (ah, al), (bh, bl) = a, b
    width = bh.shape[1]
    if width > C:
        return dot(jnp.concatenate([ah, al], axis=1), twice(bh)) + dot(ah, bl)
    rows = ah.shape[0]
    both = dot(jnp.concatenate([ah, al], axis=0), jnp.concatenate([bh, bl], axis=1))
    return both[:rows, :width] + (both[:rows, width:] + both[rows:, :width])


def iotas():
    return (
        lax.broadcasted_iota(jnp.int32, (C, C), 0),
        lax.broadcasted_iota(jnp.int32, (C, C), 1),
    )


def to_column(row, eye):
    return jnp.sum(jnp.where(eye, row, 0.0), axis=1, keepdims=True)


def to_row(column, eye):
    return jnp.sum(jnp.where(eye, column, 0.0), axis=0, keepdims=True)


def inverse_scale(rows):
    return lax.rsqrt(jnp.sum(rows * rows, axis=1, keepdims=True) + 1e-06)


def three(x):
    high, rest = x.astype(BF16), x
    rest = rest - high.astype(F32)
    return (high,) + split(rest)


def running_sums(rows, upper):
    return sum(dot(x, upper) for x in reversed(three(rows)))


def base_inverse(lower, row, col):
    on_block = (row // B) == (col // B)
    blocks = jnp.where(on_block, lower, 0.0)
    packed = sum(blocks[i * B : (i + 1) * B] for i in range(1, C // B)) + blocks[:B]
    r, c = row[:B], col[:B]
    found = jnp.where(r == c % B, 1.0, 0.0)
    first = (c // B) * B
    for j in range(B - 1):
        factor = jnp.take_along_axis(packed, first + j, axis=1)
        found = found - factor * found[j : j + 1]
    return jnp.where(on_block, jnp.concatenate([found] * (C // B), axis=0), 0.0)


def odd_rows(x, size):
    return jnp.concatenate([x[i : i + size] for i in range(size, C, 2 * size)], axis=0)


def weave(even, odd, size):
    parts = []
    for i in range(0, C // 2, size):
        parts += [even[i : i + size], odd[i : i + size]]
    return jnp.concatenate(parts, axis=0)


def even_rows(x, size):
    return jnp.concatenate([x[i : i + size] for i in range(0, C, 2 * size)], axis=0)


def inverses(lowers, row, col):
    found = [base_inverse(a, row, col) for a in lowers]
    parts = [split(a) for a in lowers]
    halves = [split(x) for x in found]
    size = B
    while size < C:
        r, c = odd_rows(row, size), odd_rows(col, size)
        mask = ((r // (2 * size)) == (c // (2 * size))) & ((r // size) != (c // size))
        nothing = jnp.zeros((C // 2, C), BF16)
        mask = jnp.where(mask, 1.0, 0.0).astype(BF16)
        joins = [tuple(odd_rows(x, size) * mask for x in part) for part in parts]
        middle = [split(dot3(a, x)) for a, x in zip(joins, halves)]
        middle = [tuple(weave(nothing, x, size) for x in part) for part in middle]
        lows = [dot3(tuple(odd_rows(x, size) for x in h), y) for h, y in zip(halves, middle)]
        lows = [odd_rows(x, size) - y for x, y in zip(found, lows)]
        found = [weave(even_rows(x, size), y, size) for x, y in zip(found, lows)]
        if 2 * size < C:
            halves = [
                tuple(weave(even_rows(x, size), y, size) for x, y in zip(h, split(low)))
                for h, low in zip(halves, lows)
            ]
        size *= 2
    return found


def in_hbm(*arrays):
    return [pltpu.with_memory_space_constraint(x, pltpu.HBM) for x in arrays]


def join(moved, added):
    return jnp.concatenate([moved, added], axis=1)


def after(later, earlier):
    total = dot3(split(later[:, :C]), split(earlier))
    return join(total[:, :C], total[:, C:] + later[:, C:])


def per_chunk(ref):
    return jnp.concatenate([ref[:, i : i + C] for i in range(0, ref.shape[1], C)], axis=0)


def chunk_rows(heads, head, c):
    return pl.ds(c * C * heads + head, C, stride=heads)


def places(heads):
    place = lax.rem(lax.axis_index("seq"), heads)
    return place, [lax.bitwise_xor(place, r) for r in range(heads - 1, -1, -1)]


def local_heads(heads, mine, k32, v32, sums_ref, betas_ref, mix_ref, wu_ref, n_ref):
    chunks = sums_ref.shape[0] // heads
    row, col = iotas()
    eye = row == col
    within = row >= col
    strict = row > col
    eye16 = jnp.where(eye, 1.0, 0.0).astype(BF16)
    jobs = [(head, c) for head in mine for c in range(chunks)]
    sums = jnp.concatenate([sums_ref[pl.ds(head, chunks, stride=heads), :] for head in mine], axis=0)
    betas = jnp.concatenate([betas_ref[pl.ds(head, chunks, stride=heads), :] for head in mine], axis=0)
    filled = jnp.concatenate([sums, jnp.zeros((C - sums.shape[0], C), F32)], axis=0)
    columns = filled.T
    grown = jnp.exp(sums)
    faded = jnp.exp(sums[:, C - 1 :] - sums)
    lowers, raws, values, fades, lengths = [], [], [], [], []
    for i, (head, c) in enumerate(jobs):
        at = slice(i, i + 1)
        raw = k32[chunk_rows(heads, head, c), :].astype(BF16)
        raws.append(raw)
        values.append(v32[chunk_rows(heads, head, c), :].astype(BF16))
        both = dot(jnp.concatenate([raw, eye16], axis=0), raw, NT)
        gram, turned = both[:C], both[C:]
        square = to_row(gram, eye) + 1e-06
        scale = lax.rsqrt(square)
        lengths.append(square * scale)
        strength = betas[at] * (scale * scale)
        mix = jnp.where(within, jnp.exp(columns[:, at] - sums[at]), 0.0) * strength
        mix_ref[i] = mix
        lowers.append(jnp.where(strict, gram * mix, 0.0))
        fades.append(turned * (strength * faded[at]))
    solved = []
    for i, found in enumerate(inverses(lowers, row, col)):
        at = slice(i, i + 1)
        kept = dot(jnp.concatenate(split(found * grown[at]), axis=1), twice(raws[i]))
        fresh = dot(jnp.concatenate(split(found * lengths[i]), axis=1), twice(values[i]))
        solved.append(join(kept, fresh))
    maps = []
    for i in range(len(jobs)):
        wu_ref[i] = solved[i]
        both = dot3(split(fades[i]), split(solved[i]))
        maps.append(join(jnp.where(eye, grown[i : i + 1, C - 1 :], 0.0) - both[:, :C], both[:, C:]))
    totals = []
    for j in range(len(mine)):
        first, second, third, last = maps[j * chunks : (j + 1) * chunks]
        early = after(second, first)
        n_ref[j * chunks + 1] = first
        n_ref[j * chunks + 2] = early
        n_ref[j * chunks + 3] = after(third, early)
        totals.append(after(after(last, third), early))
    return totals


def first_kernel(
    heads, k_hbm, v_hbm, beta_hbm, log_hbm, q_hbm, q16, k32, v32, sums_ref, betas_ref, mix_ref, wu_ref, n_ref, *refs
):
    sends, (k16, v16, beta_ref, log_ref, sems) = refs[: heads - 1], refs[heads - 1 :]
    pairs = ((log_hbm, log_ref), (beta_hbm, beta_ref), (k_hbm, k16), (v_hbm, v16), (q_hbm, q16))
    copies = [pltpu.make_async_copy(x, y, sems.at[i]) for i, (x, y) in enumerate(pairs)]
    *early, late = copies
    for copy in early:
        copy.start()
    for copy in early[:2]:
        copy.wait()
    row, col = iotas()
    sums_ref[...] = running_sums(per_chunk(log_ref), jnp.where(row <= col, 1.0, 0.0).astype(BF16))
    betas_ref[...] = per_chunk(beta_ref)
    early[2].wait()
    k32[...] = k16[...].astype(F32)
    early[3].wait()
    late.start()
    v32[...] = v16[...].astype(F32)
    mine = places(heads)[1][: heads - 1]
    totals = local_heads(heads, mine, k32, v32, sums_ref, betas_ref, mix_ref, wu_ref, n_ref)
    for send, total in zip(sends, totals):
        send[...] = total.astype(BF16)
    late.wait()


def maps_shapes(heads, chunks):
    return [
        jax.ShapeDtypeStruct((heads * chunks, C, C), F32),
        jax.ShapeDtypeStruct((heads * chunks, C, 2 * C), F32),
        jax.ShapeDtypeStruct((heads * chunks, C, 2 * C), F32),
    ] + [jax.ShapeDtypeStruct((C, 2 * C), BF16)] * heads


def first_maps(key, value, beta, log_decay, query):
    heads, tokens = beta.shape
    chunks = tokens // C
    here = pl.BlockSpec(memory_space=pltpu.VMEM)
    rows = jax.ShapeDtypeStruct((chunks * heads, C), F32)
    wide = jax.ShapeDtypeStruct(key.shape, F32)
    out_shape = [jax.ShapeDtypeStruct(query.shape, BF16), wide, wide, rows, rows] + maps_shapes(heads - 1, chunks)
    return pl.pallas_call(
        functools.partial(first_kernel, heads),
        in_specs=[pl.BlockSpec(memory_space=pltpu.HBM)] * 5,
        out_specs=[here] * len(out_shape),
        out_shape=out_shape,
        scratch_shapes=[
            pltpu.VMEM(key.shape, BF16),
            pltpu.VMEM(key.shape, BF16),
            pltpu.VMEM(beta.shape, F32),
            pltpu.VMEM(beta.shape, F32),
            pltpu.SemaphoreType.DMA((5,)),
        ],
        compiler_params=pltpu.CompilerParams(vmem_limit_bytes=32 * MIB),
        name="first_maps",
    )(*in_hbm(key, value, beta, log_decay, query))


def own_kernel(heads, k32, v32, sums_ref, betas_ref, mix_ref, wu_ref, n_ref, own_ref):
    mine = places(heads)[1][heads - 1 :]
    (total,) = local_heads(heads, mine, k32, v32, sums_ref, betas_ref, mix_ref, wu_ref, n_ref)
    own_ref[...] = total.astype(BF16)


def own_maps(heads, k32, v32, sums, betas):
    here = pl.BlockSpec(memory_space=pltpu.VMEM)
    out_shape = maps_shapes(1, sums.shape[0] // heads)
    return pl.pallas_call(
        functools.partial(own_kernel, heads),
        in_specs=[here] * 4,
        out_specs=[here] * len(out_shape),
        out_shape=out_shape,
        compiler_params=pltpu.CompilerParams(vmem_limit_bytes=16 * MIB),
        cost_estimate=pl.CostEstimate(flops=2000000000, bytes_accessed=8000000, transcendentals=0),
        name="own_maps",
    )(k32, v32, sums, betas)


def rows_kernel(heads, spot, slot, q_ref, k32, sums_ref, mix_ref, wu_ref, n_ref, out_ref, *wide):
    if wide:
        wide[0][...] = q_ref[...].astype(F32)
    q32 = wide[0] if wide else q_ref
    chunks = sums_ref.shape[0] // heads
    row, col = iotas()
    eye = row == col
    head = places(heads)[1][spot]
    grown = jnp.exp(sums_ref[pl.ds(head, chunks, stride=heads), :])
    for c in range(chunks):
        i = slot * chunks + c
        query, raw = q32[chunk_rows(heads, head, c), :], k32[chunk_rows(heads, head, c), :]
        pairs = dot(query.astype(BF16), raw.astype(BF16), NT) * mix_ref[i]
        both = dot3(split(pairs), split(wu_ref[i]))
        scale = inverse_scale(query)
        reach = (query * to_column(grown[c : c + 1], eye) - both[:, :C]) * scale
        fresh = both[:, C:] * scale
        if c > 0:
            earlier = dot3(split(reach), split(n_ref[i]))
            reach = earlier[:, :C]
            fresh = fresh + earlier[:, C:]
        out_ref[c * C : (c + 1) * C, :] = join(reach, fresh)


def row_maps(heads, spot, slot, query, *maps):
    tokens = query.shape[0] // heads
    here = pl.BlockSpec(memory_space=pltpu.VMEM)
    out_shape = [jax.ShapeDtypeStruct((tokens, 2 * C), F32)]
    if query.dtype == BF16:
        out_shape.append(jax.ShapeDtypeStruct(query.shape, F32))
    return pl.pallas_call(
        functools.partial(rows_kernel, heads, spot, slot),
        in_specs=[here] * (1 + len(maps)),
        out_specs=[here] * len(out_shape),
        out_shape=out_shape,
        compiler_params=pltpu.CompilerParams(vmem_limit_bytes=16 * MIB),
        cost_estimate=pl.CostEstimate(flops=1000000000, bytes_accessed=4000000, transcendentals=0),
        name="row_maps",
    )(query, *maps)


def small_call(kernel, out_shape, *args):
    here = pl.BlockSpec(memory_space=pltpu.VMEM)
    return pl.pallas_call(
        kernel,
        in_specs=[here] * len(args),
        out_specs=[here] * len(out_shape),
        out_shape=out_shape,
        compiler_params=pltpu.CompilerParams(vmem_limit_bytes=8 * MIB),
        name=kernel.__name__,
    )(*args)


def moved_on(maps, state16, added):
    high, low = split(maps)
    return dot(jnp.concatenate([high, low], axis=1), twice(state16)) + added


def times_parts(maps16, x):
    width = x.shape[1]
    both = dot(maps16, jnp.concatenate(split(x), axis=1))
    return both[:, :width] + both[:, width:]


def by_place(parts, work):
    heads = len(parts)
    place = places(heads)[0]
    for p in range(heads):

        @pl.when(place == p)
        def _(p=p):
            members = [i ^ p for i in range(heads)]
            work([parts[heads - 1 - r] for r in members], members)


def group_state(*refs):
    out_ref = refs[-1]

    def work(parts, _):
        first, second, third, last = parts
        state = dot(second[:, :C], first[:, C:]) + second[:, C:].astype(F32)
        both = dot(last[:, :C], third[...])
        state = dot3(split(both[:, :C]), split(state)) + (both[:, C:] + last[:, C:].astype(F32))
        out_ref[...] = state.astype(BF16)

    by_place(refs[:-1], work)


def group_prefix(*refs):
    parts, (maps_ref, added_ref, total_ref) = refs[:-3], refs[-3:]
    row, col = iotas()

    def work(parts, members):
        total = join(jnp.where(row == col, 1.0, 0.0), jnp.zeros((C, C), F32))
        for i, (part, r) in enumerate(zip(parts, members)):
            maps_ref[r] = jnp.concatenate(split(total[:, :C]), axis=1)
            added_ref[r] = total[:, C:]
            if i == 0:
                total = part[...].astype(F32)
            else:
                total = times_parts(part[:, :C], total)
                total = join(total[:, :C], total[:, C:] + part[:, C:].astype(F32))
        total_ref[...] = total.astype(BF16)

    by_place(parts, work)


def group_states(upper_only, maps_ref, added_ref, state_ref, *outs):
    state = state_ref[...]
    if upper_only:
        state = jnp.where(lax.axis_index("seq") < len(outs), jnp.zeros_like(state), state)
    both = twice(state)
    for r, out_ref in enumerate(outs):
        out_ref[...] = (dot(maps_ref[r], both) + added_ref[r]).astype(BF16)


def states_of_upper(*refs):
    group_states(True, *refs)


def states_given(*refs):
    group_states(False, *refs)


def prefix(total, heads):
    count = lax.axis_size("seq")
    groups = [list(range(i, count, heads)) for i in range(heads)]
    me = lax.axis_index("seq") // heads
    totals = lax.all_gather(total, "seq", axis_index_groups=groups)

    def step(d, state):
        longer = jnp.einsum("ik,pkw->iw", totals[d, :, :C], jnp.stack(split(state)), preferred_element_type=F32)
        return jnp.where(d < me, longer + totals[d, :, C:].astype(F32), state)

    start = jnp.zeros((C, C), F32)
    return lax.fori_loop(0, count // heads - 1, step, start).astype(BF16)


def apply_kernel(groups, other, *refs):
    heads = (len(refs) - 2) // 2
    rows_refs, states, (keep_ref, send_ref) = refs[:heads], refs[heads : 2 * heads], refs[2 * heads :]
    block = rows_refs[0].shape[0] // groups
    order = places(heads)[1]
    member = lax.axis_index("head")
    pair, core = member // 2, lax.rem(member, 2)
    pair = 1 - pair if other else pair
    for out_ref, parity in ((send_ref, 1 - core), (keep_ref, core)):
        rows = pl.ds(pl.multiple_of((2 * pair + parity) * block, block), block)
        for head, rows_ref, state in zip(order, rows_refs, states):
            attended = moved_on(rows_ref[rows, :C], state[...], rows_ref[rows, C:])
            out_ref[:, pl.ds(pl.multiple_of(head * C, C), C)] = attended.astype(BF16)


def apply(other, rows, states, groups):
    heads = len(states)
    here = pl.BlockSpec(memory_space=pltpu.VMEM)
    out = jax.ShapeDtypeStruct((rows[0].shape[0] // groups, heads * C), BF16)
    return pl.pallas_call(
        functools.partial(apply_kernel, groups, other),
        in_specs=[here] * (2 * heads),
        out_specs=[here] * 2,
        out_shape=[out, out],
        compiler_params=pltpu.CompilerParams(vmem_limit_bytes=8 * MIB),
        cost_estimate=pl.CostEstimate(flops=200000000, bytes_accessed=1000000, transcendentals=0),
        name="apply",
    )(*rows, *states)


def project_kernel(start, keep_ref, got_ref, w_ref, w2_ref, out_ref):
    columns = slice(start, start + out_ref.shape[1])
    shares = dot(keep_ref[...], w_ref[:, columns]) + dot(got_ref[...], w2_ref[:, columns])
    out_ref[...] = shares.astype(out_ref.dtype)


def project(dtype, start, width, keep, got, weight, weight2):
    block, depth = keep.shape
    return pl.pallas_call(
        functools.partial(project_kernel, start),
        out_shape=jax.ShapeDtypeStruct((block, width), dtype),
        compiler_params=pltpu.CompilerParams(vmem_limit_bytes=20 * MIB),
        cost_estimate=pl.CostEstimate(
            flops=4 * block * depth * width, bytes_accessed=4 * depth * width, transcendentals=0
        ),
        name="project",
    )(keep, got, weight, weight2)


def add_kernel(mine_ref, theirs_ref, *refs):
    refs[-1][...] = (mine_ref[...] + theirs_ref[...].astype(F32)).astype(BF16)


def add_part(index, parts, mine, theirs, earlier):
    block, width = mine.shape
    here = pl.BlockSpec(memory_space=pltpu.VMEM)
    return pl.pallas_call(
        add_kernel,
        grid=(1,),
        in_specs=[here, here] + [pl.BlockSpec(memory_space=pl.ANY)] * len(earlier),
        out_specs=pl.BlockSpec((block, width), lambda i: (0, index)),
        out_shape=jax.ShapeDtypeStruct((block, width * parts), BF16),
        input_output_aliases={2: 0} if earlier else {},
        compiler_params=pltpu.CompilerParams(vmem_limit_bytes=8 * MIB),
        name="add_part",
    )(mine, theirs, *earlier)


def swap(x, axis, bit):
    count = lax.axis_size(axis)
    return lax.ppermute(x, axis, [(i, i ^ bit) for i in range(count)])


def body(query, key, value, beta, log_decay, out_weight):
    tokens, heads, _ = key.shape
    count = lax.axis_size("seq")
    flat = lambda x: x.reshape(tokens * heads, C)
    weight2 = swap(out_weight, "head", 1)
    q16, k32, v32, sums, betas, mix, wu, states, *sends = first_maps(
        flat(key), flat(value), beta, log_decay, flat(query)
    )
    away = range(heads - 1, 0, -1)
    parts = [swap(x, "seq", r) for r, x in zip(away, sends)]
    *own_chunks, own = own_maps(heads, k32, v32, sums, betas)
    first = (k32, sums, mix, wu, states)
    own_maps_here = (k32, sums, *own_chunks)
    rows3, q32 = row_maps(heads, 0, 0, q16, *first)
    rows3, *parts = lax.optimization_barrier([rows3] + parts + [own])
    square = jax.ShapeDtypeStruct((C, C), BF16)
    both = jax.ShapeDtypeStruct((heads, C, 2 * C), BF16)
    added = jax.ShapeDtypeStruct((heads, C, C), F32)
    (state,) = small_call(group_state, [square], *parts)
    state, q32 = lax.optimization_barrier((state, q32))
    (rows2,) = row_maps(heads, 1, 1, q32, *first)
    *maps, total = small_call(group_prefix, [both, added, jax.ShapeDtypeStruct((C, 2 * C), BF16)], *parts)
    if count == 2 * heads:
        lower = swap(state, "seq", heads)
        rows2, maps, lower = lax.optimization_barrier((rows2, maps, lower))
        keep, *sends = small_call(states_of_upper, [square] * heads, *maps, lower)
    else:
        keep, *sends = small_call(states_given, [square] * heads, *maps, prefix(total, heads))
    keep, q32 = lax.optimization_barrier((keep, q32))
    (rows1,) = row_maps(heads, 2, 2, q32, *first)
    (rows0,) = row_maps(heads, 3, 0, q32, *own_maps_here)
    entering = [swap(sends[r - 1], "seq", r) for r in away] + [keep]
    rows = (rows3, rows2, rows1, rows0)
    groups = lax.axis_size("head")
    keep, send = apply(True, rows, entering, groups)
    across = (keep, swap(send, "head", 1), out_weight, weight2)
    keep, send = apply(False, rows, entering, groups)
    here = (keep, swap(send, "head", 1), out_weight, weight2)
    parts = 4
    width = out_weight.shape[1] // parts
    ranges = [(i * width, width) for i in range(parts)]
    theirs = [swap(project(BF16, *x, *across), "head", 2) for x in ranges]
    mine = [project(F32, *x, *here) for x in ranges]
    mixed = []
    for i in range(parts):
        mixed = [add_part(i, parts, mine[i], theirs[i], mixed)]
    return mixed[0]


def solution(mesh):
    in_specs = (
        P("seq", "head", None),
        P("seq", "head", None),
        P("seq", "head", None),
        P("head", "seq"),
        P("head", "seq"),
        P("head", None),
    )
    out_specs = P(("seq", "head"), None)
    return jax.shard_map(body, mesh=mesh, in_specs=in_specs, out_specs=out_specs, check_vma=False)
```

```python
import functools

import jax
import jax.numpy as jnp
from jax import lax
from jax.experimental import pallas as pl
from jax.experimental.pallas import tpu as pltpu
from jax.sharding import PartitionSpec as P

C = 128
B = 16
F32 = jnp.float32
BF16 = jnp.bfloat16
NN = (((1,), (0,)), ((), ()))
NT = (((1,), (1,)), ((), ()))
TN = (((0,), (0,)), ((), ()))
MIB = 1024 * 1024


def dot(a, b, dims=NN):
    return lax.dot_general(a, b, dims, preferred_element_type=F32)


def split(x):
    high = x.astype(BF16)
    return high, (x - high.astype(F32)).astype(BF16)


def twice(x):
    return jnp.concatenate([x, x], axis=0)


def dot3(a, b):
    (ah, al), (bh, bl) = a, b
    width = bh.shape[1]
    if width > C:
        return dot(jnp.concatenate([ah, al], axis=1), twice(bh)) + dot(ah, bl)
    rows = ah.shape[0]
    both = dot(jnp.concatenate([ah, al], axis=0), jnp.concatenate([bh, bl], axis=1))
    return both[:rows, :width] + (both[:rows, width:] + both[rows:, :width])


def iotas():
    return (
        lax.broadcasted_iota(jnp.int32, (C, C), 0),
        lax.broadcasted_iota(jnp.int32, (C, C), 1),
    )


def to_column(row, eye):
    return jnp.sum(jnp.where(eye, row, 0.0), axis=1, keepdims=True)


def to_row(column, eye):
    return jnp.sum(jnp.where(eye, column, 0.0), axis=0, keepdims=True)


def inverse_scale(rows):
    return lax.rsqrt(jnp.sum(rows * rows, axis=1, keepdims=True) + 1e-06)


def three(x):
    high, rest = x.astype(BF16), x
    rest = rest - high.astype(F32)
    return (high,) + split(rest)


def running_sums(rows, upper):
    return sum(dot(x, upper) for x in reversed(three(rows)))


def base_inverse(lower, row, col):
    on_block = (row // B) == (col // B)
    blocks = jnp.where(on_block, lower, 0.0)
    packed = sum(blocks[i * B : (i + 1) * B] for i in range(1, C // B)) + blocks[:B]
    r, c = row[:B], col[:B]
    found = jnp.where(r == c % B, 1.0, 0.0)
    first = (c // B) * B
    for j in range(B - 1):
        factor = jnp.take_along_axis(packed, first + j, axis=1)
        found = found - factor * found[j : j + 1]
    return jnp.where(on_block, jnp.concatenate([found] * (C // B), axis=0), 0.0)


def odd_rows(x, size):
    return jnp.concatenate([x[i : i + size] for i in range(size, C, 2 * size)], axis=0)


def weave(even, odd, size):
    parts = []
    for i in range(0, C // 2, size):
        parts += [even[i : i + size], odd[i : i + size]]
    return jnp.concatenate(parts, axis=0)


def even_rows(x, size):
    return jnp.concatenate([x[i : i + size] for i in range(0, C, 2 * size)], axis=0)


def inverses(lowers, row, col):
    found = [base_inverse(a, row, col) for a in lowers]
    parts = [split(a) for a in lowers]
    halves = [split(x) for x in found]
    size = B
    while size < C:
        r, c = odd_rows(row, size), odd_rows(col, size)
        mask = ((r // (2 * size)) == (c // (2 * size))) & ((r // size) != (c // size))
        nothing = jnp.zeros((C // 2, C), BF16)
        mask = jnp.where(mask, 1.0, 0.0).astype(BF16)
        joins = [tuple(odd_rows(x, size) * mask for x in part) for part in parts]
        middle = [split(dot3(a, x)) for a, x in zip(joins, halves)]
        middle = [tuple(weave(nothing, x, size) for x in part) for part in middle]
        lows = [dot3(tuple(odd_rows(x, size) for x in h), y) for h, y in zip(halves, middle)]
        lows = [odd_rows(x, size) - y for x, y in zip(found, lows)]
        found = [weave(even_rows(x, size), y, size) for x, y in zip(found, lows)]
        if 2 * size < C:
            halves = [
                tuple(weave(even_rows(x, size), y, size) for x, y in zip(h, split(low)))
                for h, low in zip(halves, lows)
            ]
        size *= 2
    return found


def in_hbm(*arrays):
    return [pltpu.with_memory_space_constraint(x, pltpu.HBM) for x in arrays]


def join(moved, added):
    return jnp.concatenate([moved, added], axis=1)


def after(later, earlier):
    total = dot3(split(later[:, :C]), split(earlier))
    return join(total[:, :C], total[:, C:] + later[:, C:])


def per_chunk(ref):
    return jnp.concatenate([ref[:, i : i + C] for i in range(0, ref.shape[1], C)], axis=0)


def chunk_rows(heads, head, c):
    return pl.ds(c * C * heads + head, C, stride=heads)


def places(heads):
    place = lax.rem(lax.axis_index("seq"), heads)
    return place, [lax.bitwise_xor(place, r) for r in range(heads - 1, -1, -1)]


def local_heads(heads, mine, k32, v32, sums_ref, betas_ref, mix_ref, wu_ref, n_ref):
    chunks = sums_ref.shape[0] // heads
    row, col = iotas()
    eye = row == col
    within = row >= col
    strict = row > col
    eye16 = jnp.where(eye, 1.0, 0.0).astype(BF16)
    jobs = [(head, c) for head in mine for c in range(chunks)]
    sums = jnp.concatenate([sums_ref[pl.ds(head, chunks, stride=heads), :] for head in mine], axis=0)
    betas = jnp.concatenate([betas_ref[pl.ds(head, chunks, stride=heads), :] for head in mine], axis=0)
    filled = jnp.concatenate([sums, jnp.zeros((C - sums.shape[0], C), F32)], axis=0)
    columns = filled.T
    grown = jnp.exp(sums)
    faded = jnp.exp(sums[:, C - 1 :] - sums)
    lowers, raws, values, fades, lengths = [], [], [], [], []
    for i, (head, c) in enumerate(jobs):
        at = slice(i, i + 1)
        raw = k32[chunk_rows(heads, head, c), :].astype(BF16)
        raws.append(raw)
        values.append(v32[chunk_rows(heads, head, c), :].astype(BF16))
        both = dot(jnp.concatenate([raw, eye16], axis=0), raw, NT)
        gram, turned = both[:C], both[C:]
        square = to_row(gram, eye) + 1e-06
        scale = lax.rsqrt(square)
        lengths.append(square * scale)
        strength = betas[at] * (scale * scale)
        mix = jnp.where(within, jnp.exp(columns[:, at] - sums[at]), 0.0) * strength
        mix_ref[i] = mix
        lowers.append(jnp.where(strict, gram * mix, 0.0))
        fades.append(turned * (strength * faded[at]))
    solved = []
    for i, found in enumerate(inverses(lowers, row, col)):
        at = slice(i, i + 1)
        kept = dot(jnp.concatenate(split(found * grown[at]), axis=1), twice(raws[i]))
        fresh = dot(jnp.concatenate(split(found * lengths[i]), axis=1), twice(values[i]))
        solved.append(join(kept, fresh))
    maps = []
    for i in range(len(jobs)):
        wu_ref[i] = solved[i]
        both = dot3(split(fades[i]), split(solved[i]))
        maps.append(join(jnp.where(eye, grown[i : i + 1, C - 1 :], 0.0) - both[:, :C], both[:, C:]))
    totals = []
    for j in range(len(mine)):
        first, second, third, last = maps[j * chunks : (j + 1) * chunks]
        early = after(second, first)
        n_ref[j * chunks + 1] = first
        n_ref[j * chunks + 2] = early
        n_ref[j * chunks + 3] = after(third, early)
        totals.append(after(after(last, third), early))
    return totals


def first_kernel(
    heads, k_hbm, v_hbm, beta_hbm, log_hbm, q_hbm, q16, k32, v32, sums_ref, betas_ref, mix_ref, wu_ref, n_ref, *refs
):
    sends, (k16, v16, beta_ref, log_ref, sems) = refs[: heads - 1], refs[heads - 1 :]
    pairs = ((log_hbm, log_ref), (beta_hbm, beta_ref), (k_hbm, k16), (v_hbm, v16), (q_hbm, q16))
    copies = [pltpu.make_async_copy(x, y, sems.at[i]) for i, (x, y) in enumerate(pairs)]
    *early, late = copies
    for copy in early:
        copy.start()
    for copy in early[:2]:
        copy.wait()
    row, col = iotas()
    sums_ref[...] = running_sums(per_chunk(log_ref), jnp.where(row <= col, 1.0, 0.0).astype(BF16))
    betas_ref[...] = per_chunk(beta_ref)
    early[2].wait()
    k32[...] = k16[...].astype(F32)
    early[3].wait()
    late.start()
    v32[...] = v16[...].astype(F32)
    mine = places(heads)[1][: heads - 1]
    totals = local_heads(heads, mine, k32, v32, sums_ref, betas_ref, mix_ref, wu_ref, n_ref)
    for send, total in zip(sends, totals):
        send[...] = total.astype(BF16)
    late.wait()


def maps_shapes(heads, chunks):
    return [
        jax.ShapeDtypeStruct((heads * chunks, C, C), F32),
        jax.ShapeDtypeStruct((heads * chunks, C, 2 * C), F32),
        jax.ShapeDtypeStruct((heads * chunks, C, 2 * C), F32),
    ] + [jax.ShapeDtypeStruct((C, 2 * C), BF16)] * heads


def first_maps(key, value, beta, log_decay, query):
    heads, tokens = beta.shape
    chunks = tokens // C
    here = pl.BlockSpec(memory_space=pltpu.VMEM)
    rows = jax.ShapeDtypeStruct((chunks * heads, C), F32)
    wide = jax.ShapeDtypeStruct(key.shape, F32)
    out_shape = [jax.ShapeDtypeStruct(query.shape, BF16), wide, wide, rows, rows] + maps_shapes(heads - 1, chunks)
    return pl.pallas_call(
        functools.partial(first_kernel, heads),
        in_specs=[pl.BlockSpec(memory_space=pltpu.HBM)] * 5,
        out_specs=[here] * len(out_shape),
        out_shape=out_shape,
        scratch_shapes=[
            pltpu.VMEM(key.shape, BF16),
            pltpu.VMEM(key.shape, BF16),
            pltpu.VMEM(beta.shape, F32),
            pltpu.VMEM(beta.shape, F32),
            pltpu.SemaphoreType.DMA((5,)),
        ],
        compiler_params=pltpu.CompilerParams(vmem_limit_bytes=32 * MIB),
        name="first_maps",
    )(*in_hbm(key, value, beta, log_decay, query))


def own_kernel(heads, k32, v32, sums_ref, betas_ref, mix_ref, wu_ref, n_ref, own_ref):
    mine = places(heads)[1][heads - 1 :]
    (total,) = local_heads(heads, mine, k32, v32, sums_ref, betas_ref, mix_ref, wu_ref, n_ref)
    own_ref[...] = total.astype(BF16)


def own_maps(heads, k32, v32, sums, betas):
    here = pl.BlockSpec(memory_space=pltpu.VMEM)
    out_shape = maps_shapes(1, sums.shape[0] // heads)
    return pl.pallas_call(
        functools.partial(own_kernel, heads),
        in_specs=[here] * 4,
        out_specs=[here] * len(out_shape),
        out_shape=out_shape,
        compiler_params=pltpu.CompilerParams(vmem_limit_bytes=16 * MIB),
        cost_estimate=pl.CostEstimate(flops=2000000000, bytes_accessed=8000000, transcendentals=0),
        name="own_maps",
    )(k32, v32, sums, betas)


def rows_kernel(heads, spot, slot, q_ref, k32, sums_ref, mix_ref, wu_ref, n_ref, out_ref, *wide):
    if wide:
        wide[0][...] = q_ref[...].astype(F32)
    q32 = wide[0] if wide else q_ref
    chunks = sums_ref.shape[0] // heads
    row, col = iotas()
    eye = row == col
    head = places(heads)[1][spot]
    grown = jnp.exp(sums_ref[pl.ds(head, chunks, stride=heads), :])
    for c in range(chunks):
        i = slot * chunks + c
        query, raw = q32[chunk_rows(heads, head, c), :], k32[chunk_rows(heads, head, c), :]
        pairs = dot(query.astype(BF16), raw.astype(BF16), NT) * mix_ref[i]
        both = dot3(split(pairs), split(wu_ref[i]))
        scale = inverse_scale(query)
        reach = (query * to_column(grown[c : c + 1], eye) - both[:, :C]) * scale
        fresh = both[:, C:] * scale
        if c > 0:
            earlier = dot3(split(reach), split(n_ref[i]))
            reach = earlier[:, :C]
            fresh = fresh + earlier[:, C:]
        out_ref[c * C : (c + 1) * C, :] = join(reach, fresh)


def row_maps(heads, spot, slot, query, *maps):
    tokens = query.shape[0] // heads
    here = pl.BlockSpec(memory_space=pltpu.VMEM)
    out_shape = [jax.ShapeDtypeStruct((tokens, 2 * C), F32)]
    if query.dtype == BF16:
        out_shape.append(jax.ShapeDtypeStruct(query.shape, F32))
    return pl.pallas_call(
        functools.partial(rows_kernel, heads, spot, slot),
        in_specs=[here] * (1 + len(maps)),
        out_specs=[here] * len(out_shape),
        out_shape=out_shape,
        compiler_params=pltpu.CompilerParams(vmem_limit_bytes=16 * MIB),
        cost_estimate=pl.CostEstimate(flops=1000000000, bytes_accessed=4000000, transcendentals=0),
        name="row_maps",
    )(query, *maps)


def small_call(kernel, out_shape, *args):
    here = pl.BlockSpec(memory_space=pltpu.VMEM)
    return pl.pallas_call(
        kernel,
        in_specs=[here] * len(args),
        out_specs=[here] * len(out_shape),
        out_shape=out_shape,
        compiler_params=pltpu.CompilerParams(vmem_limit_bytes=8 * MIB),
        name=kernel.__name__,
    )(*args)


def moved_on(maps, state16, added):
    high, low = split(maps)
    return dot(jnp.concatenate([high, low], axis=1), twice(state16)) + added


def times_parts(maps16, x):
    width = x.shape[1]
    both = dot(maps16, jnp.concatenate(split(x), axis=1))
    return both[:, :width] + both[:, width:]


def by_place(parts, work):
    heads = len(parts)
    place = places(heads)[0]
    for p in range(heads):

        @pl.when(place == p)
        def _(p=p):
            members = [i ^ p for i in range(heads)]
            work([parts[heads - 1 - r] for r in members], members)


def group_state(*refs):
    out_ref = refs[-1]

    def work(parts, _):
        first, second, third, last = parts
        state = dot(second[:, :C], first[:, C:]) + second[:, C:].astype(F32)
        both = dot(last[:, :C], third[...])
        state = dot3(split(both[:, :C]), split(state)) + (both[:, C:] + last[:, C:].astype(F32))
        out_ref[...] = state.astype(BF16)

    by_place(refs[:-1], work)


def group_prefix(*refs):
    parts, (maps_ref, added_ref, total_ref) = refs[:-3], refs[-3:]
    row, col = iotas()

    def work(parts, members):
        total = join(jnp.where(row == col, 1.0, 0.0), jnp.zeros((C, C), F32))
        for i, (part, r) in enumerate(zip(parts, members)):
            maps_ref[r] = jnp.concatenate(split(total[:, :C]), axis=1)
            added_ref[r] = total[:, C:]
            if i == 0:
                total = part[...].astype(F32)
            else:
                total = times_parts(part[:, :C], total)
                total = join(total[:, :C], total[:, C:] + part[:, C:].astype(F32))
        total_ref[...] = total.astype(BF16)

    by_place(parts, work)


def group_states(upper_only, maps_ref, added_ref, state_ref, *outs):
    state = state_ref[...]
    if upper_only:
        state = jnp.where(lax.axis_index("seq") < len(outs), jnp.zeros_like(state), state)
    both = twice(state)
    for r, out_ref in enumerate(outs):
        out_ref[...] = (dot(maps_ref[r], both) + added_ref[r]).astype(BF16)


def states_of_upper(*refs):
    group_states(True, *refs)


def states_given(*refs):
    group_states(False, *refs)


def prefix(total, heads):
    count = lax.axis_size("seq")
    groups = [list(range(i, count, heads)) for i in range(heads)]
    me = lax.axis_index("seq") // heads
    totals = lax.all_gather(total, "seq", axis_index_groups=groups)

    def step(d, state):
        longer = jnp.einsum("ik,pkw->iw", totals[d, :, :C], jnp.stack(split(state)), preferred_element_type=F32)
        return jnp.where(d < me, longer + totals[d, :, C:].astype(F32), state)

    start = jnp.zeros((C, C), F32)
    return lax.fori_loop(0, count // heads - 1, step, start).astype(BF16)


def apply_kernel(groups, other, *refs):
    heads = (len(refs) - 2) // 2
    rows_refs, states, (keep_ref, send_ref) = refs[:heads], refs[heads : 2 * heads], refs[2 * heads :]
    block = rows_refs[0].shape[0] // groups
    order = places(heads)[1]
    member = lax.axis_index("head")
    pair, core = member // 2, lax.rem(member, 2)
    pair = 1 - pair if other else pair
    for out_ref, parity in ((send_ref, 1 - core), (keep_ref, core)):
        rows = pl.ds(pl.multiple_of((2 * pair + parity) * block, block), block)
        for head, rows_ref, state in zip(order, rows_refs, states):
            attended = moved_on(rows_ref[rows, :C], state[...], rows_ref[rows, C:])
            out_ref[:, pl.ds(pl.multiple_of(head * C, C), C)] = attended.astype(BF16)


def apply(other, rows, states, groups):
    heads = len(states)
    here = pl.BlockSpec(memory_space=pltpu.VMEM)
    out = jax.ShapeDtypeStruct((rows[0].shape[0] // groups, heads * C), BF16)
    return pl.pallas_call(
        functools.partial(apply_kernel, groups, other),
        in_specs=[here] * (2 * heads),
        out_specs=[here] * 2,
        out_shape=[out, out],
        compiler_params=pltpu.CompilerParams(vmem_limit_bytes=8 * MIB),
        cost_estimate=pl.CostEstimate(flops=200000000, bytes_accessed=1000000, transcendentals=0),
        name="apply",
    )(*rows, *states)


def project_kernel(start, keep_ref, got_ref, w_ref, w2_ref, out_ref):
    columns = slice(start, start + out_ref.shape[1])
    shares = dot(keep_ref[...], w_ref[:, columns]) + dot(got_ref[...], w2_ref[:, columns])
    out_ref[...] = shares.astype(out_ref.dtype)


def project(dtype, start, width, keep, got, weight, weight2):
    block, depth = keep.shape
    return pl.pallas_call(
        functools.partial(project_kernel, start),
        out_shape=jax.ShapeDtypeStruct((block, width), dtype),
        compiler_params=pltpu.CompilerParams(vmem_limit_bytes=20 * MIB),
        cost_estimate=pl.CostEstimate(
            flops=4 * block * depth * width, bytes_accessed=4 * depth * width, transcendentals=0
        ),
        name="project",
    )(keep, got, weight, weight2)


def add_kernel(mine_ref, theirs_ref, *refs):
    refs[-1][...] = (mine_ref[...] + theirs_ref[...].astype(F32)).astype(BF16)


def add_part(index, parts, mine, theirs, earlier):
    block, width = mine.shape
    here = pl.BlockSpec(memory_space=pltpu.VMEM)
    return pl.pallas_call(
        add_kernel,
        grid=(1,),
        in_specs=[here, here] + [pl.BlockSpec(memory_space=pl.ANY)] * len(earlier),
        out_specs=pl.BlockSpec((block, width), lambda i: (0, index)),
        out_shape=jax.ShapeDtypeStruct((block, width * parts), BF16),
        input_output_aliases={2: 0} if earlier else {},
        compiler_params=pltpu.CompilerParams(vmem_limit_bytes=8 * MIB),
        name="add_part",
    )(mine, theirs, *earlier)


def swap(x, axis, bit):
    count = lax.axis_size(axis)
    return lax.ppermute(x, axis, [(i, i ^ bit) for i in range(count)])


def body(query, key, value, beta, log_decay, out_weight):
    tokens, heads, _ = key.shape
    count = lax.axis_size("seq")
    flat = lambda x: x.reshape(tokens * heads, C)
    weight2 = swap(out_weight, "head", 1)
    q16, k32, v32, sums, betas, mix, wu, states, *sends = first_maps(
        flat(key), flat(value), beta, log_decay, flat(query)
    )
    away = range(heads - 1, 0, -1)
    parts = [swap(x, "seq", r) for r, x in zip(away, sends)]
    *own_chunks, own = own_maps(heads, k32, v32, sums, betas)
    first = (k32, sums, mix, wu, states)
    own_maps_here = (k32, sums, *own_chunks)
    rows3, q32 = row_maps(heads, 0, 0, q16, *first)
    rows3, *parts = lax.optimization_barrier([rows3] + parts + [own])
    square = jax.ShapeDtypeStruct((C, C), BF16)
    both = jax.ShapeDtypeStruct((heads, C, 2 * C), BF16)
    added = jax.ShapeDtypeStruct((heads, C, C), F32)
    (state,) = small_call(group_state, [square], *parts)
    *maps, total = small_call(group_prefix, [both, added, jax.ShapeDtypeStruct((C, 2 * C), BF16)], *parts)
    if count == 2 * heads:
        lower = swap(state, "seq", heads)
        maps, lower = lax.optimization_barrier((maps, lower))
        keep, *sends = small_call(states_of_upper, [square] * heads, *maps, lower)
    else:
        keep, *sends = small_call(states_given, [square] * heads, *maps, prefix(total, heads))
    keep, q32 = lax.optimization_barrier((keep, q32))
    (rows2,) = row_maps(heads, 1, 1, q32, *first)
    (rows1,) = row_maps(heads, 2, 2, q32, *first)
    (rows0,) = row_maps(heads, 3, 0, q32, *own_maps_here)
    entering = [swap(sends[r - 1], "seq", r) for r in away] + [keep]
    rows = (rows3, rows2, rows1, rows0)
    groups = lax.axis_size("head")
    keep, send = apply(True, rows, entering, groups)
    across = (keep, swap(send, "head", 1), out_weight, weight2)
    keep, send = apply(False, rows, entering, groups)
    here = (keep, swap(send, "head", 1), out_weight, weight2)
    parts = 4
    width = out_weight.shape[1] // parts
    ranges = [(i * width, width) for i in range(parts)]
    theirs = [swap(project(BF16, *x, *across), "head", 2) for x in ranges]
    mine = [project(F32, *x, *here) for x in ranges]
    mixed = []
    for i in range(parts):
        mixed = [add_part(i, parts, mine[i], theirs[i], mixed)]
    return mixed[0]


def solution(mesh):
    in_specs = (
        P("seq", "head", None),
        P("seq", "head", None),
        P("seq", "head", None),
        P("head", "seq"),
        P("head", "seq"),
        P("head", None),
    )
    out_specs = P(("seq", "head"), None)
    return jax.shard_map(body, mesh=mesh, in_specs=in_specs, out_specs=out_specs, check_vma=False)
```

```python
import functools

import jax
import jax.numpy as jnp
from jax import lax
from jax.experimental import pallas as pl
from jax.experimental.pallas import tpu as pltpu
from jax.sharding import PartitionSpec as P

C = 128
B = 16
F32 = jnp.float32
BF16 = jnp.bfloat16
NN = (((1,), (0,)), ((), ()))
NT = (((1,), (1,)), ((), ()))
TN = (((0,), (0,)), ((), ()))
MIB = 1024 * 1024


def dot(a, b, dims=NN):
    return lax.dot_general(a, b, dims, preferred_element_type=F32)


def split(x):
    high = x.astype(BF16)
    return high, (x - high.astype(F32)).astype(BF16)


def twice(x):
    return jnp.concatenate([x, x], axis=0)


def dot3(a, b):
    (ah, al), (bh, bl) = a, b
    width = bh.shape[1]
    if width > C:
        return dot(jnp.concatenate([ah, al], axis=1), twice(bh)) + dot(ah, bl)
    both = dot(jnp.concatenate([ah, al], axis=1), twice(jnp.concatenate([bh, bl], axis=1)))
    return both[:, :width] + both[:, width:]


def iotas():
    return (
        lax.broadcasted_iota(jnp.int32, (C, C), 0),
        lax.broadcasted_iota(jnp.int32, (C, C), 1),
    )


def to_column(row, eye):
    return jnp.sum(jnp.where(eye, row, 0.0), axis=1, keepdims=True)


def to_row(column, eye):
    return jnp.sum(jnp.where(eye, column, 0.0), axis=0, keepdims=True)


def inverse_scale(rows):
    return lax.rsqrt(jnp.sum(rows * rows, axis=1, keepdims=True) + 1e-06)


def three(x):
    high, rest = x.astype(BF16), x
    rest = rest - high.astype(F32)
    return (high,) + split(rest)


def running_sums(rows, upper):
    return sum(dot(x, upper) for x in reversed(three(rows)))


def base_inverse(lower, row, col):
    on_block = (row // B) == (col // B)
    blocks = jnp.where(on_block, lower, 0.0)
    packed = sum(blocks[i * B : (i + 1) * B] for i in range(1, C // B)) + blocks[:B]
    r, c = row[:B], col[:B]
    found = jnp.where(r == c % B, 1.0, 0.0)
    first = (c // B) * B
    for j in range(B - 1):
        factor = jnp.take_along_axis(packed, first + j, axis=1)
        found = found - factor * found[j : j + 1]
    return jnp.where(on_block, jnp.concatenate([found] * (C // B), axis=0), 0.0)


def odd_rows(x, size):
    return jnp.concatenate([x[i : i + size] for i in range(size, C, 2 * size)], axis=0)


def weave(even, odd, size):
    parts = []
    for i in range(0, C // 2, size):
        parts += [even[i : i + size], odd[i : i + size]]
    return jnp.concatenate(parts, axis=0)


def even_rows(x, size):
    return jnp.concatenate([x[i : i + size] for i in range(0, C, 2 * size)], axis=0)


def inverses(lowers, row, col):
    found = [base_inverse(a, row, col) for a in lowers]
    parts = [split(a) for a in lowers]
    halves = [split(x) for x in found]
    size = B
    while size < C:
        r, c = odd_rows(row, size), odd_rows(col, size)
        mask = ((r // (2 * size)) == (c // (2 * size))) & ((r // size) != (c // size))
        nothing = jnp.zeros((C // 2, C), BF16)
        mask = jnp.where(mask, 1.0, 0.0).astype(BF16)
        joins = [tuple(odd_rows(x, size) * mask for x in part) for part in parts]
        middle = [split(dot3(a, x)) for a, x in zip(joins, halves)]
        middle = [tuple(weave(nothing, x, size) for x in part) for part in middle]
        lows = [dot3(tuple(odd_rows(x, size) for x in h), y) for h, y in zip(halves, middle)]
        lows = [odd_rows(x, size) - y for x, y in zip(found, lows)]
        found = [weave(even_rows(x, size), y, size) for x, y in zip(found, lows)]
        if 2 * size < C:
            halves = [
                tuple(weave(even_rows(x, size), y, size) for x, y in zip(h, split(low)))
                for h, low in zip(halves, lows)
            ]
        size *= 2
    return found


def in_hbm(*arrays):
    return [pltpu.with_memory_space_constraint(x, pltpu.HBM) for x in arrays]


def join(moved, added):
    return jnp.concatenate([moved, added], axis=1)


def after(later, earlier):
    total = dot3(split(later[:, :C]), split(earlier))
    return join(total[:, :C], total[:, C:] + later[:, C:])


def per_chunk(ref):
    return jnp.concatenate([ref[:, i : i + C] for i in range(0, ref.shape[1], C)], axis=0)


def chunk_rows(heads, head, c):
    return pl.ds(c * C * heads + head, C, stride=heads)


def places(heads):
    place = lax.rem(lax.axis_index("seq"), heads)
    return place, [lax.bitwise_xor(place, r) for r in range(heads - 1, -1, -1)]


def local_heads(heads, mine, k32, v32, sums_ref, betas_ref, mix_ref, wu_ref, n_ref):
    chunks = sums_ref.shape[0] // heads
    row, col = iotas()
    eye = row == col
    within = row >= col
    strict = row > col
    eye16 = jnp.where(eye, 1.0, 0.0).astype(BF16)
    jobs = [(head, c) for head in mine for c in range(chunks)]
    sums = jnp.concatenate([sums_ref[pl.ds(head, chunks, stride=heads), :] for head in mine], axis=0)
    betas = jnp.concatenate([betas_ref[pl.ds(head, chunks, stride=heads), :] for head in mine], axis=0)
    filled = jnp.concatenate([sums, jnp.zeros((C - sums.shape[0], C), F32)], axis=0)
    columns = filled.T
    grown = jnp.exp(sums)
    faded = jnp.exp(sums[:, C - 1 :] - sums)
    lowers, raws, values, fades, lengths = [], [], [], [], []
    for i, (head, c) in enumerate(jobs):
        at = slice(i, i + 1)
        raw = k32[chunk_rows(heads, head, c), :].astype(BF16)
        raws.append(raw)
        values.append(v32[chunk_rows(heads, head, c), :].astype(BF16))
        both = dot(jnp.concatenate([raw, eye16], axis=0), raw, NT)
        gram, turned = both[:C], both[C:]
        square = to_row(gram, eye) + 1e-06
        scale = lax.rsqrt(square)
        lengths.append(square * scale)
        strength = betas[at] * (scale * scale)
        mix = jnp.where(within, jnp.exp(columns[:, at] - sums[at]), 0.0) * strength
        mix_ref[i] = mix
        lowers.append(jnp.where(strict, gram * mix, 0.0))
        fades.append(turned * (strength * faded[at]))
    solved = []
    for i, found in enumerate(inverses(lowers, row, col)):
        at = slice(i, i + 1)
        kept = dot(jnp.concatenate(split(found * grown[at]), axis=1), twice(raws[i]))
        fresh = dot(jnp.concatenate(split(found * lengths[i]), axis=1), twice(values[i]))
        solved.append(join(kept, fresh))
    maps = []
    for i in range(len(jobs)):
        wu_ref[i] = solved[i]
        both = dot3(split(fades[i]), split(solved[i]))
        maps.append(join(jnp.where(eye, grown[i : i + 1, C - 1 :], 0.0) - both[:, :C], both[:, C:]))
    totals = []
    for j in range(len(mine)):
        first, second, third, last = maps[j * chunks : (j + 1) * chunks]
        early = after(second, first)
        n_ref[j * chunks + 1] = first
        n_ref[j * chunks + 2] = early
        n_ref[j * chunks + 3] = after(third, early)
        totals.append(after(after(last, third), early))
    return totals


def first_kernel(
    heads, k_hbm, v_hbm, beta_hbm, log_hbm, q_hbm, q16, k32, v32, sums_ref, betas_ref, mix_ref, wu_ref, n_ref, *refs
):
    sends, (k16, v16, beta_ref, log_ref, sems) = refs[: heads - 1], refs[heads - 1 :]
    pairs = ((log_hbm, log_ref), (beta_hbm, beta_ref), (k_hbm, k16), (v_hbm, v16), (q_hbm, q16))
    copies = [pltpu.make_async_copy(x, y, sems.at[i]) for i, (x, y) in enumerate(pairs)]
    *early, late = copies
    for copy in early:
        copy.start()
    for copy in early[:2]:
        copy.wait()
    row, col = iotas()
    sums_ref[...] = running_sums(per_chunk(log_ref), jnp.where(row <= col, 1.0, 0.0).astype(BF16))
    betas_ref[...] = per_chunk(beta_ref)
    early[2].wait()
    k32[...] = k16[...].astype(F32)
    early[3].wait()
    late.start()
    v32[...] = v16[...].astype(F32)
    mine = places(heads)[1][: heads - 1]
    totals = local_heads(heads, mine, k32, v32, sums_ref, betas_ref, mix_ref, wu_ref, n_ref)
    for send, total in zip(sends, totals):
        send[...] = total.astype(BF16)
    late.wait()


def maps_shapes(heads, chunks):
    return [
        jax.ShapeDtypeStruct((heads * chunks, C, C), F32),
        jax.ShapeDtypeStruct((heads * chunks, C, 2 * C), F32),
        jax.ShapeDtypeStruct((heads * chunks, C, 2 * C), F32),
    ] + [jax.ShapeDtypeStruct((C, 2 * C), BF16)] * heads


def first_maps(key, value, beta, log_decay, query):
    heads, tokens = beta.shape
    chunks = tokens // C
    here = pl.BlockSpec(memory_space=pltpu.VMEM)
    rows = jax.ShapeDtypeStruct((chunks * heads, C), F32)
    wide = jax.ShapeDtypeStruct(key.shape, F32)
    out_shape = [jax.ShapeDtypeStruct(query.shape, BF16), wide, wide, rows, rows] + maps_shapes(heads - 1, chunks)
    return pl.pallas_call(
        functools.partial(first_kernel, heads),
        in_specs=[pl.BlockSpec(memory_space=pltpu.HBM)] * 5,
        out_specs=[here] * len(out_shape),
        out_shape=out_shape,
        scratch_shapes=[
            pltpu.VMEM(key.shape, BF16),
            pltpu.VMEM(key.shape, BF16),
            pltpu.VMEM(beta.shape, F32),
            pltpu.VMEM(beta.shape, F32),
            pltpu.SemaphoreType.DMA((5,)),
        ],
        compiler_params=pltpu.CompilerParams(vmem_limit_bytes=32 * MIB),
        name="first_maps",
    )(*in_hbm(key, value, beta, log_decay, query))


def own_kernel(heads, k32, v32, sums_ref, betas_ref, mix_ref, wu_ref, n_ref, own_ref):
    mine = places(heads)[1][heads - 1 :]
    (total,) = local_heads(heads, mine, k32, v32, sums_ref, betas_ref, mix_ref, wu_ref, n_ref)
    own_ref[...] = total.astype(BF16)


def own_maps(heads, k32, v32, sums, betas):
    here = pl.BlockSpec(memory_space=pltpu.VMEM)
    out_shape = maps_shapes(1, sums.shape[0] // heads)
    return pl.pallas_call(
        functools.partial(own_kernel, heads),
        in_specs=[here] * 4,
        out_specs=[here] * len(out_shape),
        out_shape=out_shape,
        compiler_params=pltpu.CompilerParams(vmem_limit_bytes=16 * MIB),
        cost_estimate=pl.CostEstimate(flops=2000000000, bytes_accessed=8000000, transcendentals=0),
        name="own_maps",
    )(k32, v32, sums, betas)


def rows_kernel(heads, spot, slot, q_ref, k32, sums_ref, mix_ref, wu_ref, n_ref, out_ref, *wide):
    if wide:
        wide[0][...] = q_ref[...].astype(F32)
    q32 = wide[0] if wide else q_ref
    chunks = sums_ref.shape[0] // heads
    row, col = iotas()
    eye = row == col
    head = places(heads)[1][spot]
    grown = jnp.exp(sums_ref[pl.ds(head, chunks, stride=heads), :])
    for c in range(chunks):
        i = slot * chunks + c
        query, raw = q32[chunk_rows(heads, head, c), :], k32[chunk_rows(heads, head, c), :]
        pairs = dot(query.astype(BF16), raw.astype(BF16), NT) * mix_ref[i]
        both = dot3(split(pairs), split(wu_ref[i]))
        scale = inverse_scale(query)
        reach = (query * to_column(grown[c : c + 1], eye) - both[:, :C]) * scale
        fresh = both[:, C:] * scale
        if c > 0:
            earlier = dot3(split(reach), split(n_ref[i]))
            reach = earlier[:, :C]
            fresh = fresh + earlier[:, C:]
        out_ref[c * C : (c + 1) * C, :] = join(reach, fresh)


def row_maps(heads, spot, slot, query, *maps):
    tokens = query.shape[0] // heads
    here = pl.BlockSpec(memory_space=pltpu.VMEM)
    out_shape = [jax.ShapeDtypeStruct((tokens, 2 * C), F32)]
    if query.dtype == BF16:
        out_shape.append(jax.ShapeDtypeStruct(query.shape, F32))
    return pl.pallas_call(
        functools.partial(rows_kernel, heads, spot, slot),
        in_specs=[here] * (1 + len(maps)),
        out_specs=[here] * len(out_shape),
        out_shape=out_shape,
        compiler_params=pltpu.CompilerParams(vmem_limit_bytes=16 * MIB),
        cost_estimate=pl.CostEstimate(flops=1000000000, bytes_accessed=4000000, transcendentals=0),
        name="row_maps",
    )(query, *maps)


def small_call(kernel, out_shape, *args):
    here = pl.BlockSpec(memory_space=pltpu.VMEM)
    return pl.pallas_call(
        kernel,
        in_specs=[here] * len(args),
        out_specs=[here] * len(out_shape),
        out_shape=out_shape,
        compiler_params=pltpu.CompilerParams(vmem_limit_bytes=8 * MIB),
        name=kernel.__name__,
    )(*args)


def moved_on(maps, state16, added):
    high, low = split(maps)
    return dot(jnp.concatenate([high, low], axis=1), twice(state16)) + added


def times_parts(maps16, x):
    width = x.shape[1]
    both = dot(maps16, jnp.concatenate(split(x), axis=1))
    return both[:, :width] + both[:, width:]


def by_place(parts, work):
    heads = len(parts)
    place = places(heads)[0]
    for p in range(heads):

        @pl.when(place == p)
        def _(p=p):
            members = [i ^ p for i in range(heads)]
            work([parts[heads - 1 - r] for r in members], members)


def group_state(*refs):
    out_ref = refs[-1]

    def work(parts, _):
        first, second, third, last = parts
        state = dot(second[:, :C], first[:, C:]) + second[:, C:].astype(F32)
        both = dot(last[:, :C], third[...])
        state = dot3(split(both[:, :C]), split(state)) + (both[:, C:] + last[:, C:].astype(F32))
        out_ref[...] = state.astype(BF16)

    by_place(refs[:-1], work)


def group_prefix(*refs):
    parts, (maps_ref, added_ref, total_ref) = refs[:-3], refs[-3:]
    row, col = iotas()

    def work(parts, members):
        total = join(jnp.where(row == col, 1.0, 0.0), jnp.zeros((C, C), F32))
        for i, (part, r) in enumerate(zip(parts, members)):
            maps_ref[r] = jnp.concatenate(split(total[:, :C]), axis=1)
            added_ref[r] = total[:, C:]
            if i == 0:
                total = part[...].astype(F32)
            else:
                total = times_parts(part[:, :C], total)
                total = join(total[:, :C], total[:, C:] + part[:, C:].astype(F32))
        total_ref[...] = total.astype(BF16)

    by_place(parts, work)


def group_states(upper_only, maps_ref, added_ref, state_ref, *outs):
    state = state_ref[...]
    if upper_only:
        state = jnp.where(lax.axis_index("seq") < len(outs), jnp.zeros_like(state), state)
    both = twice(state)
    for r, out_ref in enumerate(outs):
        out_ref[...] = (dot(maps_ref[r], both) + added_ref[r]).astype(BF16)


def states_of_upper(*refs):
    group_states(True, *refs)


def states_given(*refs):
    group_states(False, *refs)


def prefix(total, heads):
    count = lax.axis_size("seq")
    groups = [list(range(i, count, heads)) for i in range(heads)]
    me = lax.axis_index("seq") // heads
    totals = lax.all_gather(total, "seq", axis_index_groups=groups)

    def step(d, state):
        longer = jnp.einsum("ik,pkw->iw", totals[d, :, :C], jnp.stack(split(state)), preferred_element_type=F32)
        return jnp.where(d < me, longer + totals[d, :, C:].astype(F32), state)

    start = jnp.zeros((C, C), F32)
    return lax.fori_loop(0, count // heads - 1, step, start).astype(BF16)


def apply_kernel(groups, other, *refs):
    heads = (len(refs) - 2) // 2
    rows_refs, states, (keep_ref, send_ref) = refs[:heads], refs[heads : 2 * heads], refs[2 * heads :]
    block = rows_refs[0].shape[0] // groups
    order = places(heads)[1]
    member = lax.axis_index("head")
    pair, core = member // 2, lax.rem(member, 2)
    pair = 1 - pair if other else pair
    for out_ref, parity in ((send_ref, 1 - core), (keep_ref, core)):
        rows = pl.ds(pl.multiple_of((2 * pair + parity) * block, block), block)
        for head, rows_ref, state in zip(order, rows_refs, states):
            attended = moved_on(rows_ref[rows, :C], state[...], rows_ref[rows, C:])
            out_ref[:, pl.ds(pl.multiple_of(head * C, C), C)] = attended.astype(BF16)


def apply(other, rows, states, groups):
    heads = len(states)
    here = pl.BlockSpec(memory_space=pltpu.VMEM)
    out = jax.ShapeDtypeStruct((rows[0].shape[0] // groups, heads * C), BF16)
    return pl.pallas_call(
        functools.partial(apply_kernel, groups, other),
        in_specs=[here] * (2 * heads),
        out_specs=[here] * 2,
        out_shape=[out, out],
        compiler_params=pltpu.CompilerParams(vmem_limit_bytes=8 * MIB),
        cost_estimate=pl.CostEstimate(flops=200000000, bytes_accessed=1000000, transcendentals=0),
        name="apply",
    )(*rows, *states)


def project_kernel(start, keep_ref, got_ref, w_ref, w2_ref, out_ref):
    columns = slice(start, start + out_ref.shape[1])
    shares = dot(keep_ref[...], w_ref[:, columns]) + dot(got_ref[...], w2_ref[:, columns])
    out_ref[...] = shares.astype(out_ref.dtype)


def project(dtype, start, width, keep, got, weight, weight2):
    block, depth = keep.shape
    return pl.pallas_call(
        functools.partial(project_kernel, start),
        out_shape=jax.ShapeDtypeStruct((block, width), dtype),
        compiler_params=pltpu.CompilerParams(vmem_limit_bytes=20 * MIB),
        cost_estimate=pl.CostEstimate(
            flops=4 * block * depth * width, bytes_accessed=4 * depth * width, transcendentals=0
        ),
        name="project",
    )(keep, got, weight, weight2)


def add_kernel(mine_ref, theirs_ref, *refs):
    refs[-1][...] = (mine_ref[...] + theirs_ref[...].astype(F32)).astype(BF16)


def add_part(index, parts, mine, theirs, earlier):
    block, width = mine.shape
    here = pl.BlockSpec(memory_space=pltpu.VMEM)
    return pl.pallas_call(
        add_kernel,
        grid=(1,),
        in_specs=[here, here] + [pl.BlockSpec(memory_space=pl.ANY)] * len(earlier),
        out_specs=pl.BlockSpec((block, width), lambda i: (0, index)),
        out_shape=jax.ShapeDtypeStruct((block, width * parts), BF16),
        input_output_aliases={2: 0} if earlier else {},
        compiler_params=pltpu.CompilerParams(vmem_limit_bytes=8 * MIB),
        name="add_part",
    )(mine, theirs, *earlier)


def swap(x, axis, bit):
    count = lax.axis_size(axis)
    return lax.ppermute(x, axis, [(i, i ^ bit) for i in range(count)])


def body(query, key, value, beta, log_decay, out_weight):
    tokens, heads, _ = key.shape
    count = lax.axis_size("seq")
    flat = lambda x: x.reshape(tokens * heads, C)
    weight2 = swap(out_weight, "head", 1)
    q16, k32, v32, sums, betas, mix, wu, states, *sends = first_maps(
        flat(key), flat(value), beta, log_decay, flat(query)
    )
    away = range(heads - 1, 0, -1)
    parts = [swap(x, "seq", r) for r, x in zip(away, sends)]
    *own_chunks, own = own_maps(heads, k32, v32, sums, betas)
    first = (k32, sums, mix, wu, states)
    own_maps_here = (k32, sums, *own_chunks)
    rows3, q32 = row_maps(heads, 0, 0, q16, *first)
    rows3, *parts = lax.optimization_barrier([rows3] + parts + [own])
    square = jax.ShapeDtypeStruct((C, C), BF16)
    both = jax.ShapeDtypeStruct((heads, C, 2 * C), BF16)
    added = jax.ShapeDtypeStruct((heads, C, C), F32)
    (state,) = small_call(group_state, [square], *parts)
    state, q32 = lax.optimization_barrier((state, q32))
    (rows2,) = row_maps(heads, 1, 1, q32, *first)
    *maps, total = small_call(group_prefix, [both, added, jax.ShapeDtypeStruct((C, 2 * C), BF16)], *parts)
    if count == 2 * heads:
        lower = swap(state, "seq", heads)
        rows2, maps, lower = lax.optimization_barrier((rows2, maps, lower))
        keep, *sends = small_call(states_of_upper, [square] * heads, *maps, lower)
    else:
        keep, *sends = small_call(states_given, [square] * heads, *maps, prefix(total, heads))
    keep, q32 = lax.optimization_barrier((keep, q32))
    (rows1,) = row_maps(heads, 2, 2, q32, *first)
    (rows0,) = row_maps(heads, 3, 0, q32, *own_maps_here)
    entering = [swap(sends[r - 1], "seq", r) for r in away] + [keep]
    rows = (rows3, rows2, rows1, rows0)
    groups = lax.axis_size("head")
    keep, send = apply(True, rows, entering, groups)
    across = (keep, swap(send, "head", 1), out_weight, weight2)
    keep, send = apply(False, rows, entering, groups)
    here = (keep, swap(send, "head", 1), out_weight, weight2)
    parts = 4
    width = out_weight.shape[1] // parts
    ranges = [(i * width, width) for i in range(parts)]
    theirs = [swap(project(BF16, *x, *across), "head", 2) for x in ranges]
    mine = [project(F32, *x, *here) for x in ranges]
    mixed = []
    for i in range(parts):
        mixed = [add_part(i, parts, mine[i], theirs[i], mixed)]
    return mixed[0]


def solution(mesh):
    in_specs = (
        P("seq", "head", None),
        P("seq", "head", None),
        P("seq", "head", None),
        P("head", "seq"),
        P("head", "seq"),
        P("head", None),
    )
    out_specs = P(("seq", "head"), None)
    return jax.shard_map(body, mesh=mesh, in_specs=in_specs, out_specs=out_specs, check_vma=False)
```

```python
import functools

import jax
import jax.numpy as jnp
from jax import lax
from jax.experimental import pallas as pl
from jax.experimental.pallas import tpu as pltpu
from jax.sharding import PartitionSpec as P

C = 128
B = 16
F32 = jnp.float32
BF16 = jnp.bfloat16
NN = (((1,), (0,)), ((), ()))
NT = (((1,), (1,)), ((), ()))
TN = (((0,), (0,)), ((), ()))
MIB = 1024 * 1024


def dot(a, b, dims=NN):
    return lax.dot_general(a, b, dims, preferred_element_type=F32)


def split(x):
    high = x.astype(BF16)
    return high, (x - high.astype(F32)).astype(BF16)


def twice(x):
    return jnp.concatenate([x, x], axis=0)


def dot3(a, b):
    (ah, al), (bh, bl) = a, b
    width = bh.shape[1]
    if width > C:
        return dot(jnp.concatenate([ah, al], axis=1), twice(bh)) + dot(ah, bl)
    rows = ah.shape[0]
    both = dot(jnp.concatenate([ah, al], axis=0), jnp.concatenate([bh, bl], axis=1))
    return both[:rows, :width] + (both[:rows, width:] + both[rows:, :width])


def iotas():
    return (
        lax.broadcasted_iota(jnp.int32, (C, C), 0),
        lax.broadcasted_iota(jnp.int32, (C, C), 1),
    )


def to_column(row, eye):
    return jnp.sum(jnp.where(eye, row, 0.0), axis=1, keepdims=True)


def to_row(column, eye):
    return jnp.sum(jnp.where(eye, column, 0.0), axis=0, keepdims=True)


def inverse_scale(rows):
    return lax.rsqrt(jnp.sum(rows * rows, axis=1, keepdims=True) + 1e-06)


def three(x):
    high, rest = x.astype(BF16), x
    rest = rest - high.astype(F32)
    return (high,) + split(rest)


def running_sums(rows, upper):
    return sum(dot(x, upper) for x in reversed(three(rows)))


def base_inverse(lower, row, col):
    on_block = (row // B) == (col // B)
    blocks = jnp.where(on_block, lower, 0.0)
    packed = sum(blocks[i * B : (i + 1) * B] for i in range(1, C // B)) + blocks[:B]
    r, c = row[:B], col[:B]
    found = jnp.where(r == c % B, 1.0, 0.0)
    first = (c // B) * B
    for j in range(B - 1):
        factor = jnp.take_along_axis(packed, first + j, axis=1)
        found = found - factor * found[j : j + 1]
    return jnp.where(on_block, jnp.concatenate([found] * (C // B), axis=0), 0.0)


def odd_rows(x, size):
    return jnp.concatenate([x[i : i + size] for i in range(size, C, 2 * size)], axis=0)


def weave(even, odd, size):
    parts = []
    for i in range(0, C // 2, size):
        parts += [even[i : i + size], odd[i : i + size]]
    return jnp.concatenate(parts, axis=0)


def even_rows(x, size):
    return jnp.concatenate([x[i : i + size] for i in range(0, C, 2 * size)], axis=0)


def inverses(lowers, row, col):
    found = [base_inverse(a, row, col) for a in lowers]
    parts = [split(a) for a in lowers]
    halves = [split(x) for x in found]
    size = B
    while size < C:
        r, c = odd_rows(row, size), odd_rows(col, size)
        mask = ((r // (2 * size)) == (c // (2 * size))) & ((r // size) != (c // size))
        nothing = jnp.zeros((C // 2, C), BF16)
        mask = jnp.where(mask, 1.0, 0.0).astype(BF16)
        joins = [tuple(odd_rows(x, size) * mask for x in part) for part in parts]
        middle = [split(dot3(a, x)) for a, x in zip(joins, halves)]
        middle = [tuple(weave(nothing, x, size) for x in part) for part in middle]
        lows = [dot3(tuple(odd_rows(x, size) for x in h), y) for h, y in zip(halves, middle)]
        lows = [odd_rows(x, size) - y for x, y in zip(found, lows)]
        found = [weave(even_rows(x, size), y, size) for x, y in zip(found, lows)]
        if 2 * size < C:
            halves = [
                tuple(weave(even_rows(x, size), y, size) for x, y in zip(h, split(low)))
                for h, low in zip(halves, lows)
            ]
        size *= 2
    return found


def in_hbm(*arrays):
    return [pltpu.with_memory_space_constraint(x, pltpu.HBM) for x in arrays]


def join(moved, added):
    return jnp.concatenate([moved, added], axis=1)


def after(later, earlier):
    total = dot3(split(later[:, :C]), split(earlier))
    return join(total[:, :C], total[:, C:] + later[:, C:])


def per_chunk(ref):
    return jnp.concatenate([ref[:, i : i + C] for i in range(0, ref.shape[1], C)], axis=0)


def chunk_rows(heads, head, c):
    return pl.ds(c * C * heads + head, C, stride=heads)


def places(heads):
    place = lax.rem(lax.axis_index("seq"), heads)
    return place, [lax.bitwise_xor(place, r) for r in range(heads - 1, -1, -1)]


def local_heads(heads, mine, k32, v32, sums_ref, betas_ref, mix_ref, wu_ref, n_ref):
    chunks = sums_ref.shape[0] // heads
    row, col = iotas()
    eye = row == col
    within = row >= col
    strict = row > col
    eye16 = jnp.where(eye, 1.0, 0.0).astype(BF16)
    jobs = [(head, c) for head in mine for c in range(chunks)]
    sums = jnp.concatenate([sums_ref[pl.ds(head, chunks, stride=heads), :] for head in mine], axis=0)
    betas = jnp.concatenate([betas_ref[pl.ds(head, chunks, stride=heads), :] for head in mine], axis=0)
    filled = jnp.concatenate([sums, jnp.zeros((C - sums.shape[0], C), F32)], axis=0)
    columns = filled.T
    grown = jnp.exp(sums)
    faded = jnp.exp(sums[:, C - 1 :] - sums)
    lowers, raws, values, fades, lengths = [], [], [], [], []
    for i, (head, c) in enumerate(jobs):
        at = slice(i, i + 1)
        raw = k32[chunk_rows(heads, head, c), :].astype(BF16)
        raws.append(raw)
        values.append(v32[chunk_rows(heads, head, c), :].astype(BF16))
        both = dot(jnp.concatenate([raw, eye16], axis=0), raw, NT)
        gram, turned = both[:C], both[C:]
        square = to_row(gram, eye) + 1e-06
        scale = lax.rsqrt(square)
        lengths.append(square * scale)
        strength = betas[at] * (scale * scale)
        mix = jnp.where(within, jnp.exp(columns[:, at] - sums[at]), 0.0) * strength
        mix_ref[i] = mix
        lowers.append(jnp.where(strict, gram * mix, 0.0))
        fades.append(turned * (strength * faded[at]))
    solved = []
    for i, found in enumerate(inverses(lowers, row, col)):
        at = slice(i, i + 1)
        kept = dot(jnp.concatenate(split(found * grown[at]), axis=1), twice(raws[i]))
        fresh = dot(jnp.concatenate(split(found * lengths[i]), axis=1), twice(values[i]))
        solved.append(join(kept, fresh))
    maps = []
    for i in range(len(jobs)):
        wu_ref[i] = solved[i]
        both = dot3(split(fades[i]), split(solved[i]))
        maps.append(join(jnp.where(eye, grown[i : i + 1, C - 1 :], 0.0) - both[:, :C], both[:, C:]))
    totals = []
    for j in range(len(mine)):
        first, second, third, last = maps[j * chunks : (j + 1) * chunks]
        early = after(second, first)
        n_ref[j * chunks + 1] = first
        n_ref[j * chunks + 2] = early
        n_ref[j * chunks + 3] = after(third, early)
        totals.append(after(after(last, third), early))
    return totals


def first_kernel(
    heads, k_hbm, v_hbm, beta_hbm, log_hbm, q_hbm, q16, k32, v32, sums_ref, betas_ref, mix_ref, wu_ref, n_ref, *refs
):
    sends, (k16, v16, beta_ref, log_ref, sems) = refs[: heads - 1], refs[heads - 1 :]
    pairs = ((log_hbm, log_ref), (beta_hbm, beta_ref), (k_hbm, k16), (v_hbm, v16), (q_hbm, q16))
    copies = [pltpu.make_async_copy(x, y, sems.at[i]) for i, (x, y) in enumerate(pairs)]
    *early, late = copies
    for copy in early:
        copy.start()
    for copy in early[:2]:
        copy.wait()
    row, col = iotas()
    sums_ref[...] = running_sums(per_chunk(log_ref), jnp.where(row <= col, 1.0, 0.0).astype(BF16))
    betas_ref[...] = per_chunk(beta_ref)
    early[2].wait()
    k32[...] = k16[...].astype(F32)
    early[3].wait()
    late.start()
    v32[...] = v16[...].astype(F32)
    mine = places(heads)[1][: heads - 1]
    totals = local_heads(heads, mine, k32, v32, sums_ref, betas_ref, mix_ref, wu_ref, n_ref)
    for send, total in zip(sends, totals):
        send[...] = total.astype(BF16)
    late.wait()


def maps_shapes(heads, chunks):
    return [
        jax.ShapeDtypeStruct((heads * chunks, C, C), F32),
        jax.ShapeDtypeStruct((heads * chunks, C, 2 * C), F32),
        jax.ShapeDtypeStruct((heads * chunks, C, 2 * C), F32),
    ] + [jax.ShapeDtypeStruct((C, 2 * C), BF16)] * heads


def first_maps(key, value, beta, log_decay, query):
    heads, tokens = beta.shape
    chunks = tokens // C
    here = pl.BlockSpec(memory_space=pltpu.VMEM)
    rows = jax.ShapeDtypeStruct((chunks * heads, C), F32)
    wide = jax.ShapeDtypeStruct(key.shape, F32)
    out_shape = [jax.ShapeDtypeStruct(query.shape, BF16), wide, wide, rows, rows] + maps_shapes(heads - 1, chunks)
    return pl.pallas_call(
        functools.partial(first_kernel, heads),
        in_specs=[pl.BlockSpec(memory_space=pltpu.HBM)] * 5,
        out_specs=[here] * len(out_shape),
        out_shape=out_shape,
        scratch_shapes=[
            pltpu.VMEM(key.shape, BF16),
            pltpu.VMEM(key.shape, BF16),
            pltpu.VMEM(beta.shape, F32),
            pltpu.VMEM(beta.shape, F32),
            pltpu.SemaphoreType.DMA((5,)),
        ],
        compiler_params=pltpu.CompilerParams(vmem_limit_bytes=32 * MIB),
        name="first_maps",
    )(*in_hbm(key, value, beta, log_decay, query))


def own_kernel(heads, k32, v32, sums_ref, betas_ref, mix_ref, wu_ref, n_ref, own_ref):
    mine = places(heads)[1][heads - 1 :]
    (total,) = local_heads(heads, mine, k32, v32, sums_ref, betas_ref, mix_ref, wu_ref, n_ref)
    own_ref[...] = total.astype(BF16)


def own_maps(heads, k32, v32, sums, betas):
    here = pl.BlockSpec(memory_space=pltpu.VMEM)
    out_shape = maps_shapes(1, sums.shape[0] // heads)
    return pl.pallas_call(
        functools.partial(own_kernel, heads),
        in_specs=[here] * 4,
        out_specs=[here] * len(out_shape),
        out_shape=out_shape,
        compiler_params=pltpu.CompilerParams(vmem_limit_bytes=16 * MIB),
        cost_estimate=pl.CostEstimate(flops=2000000000, bytes_accessed=8000000, transcendentals=0),
        name="own_maps",
    )(k32, v32, sums, betas)


def rows_kernel(heads, spot, slot, q_ref, k32, sums_ref, mix_ref, wu_ref, n_ref, out_ref, *wide):
    if wide:
        wide[0][...] = q_ref[...].astype(F32)
    q32 = wide[0] if wide else q_ref
    chunks = sums_ref.shape[0] // heads
    row, col = iotas()
    eye = row == col
    head = places(heads)[1][spot]
    grown = jnp.exp(sums_ref[pl.ds(head, chunks, stride=heads), :])
    for c in range(chunks):
        i = slot * chunks + c
        query, raw = q32[chunk_rows(heads, head, c), :], k32[chunk_rows(heads, head, c), :]
        pairs = dot(query.astype(BF16), raw.astype(BF16), NT) * mix_ref[i]
        both = dot3(split(pairs), split(wu_ref[i]))
        scale = inverse_scale(query)
        reach = (query * to_column(grown[c : c + 1], eye) - both[:, :C]) * scale
        fresh = both[:, C:] * scale
        if c > 0:
            earlier = dot3(split(reach), split(n_ref[i]))
            reach = earlier[:, :C]
            fresh = fresh + earlier[:, C:]
        out_ref[c * C : (c + 1) * C, :] = join(reach, fresh)


def row_maps(heads, spot, slot, query, *maps):
    tokens = query.shape[0] // heads
    here = pl.BlockSpec(memory_space=pltpu.VMEM)
    out_shape = [jax.ShapeDtypeStruct((tokens, 2 * C), F32)]
    if query.dtype == BF16:
        out_shape.append(jax.ShapeDtypeStruct(query.shape, F32))
    return pl.pallas_call(
        functools.partial(rows_kernel, heads, spot, slot),
        in_specs=[here] * (1 + len(maps)),
        out_specs=[here] * len(out_shape),
        out_shape=out_shape,
        compiler_params=pltpu.CompilerParams(vmem_limit_bytes=16 * MIB),
        cost_estimate=pl.CostEstimate(flops=1000000000, bytes_accessed=4000000, transcendentals=0),
        name="row_maps",
    )(query, *maps)


def small_call(kernel, out_shape, *args):
    here = pl.BlockSpec(memory_space=pltpu.VMEM)
    return pl.pallas_call(
        kernel,
        in_specs=[here] * len(args),
        out_specs=[here] * len(out_shape),
        out_shape=out_shape,
        compiler_params=pltpu.CompilerParams(vmem_limit_bytes=8 * MIB),
        name=kernel.__name__,
    )(*args)


def moved_on(maps, state16, added):
    high, low = split(maps)
    return dot(jnp.concatenate([high, low], axis=1), twice(state16)) + added


def times_parts(maps16, x):
    width = x.shape[1]
    both = dot(maps16, jnp.concatenate(split(x), axis=1))
    return both[:, :width] + both[:, width:]


def by_place(parts, work):
    heads = len(parts)
    place = places(heads)[0]
    for p in range(heads):

        @pl.when(place == p)
        def _(p=p):
            members = [i ^ p for i in range(heads)]
            work([parts[heads - 1 - r] for r in members], members)


def group_state(*refs):
    out_ref = refs[-1]

    def work(parts, _):
        first, second, third, last = parts
        state = dot(second[:, :C], first[:, C:]) + second[:, C:].astype(F32)
        both = dot(last[:, :C], third[...])
        state = dot3(split(both[:, :C]), split(state)) + (both[:, C:] + last[:, C:].astype(F32))
        out_ref[...] = state.astype(BF16)

    by_place(refs[:-1], work)


def group_prefix(*refs):
    parts, (maps_ref, added_ref, total_ref) = refs[:-3], refs[-3:]
    row, col = iotas()

    def work(parts, members):
        total = join(jnp.where(row == col, 1.0, 0.0), jnp.zeros((C, C), F32))
        for i, (part, r) in enumerate(zip(parts, members)):
            maps_ref[r] = jnp.concatenate(split(total[:, :C]), axis=1)
            added_ref[r] = total[:, C:]
            if i == 0:
                total = part[...].astype(F32)
            else:
                total = times_parts(part[:, :C], total)
                total = join(total[:, :C], total[:, C:] + part[:, C:].astype(F32))
        total_ref[...] = total.astype(BF16)

    by_place(parts, work)


def group_states(upper_only, maps_ref, added_ref, state_ref, *outs):
    state = state_ref[...]
    if upper_only:
        state = jnp.where(lax.axis_index("seq") < len(outs), jnp.zeros_like(state), state)
    both = twice(state)
    for r, out_ref in enumerate(outs):
        out_ref[...] = (dot(maps_ref[r], both) + added_ref[r]).astype(BF16)


def states_of_upper(*refs):
    group_states(True, *refs)


def states_given(*refs):
    group_states(False, *refs)


def prefix(total, heads):
    count = lax.axis_size("seq")
    groups = [list(range(i, count, heads)) for i in range(heads)]
    me = lax.axis_index("seq") // heads
    totals = lax.all_gather(total, "seq", axis_index_groups=groups)

    def step(d, state):
        longer = jnp.einsum("ik,pkw->iw", totals[d, :, :C], jnp.stack(split(state)), preferred_element_type=F32)
        return jnp.where(d < me, longer + totals[d, :, C:].astype(F32), state)

    start = jnp.zeros((C, C), F32)
    return lax.fori_loop(0, count // heads - 1, step, start).astype(BF16)


def apply_kernel(groups, other, *refs):
    heads = (len(refs) - 2) // 2
    rows_refs, states, (keep_ref, send_ref) = refs[:heads], refs[heads : 2 * heads], refs[2 * heads :]
    block = rows_refs[0].shape[0] // groups
    order = places(heads)[1]
    member = lax.axis_index("head")
    pair, core = member // 2, lax.rem(member, 2)
    pair = 1 - pair if other else pair
    for out_ref, parity in ((send_ref, 1 - core), (keep_ref, core)):
        rows = pl.ds(pl.multiple_of((2 * pair + parity) * block, block), block)
        for head, rows_ref, state in zip(order, rows_refs, states):
            attended = moved_on(rows_ref[rows, :C], state[...], rows_ref[rows, C:])
            out_ref[:, pl.ds(pl.multiple_of(head * C, C), C)] = attended.astype(BF16)


def apply(other, rows, states, groups):
    heads = len(states)
    here = pl.BlockSpec(memory_space=pltpu.VMEM)
    out = jax.ShapeDtypeStruct((rows[0].shape[0] // groups, heads * C), BF16)
    return pl.pallas_call(
        functools.partial(apply_kernel, groups, other),
        in_specs=[here] * (2 * heads),
        out_specs=[here] * 2,
        out_shape=[out, out],
        compiler_params=pltpu.CompilerParams(vmem_limit_bytes=8 * MIB),
        cost_estimate=pl.CostEstimate(flops=200000000, bytes_accessed=1000000, transcendentals=0),
        name="apply",
    )(*rows, *states)


def project_kernel(start, keep_ref, got_ref, w_ref, w2_ref, out_ref):
    columns = slice(start, start + out_ref.shape[1])
    shares = dot(keep_ref[...], w_ref[:, columns]) + dot(got_ref[...], w2_ref[:, columns])
    out_ref[...] = shares.astype(out_ref.dtype)


def project(dtype, start, width, keep, got, weight, weight2):
    block, depth = keep.shape
    return pl.pallas_call(
        functools.partial(project_kernel, start),
        out_shape=jax.ShapeDtypeStruct((block, width), dtype),
        compiler_params=pltpu.CompilerParams(vmem_limit_bytes=20 * MIB),
        cost_estimate=pl.CostEstimate(
            flops=4 * block * depth * width, bytes_accessed=4 * depth * width, transcendentals=0
        ),
        name="project",
    )(keep, got, weight, weight2)


def add_kernel(mine_ref, theirs_ref, *refs):
    refs[-1][...] = (mine_ref[...] + theirs_ref[...].astype(F32)).astype(BF16)


def add_part(index, parts, mine, theirs, earlier):
    block, width = mine.shape
    here = pl.BlockSpec(memory_space=pltpu.VMEM)
    return pl.pallas_call(
        add_kernel,
        grid=(1,),
        in_specs=[here, here] + [pl.BlockSpec(memory_space=pl.ANY)] * len(earlier),
        out_specs=pl.BlockSpec((block, width), lambda i: (0, index)),
        out_shape=jax.ShapeDtypeStruct((block, width * parts), BF16),
        input_output_aliases={2: 0} if earlier else {},
        compiler_params=pltpu.CompilerParams(vmem_limit_bytes=8 * MIB),
        name="add_part",
    )(mine, theirs, *earlier)


def swap(x, axis, bit):
    count = lax.axis_size(axis)
    return lax.ppermute(x, axis, [(i, i ^ bit) for i in range(count)])


def body(query, key, value, beta, log_decay, out_weight):
    tokens, heads, _ = key.shape
    count = lax.axis_size("seq")
    flat = lambda x: x.reshape(tokens * heads, C)
    q16, k32, v32, sums, betas, mix, wu, states, *sends = first_maps(
        flat(key), flat(value), beta, log_decay, flat(query)
    )
    away = range(heads - 1, 0, -1)
    parts = [swap(x, "seq", r) for r, x in zip(away, sends)]
    *own_chunks, own = own_maps(heads, k32, v32, sums, betas)
    first = (k32, sums, mix, wu, states)
    own_maps_here = (k32, sums, *own_chunks)
    rows3, q32 = row_maps(heads, 0, 0, q16, *first)
    rows3, *parts = lax.optimization_barrier([rows3] + parts + [own])
    square = jax.ShapeDtypeStruct((C, C), BF16)
    both = jax.ShapeDtypeStruct((heads, C, 2 * C), BF16)
    added = jax.ShapeDtypeStruct((heads, C, C), F32)
    (state,) = small_call(group_state, [square], *parts)
    state, q32, sent_weight = lax.optimization_barrier((state, q32, out_weight))
    weight2 = swap(sent_weight, "head", 1)
    (rows2,) = row_maps(heads, 1, 1, q32, *first)
    *maps, total = small_call(group_prefix, [both, added, jax.ShapeDtypeStruct((C, 2 * C), BF16)], *parts)
    if count == 2 * heads:
        lower = swap(state, "seq", heads)
        rows2, maps, lower = lax.optimization_barrier((rows2, maps, lower))
        keep, *sends = small_call(states_of_upper, [square] * heads, *maps, lower)
    else:
        keep, *sends = small_call(states_given, [square] * heads, *maps, prefix(total, heads))
    keep, q32 = lax.optimization_barrier((keep, q32))
    (rows1,) = row_maps(heads, 2, 2, q32, *first)
    (rows0,) = row_maps(heads, 3, 0, q32, *own_maps_here)
    entering = [swap(sends[r - 1], "seq", r) for r in away] + [keep]
    rows = (rows3, rows2, rows1, rows0)
    groups = lax.axis_size("head")
    keep, send = apply(True, rows, entering, groups)
    across = (keep, swap(send, "head", 1), out_weight, weight2)
    keep, send = apply(False, rows, entering, groups)
    here = (keep, swap(send, "head", 1), out_weight, weight2)
    parts = 4
    width = out_weight.shape[1] // parts
    ranges = [(i * width, width) for i in range(parts)]
    theirs = [swap(project(BF16, *x, *across), "head", 2) for x in ranges]
    mine = [project(F32, *x, *here) for x in ranges]
    mixed = []
    for i in range(parts):
        mixed = [add_part(i, parts, mine[i], theirs[i], mixed)]
    return mixed[0]


def solution(mesh):
    in_specs = (
        P("seq", "head", None),
        P("seq", "head", None),
        P("seq", "head", None),
        P("head", "seq"),
        P("head", "seq"),
        P("head", None),
    )
    out_specs = P(("seq", "head"), None)
    return jax.shard_map(body, mesh=mesh, in_specs=in_specs, out_specs=out_specs, check_vma=False)
```
